32 devices in a mesh: seq: 16 (over z, y, x), head: 2 (over core).
Axes of the slice: x: 2, y: 2, z: 4, core: 2. Of those that a mesh axis runs over, the one named last changes fastest.
Arguments:
- tokens: bfloat16 [2, 2048, 512], P(None, 'seq'), may hold values from -6 to 6
- cotangent: bfloat16 [2, 2048, 512], P(None, 'seq'), may hold values from -6 to 6
- lengths: int32 [2, 1], replicated, may hold values from 2048 to 2048, as said below
- order: int32 [2, 32], replicated, may hold values from 0 to 31, as said below
- mix_gain: float32 [512], replicated, may hold values from 0.5 to 1.5
- in_value: bfloat16 [512, 1024], P('seq', 'head'), may hold values from -0.25 to 0.25
- in_gate: bfloat16 [512, 1024], P('seq', 'head'), may hold values from -0.25 to 0.25
- in_state: bfloat16 [512, 64], P('seq', 'head'), may hold values from -0.25 to 0.25
- in_rate: bfloat16 [512, 16], P('seq', 'head'), may hold values from -0.25 to 0.25
- rate_bias: float32 [16], P('head'), may hold values from -8 to -2
- decay_log: float32 [16], P('head'), may hold values from -0.7 to 0.7
- conv_taps: float32 [4, 1024], P(None, 'head'), may hold values from -3 to 3
- conv_bias: float32 [1024], P('head'), may hold values from -0.5 to 0.5
- skip_gain: float32 [1024], P('head'), may hold values from 0.5 to 1.5
- mix_out: bfloat16 [1024, 512], P('head', 'seq'), may hold values from -0.1875 to 0.1875
- att_gain: float32 [512], replicated, may hold values from 0.5 to 1.5
- qkv_proj: bfloat16 [512, 3, 512], P('seq', None, 'head'), may hold values from -0.25 to 0.25
- att_out: bfloat16 [512, 512], P('head', 'seq'), may hold values from -12 to 12
- mlp_gain: float32 [512], replicated, may hold values from 0.5 to 1.5
- mlp_up: bfloat16 [512, 2048], P('seq', 'head'), may hold values from -0.25 to 0.25
- mlp_down: bfloat16 [2048, 512], P('head', 'seq'), may hold values from -0.125 to 0.125
Outputs:
- layer_out: bfloat16 [2, 2048, 512], P(None, 'seq')
- tokens_grad: bfloat16 [2, 2048, 512], P(None, 'seq')
- mixgain_grad: float32 [512], replicated
- invalue_grad: float32 [512, 1024], P('seq', 'head')
- ingate_grad: float32 [512, 1024], P('seq', 'head')
- instate_grad: float32 [512, 64], P('seq', 'head')
- inrate_grad: float32 [512, 16], P('seq', 'head')
- ratebias_grad: float32 [16], P('head')
- decaylog_grad: float32 [16], P('head')
- convtaps_grad: float32 [4, 1024], P(None, 'head')
- convbias_grad: float32 [1024], P('head')
- skipgain_grad: float32 [1024], P('head')
- mixout_grad: float32 [1024, 512], P('head', 'seq')
- attgain_grad: float32 [512], replicated
- qkvproj_grad: float32 [512, 3, 512], P('seq', None, 'head')
- attout_grad: float32 [512, 512], P('head', 'seq')
- mlpgain_grad: float32 [512], replicated
- mlpup_grad: float32 [512, 2048], P('seq', 'head')
- mlpdown_grad: float32 [2048, 512], P('head', 'seq')
The draws below stay inside these ranges and needn't reach their ends.
Inputs may be any that keep to these rules, and one draw needn't show every extreme that they name: Row b holds the lengths of the 1 sequence packed in micro-batch b, in stream order; they sum to 2048, and one of them is exactly 2048. `order`: row b is a permutation of the 32 stream blocks. One sequence of each micro-batch has places in the blocks held at positions 0, 16 and 31 of row b.
All inputs are finite; a program needn't handle non-finite values.
Results may differ from the reference program's by a relative error of at most 0.04.
Values may be sent and summed in bfloat16 or wider, within the bound.
No kernel may reach another device: no remote copies, remote signals or barrier semaphores. Data moves between devices by JAX's collectives and lax.ppermute only.
A program may use at most 256 MiB of HBM per device.

```python
import functools
import math
import jax
import jax.numpy as jnp
from jax import lax

D = 512
DI = 1024
NSTATE = 16
MHEAD_DIM = 64
MHEADS = 16
GROUPS = 2
CONV = 4
AHEADS = 8
AHEAD_DIM = 64
FF = 2048
TOK_DEV = 128
MB = 2
MIN_LEN = 4096
TOKENS = 2048
SEQS = 1
LONGEST = 2048
BLOCKS = 32


def place_block(shuffled, target_slot, wanted):
    slot_table = jnp.arange(BLOCKS, dtype=jnp.int32)
    found = jnp.sum(jnp.where(shuffled == wanted, slot_table, 0))
    current = jnp.sum(jnp.where(slot_table == target_slot, shuffled, 0))
    return jnp.where(slot_table == target_slot, wanted, jnp.where(slot_table == found, current, shuffled)).astype(jnp.int32)


def deal_plan(key, batch_index):
    key = jax.random.fold_in(key, batch_index)
    half_rows = TOK_DEV // 2
    long_at = jax.random.randint(jax.random.fold_in(key, 1), (), 0, SEQS)
    slot_ids = jnp.arange(SEQS, dtype=jnp.int32)
    if SEQS > 1:
        others = SEQS - 1
        spare_rows = TOKENS - LONGEST - others * MIN_LEN
        even_share = spare_rows // others
        leftover = spare_rows - even_share * others
        other_ids = jnp.arange(others, dtype=jnp.int32)
        extras = even_share + (other_ids < leftover).astype(jnp.int32)
        pair_count = others // 2
        shifts = jax.random.randint(jax.random.fold_in(key, 2), (pair_count,), 0, even_share + 1).astype(jnp.int32)
        signed = jnp.concatenate([jnp.stack([shifts, -shifts], axis=1).reshape(-1), jnp.zeros((others - 2 * pair_count,), jnp.int32)])
        remaining = jnp.concatenate([MIN_LEN + extras + signed, jnp.zeros((1,), jnp.int32)])
        seq_lengths = jnp.where(slot_ids < long_at, remaining[slot_ids], jnp.where(slot_ids == long_at, LONGEST, remaining[jnp.maximum(slot_ids - 1, 0)]))
    else:
        seq_lengths = jnp.full((1,), LONGEST, jnp.int32)
    seq_lengths = seq_lengths.astype(jnp.int32)
    starts = jnp.cumsum(seq_lengths) - seq_lengths
    long_start = jnp.sum(jnp.where(slot_ids == long_at, starts, 0))
    first_block = long_start // half_rows
    last_block = (long_start + LONGEST - 1) // half_rows
    middle_block = (first_block + last_block) // 2
    shuffled = jax.random.permutation(jax.random.fold_in(key, 3), BLOCKS).astype(jnp.int32)
    shuffled = place_block(shuffled, 0, first_block)
    shuffled = place_block(shuffled, BLOCKS // 2, middle_block)
    shuffled = place_block(shuffled, BLOCKS - 1, last_block)
    return (seq_lengths, shuffled)


def draw_lengths(key, part):
    plans = [deal_plan(key, batch_index) for batch_index in range(MB)]
    return jnp.stack([plan[0] for plan in plans]).astype(jnp.int32)


def draw_order(key, part):
    plans = [deal_plan(key, batch_index) for batch_index in range(MB)]
    return jnp.stack([plan[1] for plan in plans]).astype(jnp.int32)


def block_scale(stream_key, extent, shards, smallest, largest):
    def one(dim, shards_of):
        draws = jax.random.uniform(jax.random.fold_in(jax.random.fold_in(stream_key, 6), dim), (shards_of,), jnp.float32, smallest / len(shards), largest / len(shards))
        return jnp.repeat(jnp.exp(draws), extent[dim] // shards_of).reshape((-1,) + (1,) * (len(extent) - dim - 1))

    loudness = one(*shards[0])
    for cut in shards[1:]:
        loudness = loudness * one(*cut)
    return loudness


def gaussian(key, dims, scale, most, shards=(), kind=jnp.bfloat16):
    entries = jax.random.normal(key, dims, jnp.float32) * scale
    if len(shards) > 0:
        entries = block_scale(key, dims, shards, -0.22, 0.18) * entries
    return jnp.clip(entries, min=-most, max=most).astype(kind)


def setup_inputs(seed: int = 0) -> dict:
    streams_of = jax.random.split(jax.random.key(seed), 22)
    return {
        "tokens": gaussian(streams_of[0], (MB, TOKENS, D), 1.0, 6.0, ((1, 16),)),
        "cotangent": gaussian(streams_of[1], (MB, TOKENS, D), 1.0, 6.0, ((1, 16),)),
        "lengths": draw_lengths(jax.random.fold_in(streams_of[21], 71), 0),
        "order": draw_order(jax.random.fold_in(streams_of[21], 71), 0),
        "mix_gain": jnp.clip(1.0 + 0.1 * jax.random.normal(streams_of[4], (D,), jnp.float32), 0.5, 1.5),
        "in_value": gaussian(streams_of[5], (D, DI), D ** -0.5, 0.25, ((0, 16), (1, 2))),
        "in_gate": gaussian(streams_of[6], (D, DI), D ** -0.5, 0.25, ((0, 16), (1, 2))),
        "in_state": gaussian(streams_of[7], (D, GROUPS * 2 * NSTATE), D ** -0.5, 0.25, ((0, 16), (1, 2))),
        "in_rate": gaussian(streams_of[8], (D, MHEADS), D ** -0.5, 0.25, ((0, 16), (1, 2))),
        "rate_bias": jnp.clip(-8.0 + 6.0 * jax.random.uniform(streams_of[9], (MHEADS,), jnp.float32) ** block_scale(streams_of[9], (MHEADS,), ((0, 2),), -0.2, 0.2), -8.0, -2.0),
        "decay_log": jnp.clip(jax.random.uniform(streams_of[10], (MHEADS,), jnp.float32, -0.7, 0.7) * block_scale(streams_of[10], (MHEADS,), ((0, 2),), -0.4, 0.0), -0.7, 0.7),
        "conv_taps": gaussian(streams_of[11], (CONV, DI), CONV ** -0.5, 3.0, ((1, 2),), jnp.float32),
        "conv_bias": jnp.clip(jax.random.uniform(streams_of[12], (DI,), jnp.float32, -0.5, 0.5) * block_scale(streams_of[12], (DI,), ((0, 2),), -0.4, 0.0), -0.5, 0.5),
        "skip_gain": jnp.clip(0.5 + 1.0 * jax.random.uniform(streams_of[13], (DI,), jnp.float32) ** block_scale(streams_of[13], (DI,), ((0, 2),), -0.2, 0.2), 0.5, 1.5),
        "mix_out": gaussian(streams_of[14], (DI, D), DI ** -0.5, 0.1875, ((0, 2), (1, 16))),
        "att_gain": jnp.clip(1.0 + 0.1 * jax.random.normal(streams_of[15], (D,), jnp.float32), 0.5, 1.5),
        "qkv_proj": gaussian(streams_of[16], (D, 3, D), D ** -0.5, 0.25, ((0, 16), (2, 2))),
        "att_out": gaussian(streams_of[17], (D, D), 2.0, 12.0, ((0, 2), (1, 16))),
        "mlp_gain": jnp.clip(1.0 + 0.1 * jax.random.normal(streams_of[18], (D,), jnp.float32), 0.5, 1.5),
        "mlp_up": gaussian(streams_of[19], (D, FF), D ** -0.5, 0.25, ((0, 16), (1, 2))),
        "mlp_down": gaussian(streams_of[20], (FF, D), FF ** -0.5, 0.125, ((0, 2), (1, 16))),
    }


@jax.custom_vjp
def low(v):
    return lax.optimization_barrier(v.astype(jnp.bfloat16)).astype(jnp.float32)

@jax.custom_vjp
def low_back(v):
    return v

def low_keep(v):
    return (low(v), None)

def low_pass(kept, grad):
    return (grad,)

def back_keep(v):
    return (v, None)

def back_low(kept, grad):
    return (low(grad),)
low.defvjp(low_keep, low_pass)
low_back.defvjp(back_keep, back_low)
epsilon = 1e-05
highest = lax.Precision.HIGHEST

def product(left_op, right_op):
    return jnp.dot(left_op, right_op, preferred_element_type=jnp.float32, precision=highest)

def rms_norm(values, gain_row):
    return values * lax.rsqrt(lax.optimization_barrier(jnp.mean(values * values, axis=-1, keepdims=True)) + epsilon) * gain_row

def segment_of(position, seq_ends):
    bounds = seq_ends[:-1]
    return lax.optimization_barrier(jnp.sum((jnp.asarray(position)[..., None] >= bounds).astype(jnp.int32), axis=-1)).astype(jnp.int32)

def scan_block(states, inputs):
    driving_in, step_in, b_rows, c_rows, log_rates, segment, seg_before = inputs
    length = segment.shape[0]
    row_ids = jnp.arange(length, dtype=jnp.int32)
    cumulative = jnp.cumsum(log_rates, axis=0)
    allowed = ((row_ids[:, None] >= row_ids[None, :]) & (segment[:, None] == segment[None, :]))[:, :, None]
    decays = jnp.where(allowed, jnp.exp(jnp.where(allowed, cumulative[:, None, :] - cumulative[None, :, :], 0.0)), 0.0)
    inner_cb = jnp.einsum('thn,shn->tsh', c_rows, b_rows, precision=highest)
    driving = step_in[:, :, None] * driving_in
    output = jnp.einsum('tsh,shp->thp', decays * inner_cb, driving, precision=highest)
    inflow = jnp.exp(cumulative) * (segment == seg_before).astype(jnp.float32)[:, None]
    output = output + inflow[:, :, None] * jnp.einsum('thn,hpn->thp', c_rows, states, precision=highest)
    tail_weight = jnp.exp(cumulative[-1][None, :] - cumulative) * (segment == segment[-1]).astype(jnp.float32)[:, None]
    local_state = jnp.einsum('sh,shp,shn->hpn', tail_weight, driving, b_rows, precision=highest)
    through = jnp.exp(cumulative[-1]) * (segment[-1] == seg_before).astype(jnp.float32)
    return (through[:, None, None] * states + local_state, output)

def whole_layer(hidden, mix_gain, in_value, in_gate, in_state, in_rate, rate_bias, decay_log, conv_taps, conv_bias, skip_gain, mix_out, att_gain, qkv_proj, att_out, mlp_gain, mlp_up, mlp_down, seq_ends=None):
    count_rows = hidden.shape[0]
    position = jnp.arange(count_rows, dtype=jnp.int32)
    segment = segment_of(position, seq_ends)
    normed_one = low(rms_norm(hidden, mix_gain))
    x_in = low_back(low(product(normed_one, in_value)))
    gate_in = low_back(product(normed_one, in_gate))
    bc_rows = product(normed_one, in_state).reshape(count_rows, GROUPS, 2, NSTATE)
    rate_in = product(normed_one, in_rate)
    step_size = jax.nn.softplus(rate_in + rate_bias)
    padded = jnp.concatenate([jnp.zeros((CONV - 1, DI), jnp.float32), x_in], axis=0)
    conv_sum = jnp.zeros((count_rows, DI), jnp.float32) + conv_bias
    for tap_index in range(CONV):
        source = position - (CONV - 1 - tap_index)
        valid_tap = ((source >= 0) & (segment_of(source, seq_ends) == segment)).astype(jnp.float32)
        conv_sum = conv_sum + conv_taps[tap_index] * padded[tap_index:tap_index + count_rows] * valid_tap[:, None]
    mixed_x = jax.nn.silu(conv_sum)
    per_group = MHEADS // GROUPS
    b_heads = jnp.repeat(bc_rows[:, :, 0, :], per_group, axis=1)
    c_heads = jnp.repeat(bc_rows[:, :, 1, :], per_group, axis=1)
    log_decay = -step_size * jnp.exp(decay_log)
    blocks_n = count_rows // TOK_DEV

    def blocked(values):
        return values.reshape((blocks_n, TOK_DEV) + values.shape[1:])
    seg_before = segment_of(jnp.arange(blocks_n, dtype=jnp.int32) * TOK_DEV - 1, seq_ends)
    inputs = (blocked(mixed_x.reshape(count_rows, MHEADS, MHEAD_DIM)), blocked(step_size), blocked(b_heads), blocked(c_heads), blocked(log_decay), blocked(segment), seg_before)
    initial = jnp.zeros((MHEADS, MHEAD_DIM, NSTATE), jnp.float32)
    final_state, mixer_y = lax.scan(jax.checkpoint(scan_block), initial, inputs)
    mixer_y = mixer_y.reshape(count_rows, DI) + skip_gain * mixed_x
    gated_low = low(mixer_y * jax.nn.silu(gate_in))
    hidden_one = hidden + low_back(product(gated_low, mix_out))
    normed_two = low(rms_norm(hidden_one, att_gain))
    qkv_rows = product(normed_two, qkv_proj.reshape(D, 3 * D)).reshape(count_rows, 3, AHEADS, AHEAD_DIM)
    queries = low_back(low(qkv_rows[:, 0]))
    key_heads = low_back(low(qkv_rows[:, 1]))
    value_heads = low_back(low(qkv_rows[:, 2]))
    scaling = AHEAD_DIM ** (-0.5)
    query_block = math.gcd(count_rows, 512)
    blocks_q = count_rows // query_block

    def attend(inputs_q):
        query_rows, query_pos, query_seg = inputs_q
        scores = low_back(jnp.einsum('qhd,khd->qhk', query_rows, key_heads, precision=highest) * scaling)
        allowed = ((position[None, :] <= query_pos[:, None]) & (segment[None, :] == query_seg[:, None]))[:, None, :]
        scores = jnp.where(allowed, scores, -jnp.inf)
        weights = jnp.exp(scores - lax.optimization_barrier(jnp.max(scores, axis=-1, keepdims=True)))
        weights = low(weights / lax.optimization_barrier(jnp.sum(weights, axis=-1, keepdims=True)))
        return jnp.einsum('qhk,khd->qhd', weights, value_heads, precision=highest)
    attended = lax.map(jax.checkpoint(attend), (queries.reshape(blocks_q, query_block, AHEADS, AHEAD_DIM), position.reshape(blocks_q, query_block), segment.reshape(blocks_q, query_block)))
    attended = low_back(low(attended.reshape(count_rows, D)))
    hidden_two = hidden_one + low_back(product(attended, att_out))
    normed_three = low(rms_norm(hidden_two, mlp_gain))
    up_rows = low_back(product(normed_three, mlp_up))
    activated = low(jax.nn.gelu(up_rows, approximate=True))
    return hidden_two + product(activated, mlp_down)

def to_stream(rows, picks):
    return rows.reshape(BLOCKS, TOKENS // BLOCKS, D)[picks].reshape(TOKENS, D)

def reference(tokens, cotangent, lengths, order, mix_gain, in_value, in_gate, in_state, in_rate, rate_bias, decay_log, conv_taps, conv_bias, skip_gain, mix_out, att_gain, qkv_proj, att_out, mlp_gain, mlp_up, mlp_down):
    weights = tuple((member.astype(jnp.float32) for member in (mix_gain, in_value, in_gate, in_state, in_rate, rate_bias, decay_log, conv_taps, conv_bias, skip_gain, mix_out, att_gain, qkv_proj, att_out, mlp_gain, mlp_up, mlp_down)))
    outputs = []
    input_grads = []
    running = [jnp.zeros(member.shape, jnp.float32) for member in weights]
    for batch_index in range(MB):
        seq_ends = jnp.cumsum(lengths[batch_index]).astype(jnp.int32)
        order_row = order[batch_index].astype(jnp.int32)
        source_slot = jnp.argsort(order_row).astype(jnp.int32)
        layer_call = functools.partial(whole_layer, seq_ends=seq_ends)
        stream_in = to_stream(tokens[batch_index].astype(jnp.float32), source_slot)
        stream_cot = to_stream(cotangent[batch_index].astype(jnp.float32), source_slot)
        result, pullback = jax.vjp(layer_call, stream_in, *weights)
        gradients = pullback(stream_cot)
        outputs.append(to_stream(result, order_row).astype(jnp.bfloat16))
        input_grads.append(to_stream(gradients[0], order_row).astype(jnp.bfloat16))
        running = [summed + part_grad for summed, part_grad in zip(running, gradients[1:])]
    return (jnp.stack(outputs), jnp.stack(input_grads), running[0], running[1], running[2], running[3], running[4], running[5], running[6], running[7], running[8], running[9], running[10], running[11], running[12], running[13], running[14], running[15], running[16])
```

```python
import math

import jax
import jax.numpy as jnp
from jax import lax
from jax.experimental import pallas as pl
from jax.experimental.pallas import tpu as pltpu
from jax.sharding import PartitionSpec as P

NSTATE = 16
CONV = 4
AHEAD_DIM = 64


epsilon = 1e-05
highest = lax.Precision.HIGHEST


def rms_norm(values, gain_row):
    return (
        values * lax.rsqrt(jnp.mean(values * values, axis=-1, keepdims=True) + epsilon) * gain_row
    )


def gelu_tanh(values):
    return jax.nn.gelu(values, approximate=True)


def segment_of(position, seq_ends):
    bounds = seq_ends[:-1]
    return jnp.sum((jnp.asarray(position)[..., None] >= bounds).astype(jnp.int32), axis=-1)


def tap_valid(position, lag_rows, seq_ends):
    source = position - lag_rows
    return (
        (source >= 0) & (segment_of(source, seq_ends) == segment_of(position, seq_ends))
    ).astype(jnp.float32)


def slot_position(order_row, row_ids, half_rows):
    slot = row_ids // half_rows
    slot_table = jnp.arange(order_row.shape[0], dtype=jnp.int32)
    block = jnp.sum(jnp.where(slot[:, None] == slot_table[None, :], order_row[None, :], 0), axis=1)
    return block * half_rows + row_ids % half_rows


def stream_slots(order_row):
    slot_table = jnp.arange(order_row.shape[0], dtype=jnp.int32)
    return jnp.sum(
        jnp.where(order_row[None, :] == slot_table[:, None], slot_table[None, :], 0), axis=1
    )


def matmul(left_op, right_op):
    return jnp.dot(left_op, right_op, preferred_element_type=jnp.float32)


def transposed(left_op, right_op):
    return lax.dot_general(
        left_op, right_op, (((1,), (1,)), ((), ())), preferred_element_type=jnp.float32
    )


def left_gram(left_op, right_op):
    return lax.dot_general(
        left_op, right_op, (((0,), (0,)), ((), ())), preferred_element_type=jnp.float32
    )


def transposed_exact(left_op, right_op):
    return lax.dot_general(
        left_op,
        right_op,
        (((1,), (1,)), ((), ())),
        preferred_element_type=jnp.float32,
        precision=highest,
    )


def left_gram_exact(left_op, right_op):
    return lax.dot_general(
        left_op,
        right_op,
        (((0,), (0,)), ((), ())),
        preferred_element_type=jnp.float32,
        precision=highest,
    )


def keep_same(current):
    return current


def head_total(partial_rows):
    return lax.psum(partial_rows, "head")


def collect(in_value, in_gate, in_state, in_rate, qkv_proj, mlp_up, mix_out, att_out, mlp_down):
    return (
        lax.all_gather(in_value, "seq", axis=0, tiled=True),
        lax.all_gather(in_gate, "seq", axis=0, tiled=True),
        lax.all_gather(in_state, "seq", axis=0, tiled=True),
        lax.all_gather(in_rate, "seq", axis=0, tiled=True),
        lax.all_gather(qkv_proj, "seq", axis=0, tiled=True),
        lax.all_gather(mlp_up, "seq", axis=0, tiled=True),
        lax.all_gather(mix_out, "seq", axis=1, tiled=True),
        lax.all_gather(att_out, "seq", axis=1, tiled=True),
        lax.all_gather(mlp_down, "seq", axis=1, tiled=True),
    )


def reduce_grads(grad_parts):
    return (
        lax.psum_scatter(grad_parts[0], "seq", scatter_dimension=0, tiled=True),
        lax.psum_scatter(grad_parts[1], "seq", scatter_dimension=0, tiled=True),
        lax.psum_scatter(grad_parts[2], "seq", scatter_dimension=0, tiled=True),
        lax.psum_scatter(grad_parts[3], "seq", scatter_dimension=0, tiled=True),
        lax.psum_scatter(grad_parts[4], "seq", scatter_dimension=0, tiled=True),
        lax.psum_scatter(grad_parts[5], "seq", scatter_dimension=0, tiled=True),
        lax.psum_scatter(grad_parts[6], "seq", scatter_dimension=1, tiled=True),
        lax.psum_scatter(grad_parts[7], "seq", scatter_dimension=1, tiled=True),
        lax.psum_scatter(grad_parts[8], "seq", scatter_dimension=1, tiled=True),
    )


def fold_blocks(fold_fn, initial, arrays, block_rows):
    blocks_n = arrays[0].shape[0] // block_rows

    def one_step(block_index, current):
        offset = block_index * block_rows
        shards = tuple(
            (lax.dynamic_slice_in_dim(member, offset, block_rows, 0) for member in arrays)
        )
        return fold_fn(current, shards, offset)

    return lax.fori_loop(0, blocks_n, one_step, initial)


def add_parts(left_op, right_op):
    if left_op is None:
        return right_op
    return tuple((first_part + second_part for first_part, second_part in zip(left_op, right_op)))


def combine_state(earlier, later):
    return (earlier[0] * later[0], later[0][..., None, None] * earlier[1] + later[1])


def attention_probs(
    query_rows, key_rows, query_pos, key_pos, query_seg, key_seg, log_total, scaling
):
    allowed = ((key_pos[None, :] <= query_pos[:, None]) & (key_seg[None, :] == query_seg[:, None]))[
        :, None, :
    ]
    scores = (
        jnp.einsum("qhd,khd->qhk", query_rows, key_rows, preferred_element_type=jnp.float32)
        * scaling
    )
    return jnp.where(allowed, jnp.exp(jnp.where(allowed, scores - log_total[:, :, None], 0.0)), 0.0)


def scan_terms(mixed_x, step_size, bc_rows, decay_log, segment, seg_before):
    rows_n, heads_n = step_size.shape
    log_decay = -step_size * jnp.exp(decay_log)
    cumulative = jnp.cumsum(log_decay, axis=0)
    driving = step_size[:, :, None] * mixed_x.reshape(rows_n, heads_n, -1)
    tail_weight = (
        jnp.exp(cumulative[-1][None, :] - cumulative)
        * (segment == segment[-1]).astype(jnp.float32)[:, None]
    )
    local_state = jnp.einsum(
        "sh,shp,sn->hpn", tail_weight, driving, bc_rows[:, :NSTATE], precision=highest
    )
    through = jnp.exp(cumulative[-1]) * (segment[-1] == seg_before).astype(jnp.float32)
    return (cumulative, driving, through, local_state)


def scan_output(cumulative, driving, bc_rows, incoming, segment, seg_before):
    rows_n = cumulative.shape[0]
    row_ids = jnp.arange(rows_n, dtype=jnp.int32)
    allowed = ((row_ids[:, None] >= row_ids[None, :]) & (segment[:, None] == segment[None, :]))[
        :, :, None
    ]
    decays = jnp.where(
        allowed,
        jnp.exp(jnp.where(allowed, cumulative[:, None, :] - cumulative[None, :, :], 0.0)),
        0.0,
    )
    inner_cb = jnp.dot(bc_rows[:, NSTATE:], bc_rows[:, :NSTATE].T, precision=highest)
    output = jnp.einsum("tsh,shp->thp", decays * inner_cb[:, :, None], driving, precision=highest)
    inflow = jnp.exp(cumulative) * (segment == seg_before).astype(jnp.float32)[:, None]
    output = output + inflow[:, :, None] * jnp.einsum(
        "tn,hpn->thp", bc_rows[:, NSTATE:], incoming, precision=highest
    )
    return output.reshape(rows_n, -1)


def scan_whole(mixed_x, step_size, bc_rows, decay_log, incoming, segment, seg_before):
    cumulative, driving, through, local_state = scan_terms(
        mixed_x, step_size, bc_rows, decay_log, segment, seg_before
    )
    output = scan_output(cumulative, driving, bc_rows, incoming, segment, seg_before)
    return (output, through[:, None, None] * incoming + local_state)


def on_device(
    tokens,
    cotangent,
    lengths,
    order,
    mix_gain,
    in_value,
    in_gate,
    in_state,
    in_rate,
    rate_bias,
    decay_log,
    conv_taps,
    conv_bias,
    skip_gain,
    mix_out,
    att_gain,
    qkv_proj,
    att_out,
    mlp_gain,
    mlp_up,
    mlp_down,
):
    rows_n = tokens.shape[1]
    half_rows = rows_n // 2
    slots_n = 2 * lax.axis_size("seq")
    my_slot = 2 * lax.axis_index("seq")
    total_rows = rows_n * lax.axis_size("seq")
    block_rows = math.gcd(total_rows, 1024)
    scaling = AHEAD_DIM ** (-0.5)
    local_ids = jnp.arange(half_rows, dtype=jnp.int32)
    ext_ids = jnp.arange(half_rows + CONV - 1, dtype=jnp.int32)
    terms_all = jax.vmap(scan_terms, in_axes=(0, 0, 0, None, 0, 0))
    output_all = jax.vmap(scan_output, in_axes=(0, 0, 0, 0, 0, 0))
    whole_all = jax.vmap(scan_whole, in_axes=(0, 0, 0, None, 0, 0, 0))
    layer_list = []
    input_list = []
    big_sums = None
    small_sums = None
    for batch_index in range(tokens.shape[0]):
        (
            value_full,
            gate_full,
            state_full,
            rate_full,
            qkv_full,
            up_full,
            mixout_full,
            attout_full,
            down_full,
        ) = collect(
            in_value, in_gate, in_state, in_rate, qkv_proj, mlp_up, mix_out, att_out, mlp_down
        )
        seq_ends = jnp.cumsum(lengths[batch_index])
        order_row = order[batch_index]
        inverse = stream_slots(order_row)
        my_blocks = lax.dynamic_slice_in_dim(order_row, my_slot, 2)
        position = (my_blocks[:, None] * half_rows + local_ids[None, :]).reshape(rows_n)
        segment = segment_of(position, seq_ends)
        seg_blocks = segment.reshape(2, half_rows)
        seg_before = segment_of(my_blocks * half_rows - 1, seq_ends)
        hidden_in = tokens[batch_index].astype(jnp.float32)
        normed_one = rms_norm(hidden_in, mix_gain).astype(jnp.bfloat16)
        x_in = matmul(normed_one, value_full).astype(jnp.bfloat16)
        gate_in = matmul(normed_one, gate_full)
        bc_rows = matmul(normed_one, state_full)
        rate_in = matmul(normed_one, rate_full)
        step_size = jax.nn.softplus(rate_in + rate_bias)
        x_blocks = x_in.reshape(2, half_rows, -1)
        all_tails = lax.all_gather(x_blocks[:, half_rows - (CONV - 1) :], "seq", axis=0, tiled=True)
        pick_prev = (order_row[None, :] == my_blocks[:, None] - 1).astype(jnp.bfloat16)
        edge_rows = jnp.einsum(
            "bs,srd->brd", pick_prev, all_tails, preferred_element_type=jnp.float32
        )
        extended = jnp.concatenate([edge_rows, x_blocks.astype(jnp.float32)], axis=1)
        valid_taps = [
            tap_valid(position, CONV - 1 - tap_index, seq_ends).reshape(2, half_rows)
            for tap_index in range(CONV)
        ]
        conv_blocks = jnp.zeros(x_blocks.shape, jnp.float32) + conv_bias
        for tap_index in range(CONV):
            conv_blocks = (
                conv_blocks
                + conv_taps[tap_index]
                * extended[:, tap_index : tap_index + half_rows]
                * valid_taps[tap_index][:, :, None]
            )
        conv_sum = conv_blocks.reshape(rows_n, -1)
        mixed_x = jax.nn.silu(conv_sum)
        mixed_b = mixed_x.reshape(2, half_rows, -1)
        step_b = step_size.reshape(2, half_rows, -1)
        bc_b = bc_rows.reshape(2, half_rows, -1)
        cumulative, driving, through, local_state = terms_all(
            mixed_b, step_b, bc_b, decay_log, seg_blocks, seg_before
        )
        all_through, all_state = (
            lax.all_gather(through, "seq", axis=0, tiled=True),
            lax.all_gather(local_state, "seq", axis=0, tiled=True),
        )
        through_stream = all_through[inverse]
        state_stream = all_state[inverse]
        acc_through, acc_state = lax.associative_scan(
            combine_state, (through_stream, state_stream), axis=0
        )
        before = my_blocks - 1
        incoming = (
            acc_state[jnp.maximum(before, 0)]
            * (before >= 0).astype(jnp.float32)[:, None, None, None]
        )
        ssm_out = output_all(cumulative, driving, bc_b, incoming, seg_blocks, seg_before).reshape(
            rows_n, -1
        )
        full_y = ssm_out + skip_gain * mixed_x
        gating = jax.nn.silu(gate_in)
        gated_low = (full_y * gating).astype(jnp.bfloat16)
        hidden_one = hidden_in + head_total(matmul(gated_low, mixout_full))
        normed_two = rms_norm(hidden_one, att_gain).astype(jnp.bfloat16)
        qkv_rows = jnp.einsum(
            "rd,dcn->rcn", normed_two, qkv_full, preferred_element_type=jnp.float32
        ).astype(jnp.bfloat16)
        heads_att = qkv_rows.shape[2] // AHEAD_DIM
        queries = qkv_rows[:, 0].reshape(rows_n, heads_att, AHEAD_DIM)
        key_heads = qkv_rows[:, 1].reshape(rows_n, heads_att, AHEAD_DIM)
        value_heads = qkv_rows[:, 2].reshape(rows_n, heads_att, AHEAD_DIM)

        def forward_fold(totals, shards, offset):
            key_rows, value_rows = shards
            key_pos = slot_position(
                order_row, offset + jnp.arange(key_rows.shape[0], dtype=jnp.int32), half_rows
            )
            allowed = (
                (key_pos[None, :] <= position[:, None])
                & (segment_of(key_pos, seq_ends)[None, :] == segment[:, None])
            )[:, None, :]

            def forward_compute(current):
                running_max, running_sum, weighted = current
                scores = (
                    jnp.einsum(
                        "qhd,khd->qhk", queries, key_rows, preferred_element_type=jnp.float32
                    )
                    * scaling
                )
                scores = jnp.where(allowed, scores, -jnp.inf)
                new_max = jnp.maximum(running_max, jnp.max(scores, axis=-1))
                safe_max = jnp.where(new_max == -jnp.inf, 0.0, new_max)
                exp_scores = jnp.exp(scores - safe_max[:, :, None])
                factor = jnp.exp(running_max - safe_max)
                running_sum = running_sum * factor + jnp.sum(exp_scores, axis=-1)
                weighted = weighted * factor[:, :, None] + jnp.einsum(
                    "qhk,khd->qhd",
                    exp_scores.astype(jnp.bfloat16),
                    value_rows,
                    preferred_element_type=jnp.float32,
                )
                return (new_max, running_sum, weighted)

            return lax.cond(jnp.any(allowed), forward_compute, keep_same, totals)

        init_fwd = (
            jnp.full((rows_n, heads_att), -jnp.inf, jnp.float32),
            jnp.zeros((rows_n, heads_att), jnp.float32),
            jnp.zeros((rows_n, heads_att, AHEAD_DIM), jnp.float32),
        )
        all_keys, all_values = (
            lax.all_gather(key_heads, "seq", axis=0, tiled=True),
            lax.all_gather(value_heads, "seq", axis=0, tiled=True),
        )
        running_max, running_sum, weighted = fold_blocks(
            forward_fold, init_fwd, (all_keys, all_values), block_rows
        )
        attended = weighted / running_sum[:, :, None]
        log_total = running_max + jnp.log(running_sum)
        att_low = attended.reshape(rows_n, -1).astype(jnp.bfloat16)
        hidden_two = hidden_one + head_total(matmul(att_low, attout_full))
        normed_three = rms_norm(hidden_two, mlp_gain).astype(jnp.bfloat16)
        up_rows = matmul(normed_three, up_full)
        act_low = gelu_tanh(up_rows).astype(jnp.bfloat16)
        layer_rows = hidden_two + head_total(matmul(act_low, down_full))
        layer_list.append(layer_rows.astype(jnp.bfloat16))
        cot_low = cotangent[batch_index]
        down_wgrad = left_gram(act_low, cot_low)
        act_grad = transposed(cot_low, down_full)
        up_grad = jax.vjp(gelu_tanh, up_rows)[1](act_grad)[0].astype(jnp.bfloat16)
        up_wgrad = left_gram(normed_three, up_grad)
        three_grad = head_total(transposed(up_grad, up_full))
        hidden_part, mlpgain_part = jax.vjp(rms_norm, hidden_two, mlp_gain)[1](three_grad)
        hidden_two_grad = cot_low.astype(jnp.float32) + hidden_part
        branch_low = hidden_two_grad.astype(jnp.bfloat16)
        attout_wgrad = left_gram(att_low, branch_low)
        attended_grad = (
            transposed(branch_low, attout_full)
            .astype(jnp.bfloat16)
            .reshape(rows_n, heads_att, AHEAD_DIM)
        )
        delta_rows = jnp.sum(attended_grad.astype(jnp.float32) * attended, axis=-1)

        def query_fold(totals, shards, offset):
            key_rows, value_rows = shards
            key_pos = slot_position(
                order_row, offset + jnp.arange(key_rows.shape[0], dtype=jnp.int32), half_rows
            )
            key_seg = segment_of(key_pos, seq_ends)
            any_allowed = jnp.any(
                (key_pos[None, :] <= position[:, None]) & (key_seg[None, :] == segment[:, None])
            )

            def query_compute(current):
                probabilities = attention_probs(
                    queries, key_rows, position, key_pos, segment, key_seg, log_total, scaling
                )
                prob_grad = jnp.einsum(
                    "qhd,khd->qhk", attended_grad, value_rows, preferred_element_type=jnp.float32
                )
                score_grad = (probabilities * (prob_grad - delta_rows[:, :, None])).astype(
                    jnp.bfloat16
                )
                return current + jnp.einsum(
                    "qhk,khd->qhd", score_grad, key_rows, preferred_element_type=jnp.float32
                )

            return lax.cond(any_allowed, query_compute, keep_same, totals)

        zero_heads = jnp.zeros((rows_n, heads_att, AHEAD_DIM), jnp.float32)
        query_sum = fold_blocks(query_fold, zero_heads, (all_keys, all_values), block_rows)
        query_rows = lax.all_gather(queries.astype(jnp.float32), "seq", axis=0, tiled=True)
        grad_rows = lax.all_gather(attended_grad.astype(jnp.float32), "seq", axis=0, tiled=True)
        log_rows = lax.all_gather(log_total, "seq", axis=0, tiled=True)
        delta_part = lax.all_gather(delta_rows, "seq", axis=0, tiled=True)
        query_pos = slot_position(
            order_row, jnp.arange(query_rows.shape[0], dtype=jnp.int32), half_rows
        )
        query_seg = segment_of(query_pos, seq_ends)
        key_any_allowed = jnp.any(
            (position[None, :] <= query_pos[:, None]) & (segment[None, :] == query_seg[:, None])
        )

        def key_compute(current):
            query_low = query_rows.astype(jnp.bfloat16)
            grad_low = grad_rows.astype(jnp.bfloat16)
            probabilities = attention_probs(
                query_low, key_heads, query_pos, position, query_seg, segment, log_rows, scaling
            )
            value_grad = jnp.einsum(
                "qhk,qhd->khd",
                probabilities.astype(jnp.bfloat16),
                grad_low,
                preferred_element_type=jnp.float32,
            )
            prob_grad = jnp.einsum(
                "qhd,khd->qhk", grad_low, value_heads, preferred_element_type=jnp.float32
            )
            score_grad = (probabilities * (prob_grad - delta_part[:, :, None])).astype(jnp.bfloat16)
            key_grad = jnp.einsum(
                "qhk,qhd->khd", score_grad, query_low, preferred_element_type=jnp.float32
            )
            return (key_grad, value_grad)

        key_sum, value_sum = lax.cond(
            key_any_allowed, key_compute, keep_same, (zero_heads, zero_heads)
        )
        qkv_grad = jnp.stack(
            [
                (query_sum * scaling).astype(jnp.bfloat16),
                (key_sum * scaling).astype(jnp.bfloat16),
                value_sum.astype(jnp.bfloat16),
            ],
            axis=1,
        ).reshape(rows_n, 3, -1)
        qkv_wgrad = jnp.einsum(
            "rd,rcn->dcn", normed_two, qkv_grad, preferred_element_type=jnp.float32
        )
        two_grad = head_total(
            jnp.einsum("rcn,dcn->rd", qkv_grad, qkv_full, preferred_element_type=jnp.float32)
        )
        hidden_part, attgain_part = jax.vjp(rms_norm, hidden_one, att_gain)[1](two_grad)
        hidden_one_grad = hidden_two_grad + hidden_part
        mix_low = hidden_one_grad.astype(jnp.bfloat16)
        mixout_wgrad = left_gram(gated_low, mix_low)
        gated_grad = transposed(mix_low, mixout_full)
        y_grad = gated_grad * gating
        gate_grad = jax.vjp(jax.nn.silu, gate_in)[1](gated_grad * full_y)[0].astype(jnp.bfloat16)
        skip_part = jnp.sum(y_grad * mixed_x, axis=0)
        heads_mix = step_size.shape[1]
        y_blocks = y_grad.reshape(2, half_rows, -1)
        inflow = (
            jnp.exp(cumulative)
            * (seg_blocks == seg_before[:, None]).astype(jnp.float32)[:, :, None]
        )
        back_local = jnp.einsum(
            "bth,bthp,btn->bhpn",
            inflow,
            y_blocks.reshape(2, half_rows, heads_mix, -1),
            bc_b[:, :, NSTATE:],
            precision=highest,
        )
        all_back = lax.all_gather(back_local, "seq", axis=0, tiled=True)
        back_stream = all_back[inverse]
        rev_through, rev_state = lax.associative_scan(
            combine_state, (through_stream[::-1], back_stream[::-1]), axis=0
        )
        after_index = slots_n - 2 - my_blocks
        outgoing_grad = (
            rev_state[jnp.maximum(after_index, 0)]
            * (after_index >= 0).astype(jnp.float32)[:, None, None, None]
        )

        def scan_call(mixed_arg, step_arg, bc_arg, decay_arg, incoming_arg):
            return whole_all(
                mixed_arg, step_arg, bc_arg, decay_arg, incoming_arg, seg_blocks, seg_before
            )

        scan_pull = jax.vjp(scan_call, mixed_b, step_b, bc_b, decay_log, incoming)[1]
        x_scan_grad, step_grad, bc_grad, decay_part, incoming_grad = scan_pull(
            (y_blocks, outgoing_grad)
        )
        mixed_grad = y_grad * skip_gain + x_scan_grad.reshape(rows_n, -1)
        conv_grad = jax.vjp(jax.nn.silu, conv_sum)[1](mixed_grad)[0]
        conv_grad_b = conv_grad.reshape(2, half_rows, -1)
        convbias_part = jnp.sum(conv_grad, axis=0)
        convtaps_part = jnp.stack(
            [
                jnp.sum(
                    extended[:, tap_index : tap_index + half_rows]
                    * valid_taps[tap_index][:, :, None]
                    * conv_grad_b,
                    axis=(0, 1),
                )
                for tap_index in range(CONV)
            ]
        )
        all_heads = lax.all_gather(conv_grad_b[:, : CONV - 1], "seq", axis=0, tiled=True)
        pick_next = (order_row[None, :] == my_blocks[:, None] + 1).astype(jnp.float32)
        next_rows = jnp.einsum("bs,srd->brd", pick_next, all_heads, precision=highest)
        grad_ext = jnp.concatenate([conv_grad_b, next_rows], axis=1)
        position_ext = (my_blocks[:, None] * half_rows + ext_ids[None, :]).reshape(-1)
        x_blocks_grad = jnp.zeros(conv_grad_b.shape, jnp.float32)
        for tap_index in range(CONV):
            lag_rows = CONV - 1 - tap_index
            masked_grad = (
                grad_ext
                * tap_valid(position_ext, lag_rows, seq_ends).reshape(2, half_rows + CONV - 1)[
                    :, :, None
                ]
            )
            x_blocks_grad = (
                x_blocks_grad
                + conv_taps[tap_index] * masked_grad[:, lag_rows : lag_rows + half_rows]
            )
        x_low = x_blocks_grad.reshape(rows_n, -1).astype(jnp.bfloat16)
        rate_grad = step_grad.reshape(rows_n, -1) * jax.nn.sigmoid(rate_in + rate_bias)
        ratebias_part = jnp.sum(rate_grad, axis=0)
        bc_flat = bc_grad.reshape(rows_n, -1)
        normed_wide = normed_one.astype(jnp.float32)
        value_wgrad = left_gram(normed_one, x_low)
        gate_wgrad = left_gram(normed_one, gate_grad)
        state_wgrad = left_gram_exact(normed_wide, bc_flat)
        rate_wgrad = left_gram_exact(normed_wide, rate_grad)
        one_grad = head_total(
            transposed(x_low, value_full)
            + transposed(gate_grad, gate_full)
            + transposed_exact(bc_flat, state_full.astype(jnp.float32))
            + transposed_exact(rate_grad, rate_full.astype(jnp.float32))
        )
        hidden_part, mixgain_part = jax.vjp(rms_norm, hidden_in, mix_gain)[1](one_grad)
        input_list.append((hidden_one_grad + hidden_part).astype(jnp.bfloat16))
        big_part = (
            value_wgrad,
            gate_wgrad,
            state_wgrad,
            rate_wgrad,
            qkv_wgrad,
            up_wgrad,
            mixout_wgrad,
            attout_wgrad,
            down_wgrad,
        )
        small_part = (
            mixgain_part,
            attgain_part,
            mlpgain_part,
            ratebias_part,
            decay_part,
            convtaps_part,
            convbias_part,
            skip_part,
        )
        big_part = reduce_grads(big_part)
        big_sums = add_parts(big_sums, big_part)
        small_sums = add_parts(small_sums, small_part)
    small_total = lax.psum(
        (
            small_sums[0],
            small_sums[1],
            small_sums[2],
            small_sums[3],
            small_sums[4],
            small_sums[5],
            small_sums[6],
            small_sums[7],
        ),
        "seq",
    )
    return (
        jnp.stack(layer_list),
        jnp.stack(input_list),
        small_total[0],
        big_sums[0],
        big_sums[1],
        big_sums[2],
        big_sums[3],
        small_total[3],
        small_total[4],
        small_total[5],
        small_total[6],
        small_total[7],
        big_sums[6],
        small_total[1],
        big_sums[4],
        big_sums[7],
        small_total[2],
        big_sums[5],
        big_sums[8],
    )


f32 = jnp.float32
bf16 = jnp.bfloat16
HALF = 64
TAIL = 16
EXT = HALF + TAIL
ROWS = 2 * HALF
HCH = 512
LANES = 128
RATE_AT = 32
HPG = 8
VMEM_LIMIT = 56 * 1024 * 1024


def mm(left_op, right_op):
    return jnp.dot(left_op, right_op, preferred_element_type=f32)


def mm_exact(left_op, right_op):
    return jnp.dot(left_op, right_op, preferred_element_type=f32, precision=highest)


def nt(left_op, right_op):
    return lax.dot_general(
        left_op, right_op, (((1,), (1,)), ((), ())), preferred_element_type=f32
    )


def nt_exact(left_op, right_op):
    return lax.dot_general(
        left_op,
        right_op,
        (((1,), (1,)), ((), ())),
        preferred_element_type=f32,
        precision=highest,
    )


def tn(left_op, right_op):
    return lax.dot_general(
        left_op, right_op, (((0,), (0,)), ((), ())), preferred_element_type=f32
    )


def iota(shape, axis):
    return lax.broadcasted_iota(jnp.int32, shape, axis)


def sigmoid(values):
    return 1.0 / (1.0 + jnp.exp(-values))


def softplus(values):
    return jnp.maximum(values, 0.0) + jnp.log1p(jnp.exp(-jnp.abs(values)))


def rms_rows(values):
    return lax.rsqrt(jnp.mean(values * values, axis=-1, keepdims=True) + epsilon)


def rms_back(values, gain_row, grad):
    scale = rms_rows(values)
    inner = grad * gain_row
    dot = jnp.mean(inner * values, axis=-1, keepdims=True)
    part = scale * (inner - values * (scale * scale) * dot)
    return part, jnp.sum(grad * (values * scale), axis=0, keepdims=True)


def same_block(rows_idx, cols_idx):
    return (rows_idx // HALF) == (cols_idx // HALF)


def lower_mask():
    rows_idx, cols_idx = iota((ROWS, ROWS), 0), iota((ROWS, ROWS), 1)
    return same_block(rows_idx, cols_idx) & (rows_idx >= cols_idx)


def spread_matrix():
    return (iota((LANES, HCH), 0) - RATE_AT == iota((LANES, HCH), 1) // HALF).astype(f32)


def per_block(values_0, values_1, shape):
    return jnp.where(iota(shape, 0) < HALF, values_0, values_1)


def step_terms(state_rate, params):
    lane = iota((1, LANES), 1)
    is_rate = (lane >= RATE_AT) & (lane < RATE_AT + HPG)
    shifted = state_rate + params[6:7, 0:LANES]
    step = jnp.where(is_rate, softplus(shifted), 0.0)
    rates = jnp.where(is_rate, jnp.exp(params[7:8, 0:LANES]), 0.0)
    log_decay = -step * rates
    cumulative = mm_exact(lower_mask().astype(f32), log_decay)
    return shifted, step, rates, log_decay, cumulative


def tail_decay(cum_wide):
    last = per_block(cum_wide[HALF - 1 : HALF], cum_wide[ROWS - 1 : ROWS], cum_wide.shape)
    return jnp.exp(last - cum_wide)


def decay_matrix(cumulative, cumulative_t, head, mask):
    at = RATE_AT + head
    gap = cumulative[:, at : at + 1] - cumulative_t[at : at + 1, :]
    return jnp.where(mask, jnp.exp(jnp.where(mask, gap, 0.0)), 0.0)


def silu_parts(values):
    gate = sigmoid(values)
    return values * gate, gate * (1.0 + values * (1.0 - gate))


def put_state(msg_ref, batch, group, state):
    for lane_block in range(4):
        for state_half in range(2):
            msg_ref[batch * 16 + group * 8 + lane_block * 2 + state_half, 0:8, :] = state[
                state_half * 8 : (state_half + 1) * 8,
                lane_block * LANES : (lane_block + 1) * LANES,
            ]


def get_state(msg_ref, batch, group):
    base = batch * 16 + group * 8
    return jnp.concatenate(
        [
            jnp.concatenate(
                [
                    msg_ref[base + lane_block * 2 + state_half, 0:8, :]
                    for lane_block in range(4)
                ],
                axis=1,
            )
            for state_half in range(2)
        ],
        axis=0,
    )


def in_kernel(
    core_ref, tok_ref, gain_ref, own_ref, other_ref, par_own_ref, par_other_ref,
    normed_ref, x_ref, conv_ref, gate_ref, sr_ref, cum_ref, inner_ref, local_ref, msg_ref,
    x_scr,
):
    core = core_ref[0]
    hidden = tok_ref[...].astype(f32)
    normed = (hidden * rms_rows(hidden) * gain_ref[...]).astype(bf16)
    normed_ref[...] = normed
    real = jnp.concatenate([normed[TAIL:EXT], normed[EXT + TAIL :]], axis=0)
    mask = lower_mask()
    spread = spread_matrix()
    for half, (w_ref, par_ref) in enumerate(
        ((own_ref, par_own_ref), (other_ref, par_other_ref))
    ):
        at = half * HCH
        params = par_ref[...]
        x_low = mm(normed, w_ref[:, 0:HCH]).astype(bf16)
        x_ref[:, at : at + HCH] = x_low
        x_scr[...] = x_low.astype(f32)
        gate_ref[:, at : at + HCH] = mm(real, w_ref[:, HCH : 2 * HCH])
        state_rate = mm(real, w_ref[:, 2 * HCH : 2 * HCH + LANES])
        sr_ref[:, half * LANES : (half + 1) * LANES] = state_rate
        conv_list = []
        for batch in range(2):
            conv = jnp.zeros((HALF, HCH), f32) + params[4:5]
            for tap in range(CONV):
                first = batch * EXT + TAIL - (CONV - 1) + tap
                conv = conv + params[tap : tap + 1] * x_scr[first : first + HALF, :]
            conv_list.append(conv)
        conv = jnp.concatenate(conv_list, axis=0)
        conv_ref[:, at : at + HCH] = conv
        mixed = conv * sigmoid(conv)
        _, step, _, _, cumulative = step_terms(state_rate, params)
        cum_wide = mm_exact(cumulative, spread)
        cum_ref[:, at : at + HCH] = cum_wide
        driving = mm_exact(step, spread) * mixed
        weighted = (driving * tail_decay(cum_wide)).astype(bf16)
        driving = driving.astype(bf16)
        b_rows = state_rate[:, 0:NSTATE].astype(bf16)
        c_rows = state_rate[:, NSTATE : 2 * NSTATE].astype(bf16)
        group = half ^ core
        for batch in range(2):
            rows = slice(batch * HALF, (batch + 1) * HALF)
            state = tn(b_rows[rows], weighted[rows])
            local_ref[batch, half] = state
            put_state(msg_ref, batch, group, state)
            for lane_block in range(4):
                total = cum_wide[
                    (batch + 1) * HALF - 1 : (batch + 1) * HALF,
                    lane_block * LANES : (lane_block + 1) * LANES,
                ]
                wide = jnp.broadcast_to(total, (8, LANES))
                for state_half in range(2):
                    msg_ref[batch * 16 + group * 8 + lane_block * 2 + state_half, 8:16, :] = wide
        inner_cb = nt(c_rows, b_rows)
        cumulative_t = cumulative.T
        first_head = iota((ROWS, LANES), 1) < HALF
        for pair in range(4):
            pair_rows = driving[:, pair * LANES : (pair + 1) * LANES]
            parts = [
                mm(
                    (decay_matrix(cumulative, cumulative_t, 2 * pair + k, mask) * inner_cb).astype(
                        bf16
                    ),
                    pair_rows,
                )
                for k in range(2)
            ]
            inner_ref[:, at + pair * LANES : at + (pair + 1) * LANES] = jnp.where(
                first_head, parts[0], parts[1]
            )


def forward_scan_kernel(slots_ref, in_ref, out_ref):
    state = jnp.zeros((8, LANES), f32)
    for place in range(slots_ref.shape[0]):
        slot = slots_ref[place]
        out_ref[slot] = state
        state = state * jnp.exp(in_ref[slot, 8:16, :]) + in_ref[slot, 0:8, :]


def backward_scan_kernel(slots_ref, decay_ref, in_ref, out_ref):
    state = jnp.zeros((8, LANES), f32)
    for place in reversed(range(slots_ref.shape[0])):
        slot = slots_ref[place]
        out_ref[slot] = state
        state = state * jnp.exp(decay_ref[slot, 8:16, :]) + in_ref[slot]


def mix_kernel(
    core_ref, tok_ref, state_ref, sr_ref, cum_ref, inner_ref, conv_ref, gate_ref,
    par_own_ref, par_other_ref, own_ref, other_ref, gain_ref,
    full_ref, gated_ref, hidden_ref, normed_ref, msg_ref,
):
    core = core_ref[0]
    hidden = tok_ref[...].astype(f32)
    hidden = jnp.concatenate([hidden[TAIL:EXT], hidden[EXT + TAIL :]], axis=0)
    for half, (w_ref, par_ref) in enumerate(
        ((own_ref, par_own_ref), (other_ref, par_other_ref))
    ):
        cols = slice(half * HCH, (half + 1) * HCH)
        c_rows = sr_ref[:, half * LANES + NSTATE : half * LANES + 2 * NSTATE].astype(bf16)
        carried = jnp.concatenate(
            [
                mm(
                    c_rows[batch * HALF : (batch + 1) * HALF],
                    get_state(state_ref, batch, half ^ core).astype(bf16),
                )
                for batch in range(2)
            ],
            axis=0,
        )
        conv = conv_ref[:, cols]
        mixed = conv * sigmoid(conv)
        full = inner_ref[:, cols] + jnp.exp(cum_ref[:, cols]) * carried + par_ref[5:6] * mixed
        full_ref[:, cols] = full
        gate = gate_ref[:, cols]
        gated = (full * (gate * sigmoid(gate))).astype(bf16)
        gated_ref[:, cols] = gated
        hidden = hidden + nt(gated, w_ref[:, 0:HCH])
    hidden_ref[...] = hidden
    normed = (hidden * rms_rows(hidden) * gain_ref[...]).astype(bf16)
    normed_ref[...] = normed
    for half, w_ref in enumerate((own_ref, other_ref)):
        rows_qkv = mm(normed, w_ref[:, HCH : HCH + 768]).astype(bf16)
        for batch in range(2):
            for head in range(4):
                for kind in range(3):
                    msg_ref[
                        batch * 8 + (half ^ core) * 4 + head,
                        :,
                        kind * AHEAD_DIM : (kind + 1) * AHEAD_DIM,
                    ] = rows_qkv[
                        batch * HALF : (batch + 1) * HALF,
                        kind * 256 + head * AHEAD_DIM : kind * 256 + (head + 1) * AHEAD_DIM,
                    ]


QTILE = 256


def query_places(blocks_ref, tile):
    parts = [
        iota((HALF, 1), 0) + blocks_ref[tile * (QTILE // HALF) + k] * HALF
        for k in range(QTILE // HALF)
    ]
    return jnp.concatenate(parts, axis=0)


def attend_kernel(blocks_ref, places_ref, own_ref, other_ref, out_ref, log_ref):
    kinds = [slice(k * AHEAD_DIM, (k + 1) * AHEAD_DIM) for k in range(3)]
    keys = [ref[:, kinds[1]] for ref in (own_ref, other_ref)]
    values = [ref[:, kinds[2]] for ref in (own_ref, other_ref)]
    scaling = AHEAD_DIM ** (-0.5)
    for tile in range(own_ref.shape[0] // QTILE):
        rows = slice(tile * QTILE, (tile + 1) * QTILE)
        place = query_places(blocks_ref, tile)
        queries = own_ref[rows, kinds[0]]
        scores = [
            jnp.where(
                places_ref[k : k + 1, :] <= place, nt(queries, keys[k]) * scaling, -jnp.inf
            )
            for k in range(2)
        ]
        most = jnp.maximum(
            jnp.max(scores[0], axis=-1, keepdims=True), jnp.max(scores[1], axis=-1, keepdims=True)
        )
        exps = [jnp.exp(member - most) for member in scores]
        total = jnp.sum(exps[0], axis=-1, keepdims=True) + jnp.sum(exps[1], axis=-1, keepdims=True)
        mixed = mm(exps[0].astype(bf16), values[0]) + mm(exps[1].astype(bf16), values[1])
        out_ref[rows, :] = (mixed / total).astype(bf16)
        log_ref[rows, :] = most + jnp.log(total)


def attend_back_kernel(
    blocks_ref, places_ref, own_ref, other_ref, grad_ref, log_ref, mine_ref, theirs_ref,
    key_scr, value_scr,
):
    kinds = [slice(k * AHEAD_DIM, (k + 1) * AHEAD_DIM) for k in range(3)]
    keys = [ref[:, kinds[1]] for ref in (own_ref, other_ref)]
    values = [ref[:, kinds[2]] for ref in (own_ref, other_ref)]
    scaling = AHEAD_DIM ** (-0.5)
    key_scr[...] = jnp.zeros(key_scr.shape, f32)
    value_scr[...] = jnp.zeros(value_scr.shape, f32)
    for tile in range(own_ref.shape[0] // QTILE):
        rows = slice(tile * QTILE, (tile + 1) * QTILE)
        place = query_places(blocks_ref, tile)
        queries = own_ref[rows, kinds[0]]
        grad = grad_ref[rows, :]
        log_total = log_ref[rows, :]
        probs = []
        prob_grads = []
        for k in range(2):
            scores = nt(queries, keys[k]) * scaling - log_total
            probs.append(jnp.exp(jnp.where(places_ref[k : k + 1, :] <= place, scores, -jnp.inf)))
            prob_grads.append(nt(grad, values[k]))
        delta = jnp.sum(probs[0] * prob_grads[0], axis=-1, keepdims=True) + jnp.sum(
            probs[1] * prob_grads[1], axis=-1, keepdims=True
        )
        query_grad = jnp.zeros((QTILE, AHEAD_DIM), f32)
        for k in range(2):
            score_grad = (probs[k] * (prob_grads[k] - delta)).astype(bf16)
            value_scr[k] += tn(probs[k].astype(bf16), grad)
            key_scr[k] += tn(score_grad, queries)
            query_grad = query_grad + mm(score_grad, keys[k])
        mine_ref[rows, kinds[0]] = query_grad * scaling
    mine_ref[:, kinds[1]] = key_scr[0] * scaling
    mine_ref[:, kinds[2]] = value_scr[0]
    theirs_ref[:, kinds[0]] = jnp.zeros(key_scr.shape[1:], bf16)
    theirs_ref[:, kinds[1]] = (key_scr[1] * scaling).astype(bf16)
    theirs_ref[:, kinds[2]] = value_scr[1].astype(bf16)


GELU_RATE = math.sqrt(2.0 / math.pi)
GELU_CUBE = 0.044715


def mlp_kernel(
    core_ref, att_ref, hidden_ref, cot_ref, gain_ref, own_ref, other_ref,
    out_ref, hidden_two_ref, grad_own_ref, grad_other_ref, hidden_grad_ref, gain_grad_ref,
    msg_ref,
    att_scr, result_scr,
):
    core = core_ref[0]
    weights = (own_ref, other_ref)
    grads = (grad_own_ref, grad_other_ref)
    up_cols, down_cols, att_cols = slice(0, 1024), slice(1024, 2048), slice(2048, 2304)
    hidden = hidden_ref[...]
    for half in range(2):
        for batch in range(2):
            for head in range(4):
                att_scr[
                    half,
                    batch * HALF : (batch + 1) * HALF,
                    head * AHEAD_DIM : (head + 1) * AHEAD_DIM,
                ] = att_ref[batch * 8 + (half ^ core) * 4 + head]
        hidden = hidden + nt(att_scr[half], weights[half][:, att_cols])
    normed = (hidden * rms_rows(hidden) * gain_ref[...]).astype(bf16)
    cot = cot_ref[...]
    normed_grad = jnp.zeros(hidden.shape, f32)
    for half in range(2):
        up_rows = mm(normed, weights[half][:, up_cols])
        squares = up_rows * up_rows
        bent = jnp.tanh(GELU_RATE * (up_rows + GELU_CUBE * squares * up_rows))
        act = (0.5 * up_rows * (1.0 + bent)).astype(bf16)
        slope = 0.5 * (1.0 + bent) + 0.5 * up_rows * (1.0 - bent * bent) * (
            GELU_RATE * (1.0 + 3.0 * GELU_CUBE * squares)
        )
        result_scr[half] = nt(act, weights[half][:, down_cols])
        grads[half][:, down_cols] = tn(cot, act).astype(bf16)
        up_grad = (mm(cot, weights[half][:, down_cols]) * slope).astype(bf16)
        grads[half][:, up_cols] = tn(normed, up_grad).astype(bf16)
        normed_grad = normed_grad + nt(up_grad, weights[half][:, up_cols])
    hidden_two_ref[...] = hidden
    out_ref[...] = result_scr[0] + result_scr[1]
    part, gain_grad = rms_back(hidden, gain_ref[...], normed_grad)
    gain_grad_ref[...] = gain_grad
    hidden_grad = cot.astype(f32) + part
    hidden_grad_ref[...] = hidden_grad
    branch = hidden_grad.astype(bf16)
    for half in range(2):
        grads[half][:, att_cols] = tn(branch, att_scr[half]).astype(bf16)
        att_grad = mm(branch, weights[half][:, att_cols]).astype(bf16)
        for batch in range(2):
            for head in range(4):
                msg_ref[batch * 8 + (half ^ core) * 4 + head] = att_grad[
                    batch * HALF : (batch + 1) * HALF,
                    head * AHEAD_DIM : (head + 1) * AHEAD_DIM,
                ]


def mix_back_kernel(
    core_ref, qkv_ref, normed_ref, hidden_ref, hidden_grad_ref, gain_ref, own_ref, other_ref,
    gated_ref, gate_ref, full_ref, conv_ref, cum_ref, sr_ref,
    grad_own_ref, grad_other_ref, y_grad_ref, gate_grad_ref, one_grad_ref, gain_grad_ref,
    skip_grad_ref, msg_ref,
    qkv_scr,
):
    core = core_ref[0]
    weights = (own_ref, other_ref)
    grads = (grad_own_ref, grad_other_ref)
    mix_cols, qkv_cols = slice(0, HCH), slice(HCH, HCH + 768)
    normed = normed_ref[...]
    normed_grad = jnp.zeros((ROWS, normed.shape[1]), f32)
    for half in range(2):
        for batch in range(2):
            for head in range(4):
                for kind in range(3):
                    qkv_scr[
                        batch * HALF : (batch + 1) * HALF,
                        kind * 256 + head * AHEAD_DIM : kind * 256 + (head + 1) * AHEAD_DIM,
                    ] = qkv_ref[
                        batch * 8 + (half ^ core) * 4 + head,
                        :,
                        kind * AHEAD_DIM : (kind + 1) * AHEAD_DIM,
                    ]
        rows_grad = qkv_scr[...]
        grads[half][:, qkv_cols] = tn(normed, rows_grad).astype(bf16)
        normed_grad = normed_grad + nt(rows_grad, weights[half][:, qkv_cols])
    part, gain_grad = rms_back(hidden_ref[...], gain_ref[...], normed_grad)
    gain_grad_ref[...] = gain_grad
    one_grad = hidden_grad_ref[...] + part
    one_grad_ref[...] = one_grad
    branch = one_grad.astype(bf16)
    for half in range(2):
        cols = slice(half * HCH, (half + 1) * HCH)
        grads[half][:, mix_cols] = tn(branch, gated_ref[:, cols]).astype(bf16)
        gated_grad = mm(branch, weights[half][:, mix_cols])
        silu, slope = silu_parts(gate_ref[:, cols])
        y_grad = gated_grad * silu
        y_grad_ref[:, cols] = y_grad
        gate_grad_ref[:, cols] = (gated_grad * full_ref[:, cols] * slope).astype(bf16)
        conv = conv_ref[:, cols]
        skip_grad_ref[:, cols] = jnp.sum(y_grad * (conv * sigmoid(conv)), axis=0, keepdims=True)
        carried = (jnp.exp(cum_ref[:, cols]) * y_grad).astype(bf16)
        c_rows = sr_ref[:, half * LANES + NSTATE : half * LANES + 2 * NSTATE].astype(bf16)
        for batch in range(2):
            rows = slice(batch * HALF, (batch + 1) * HALF)
            put_state(msg_ref, batch, half ^ core, tn(c_rows[rows], carried[rows]))


def in_back_kernel(
    core_ref, later_ref, state_ref, local_ref, sr_ref, cum_ref, conv_ref, x_ref, y_grad_ref,
    gate_grad_ref, normed_ref, tok_ref, gain_ref, one_grad_ref, own_ref, other_ref,
    par_own_ref, par_other_ref,
    grad_own_ref, grad_other_ref, hidden_grad_ref, gain_grad_ref, small_own_ref, small_other_ref,
    x_scr, grad_scr, sr_scr, gate_scr,
):
    core = core_ref[0]
    mask = lower_mask()
    spread = spread_matrix()
    normed = normed_ref[...]
    ext_grad = jnp.zeros((2 * EXT, normed.shape[1]), f32)
    lower_t = (
        same_block(iota((ROWS, ROWS), 0), iota((ROWS, ROWS), 1))
        & (iota((ROWS, ROWS), 0) <= iota((ROWS, ROWS), 1))
    ).astype(f32)
    lane = iota((1, LANES), 1)
    for half, (w_ref, par_ref, grad_ref, small_ref) in enumerate(
        (
            (own_ref, par_own_ref, grad_own_ref, small_own_ref),
            (other_ref, par_other_ref, grad_other_ref, small_other_ref),
        )
    ):
        cols = slice(half * HCH, (half + 1) * HCH)
        group = half ^ core
        params = par_ref[...]
        state_rate = sr_ref[:, half * LANES : (half + 1) * LANES]
        shifted, step, rates, log_decay, cumulative = step_terms(state_rate, params)
        cumulative_t = cumulative.T
        cum_wide = cum_ref[:, cols]
        step_wide = mm_exact(step, spread)
        conv = conv_ref[:, cols]
        mixed, conv_slope = silu_parts(conv)
        driving = step_wide * mixed
        tail = tail_decay(cum_wide)
        inflow = jnp.exp(cum_wide)
        y_grad = y_grad_ref[:, cols]
        y_low = y_grad.astype(bf16)
        driving_low = driving.astype(bf16)
        b_rows = state_rate[:, 0:NSTATE].astype(bf16)
        c_rows = state_rate[:, NSTATE : 2 * NSTATE].astype(bf16)
        inner_cb = nt(c_rows, b_rows)
        weighted = (driving * tail).astype(bf16)
        carried_grad = (inflow * y_grad).astype(bf16)
        through_list = []
        tail_list = []
        flow_list = []
        b_list = []
        c_list = []
        for batch in range(2):
            rows = slice(batch * HALF, (batch + 1) * HALF)
            incoming = get_state(state_ref, batch, group)
            later = get_state(later_ref, batch, group)
            total = cum_wide[(batch + 1) * HALF - 1 : (batch + 1) * HALF, :]
            outgoing = jnp.exp(total) * incoming + local_ref[batch, half]
            through_list.append(jnp.sum(later * outgoing, axis=0, keepdims=True))
            incoming = incoming.astype(bf16)
            later = later.astype(bf16)
            tail_list.append(mm(b_rows[rows], later))
            flow_list.append(mm(c_rows[rows], incoming))
            b_list.append(nt(weighted[rows], later))
            c_list.append(nt(carried_grad[rows], incoming))
        tail_part = tail * jnp.concatenate(tail_list, axis=0)
        flow_part = inflow * jnp.concatenate(flow_list, axis=0)
        first_head = iota((ROWS, LANES), 1) < HALF
        inner_grad = jnp.zeros((ROWS, ROWS), f32)
        row_sums = jnp.zeros((ROWS, LANES), f32)
        col_list = []
        drive_list = []
        for pair in range(4):
            lanes = slice(pair * LANES, (pair + 1) * LANES)
            y_pair = y_low[:, lanes]
            u_pair = driving_low[:, lanes]
            parts = []
            for k in range(2):
                head = 2 * pair + k
                mine = first_head if k == 0 else ~first_head
                decay = decay_matrix(cumulative, cumulative_t, head, mask)
                product = nt(jnp.where(mine, y_pair, jnp.zeros_like(y_pair)), u_pair)
                decayed = decay * product
                inner_grad = inner_grad + decayed
                both = decayed * inner_cb
                row_sums = row_sums + jnp.where(
                    lane == RATE_AT + head, jnp.sum(both, axis=1, keepdims=True), 0.0
                )
                col_list.append(jnp.sum(both, axis=0, keepdims=True))
                parts.append(tn((decay * inner_cb).astype(bf16), y_pair))
            drive_list.append(jnp.where(first_head, parts[0], parts[1]))
        drive_grad = jnp.concatenate(drive_list, axis=1) + tail_part
        col_rows = jnp.concatenate(
            [jnp.zeros((RATE_AT, ROWS), f32)]
            + col_list
            + [jnp.zeros((LANES - RATE_AT - HPG, ROWS), f32)],
            axis=0,
        )
        cum_grad = (
            row_sums
            - col_rows.T
            + nt_exact(y_grad * flow_part - driving * tail_part, spread)
        )
        through_rows = nt_exact(
            jnp.concatenate(through_list + [jnp.zeros((6, HCH), f32)], axis=0), spread
        )
        decay_grad = mm_exact(lower_t, cum_grad) + per_block(
            through_rows[0:1], through_rows[1:2], (ROWS, LANES)
        )
        step_grad = nt_exact(mixed * drive_grad, spread) - decay_grad * rates
        rate_grad = step_grad * sigmoid(shifted)
        inner_low = inner_grad.astype(bf16)
        b_grad = tn(inner_low, c_rows) + jnp.concatenate(b_list, axis=0)
        c_grad = mm(inner_low, b_rows) + jnp.concatenate(c_list, axis=0)
        is_rate = (lane >= RATE_AT) & (lane < RATE_AT + HPG)
        rate_grad = jnp.where(is_rate, rate_grad, 0.0)
        sr_grad = jnp.concatenate(
            [b_grad, c_grad, rate_grad[:, RATE_AT:LANES]], axis=1
        ).astype(bf16)
        mixed_grad = step_wide * drive_grad + params[5:6] * y_grad
        conv_grad = mixed_grad * conv_slope
        x_scr[...] = x_ref[:, cols].astype(f32)
        grad_scr[...] = jnp.zeros(grad_scr.shape, f32)
        sr_scr[...] = jnp.zeros(sr_scr.shape, bf16)
        gate_scr[...] = jnp.zeros(gate_scr.shape, bf16)
        gate_grad = gate_grad_ref[:, cols]
        for batch in range(2):
            rows = slice(batch * HALF, (batch + 1) * HALF)
            ext_rows = slice(batch * EXT + TAIL, (batch + 1) * EXT)
            grad_scr[batch, TAIL:EXT, :] = conv_grad[rows]
            sr_scr[ext_rows, :] = sr_grad[rows]
            gate_scr[ext_rows, :] = gate_grad[rows]
        x_list = []
        tap_list = [jnp.zeros((1, HCH), f32) for _ in range(CONV)]
        for batch in range(2):
            x_grad = jnp.zeros((EXT, HCH), f32)
            for tap in range(CONV):
                lag = CONV - 1 - tap
                x_grad = x_grad + params[tap : tap + 1] * grad_scr[batch, lag : lag + EXT, :]
                first = batch * EXT + TAIL - lag
                tap_list[tap] = tap_list[tap] + jnp.sum(
                    x_scr[first : first + HALF, :] * grad_scr[batch, TAIL:EXT, :],
                    axis=0,
                    keepdims=True,
                )
            x_list.append(x_grad)
        x_low = jnp.concatenate(x_list, axis=0).astype(bf16)
        small_ref[0:4, :] = jnp.concatenate(tap_list, axis=0)
        small_ref[4:5, :] = jnp.sum(conv_grad, axis=0, keepdims=True)
        small_ref[5:6, :] = jnp.zeros((1, HCH), f32)
        small_ref[6:8, :] = jnp.concatenate(
            [
                jnp.concatenate(
                    [
                        jnp.sum(rate_grad, axis=0, keepdims=True),
                        jnp.sum(decay_grad * log_decay, axis=0, keepdims=True),
                    ],
                    axis=0,
                ),
                jnp.zeros((2, HCH - LANES), f32),
            ],
            axis=1,
        )
        grad_ref[:, 0:HCH] = tn(normed, x_low).astype(bf16)
        grad_ref[:, HCH : 2 * HCH] = tn(normed, gate_scr[...]).astype(bf16)
        grad_ref[:, 2 * HCH : 2 * HCH + LANES] = tn(normed, sr_scr[...]).astype(bf16)
        ext_grad = (
            ext_grad
            + nt(x_low, w_ref[:, 0:HCH])
            + nt(gate_scr[...], w_ref[:, HCH : 2 * HCH])
            + nt(sr_scr[...], w_ref[:, 2 * HCH : 2 * HCH + LANES])
        )
    hidden = tok_ref[...].astype(f32)
    part, gain_grad = rms_back(hidden, gain_ref[...], ext_grad)
    gain_grad_ref[...] = gain_grad
    for batch in range(2):
        base = batch * EXT
        hidden_grad_ref[base : base + TAIL, :] = part[base : base + TAIL]
        hidden_grad_ref[base + TAIL : base + EXT, :] = (
            part[base + TAIL : base + EXT] + one_grad_ref[batch * HALF : (batch + 1) * HALF, :]
        )


SMEM_SPEC = pl.BlockSpec(memory_space=pltpu.SMEM)


def run_kernel(kernel, out_shapes, scalars_n, args, scratch=()):
    vmem_spec = pl.BlockSpec(memory_space=pltpu.VMEM)
    return pl.pallas_call(
        kernel,
        out_shape=[jax.ShapeDtypeStruct(shape, kind) for shape, kind in out_shapes],
        in_specs=[SMEM_SPEC] * scalars_n + [vmem_spec] * (len(args) - scalars_n),
        out_specs=[vmem_spec] * len(out_shapes),
        scratch_shapes=list(scratch),
        compiler_params=pltpu.CompilerParams(vmem_limit_bytes=VMEM_LIMIT),
    )(*args)


def flip(bits, ranks):
    return [(index, index ^ bits) for index in range(ranks)]


def swap_cores(values):
    return lax.ppermute(values, "head", [(0, 1), (1, 0)])


def gather_group(shard, ranks):
    stack = jnp.concatenate(
        [shard] + [lax.ppermute(shard, "seq", flip(4 * k, ranks)) for k in (1, 2, 3)], axis=0
    )
    whole = jnp.concatenate(
        [stack] + [lax.ppermute(stack, "seq", flip(k, ranks)) for k in (1, 2, 3)], axis=0
    )
    return whole, swap_cores(whole)


def reduce_group(own, other, ranks):
    whole = (own.astype(f32) + swap_cores(other).astype(f32)).astype(bf16)
    rows_n = whole.shape[0] // 4
    total = whole[0:rows_n].astype(f32)
    for k in (1, 2, 3):
        total = total + lax.ppermute(
            whole[k * rows_n : (k + 1) * rows_n], "seq", flip(k, ranks)
        ).astype(f32)
    part = total.astype(bf16)
    rows_n = rows_n // 4
    total = part[0:rows_n].astype(f32)
    for k in (1, 2, 3):
        total = total + lax.ppermute(
            part[k * rows_n : (k + 1) * rows_n], "seq", flip(4 * k, ranks)
        ).astype(f32)
    return total


def exchange(values, axes):
    return lax.all_to_all(values, axes, 0, 0, tiled=True)


def dealt_device(
    tokens, cotangent, lengths, order, mix_gain, in_value, in_gate, in_state, in_rate,
    rate_bias, decay_log, conv_taps, conv_bias, skip_gain, mix_out, att_gain, qkv_proj,
    att_out, mlp_gain, mlp_up, mlp_down,
):
    ranks = lax.axis_size("seq")
    both = ("seq", "head")
    chip = lax.axis_index("seq")
    core = lax.axis_index("head")
    core_1 = core.astype(jnp.int32).reshape(1)
    my_slot = 2 * chip + core
    width = tokens.shape[2]
    slots_n = 2 * ranks
    shard_rows = width // ranks

    first_shard = jnp.concatenate(
        [in_value, in_gate, in_state, in_rate, jnp.zeros((shard_rows, LANES - 40), bf16)], axis=1
    )
    second_shard = jnp.concatenate([mix_out.T, qkv_proj.reshape(shard_rows, -1)], axis=1)
    third_shard = jnp.concatenate([mlp_up, mlp_down.T, att_out.T], axis=1)
    first_own, first_other = gather_group(first_shard, ranks)
    second_own, second_other = gather_group(second_shard, ranks)
    third_own, third_other = gather_group(third_shard, ranks)

    par_own = jnp.concatenate(
        [
            conv_taps,
            conv_bias[None],
            skip_gain[None],
            jnp.pad(rate_bias, (RATE_AT, HCH - RATE_AT - HPG))[None],
            jnp.pad(decay_log, (RATE_AT, HCH - RATE_AT - HPG))[None],
        ],
        axis=0,
    )
    par_other = swap_cores(par_own)

    feature = jnp.arange(width, dtype=jnp.int32)
    feature_block = feature // shard_rows
    source = (chip ^ (feature_block // 4 + 4 * (feature_block % 4))) * shard_rows + (
        feature % shard_rows
    )
    deal = feature[:, None] == source[None, :]
    deal_low = deal.astype(bf16)
    gains = mm_exact(jnp.stack([mix_gain, att_gain, mlp_gain]), deal.astype(f32))

    my_blocks = jnp.sum(
        jnp.where(jnp.arange(slots_n)[None, :] == my_slot, order, 0), axis=1
    )
    halves = tokens.reshape(2, 2, HALF, width)
    tails = exchange(
        jnp.broadcast_to(
            halves[:, :, HALF - (CONV - 1) :].reshape(1, 4 * (CONV - 1), width),
            (ranks, 4 * (CONV - 1), width),
        ),
        "seq",
    )
    tails = (
        tails.reshape(ranks, 2, 2, CONV - 1, width)
        .transpose(1, 0, 2, 3, 4)
        .reshape(2, slots_n, CONV - 1, width)
    )
    pick_prev = (order == my_blocks[:, None] - 1).astype(f32)
    my_tails = jnp.sum(pick_prev[:, :, None, None] * tails.astype(f32), axis=1).astype(bf16)
    my_rows = jnp.where(core == 0, halves[:, 0], halves[:, 1])
    ext_rows = jnp.concatenate(
        [jnp.zeros((2, TAIL - (CONV - 1), width), bf16), my_tails, my_rows], axis=1
    ).reshape(2 * EXT, width)
    ext_rows = mm(ext_rows, deal_low).astype(bf16)
    cot_halves = cotangent.reshape(2, 2, HALF, width)
    cot_rows = jnp.where(core == 0, cot_halves[:, 0], cot_halves[:, 1]).reshape(ROWS, width)
    cot_rows = mm(cot_rows, deal_low).astype(bf16)

    channels = 2 * HCH
    (
        normed_one, x_in, conv_sum, gate_in, state_rate, cum_wide, inner_y, local_state, msg,
    ) = run_kernel(
        in_kernel,
        [
            ((2 * EXT, width), bf16),
            ((2 * EXT, channels), bf16),
            ((ROWS, channels), f32),
            ((ROWS, channels), f32),
            ((ROWS, 2 * LANES), f32),
            ((ROWS, channels), f32),
            ((ROWS, channels), f32),
            ((2, 2, NSTATE, HCH), f32),
            ((slots_n, 16, LANES), f32),
        ],
        1,
        (core_1, ext_rows, gains[0:1], first_own, first_other, par_own, par_other),
        (pltpu.VMEM((2 * EXT, HCH), f32),),
    )

    slot_table = jnp.arange(slots_n, dtype=jnp.int32)
    state_order = jnp.where(my_slot < ranks, order[0], order[1])
    state_slots = jnp.sum(
        jnp.where(state_order[None, :] == slot_table[:, None], slot_table[None, :], 0), axis=1
    )
    states = exchange(msg, both)
    (incoming,) = run_kernel(
        forward_scan_kernel, [((slots_n, 8, LANES), f32)], 1, (state_slots, states)
    )
    incoming = exchange(incoming, both)

    full_y, gated, hidden_one, normed_two, msg = run_kernel(
        mix_kernel,
        [
            ((ROWS, channels), f32),
            ((ROWS, channels), bf16),
            ((ROWS, width), f32),
            ((ROWS, width), bf16),
            ((ranks, HALF, 3 * AHEAD_DIM), bf16),
        ],
        1,
        (
            core_1, ext_rows, incoming, state_rate, cum_wide, inner_y, conv_sum, gate_in,
            par_own, par_other, second_own, second_other, gains[1:2],
        ),
    )

    att_order = jnp.where(chip < ranks // 2, order[0], order[1]).reshape(ranks, 2)
    own_blocks = jnp.where(core == 0, att_order[:, 0], att_order[:, 1])
    other_blocks = jnp.where(core == 0, att_order[:, 1], att_order[:, 0])
    places = (
        jnp.stack([own_blocks, other_blocks])[:, :, None] * HALF
        + jnp.arange(HALF, dtype=jnp.int32)[None, None, :]
    ).reshape(2, ranks * HALF)
    att_rows = ranks * HALF
    qkv_own = exchange(msg, "seq").reshape(att_rows, 3 * AHEAD_DIM)
    qkv_other = swap_cores(qkv_own)
    attended, log_total = run_kernel(
        attend_kernel,
        [((att_rows, AHEAD_DIM), bf16), ((att_rows, 1), f32)],
        1,
        (own_blocks, places, qkv_own, qkv_other),
    )
    attended = exchange(attended.reshape(ranks, HALF, AHEAD_DIM), "seq")

    third_cols = third_own.shape[1]
    down_rows, hidden_two, third_grad_own, third_grad_other, two_grad, mlpgain_part, msg = run_kernel(
        mlp_kernel,
        [
            ((ROWS, width), f32),
            ((ROWS, width), f32),
            ((width, third_cols), bf16),
            ((width, third_cols), bf16),
            ((ROWS, width), f32),
            ((1, width), f32),
            ((ranks, HALF, AHEAD_DIM), bf16),
        ],
        1,
        (core_1, attended, hidden_one, cot_rows, gains[2:3], third_own, third_other),
        (pltpu.VMEM((2, ROWS, 256), bf16), pltpu.VMEM((2, ROWS, width), f32)),
    )
    att_grad = exchange(msg, "seq").reshape(att_rows, AHEAD_DIM)
    mine, theirs = run_kernel(
        attend_back_kernel,
        [((att_rows, 3 * AHEAD_DIM), f32), ((att_rows, 3 * AHEAD_DIM), bf16)],
        1,
        (own_blocks, places, qkv_own, qkv_other, att_grad, log_total),
        (
            pltpu.VMEM((2, att_rows, AHEAD_DIM), f32),
            pltpu.VMEM((2, att_rows, AHEAD_DIM), f32),
        ),
    )
    qkv_grad = (mine + swap_cores(theirs).astype(f32)).astype(bf16)
    qkv_grad = exchange(qkv_grad.reshape(ranks, HALF, 3 * AHEAD_DIM), "seq")

    second_cols = second_own.shape[1]
    (
        second_grad_own, second_grad_other, y_grad, gate_grad, one_grad, attgain_part, skip_part,
        msg,
    ) = run_kernel(
        mix_back_kernel,
        [
            ((width, second_cols), bf16),
            ((width, second_cols), bf16),
            ((ROWS, channels), f32),
            ((ROWS, channels), bf16),
            ((ROWS, width), f32),
            ((1, width), f32),
            ((1, channels), f32),
            ((slots_n, 8, LANES), f32),
        ],
        1,
        (
            core_1, qkv_grad, normed_two, hidden_one, two_grad, gains[1:2], second_own,
            second_other, gated, gate_in, full_y, conv_sum, cum_wide, state_rate,
        ),
        (pltpu.VMEM((ROWS, 768), bf16),),
    )
    (later,) = run_kernel(
        backward_scan_kernel,
        [((slots_n, 8, LANES), f32)],
        1,
        (state_slots, states, exchange(msg, both)),
    )
    later = exchange(later, both)

    first_cols = first_own.shape[1]
    (
        first_grad_own, first_grad_other, hidden_grad, mixgain_part, small_own, small_other,
    ) = run_kernel(
        in_back_kernel,
        [
            ((width, first_cols), bf16),
            ((width, first_cols), bf16),
            ((2 * EXT, width), f32),
            ((1, width), f32),
            ((8, HCH), f32),
            ((8, HCH), f32),
        ],
        1,
        (
            core_1, later, incoming, local_state, state_rate, cum_wide, conv_sum, x_in, y_grad,
            gate_grad, normed_one, ext_rows, gains[0:1], one_grad, first_own, first_other,
            par_own, par_other,
        ),
        (
            pltpu.VMEM((2 * EXT, HCH), f32),
            pltpu.VMEM((2, EXT + TAIL, HCH), f32),
            pltpu.VMEM((2 * EXT, LANES), bf16),
            pltpu.VMEM((2 * EXT, HCH), bf16),
        ),
    )

    third_total = reduce_group(third_grad_own, third_grad_other, ranks)
    second_total = reduce_group(second_grad_own, second_grad_other, ranks)
    first_total = reduce_group(first_grad_own, first_grad_other, ranks)

    gain_parts = nt_exact(
        jnp.concatenate([mixgain_part, attgain_part, mlpgain_part], axis=0), deal.astype(f32)
    )
    skip_rows = skip_part.reshape(2, HCH)
    row_is_skip = jnp.arange(8)[:, None] == 5
    small_own = jnp.where(row_is_skip, skip_rows[0:1], small_own)
    small_other = jnp.where(row_is_skip, skip_rows[1:2], small_other)
    small_send = jnp.concatenate([small_other, gain_parts], axis=0)
    small_keep = jnp.concatenate([small_own, gain_parts], axis=0)
    small_chip = small_keep + swap_cores(small_send)
    hidden_grad = hidden_grad.reshape(2, EXT, width)
    tail_grads = nt(
        hidden_grad[:, TAIL - (CONV - 1) : TAIL].reshape(2 * (CONV - 1), width).astype(bf16),
        deal_low,
    )
    tail_both = swap_cores(tail_grads)
    tail_chip = jnp.where(
        core == 0,
        jnp.concatenate([tail_grads, tail_both], axis=0),
        jnp.concatenate([tail_both, tail_grads], axis=0),
    )
    last_msg = jnp.concatenate([small_chip, tail_chip], axis=0)
    last = exchange(jnp.broadcast_to(last_msg[None], (ranks,) + last_msg.shape), "seq")
    small_total = jnp.sum(last[:, 0:11], axis=0)
    next_tails = last[:, 11:].reshape(ranks, 2, 2, CONV - 1, width).transpose(2, 0, 1, 3, 4)
    next_tails = next_tails.reshape(2, slots_n, CONV - 1, width)
    pick_next = (order == my_blocks[:, None] + 1).astype(f32)
    tail_add = jnp.sum(pick_next[:, :, None, None] * next_tails, axis=1)
    tokens_grad = nt(
        hidden_grad[:, TAIL:].reshape(ROWS, width).astype(bf16), deal_low
    ).reshape(2, HALF, width)
    tokens_grad = jnp.concatenate(
        [tokens_grad[:, : HALF - (CONV - 1)], tokens_grad[:, HALF - (CONV - 1) :] + tail_add],
        axis=1,
    ).astype(bf16)
    layer_rows = nt((hidden_two + down_rows).astype(bf16), deal_low).astype(bf16).reshape(2, HALF, width)
    outs = jnp.stack([layer_rows, tokens_grad])
    outs_other = swap_cores(outs)
    outs = jnp.where(
        core == 0,
        jnp.concatenate([outs, outs_other], axis=2),
        jnp.concatenate([outs_other, outs], axis=2),
    )
    return (
        outs[0],
        outs[1],
        small_total[8],
        first_total[:, 0:HCH],
        first_total[:, HCH : 2 * HCH],
        first_total[:, 2 * HCH : 2 * HCH + 32],
        first_total[:, 2 * HCH + RATE_AT : 2 * HCH + RATE_AT + HPG],
        small_total[6, RATE_AT : RATE_AT + HPG],
        small_total[7, RATE_AT : RATE_AT + HPG],
        small_total[0:4],
        small_total[4],
        small_total[5],
        second_total[:, 0:HCH].T,
        small_total[9],
        second_total[:, HCH:].reshape(qkv_proj.shape),
        third_total[:, 2048:2304].T,
        small_total[10],
        third_total[:, 0:1024],
        third_total[:, 1024:2048].T,
    )


def layer(*args):
    tokens, lengths = args[0], args[2]
    fits = lax.axis_size("seq") == 16 and lax.axis_size("head") == 2
    fits = fits and lengths.shape == (2, 1) and tokens.shape[1] == ROWS
    return dealt_device(*args) if fits else on_device(*args)


def solution(mesh):
    return jax.shard_map(
        layer,
        mesh=mesh,
        in_specs=(
            P(None, "seq", None),
            P(None, "seq", None),
            P(),
            P(),
            P(),
            P("seq", "head"),
            P("seq", "head"),
            P("seq", "head"),
            P("seq", "head"),
            P("head"),
            P("head"),
            P(None, "head"),
            P("head"),
            P("head"),
            P("head", "seq"),
            P(),
            P("seq", None, "head"),
            P("head", "seq"),
            P(),
            P("seq", "head"),
            P("head", "seq"),
        ),
        out_specs=(
            P(None, "seq", None),
            P(None, "seq", None),
            P(),
            P("seq", "head"),
            P("seq", "head"),
            P("seq", "head"),
            P("seq", "head"),
            P("head"),
            P("head"),
            P(None, "head"),
            P("head"),
            P("head"),
            P("head", "seq"),
            P(),
            P("seq", None, "head"),
            P("head", "seq"),
            P(),
            P("seq", "head"),
            P("head", "seq"),
        ),
        check_vma=False,
    )
```

```python
import functools
import math

import jax
import jax.numpy as jnp
from jax import lax
from jax.experimental import pallas as pl
from jax.experimental.pallas import tpu as pltpu
from jax.sharding import PartitionSpec as P

NSTATE = 16
CONV = 4
AHEAD_DIM = 64


epsilon = 1e-05
highest = lax.Precision.HIGHEST


def rms_norm(values, gain_row):
    return (
        values * lax.rsqrt(jnp.mean(values * values, axis=-1, keepdims=True) + epsilon) * gain_row
    )


def gelu_tanh(values):
    return jax.nn.gelu(values, approximate=True)


def segment_of(position, seq_ends):
    bounds = seq_ends[:-1]
    return jnp.sum((jnp.asarray(position)[..., None] >= bounds).astype(jnp.int32), axis=-1)


def tap_valid(position, lag_rows, seq_ends):
    source = position - lag_rows
    return (
        (source >= 0) & (segment_of(source, seq_ends) == segment_of(position, seq_ends))
    ).astype(jnp.float32)


def slot_position(order_row, row_ids, half_rows):
    slot = row_ids // half_rows
    slot_table = jnp.arange(order_row.shape[0], dtype=jnp.int32)
    block = jnp.sum(jnp.where(slot[:, None] == slot_table[None, :], order_row[None, :], 0), axis=1)
    return block * half_rows + row_ids % half_rows


def stream_slots(order_row):
    slot_table = jnp.arange(order_row.shape[0], dtype=jnp.int32)
    return jnp.sum(
        jnp.where(order_row[None, :] == slot_table[:, None], slot_table[None, :], 0), axis=1
    )


def matmul(left_op, right_op):
    return jnp.dot(left_op, right_op, preferred_element_type=jnp.float32)


def transposed(left_op, right_op):
    return lax.dot_general(
        left_op, right_op, (((1,), (1,)), ((), ())), preferred_element_type=jnp.float32
    )


def left_gram(left_op, right_op):
    return lax.dot_general(
        left_op, right_op, (((0,), (0,)), ((), ())), preferred_element_type=jnp.float32
    )


def transposed_exact(left_op, right_op):
    return lax.dot_general(
        left_op,
        right_op,
        (((1,), (1,)), ((), ())),
        preferred_element_type=jnp.float32,
        precision=highest,
    )


def left_gram_exact(left_op, right_op):
    return lax.dot_general(
        left_op,
        right_op,
        (((0,), (0,)), ((), ())),
        preferred_element_type=jnp.float32,
        precision=highest,
    )


def keep_same(current):
    return current


def head_total(partial_rows):
    return lax.psum(partial_rows, "head")


def collect(in_value, in_gate, in_state, in_rate, qkv_proj, mlp_up, mix_out, att_out, mlp_down):
    return (
        lax.all_gather(in_value, "seq", axis=0, tiled=True),
        lax.all_gather(in_gate, "seq", axis=0, tiled=True),
        lax.all_gather(in_state, "seq", axis=0, tiled=True),
        lax.all_gather(in_rate, "seq", axis=0, tiled=True),
        lax.all_gather(qkv_proj, "seq", axis=0, tiled=True),
        lax.all_gather(mlp_up, "seq", axis=0, tiled=True),
        lax.all_gather(mix_out, "seq", axis=1, tiled=True),
        lax.all_gather(att_out, "seq", axis=1, tiled=True),
        lax.all_gather(mlp_down, "seq", axis=1, tiled=True),
    )


def reduce_grads(grad_parts):
    return (
        lax.psum_scatter(grad_parts[0], "seq", scatter_dimension=0, tiled=True),
        lax.psum_scatter(grad_parts[1], "seq", scatter_dimension=0, tiled=True),
        lax.psum_scatter(grad_parts[2], "seq", scatter_dimension=0, tiled=True),
        lax.psum_scatter(grad_parts[3], "seq", scatter_dimension=0, tiled=True),
        lax.psum_scatter(grad_parts[4], "seq", scatter_dimension=0, tiled=True),
        lax.psum_scatter(grad_parts[5], "seq", scatter_dimension=0, tiled=True),
        lax.psum_scatter(grad_parts[6], "seq", scatter_dimension=1, tiled=True),
        lax.psum_scatter(grad_parts[7], "seq", scatter_dimension=1, tiled=True),
        lax.psum_scatter(grad_parts[8], "seq", scatter_dimension=1, tiled=True),
    )


def fold_blocks(fold_fn, initial, arrays, block_rows):
    blocks_n = arrays[0].shape[0] // block_rows

    def one_step(block_index, current):
        offset = block_index * block_rows
        shards = tuple(
            (lax.dynamic_slice_in_dim(member, offset, block_rows, 0) for member in arrays)
        )
        return fold_fn(current, shards, offset)

    return lax.fori_loop(0, blocks_n, one_step, initial)


def add_parts(left_op, right_op):
    if left_op is None:
        return right_op
    return tuple((first_part + second_part for first_part, second_part in zip(left_op, right_op)))


def combine_state(earlier, later):
    return (earlier[0] * later[0], later[0][..., None, None] * earlier[1] + later[1])


def attention_probs(
    query_rows, key_rows, query_pos, key_pos, query_seg, key_seg, log_total, scaling
):
    allowed = ((key_pos[None, :] <= query_pos[:, None]) & (key_seg[None, :] == query_seg[:, None]))[
        :, None, :
    ]
    scores = (
        jnp.einsum("qhd,khd->qhk", query_rows, key_rows, preferred_element_type=jnp.float32)
        * scaling
    )
    return jnp.where(allowed, jnp.exp(jnp.where(allowed, scores - log_total[:, :, None], 0.0)), 0.0)


def scan_terms(mixed_x, step_size, bc_rows, decay_log, segment, seg_before):
    rows_n, heads_n = step_size.shape
    log_decay = -step_size * jnp.exp(decay_log)
    cumulative = jnp.cumsum(log_decay, axis=0)
    driving = step_size[:, :, None] * mixed_x.reshape(rows_n, heads_n, -1)
    tail_weight = (
        jnp.exp(cumulative[-1][None, :] - cumulative)
        * (segment == segment[-1]).astype(jnp.float32)[:, None]
    )
    local_state = jnp.einsum(
        "sh,shp,sn->hpn", tail_weight, driving, bc_rows[:, :NSTATE], precision=highest
    )
    through = jnp.exp(cumulative[-1]) * (segment[-1] == seg_before).astype(jnp.float32)
    return (cumulative, driving, through, local_state)


def scan_output(cumulative, driving, bc_rows, incoming, segment, seg_before):
    rows_n = cumulative.shape[0]
    row_ids = jnp.arange(rows_n, dtype=jnp.int32)
    allowed = ((row_ids[:, None] >= row_ids[None, :]) & (segment[:, None] == segment[None, :]))[
        :, :, None
    ]
    decays = jnp.where(
        allowed,
        jnp.exp(jnp.where(allowed, cumulative[:, None, :] - cumulative[None, :, :], 0.0)),
        0.0,
    )
    inner_cb = jnp.dot(bc_rows[:, NSTATE:], bc_rows[:, :NSTATE].T, precision=highest)
    output = jnp.einsum("tsh,shp->thp", decays * inner_cb[:, :, None], driving, precision=highest)
    inflow = jnp.exp(cumulative) * (segment == seg_before).astype(jnp.float32)[:, None]
    output = output + inflow[:, :, None] * jnp.einsum(
        "tn,hpn->thp", bc_rows[:, NSTATE:], incoming, precision=highest
    )
    return output.reshape(rows_n, -1)


def scan_whole(mixed_x, step_size, bc_rows, decay_log, incoming, segment, seg_before):
    cumulative, driving, through, local_state = scan_terms(
        mixed_x, step_size, bc_rows, decay_log, segment, seg_before
    )
    output = scan_output(cumulative, driving, bc_rows, incoming, segment, seg_before)
    return (output, through[:, None, None] * incoming + local_state)


def on_device(
    tokens,
    cotangent,
    lengths,
    order,
    mix_gain,
    in_value,
    in_gate,
    in_state,
    in_rate,
    rate_bias,
    decay_log,
    conv_taps,
    conv_bias,
    skip_gain,
    mix_out,
    att_gain,
    qkv_proj,
    att_out,
    mlp_gain,
    mlp_up,
    mlp_down,
):
    rows_n = tokens.shape[1]
    half_rows = rows_n // 2
    slots_n = 2 * lax.axis_size("seq")
    my_slot = 2 * lax.axis_index("seq")
    total_rows = rows_n * lax.axis_size("seq")
    block_rows = math.gcd(total_rows, 1024)
    scaling = AHEAD_DIM ** (-0.5)
    local_ids = jnp.arange(half_rows, dtype=jnp.int32)
    ext_ids = jnp.arange(half_rows + CONV - 1, dtype=jnp.int32)
    terms_all = jax.vmap(scan_terms, in_axes=(0, 0, 0, None, 0, 0))
    output_all = jax.vmap(scan_output, in_axes=(0, 0, 0, 0, 0, 0))
    whole_all = jax.vmap(scan_whole, in_axes=(0, 0, 0, None, 0, 0, 0))
    layer_list = []
    input_list = []
    big_sums = None
    small_sums = None
    for batch_index in range(tokens.shape[0]):
        (
            value_full,
            gate_full,
            state_full,
            rate_full,
            qkv_full,
            up_full,
            mixout_full,
            attout_full,
            down_full,
        ) = collect(
            in_value, in_gate, in_state, in_rate, qkv_proj, mlp_up, mix_out, att_out, mlp_down
        )
        seq_ends = jnp.cumsum(lengths[batch_index])
        order_row = order[batch_index]
        inverse = stream_slots(order_row)
        my_blocks = lax.dynamic_slice_in_dim(order_row, my_slot, 2)
        position = (my_blocks[:, None] * half_rows + local_ids[None, :]).reshape(rows_n)
        segment = segment_of(position, seq_ends)
        seg_blocks = segment.reshape(2, half_rows)
        seg_before = segment_of(my_blocks * half_rows - 1, seq_ends)
        hidden_in = tokens[batch_index].astype(jnp.float32)
        normed_one = rms_norm(hidden_in, mix_gain).astype(jnp.bfloat16)
        x_in = matmul(normed_one, value_full).astype(jnp.bfloat16)
        gate_in = matmul(normed_one, gate_full)
        bc_rows = matmul(normed_one, state_full)
        rate_in = matmul(normed_one, rate_full)
        step_size = jax.nn.softplus(rate_in + rate_bias)
        x_blocks = x_in.reshape(2, half_rows, -1)
        all_tails = lax.all_gather(x_blocks[:, half_rows - (CONV - 1) :], "seq", axis=0, tiled=True)
        pick_prev = (order_row[None, :] == my_blocks[:, None] - 1).astype(jnp.bfloat16)
        edge_rows = jnp.einsum(
            "bs,srd->brd", pick_prev, all_tails, preferred_element_type=jnp.float32
        )
        extended = jnp.concatenate([edge_rows, x_blocks.astype(jnp.float32)], axis=1)
        valid_taps = [
            tap_valid(position, CONV - 1 - tap_index, seq_ends).reshape(2, half_rows)
            for tap_index in range(CONV)
        ]
        conv_blocks = jnp.zeros(x_blocks.shape, jnp.float32) + conv_bias
        for tap_index in range(CONV):
            conv_blocks = (
                conv_blocks
                + conv_taps[tap_index]
                * extended[:, tap_index : tap_index + half_rows]
                * valid_taps[tap_index][:, :, None]
            )
        conv_sum = conv_blocks.reshape(rows_n, -1)
        mixed_x = jax.nn.silu(conv_sum)
        mixed_b = mixed_x.reshape(2, half_rows, -1)
        step_b = step_size.reshape(2, half_rows, -1)
        bc_b = bc_rows.reshape(2, half_rows, -1)
        cumulative, driving, through, local_state = terms_all(
            mixed_b, step_b, bc_b, decay_log, seg_blocks, seg_before
        )
        all_through, all_state = (
            lax.all_gather(through, "seq", axis=0, tiled=True),
            lax.all_gather(local_state, "seq", axis=0, tiled=True),
        )
        through_stream = all_through[inverse]
        state_stream = all_state[inverse]
        acc_through, acc_state = lax.associative_scan(
            combine_state, (through_stream, state_stream), axis=0
        )
        before = my_blocks - 1
        incoming = (
            acc_state[jnp.maximum(before, 0)]
            * (before >= 0).astype(jnp.float32)[:, None, None, None]
        )
        ssm_out = output_all(cumulative, driving, bc_b, incoming, seg_blocks, seg_before).reshape(
            rows_n, -1
        )
        full_y = ssm_out + skip_gain * mixed_x
        gating = jax.nn.silu(gate_in)
        gated_low = (full_y * gating).astype(jnp.bfloat16)
        hidden_one = hidden_in + head_total(matmul(gated_low, mixout_full))
        normed_two = rms_norm(hidden_one, att_gain).astype(jnp.bfloat16)
        qkv_rows = jnp.einsum(
            "rd,dcn->rcn", normed_two, qkv_full, preferred_element_type=jnp.float32
        ).astype(jnp.bfloat16)
        heads_att = qkv_rows.shape[2] // AHEAD_DIM
        queries = qkv_rows[:, 0].reshape(rows_n, heads_att, AHEAD_DIM)
        key_heads = qkv_rows[:, 1].reshape(rows_n, heads_att, AHEAD_DIM)
        value_heads = qkv_rows[:, 2].reshape(rows_n, heads_att, AHEAD_DIM)

        def forward_fold(totals, shards, offset):
            key_rows, value_rows = shards
            key_pos = slot_position(
                order_row, offset + jnp.arange(key_rows.shape[0], dtype=jnp.int32), half_rows
            )
            allowed = (
                (key_pos[None, :] <= position[:, None])
                & (segment_of(key_pos, seq_ends)[None, :] == segment[:, None])
            )[:, None, :]

            def forward_compute(current):
                running_max, running_sum, weighted = current
                scores = (
                    jnp.einsum(
                        "qhd,khd->qhk", queries, key_rows, preferred_element_type=jnp.float32
                    )
                    * scaling
                )
                scores = jnp.where(allowed, scores, -jnp.inf)
                new_max = jnp.maximum(running_max, jnp.max(scores, axis=-1))
                safe_max = jnp.where(new_max == -jnp.inf, 0.0, new_max)
                exp_scores = jnp.exp(scores - safe_max[:, :, None])
                factor = jnp.exp(running_max - safe_max)
                running_sum = running_sum * factor + jnp.sum(exp_scores, axis=-1)
                weighted = weighted * factor[:, :, None] + jnp.einsum(
                    "qhk,khd->qhd",
                    exp_scores.astype(jnp.bfloat16),
                    value_rows,
                    preferred_element_type=jnp.float32,
                )
                return (new_max, running_sum, weighted)

            return lax.cond(jnp.any(allowed), forward_compute, keep_same, totals)

        init_fwd = (
            jnp.full((rows_n, heads_att), -jnp.inf, jnp.float32),
            jnp.zeros((rows_n, heads_att), jnp.float32),
            jnp.zeros((rows_n, heads_att, AHEAD_DIM), jnp.float32),
        )
        all_keys, all_values = (
            lax.all_gather(key_heads, "seq", axis=0, tiled=True),
            lax.all_gather(value_heads, "seq", axis=0, tiled=True),
        )
        running_max, running_sum, weighted = fold_blocks(
            forward_fold, init_fwd, (all_keys, all_values), block_rows
        )
        attended = weighted / running_sum[:, :, None]
        log_total = running_max + jnp.log(running_sum)
        att_low = attended.reshape(rows_n, -1).astype(jnp.bfloat16)
        hidden_two = hidden_one + head_total(matmul(att_low, attout_full))
        normed_three = rms_norm(hidden_two, mlp_gain).astype(jnp.bfloat16)
        up_rows = matmul(normed_three, up_full)
        act_low = gelu_tanh(up_rows).astype(jnp.bfloat16)
        layer_rows = hidden_two + head_total(matmul(act_low, down_full))
        layer_list.append(layer_rows.astype(jnp.bfloat16))
        cot_low = cotangent[batch_index]
        down_wgrad = left_gram(act_low, cot_low)
        act_grad = transposed(cot_low, down_full)
        up_grad = jax.vjp(gelu_tanh, up_rows)[1](act_grad)[0].astype(jnp.bfloat16)
        up_wgrad = left_gram(normed_three, up_grad)
        three_grad = head_total(transposed(up_grad, up_full))
        hidden_part, mlpgain_part = jax.vjp(rms_norm, hidden_two, mlp_gain)[1](three_grad)
        hidden_two_grad = cot_low.astype(jnp.float32) + hidden_part
        branch_low = hidden_two_grad.astype(jnp.bfloat16)
        attout_wgrad = left_gram(att_low, branch_low)
        attended_grad = (
            transposed(branch_low, attout_full)
            .astype(jnp.bfloat16)
            .reshape(rows_n, heads_att, AHEAD_DIM)
        )
        delta_rows = jnp.sum(attended_grad.astype(jnp.float32) * attended, axis=-1)

        def query_fold(totals, shards, offset):
            key_rows, value_rows = shards
            key_pos = slot_position(
                order_row, offset + jnp.arange(key_rows.shape[0], dtype=jnp.int32), half_rows
            )
            key_seg = segment_of(key_pos, seq_ends)
            any_allowed = jnp.any(
                (key_pos[None, :] <= position[:, None]) & (key_seg[None, :] == segment[:, None])
            )

            def query_compute(current):
                probabilities = attention_probs(
                    queries, key_rows, position, key_pos, segment, key_seg, log_total, scaling
                )
                prob_grad = jnp.einsum(
                    "qhd,khd->qhk", attended_grad, value_rows, preferred_element_type=jnp.float32
                )
                score_grad = (probabilities * (prob_grad - delta_rows[:, :, None])).astype(
                    jnp.bfloat16
                )
                return current + jnp.einsum(
                    "qhk,khd->qhd", score_grad, key_rows, preferred_element_type=jnp.float32
                )

            return lax.cond(any_allowed, query_compute, keep_same, totals)

        zero_heads = jnp.zeros((rows_n, heads_att, AHEAD_DIM), jnp.float32)
        query_sum = fold_blocks(query_fold, zero_heads, (all_keys, all_values), block_rows)
        query_rows = lax.all_gather(queries.astype(jnp.float32), "seq", axis=0, tiled=True)
        grad_rows = lax.all_gather(attended_grad.astype(jnp.float32), "seq", axis=0, tiled=True)
        log_rows = lax.all_gather(log_total, "seq", axis=0, tiled=True)
        delta_part = lax.all_gather(delta_rows, "seq", axis=0, tiled=True)
        query_pos = slot_position(
            order_row, jnp.arange(query_rows.shape[0], dtype=jnp.int32), half_rows
        )
        query_seg = segment_of(query_pos, seq_ends)
        key_any_allowed = jnp.any(
            (position[None, :] <= query_pos[:, None]) & (segment[None, :] == query_seg[:, None])
        )

        def key_compute(current):
            query_low = query_rows.astype(jnp.bfloat16)
            grad_low = grad_rows.astype(jnp.bfloat16)
            probabilities = attention_probs(
                query_low, key_heads, query_pos, position, query_seg, segment, log_rows, scaling
            )
            value_grad = jnp.einsum(
                "qhk,qhd->khd",
                probabilities.astype(jnp.bfloat16),
                grad_low,
                preferred_element_type=jnp.float32,
            )
            prob_grad = jnp.einsum(
                "qhd,khd->qhk", grad_low, value_heads, preferred_element_type=jnp.float32
            )
            score_grad = (probabilities * (prob_grad - delta_part[:, :, None])).astype(jnp.bfloat16)
            key_grad = jnp.einsum(
                "qhk,qhd->khd", score_grad, query_low, preferred_element_type=jnp.float32
            )
            return (key_grad, value_grad)

        key_sum, value_sum = lax.cond(
            key_any_allowed, key_compute, keep_same, (zero_heads, zero_heads)
        )
        qkv_grad = jnp.stack(
            [
                (query_sum * scaling).astype(jnp.bfloat16),
                (key_sum * scaling).astype(jnp.bfloat16),
                value_sum.astype(jnp.bfloat16),
            ],
            axis=1,
        ).reshape(rows_n, 3, -1)
        qkv_wgrad = jnp.einsum(
            "rd,rcn->dcn", normed_two, qkv_grad, preferred_element_type=jnp.float32
        )
        two_grad = head_total(
            jnp.einsum("rcn,dcn->rd", qkv_grad, qkv_full, preferred_element_type=jnp.float32)
        )
        hidden_part, attgain_part = jax.vjp(rms_norm, hidden_one, att_gain)[1](two_grad)
        hidden_one_grad = hidden_two_grad + hidden_part
        mix_low = hidden_one_grad.astype(jnp.bfloat16)
        mixout_wgrad = left_gram(gated_low, mix_low)
        gated_grad = transposed(mix_low, mixout_full)
        y_grad = gated_grad * gating
        gate_grad = jax.vjp(jax.nn.silu, gate_in)[1](gated_grad * full_y)[0].astype(jnp.bfloat16)
        skip_part = jnp.sum(y_grad * mixed_x, axis=0)
        heads_mix = step_size.shape[1]
        y_blocks = y_grad.reshape(2, half_rows, -1)
        inflow = (
            jnp.exp(cumulative)
            * (seg_blocks == seg_before[:, None]).astype(jnp.float32)[:, :, None]
        )
        back_local = jnp.einsum(
            "bth,bthp,btn->bhpn",
            inflow,
            y_blocks.reshape(2, half_rows, heads_mix, -1),
            bc_b[:, :, NSTATE:],
            precision=highest,
        )
        all_back = lax.all_gather(back_local, "seq", axis=0, tiled=True)
        back_stream = all_back[inverse]
        rev_through, rev_state = lax.associative_scan(
            combine_state, (through_stream[::-1], back_stream[::-1]), axis=0
        )
        after_index = slots_n - 2 - my_blocks
        outgoing_grad = (
            rev_state[jnp.maximum(after_index, 0)]
            * (after_index >= 0).astype(jnp.float32)[:, None, None, None]
        )

        def scan_call(mixed_arg, step_arg, bc_arg, decay_arg, incoming_arg):
            return whole_all(
                mixed_arg, step_arg, bc_arg, decay_arg, incoming_arg, seg_blocks, seg_before
            )

        scan_pull = jax.vjp(scan_call, mixed_b, step_b, bc_b, decay_log, incoming)[1]
        x_scan_grad, step_grad, bc_grad, decay_part, incoming_grad = scan_pull(
            (y_blocks, outgoing_grad)
        )
        mixed_grad = y_grad * skip_gain + x_scan_grad.reshape(rows_n, -1)
        conv_grad = jax.vjp(jax.nn.silu, conv_sum)[1](mixed_grad)[0]
        conv_grad_b = conv_grad.reshape(2, half_rows, -1)
        convbias_part = jnp.sum(conv_grad, axis=0)
        convtaps_part = jnp.stack(
            [
                jnp.sum(
                    extended[:, tap_index : tap_index + half_rows]
                    * valid_taps[tap_index][:, :, None]
                    * conv_grad_b,
                    axis=(0, 1),
                )
                for tap_index in range(CONV)
            ]
        )
        all_heads = lax.all_gather(conv_grad_b[:, : CONV - 1], "seq", axis=0, tiled=True)
        pick_next = (order_row[None, :] == my_blocks[:, None] + 1).astype(jnp.float32)
        next_rows = jnp.einsum("bs,srd->brd", pick_next, all_heads, precision=highest)
        grad_ext = jnp.concatenate([conv_grad_b, next_rows], axis=1)
        position_ext = (my_blocks[:, None] * half_rows + ext_ids[None, :]).reshape(-1)
        x_blocks_grad = jnp.zeros(conv_grad_b.shape, jnp.float32)
        for tap_index in range(CONV):
            lag_rows = CONV - 1 - tap_index
            masked_grad = (
                grad_ext
                * tap_valid(position_ext, lag_rows, seq_ends).reshape(2, half_rows + CONV - 1)[
                    :, :, None
                ]
            )
            x_blocks_grad = (
                x_blocks_grad
                + conv_taps[tap_index] * masked_grad[:, lag_rows : lag_rows + half_rows]
            )
        x_low = x_blocks_grad.reshape(rows_n, -1).astype(jnp.bfloat16)
        rate_grad = step_grad.reshape(rows_n, -1) * jax.nn.sigmoid(rate_in + rate_bias)
        ratebias_part = jnp.sum(rate_grad, axis=0)
        bc_flat = bc_grad.reshape(rows_n, -1)
        normed_wide = normed_one.astype(jnp.float32)
        value_wgrad = left_gram(normed_one, x_low)
        gate_wgrad = left_gram(normed_one, gate_grad)
        state_wgrad = left_gram_exact(normed_wide, bc_flat)
        rate_wgrad = left_gram_exact(normed_wide, rate_grad)
        one_grad = head_total(
            transposed(x_low, value_full)
            + transposed(gate_grad, gate_full)
            + transposed_exact(bc_flat, state_full.astype(jnp.float32))
            + transposed_exact(rate_grad, rate_full.astype(jnp.float32))
        )
        hidden_part, mixgain_part = jax.vjp(rms_norm, hidden_in, mix_gain)[1](one_grad)
        input_list.append((hidden_one_grad + hidden_part).astype(jnp.bfloat16))
        big_part = (
            value_wgrad,
            gate_wgrad,
            state_wgrad,
            rate_wgrad,
            qkv_wgrad,
            up_wgrad,
            mixout_wgrad,
            attout_wgrad,
            down_wgrad,
        )
        small_part = (
            mixgain_part,
            attgain_part,
            mlpgain_part,
            ratebias_part,
            decay_part,
            convtaps_part,
            convbias_part,
            skip_part,
        )
        big_part = reduce_grads(big_part)
        big_sums = add_parts(big_sums, big_part)
        small_sums = add_parts(small_sums, small_part)
    small_total = lax.psum(
        (
            small_sums[0],
            small_sums[1],
            small_sums[2],
            small_sums[3],
            small_sums[4],
            small_sums[5],
            small_sums[6],
            small_sums[7],
        ),
        "seq",
    )
    return (
        jnp.stack(layer_list),
        jnp.stack(input_list),
        small_total[0],
        big_sums[0],
        big_sums[1],
        big_sums[2],
        big_sums[3],
        small_total[3],
        small_total[4],
        small_total[5],
        small_total[6],
        small_total[7],
        big_sums[6],
        small_total[1],
        big_sums[4],
        big_sums[7],
        small_total[2],
        big_sums[5],
        big_sums[8],
    )


f32 = jnp.float32
bf16 = jnp.bfloat16
HALF = 64
TAIL = 16
EXT = HALF + TAIL
ROWS = 2 * HALF
HCH = 512
LANES = 128
RATE_AT = 32
HPG = 8
TILE_ROWS = 32
SMALL_ROWS = 16
TAIL_COLS = slice(2 * HCH + LANES, 2 * HCH + 2 * LANES)
QKV_ROWS = HALF + HALF // 2
VMEM_LIMIT = 56 * 1024 * 1024


def mm(left_op, right_op):
    return jnp.dot(left_op, right_op, preferred_element_type=f32)


def mm_exact(left_op, right_op):
    return jnp.dot(left_op, right_op, preferred_element_type=f32, precision=highest)


def nt(left_op, right_op):
    return lax.dot_general(
        left_op, right_op, (((1,), (1,)), ((), ())), preferred_element_type=f32
    )


def nt_exact(left_op, right_op):
    return lax.dot_general(
        left_op,
        right_op,
        (((1,), (1,)), ((), ())),
        preferred_element_type=f32,
        precision=highest,
    )


def tn(left_op, right_op):
    return lax.dot_general(
        left_op, right_op, (((0,), (0,)), ((), ())), preferred_element_type=f32
    )


def iota(shape, axis):
    return lax.broadcasted_iota(jnp.int32, shape, axis)


def sigmoid(values):
    return 1.0 / (1.0 + jnp.exp(-values))


def softplus(values):
    return jnp.maximum(values, 0.0) + jnp.log1p(jnp.exp(-jnp.abs(values)))


def rms_rows(values):
    return lax.rsqrt(jnp.mean(values * values, axis=-1, keepdims=True) + epsilon)


def rms_back(values, gain_row, grad):
    scale = rms_rows(values)
    inner = grad * gain_row
    dot = jnp.mean(inner * values, axis=-1, keepdims=True)
    part = scale * (inner - values * (scale * scale) * dot)
    return part, jnp.sum(grad * (values * scale), axis=0, keepdims=True)


def same_block(rows_idx, cols_idx):
    return (rows_idx // HALF) == (cols_idx // HALF)


def lower_mask():
    rows_idx, cols_idx = iota((ROWS, ROWS), 0), iota((ROWS, ROWS), 1)
    return same_block(rows_idx, cols_idx) & (rows_idx >= cols_idx)


def spread_matrix():
    return (iota((LANES, HCH), 0) - RATE_AT == iota((LANES, HCH), 1) // HALF).astype(f32)


def per_block(values_0, values_1, shape):
    return jnp.where(iota(shape, 0) < HALF, values_0, values_1)


def step_terms(state_rate, params):
    lane = iota((1, LANES), 1)
    is_rate = (lane >= RATE_AT) & (lane < RATE_AT + HPG)
    shifted = state_rate + params[6:7, 0:LANES]
    step = jnp.where(is_rate, softplus(shifted), 0.0)
    rates = jnp.where(is_rate, jnp.exp(params[7:8, 0:LANES]), 0.0)
    log_decay = -step * rates
    cumulative = mm_exact(lower_mask().astype(f32), log_decay)
    return shifted, step, rates, log_decay, cumulative


def tail_decay(cum_wide):
    last = per_block(cum_wide[HALF - 1 : HALF], cum_wide[ROWS - 1 : ROWS], cum_wide.shape)
    return jnp.exp(last - cum_wide)


def decay_matrix(cumulative, cumulative_t, head, mask):
    at = RATE_AT + head
    gap = cumulative[:, at : at + 1] - cumulative_t[at : at + 1, :]
    return jnp.where(mask, jnp.exp(jnp.where(mask, gap, 0.0)), 0.0)


def silu_parts(values):
    gate = sigmoid(values)
    return values * gate, gate * (1.0 + values * (1.0 - gate))


def put_state(msg_ref, batch, group, state):
    for lane_block in range(4):
        for state_half in range(2):
            msg_ref[batch * 16 + group * 8 + lane_block * 2 + state_half, 0:8, :] = state[
                state_half * 8 : (state_half + 1) * 8,
                lane_block * LANES : (lane_block + 1) * LANES,
            ]


def get_state(msg_ref, batch, group):
    base = batch * 16 + group * 8
    return jnp.concatenate(
        [
            jnp.concatenate(
                [
                    msg_ref[base + lane_block * 2 + state_half, 0:8, :]
                    for lane_block in range(4)
                ],
                axis=1,
            )
            for state_half in range(2)
        ],
        axis=0,
    )


def my_rows(core):
    return pl.ds(pl.multiple_of(core * HALF, HALF), HALF)


def in_kernel(
    ids_ref, order_ref, tok_ref, gain_ref, own_ref, other_ref, par_own_ref, par_other_ref,
    ext_ref, normed_ref, x_ref, conv_ref, gate_ref, sr_ref, cum_ref, inner_ref, local_ref,
    msg_ref, deal_ref, gains_ref, x_scr, tail_scr,
):
    chip, core = ids_ref[0], ids_ref[1]
    width = tok_ref.shape[2]
    place = iota((1, width), 1)
    block = place // TILE_ROWS
    source = (chip ^ (block // 4 + 4 * (block % 4))) * TILE_ROWS + place % TILE_ROWS
    deal = (iota((width, width), 0) == source).astype(f32)
    deal_low = deal.astype(bf16)
    deal_ref[...] = deal_low
    gains = mm_exact(gain_ref[...], deal)
    gains_ref[...] = gains
    ext_list = []
    for batch in range(2):
        my_block = order_ref[batch, 2 * chip + core]
        before = jnp.int32(0)
        for slot in range(order_ref.shape[1]):
            before = jnp.where(order_ref[batch, slot] == my_block - 1, slot, before)
        apart = chip ^ (before // 2)
        tail_at = ((apart % 4) * 4 + apart // 4) * TILE_ROWS
        rows = pl.ds(pl.multiple_of(tail_at, TILE_ROWS), TILE_ROWS)

        @pl.when(core == batch)
        def _():
            tail_scr[batch] = own_ref[rows, TAIL_COLS].astype(f32)

        @pl.when(core != batch)
        def _():
            tail_scr[batch] = other_ref[rows, TAIL_COLS].astype(f32)

        tile = jnp.where(before % 2 == 0, tail_scr[batch, 0:12], tail_scr[batch, 12:24])
        tile = jnp.where(my_block == 0, 0.0, tile)
        tails = [
            jnp.concatenate([tile[4 * k + j : 4 * k + j + 1] for j in range(4)], axis=1)
            for k in range(CONV - 1)
        ]
        lead = jnp.zeros((TAIL - (CONV - 1), width), f32)
        ext_list.append(jnp.concatenate([lead] + tails, axis=0).astype(bf16))
        ext_list.append(tok_ref[batch, my_rows(core), :])
    ext_rows = mm(jnp.concatenate(ext_list, axis=0), deal_low).astype(bf16)
    ext_ref[...] = ext_rows
    hidden = ext_rows.astype(f32)
    normed = (hidden * rms_rows(hidden) * gains[0:1]).astype(bf16)
    normed_ref[...] = normed
    real = jnp.concatenate([normed[TAIL:EXT], normed[EXT + TAIL :]], axis=0)
    mask = lower_mask()
    spread = spread_matrix()
    for half, (w_ref, par_ref) in enumerate(
        ((own_ref, par_own_ref), (other_ref, par_other_ref))
    ):
        at = half * HCH
        params = par_ref[...]
        x_low = mm(normed, w_ref[:, 0:HCH]).astype(bf16)
        x_ref[:, at : at + HCH] = x_low
        x_scr[...] = x_low.astype(f32)
        gate_ref[:, at : at + HCH] = mm(real, w_ref[:, HCH : 2 * HCH])
        state_rate = mm(real, w_ref[:, 2 * HCH : 2 * HCH + LANES])
        sr_ref[:, half * LANES : (half + 1) * LANES] = state_rate
        conv_list = []
        for batch in range(2):
            conv = jnp.zeros((HALF, HCH), f32) + params[4:5]
            for tap in range(CONV):
                first = batch * EXT + TAIL - (CONV - 1) + tap
                conv = conv + params[tap : tap + 1] * x_scr[first : first + HALF, :]
            conv_list.append(conv)
        conv = jnp.concatenate(conv_list, axis=0)
        conv_ref[:, at : at + HCH] = conv
        mixed = conv * sigmoid(conv)
        _, step, _, _, cumulative = step_terms(state_rate, params)
        cum_wide = mm_exact(cumulative, spread)
        cum_ref[:, at : at + HCH] = cum_wide
        driving = mm_exact(step, spread) * mixed
        weighted = (driving * tail_decay(cum_wide)).astype(bf16)
        driving = driving.astype(bf16)
        b_rows = state_rate[:, 0:NSTATE].astype(bf16)
        c_rows = state_rate[:, NSTATE : 2 * NSTATE].astype(bf16)
        group = half ^ core
        for batch in range(2):
            rows = slice(batch * HALF, (batch + 1) * HALF)
            state = tn(b_rows[rows], weighted[rows])
            local_ref[batch, half] = state
            put_state(msg_ref, batch, group, state)
            for lane_block in range(4):
                total = cum_wide[
                    (batch + 1) * HALF - 1 : (batch + 1) * HALF,
                    lane_block * LANES : (lane_block + 1) * LANES,
                ]
                wide = jnp.broadcast_to(total, (8, LANES))
                for state_half in range(2):
                    msg_ref[batch * 16 + group * 8 + lane_block * 2 + state_half, 8:16, :] = wide
        inner_cb = nt(c_rows, b_rows)
        cumulative_t = cumulative.T
        first_head = iota((ROWS, LANES), 1) < HALF
        for pair in range(4):
            pair_rows = driving[:, pair * LANES : (pair + 1) * LANES]
            parts = [
                mm(
                    (decay_matrix(cumulative, cumulative_t, 2 * pair + k, mask) * inner_cb).astype(
                        bf16
                    ),
                    pair_rows,
                )
                for k in range(2)
            ]
            inner_ref[:, at + pair * LANES : at + (pair + 1) * LANES] = jnp.where(
                first_head, parts[0], parts[1]
            )


def invert_order(ids_ref, order_ref, slots_scr):
    slots_n = order_ref.shape[1]
    batch = (2 * ids_ref[0] + ids_ref[1]) // (slots_n // 2)
    for slot in range(slots_n):
        slots_scr[order_ref[batch, slot]] = slot


def forward_scan_kernel(ids_ref, order_ref, in_ref, out_ref, slots_scr):
    invert_order(ids_ref, order_ref, slots_scr)
    state = jnp.zeros((8, LANES), f32)
    for place in range(order_ref.shape[1]):
        slot = slots_scr[place]
        out_ref[slot] = state
        state = state * jnp.exp(in_ref[slot, 8:16, :]) + in_ref[slot, 0:8, :]


def backward_scan_kernel(ids_ref, order_ref, decay_ref, in_ref, out_ref, slots_scr):
    invert_order(ids_ref, order_ref, slots_scr)
    state = jnp.zeros((8, LANES), f32)
    for place in reversed(range(order_ref.shape[1])):
        slot = slots_scr[place]
        out_ref[slot] = state
        state = state * jnp.exp(decay_ref[slot, 8:16, :]) + in_ref[slot]


def mix_kernel(
    ids_ref, tok_ref, state_ref, sr_ref, cum_ref, inner_ref, conv_ref, gate_ref,
    par_own_ref, par_other_ref, own_ref, other_ref, gain_ref,
    full_ref, gated_ref, hidden_ref, normed_ref, msg_ref,
):
    core = ids_ref[1]
    hidden = tok_ref[...].astype(f32)
    hidden = jnp.concatenate([hidden[TAIL:EXT], hidden[EXT + TAIL :]], axis=0)
    for half, (w_ref, par_ref) in enumerate(
        ((own_ref, par_own_ref), (other_ref, par_other_ref))
    ):
        cols = slice(half * HCH, (half + 1) * HCH)
        c_rows = sr_ref[:, half * LANES + NSTATE : half * LANES + 2 * NSTATE].astype(bf16)
        carried = jnp.concatenate(
            [
                mm(
                    c_rows[batch * HALF : (batch + 1) * HALF],
                    get_state(state_ref, batch, half ^ core).astype(bf16),
                )
                for batch in range(2)
            ],
            axis=0,
        )
        conv = conv_ref[:, cols]
        mixed = conv * sigmoid(conv)
        full = inner_ref[:, cols] + jnp.exp(cum_ref[:, cols]) * carried + par_ref[5:6] * mixed
        full_ref[:, cols] = full
        gate = gate_ref[:, cols]
        gated = (full * (gate * sigmoid(gate))).astype(bf16)
        gated_ref[:, cols] = gated
        hidden = hidden + nt(gated, w_ref[:, 0:HCH])
    hidden_ref[...] = hidden
    normed = (hidden * rms_rows(hidden) * gain_ref[1:2]).astype(bf16)
    normed_ref[...] = normed
    for half, w_ref in enumerate((own_ref, other_ref)):
        rows_qkv = mm(normed, w_ref[:, HCH : HCH + 768]).astype(bf16)
        for batch in range(2):
            rows = slice(batch * HALF, (batch + 1) * HALF)
            for head in range(4):
                put_qkv(
                    msg_ref,
                    batch * 8 + (half ^ core) * 4 + head,
                    [
                        rows_qkv[rows, at : at + AHEAD_DIM]
                        for at in range(head * AHEAD_DIM, 768, 256)
                    ],
                )


def put_qkv(ref, at, members):
    ref[at, 0:HALF, 0:AHEAD_DIM] = members[0]
    ref[at, 0:HALF, AHEAD_DIM:LANES] = members[1]
    ref[at, HALF:QKV_ROWS, 0:AHEAD_DIM] = members[2][0 : HALF // 2]
    ref[at, HALF:QKV_ROWS, AHEAD_DIM:LANES] = members[2][HALF // 2 :]


def get_qkv(ref, at):
    return [
        ref[at, 0:HALF, 0:AHEAD_DIM],
        ref[at, 0:HALF, AHEAD_DIM:LANES],
        jnp.concatenate(
            [ref[at, HALF:QKV_ROWS, 0:AHEAD_DIM], ref[at, HALF:QKV_ROWS, AHEAD_DIM:LANES]], axis=0
        ),
    ]


def unpack_qkv(own_ref, other_ref, query_scr, key_scr, value_scr):
    for k, ref in enumerate((own_ref, other_ref)):
        for at in range(ref.shape[0]):
            rows = slice(at * HALF, (at + 1) * HALF)
            queries, keys, values = get_qkv(ref, at)
            if k == 0:
                query_scr[rows, :] = queries
            key_scr[k, rows, :] = keys
            value_scr[k, rows, :] = values


def put_rows(ref, at, member):
    ref[at, :, 0:AHEAD_DIM] = member[0 : HALF // 2]
    ref[at, :, AHEAD_DIM:LANES] = member[HALF // 2 :]


def get_rows(ref, at):
    return jnp.concatenate([ref[at, :, 0:AHEAD_DIM], ref[at, :, AHEAD_DIM:LANES]], axis=0)


QTILE = 256


def block_place(ids_ref, order_ref, block, other):
    chip, core = ids_ref[0], ids_ref[1]
    batch = chip // (order_ref.shape[1] // 4)
    return order_ref[batch, 2 * block + (core ^ other)] * HALF


def query_places(ids_ref, order_ref, tile):
    parts = [
        iota((HALF, 1), 0) + block_place(ids_ref, order_ref, tile * (QTILE // HALF) + k, 0)
        for k in range(QTILE // HALF)
    ]
    return jnp.concatenate(parts, axis=0)


def key_places(ids_ref, order_ref, other):
    lane = iota((1, LANES), 1)
    parts = []
    for pair in range(order_ref.shape[1] // 4):
        first = block_place(ids_ref, order_ref, 2 * pair, other)
        second = block_place(ids_ref, order_ref, 2 * pair + 1, other)
        parts.append(lane + jnp.where(lane < HALF, first, second - HALF))
    return jnp.concatenate(parts, axis=1)


def attend_kernel(
    ids_ref, order_ref, own_ref, other_ref, out_ref, log_ref, query_scr, key_scr, value_scr
):
    places = [key_places(ids_ref, order_ref, k) for k in range(2)]
    unpack_qkv(own_ref, other_ref, query_scr, key_scr, value_scr)
    scaling = AHEAD_DIM ** (-0.5)
    for tile in range(query_scr.shape[0] // QTILE):
        rows = slice(tile * QTILE, (tile + 1) * QTILE)
        place = query_places(ids_ref, order_ref, tile)
        queries = query_scr[rows, :]
        scores = [
            jnp.where(
                places[k] <= place, nt(queries, key_scr[k]) * scaling, -jnp.inf
            )
            for k in range(2)
        ]
        most = jnp.maximum(
            jnp.max(scores[0], axis=-1, keepdims=True), jnp.max(scores[1], axis=-1, keepdims=True)
        )
        exps = [jnp.exp(member - most) for member in scores]
        total = jnp.sum(exps[0], axis=-1, keepdims=True) + jnp.sum(exps[1], axis=-1, keepdims=True)
        mixed = mm(exps[0].astype(bf16), value_scr[0]) + mm(exps[1].astype(bf16), value_scr[1])
        mixed = (mixed / total).astype(bf16)
        for k in range(QTILE // HALF):
            put_rows(out_ref, tile * (QTILE // HALF) + k, mixed[k * HALF : (k + 1) * HALF])
        log_ref[rows, :] = most + jnp.log(total)


def attend_back_kernel(
    ids_ref, order_ref, own_ref, other_ref, grad_ref, log_ref, mine_ref, theirs_ref,
    query_scr, key_scr, value_scr, query_sum, key_sum, value_sum,
):
    places = [key_places(ids_ref, order_ref, k) for k in range(2)]
    unpack_qkv(own_ref, other_ref, query_scr, key_scr, value_scr)
    scaling = AHEAD_DIM ** (-0.5)
    key_sum[...] = jnp.zeros(key_sum.shape, f32)
    value_sum[...] = jnp.zeros(value_sum.shape, f32)
    for tile in range(query_scr.shape[0] // QTILE):
        rows = slice(tile * QTILE, (tile + 1) * QTILE)
        place = query_places(ids_ref, order_ref, tile)
        queries = query_scr[rows, :]
        grad = jnp.concatenate(
            [get_rows(grad_ref, tile * (QTILE // HALF) + k) for k in range(QTILE // HALF)],
            axis=0,
        )
        log_total = log_ref[rows, :]
        probs = []
        prob_grads = []
        for k in range(2):
            scores = nt(queries, key_scr[k]) * scaling - log_total
            probs.append(jnp.exp(jnp.where(places[k] <= place, scores, -jnp.inf)))
            prob_grads.append(nt(grad, value_scr[k]))
        delta = jnp.sum(probs[0] * prob_grads[0], axis=-1, keepdims=True) + jnp.sum(
            probs[1] * prob_grads[1], axis=-1, keepdims=True
        )
        query_grad = jnp.zeros((QTILE, AHEAD_DIM), f32)
        for k in range(2):
            score_grad = (probs[k] * (prob_grads[k] - delta)).astype(bf16)
            value_sum[k] += tn(probs[k].astype(bf16), grad)
            key_sum[k] += tn(score_grad, queries)
            query_grad = query_grad + mm(score_grad, key_scr[k])
        query_sum[rows, :] = query_grad * scaling
    for at in range(mine_ref.shape[0]):
        rows = slice(at * HALF, (at + 1) * HALF)
        put_qkv(
            mine_ref, at, [query_sum[rows, :], key_sum[0, rows, :] * scaling, value_sum[0, rows, :]]
        )
        put_qkv(
            theirs_ref,
            at,
            [
                jnp.zeros((HALF, AHEAD_DIM), bf16),
                (key_sum[1, rows, :] * scaling).astype(bf16),
                value_sum[1, rows, :].astype(bf16),
            ],
        )


GELU_RATE = math.sqrt(2.0 / math.pi)
GELU_CUBE = 0.044715


def mlp_kernel(
    ids_ref, att_ref, hidden_ref, cot_ref, deal_ref, gain_ref, own_ref, other_ref,
    out_ref, hidden_two_ref, cot_both_ref, mine_ref, theirs_ref, hidden_grad_ref, gain_grad_ref,
    msg_ref,
    att_scr, result_scr,
):
    core = ids_ref[1]
    weights = (own_ref, other_ref)
    packs = (mine_ref, theirs_ref)
    up_cols, down_cols, att_cols = slice(0, 1024), slice(1024, 2048), slice(2048, 2304)
    cot_both = mm(
        jnp.concatenate(
            [cot_ref[batch, my_rows(side), :] for side in (core, 1 - core) for batch in range(2)],
            axis=0,
        ),
        deal_ref[...],
    ).astype(bf16)
    cot_both_ref[...] = cot_both
    cot = cot_both[0:ROWS]
    hidden = hidden_ref[...]
    for half in range(2):
        for batch in range(2):
            for head in range(4):
                att_scr[
                    half,
                    batch * HALF : (batch + 1) * HALF,
                    head * AHEAD_DIM : (head + 1) * AHEAD_DIM,
                ] = get_rows(att_ref, batch * 8 + (half ^ core) * 4 + head)
        packs[half][:, att_cols] = att_scr[half]
        hidden = hidden + nt(att_scr[half], weights[half][:, att_cols])
    gain = gain_ref[2:3]
    normed = (hidden * rms_rows(hidden) * gain).astype(bf16)
    normed_grad = jnp.zeros(hidden.shape, f32)
    for half in range(2):
        up_rows = mm(normed, weights[half][:, up_cols])
        squares = up_rows * up_rows
        bent = jnp.tanh(GELU_RATE * (up_rows + GELU_CUBE * squares * up_rows))
        act = (0.5 * up_rows * (1.0 + bent)).astype(bf16)
        slope = 0.5 * (1.0 + bent) + 0.5 * up_rows * (1.0 - bent * bent) * (
            GELU_RATE * (1.0 + 3.0 * GELU_CUBE * squares)
        )
        result_scr[half] = nt(act, weights[half][:, down_cols])
        packs[half][:, down_cols] = act
        up_grad = (mm(cot, weights[half][:, down_cols]) * slope).astype(bf16)
        packs[half][:, up_cols] = up_grad
        normed_grad = normed_grad + nt(up_grad, weights[half][:, up_cols])
        packs[half][:, 2304 : 2304 + 512] = normed
    hidden_two_ref[...] = hidden
    out_ref[...] = result_scr[0] + result_scr[1]
    part, gain_grad = rms_back(hidden, gain, normed_grad)
    gain_grad_ref[...] = gain_grad
    hidden_grad = cot.astype(f32) + part
    hidden_grad_ref[...] = hidden_grad
    branch = hidden_grad.astype(bf16)
    for half in range(2):
        packs[half][:, 2816 : 2816 + 512] = branch
        att_grad = mm(branch, weights[half][:, att_cols]).astype(bf16)
        for batch in range(2):
            for head in range(4):
                put_rows(
                    msg_ref,
                    batch * 8 + (half ^ core) * 4 + head,
                    att_grad[
                        batch * HALF : (batch + 1) * HALF,
                        head * AHEAD_DIM : (head + 1) * AHEAD_DIM,
                    ],
                )


def both_rows(mine_ref, theirs_ref, cols):
    return jnp.concatenate([mine_ref[:, cols], theirs_ref[:, cols]], axis=0)


def put_pieces(piece_refs, cols, values):
    rows_n = piece_refs[0].shape[0]
    for k, piece_ref in enumerate(piece_refs):
        piece_ref[:, cols] = values[k * rows_n : (k + 1) * rows_n].astype(bf16)


def third_grad_kernel(mine_ref, theirs_ref, cot_ref, *piece_refs):
    up_cols, down_cols, att_cols = slice(0, 1024), slice(1024, 2048), slice(2048, 2304)

    def both(cols):
        return both_rows(mine_ref, theirs_ref, cols)

    put_pieces(piece_refs, up_cols, tn(both(slice(2304, 2816)), both(up_cols)))
    put_pieces(piece_refs, down_cols, tn(cot_ref[...], both(down_cols)))
    put_pieces(piece_refs, att_cols, tn(both(slice(2816, 3328)), both(att_cols)))


def second_grad_kernel(mine_ref, theirs_ref, *piece_refs):
    def both(cols):
        return both_rows(mine_ref, theirs_ref, cols)

    for cols, base in ((slice(0, 512), 2304), (slice(512, 1280), 1792), (slice(1280, 1792), 2816)):
        put_pieces(piece_refs, cols, tn(both(slice(base, base + 512)), both(cols)))


def first_grad_kernel(ids_ref, mine_ref, theirs_ref, msg_ref, *piece_refs):
    cols = slice(0, HCH + LANES)
    rows = slice(0, 2 * EXT)
    packs = (mine_ref, theirs_ref)
    put_pieces(
        piece_refs,
        cols,
        tn(
            jnp.concatenate([ref[rows, HCH + LANES : 2 * HCH + LANES] for ref in packs], axis=0),
            jnp.concatenate([ref[rows, cols] for ref in packs], axis=0),
        ),
    )
    rows = slice(2 * EXT, 2 * EXT + SMALL_ROWS)
    small = mine_ref[rows, 0:HCH].astype(f32) + theirs_ref[rows, 0:HCH].astype(f32)
    tails = [ref[rows, HCH : 2 * HCH].astype(f32) for ref in packs]
    ordered = [jnp.where(ids_ref[1] == k, tails[0], tails[1]) for k in range(2)]
    tails = jnp.concatenate(
        [ordered[0][0:6], ordered[1][0:6], jnp.zeros((SMALL_ROWS - 12, HCH), f32)], axis=0
    )
    block = jnp.concatenate([small, tails], axis=1).astype(bf16)
    for k in range(msg_ref.shape[0]):
        msg_ref[k] = block


def sum_kernel(*refs):
    total = refs[0][...].astype(f32)
    for ref in refs[1:4]:
        total = total + ref[...].astype(f32)
    put_pieces(refs[4:], slice(0, total.shape[1]), total)


def sum_both_kernel(*refs):
    at = 0
    for group in (refs[0:4], refs[4:8]):
        total = group[0][...].astype(f32)
        for ref in group[1:]:
            total = total + ref[...].astype(f32)
        put_pieces(refs[8:], slice(at, at + total.shape[1]), total)
        at += total.shape[1]


def stack_kernel(first_col, *refs):
    out_ref = refs[-1]
    rows_n = refs[0].shape[0]
    for k, ref in enumerate(refs[:-1]):
        out_ref[k * rows_n : (k + 1) * rows_n, :] = ref[
            :, first_col : first_col + out_ref.shape[1]
        ]


def mix_back_kernel(
    ids_ref, qkv_ref, first_ref, normed_ref, hidden_ref, hidden_grad_ref, gain_ref, own_ref,
    other_ref, gated_ref, gate_ref, full_ref, conv_ref, cum_ref, sr_ref,
    mine_ref, theirs_ref, y_grad_ref, gate_grad_ref, one_grad_ref, gain_grad_ref, skip_grad_ref,
    msg_ref, qkv_scr,
):
    core = ids_ref[1]
    weights = (own_ref, other_ref)
    packs = (mine_ref, theirs_ref)
    mix_cols, qkv_cols, gate_cols = slice(0, 512), slice(512, 1280), slice(1280, 1792)
    first = jnp.concatenate([first_ref[TAIL:EXT], first_ref[EXT + TAIL :]], axis=0)
    normed_grad = jnp.zeros(hidden_ref.shape, f32)
    for half in range(2):
        for batch in range(2):
            for head in range(4):
                members = get_qkv(qkv_ref, batch * 8 + (half ^ core) * 4 + head)
                for kind, member in enumerate(members):
                    at = kind * 256 + head * AHEAD_DIM
                    qkv_scr[batch * HALF : (batch + 1) * HALF, at : at + AHEAD_DIM] = member
        rows_grad = qkv_scr[...]
        packs[half][:, qkv_cols] = rows_grad
        normed_grad = normed_grad + nt(rows_grad, weights[half][:, qkv_cols])
    part, gain_grad = rms_back(hidden_ref[...], gain_ref[1:2], normed_grad)
    gain_grad_ref[...] = gain_grad
    one_grad = hidden_grad_ref[...] + part
    one_grad_ref[...] = one_grad
    branch = one_grad.astype(bf16)
    for half in range(2):
        cols = slice(half * HCH, (half + 1) * HCH)
        packs[half][:, mix_cols] = gated_ref[:, cols]
        packs[half][:, 1792:2304] = normed_ref[...]
        packs[half][:, 2304:2816] = branch
        packs[half][:, 2816:3328] = first
        gated_grad = mm(branch, weights[half][:, mix_cols])
        silu, slope = silu_parts(gate_ref[:, cols])
        y_grad = gated_grad * silu
        y_grad_ref[:, cols] = y_grad
        gate_grad = (gated_grad * full_ref[:, cols] * slope).astype(bf16)
        gate_grad_ref[:, cols] = gate_grad
        packs[half][:, gate_cols] = gate_grad
        conv = conv_ref[:, cols]
        skip_grad_ref[:, cols] = jnp.sum(y_grad * (conv * sigmoid(conv)), axis=0, keepdims=True)
        carried = (jnp.exp(cum_ref[:, cols]) * y_grad).astype(bf16)
        c_rows = sr_ref[:, half * LANES + NSTATE : half * LANES + 2 * NSTATE].astype(bf16)
        for batch in range(2):
            rows = slice(batch * HALF, (batch + 1) * HALF)
            put_state(msg_ref, batch, half ^ core, tn(c_rows[rows], carried[rows]))


def in_back_kernel(
    ids_ref, later_ref, state_ref, local_ref, sr_ref, cum_ref, conv_ref, x_ref, y_grad_ref,
    gate_grad_ref, normed_ref, tok_ref, gain_ref, one_grad_ref, own_ref, other_ref,
    par_own_ref, par_other_ref, deal_ref, skip_grad_ref, attgain_ref, mlpgain_ref,
    mine_ref, theirs_ref, hidden_grad_ref,
    x_scr, grad_scr, sr_scr, gate_scr,
):
    core = ids_ref[1]
    mask = lower_mask()
    spread = spread_matrix()
    normed = normed_ref[...]
    ext_grad = jnp.zeros((2 * EXT, normed.shape[1]), f32)
    lower_t = (
        same_block(iota((ROWS, ROWS), 0), iota((ROWS, ROWS), 1))
        & (iota((ROWS, ROWS), 0) <= iota((ROWS, ROWS), 1))
    ).astype(f32)
    lane = iota((1, LANES), 1)
    small_list = []
    for half, (w_ref, par_ref, pack_ref) in enumerate(
        ((own_ref, par_own_ref, mine_ref), (other_ref, par_other_ref, theirs_ref))
    ):
        cols = slice(half * HCH, (half + 1) * HCH)
        group = half ^ core
        params = par_ref[...]
        state_rate = sr_ref[:, half * LANES : (half + 1) * LANES]
        shifted, step, rates, log_decay, cumulative = step_terms(state_rate, params)
        cumulative_t = cumulative.T
        cum_wide = cum_ref[:, cols]
        step_wide = mm_exact(step, spread)
        conv = conv_ref[:, cols]
        mixed, conv_slope = silu_parts(conv)
        driving = step_wide * mixed
        tail = tail_decay(cum_wide)
        inflow = jnp.exp(cum_wide)
        y_grad = y_grad_ref[:, cols]
        y_low = y_grad.astype(bf16)
        driving_low = driving.astype(bf16)
        b_rows = state_rate[:, 0:NSTATE].astype(bf16)
        c_rows = state_rate[:, NSTATE : 2 * NSTATE].astype(bf16)
        inner_cb = nt(c_rows, b_rows)
        weighted = (driving * tail).astype(bf16)
        carried_grad = (inflow * y_grad).astype(bf16)
        through_list = []
        tail_list = []
        flow_list = []
        b_list = []
        c_list = []
        for batch in range(2):
            rows = slice(batch * HALF, (batch + 1) * HALF)
            incoming = get_state(state_ref, batch, group)
            later = get_state(later_ref, batch, group)
            total = cum_wide[(batch + 1) * HALF - 1 : (batch + 1) * HALF, :]
            outgoing = jnp.exp(total) * incoming + local_ref[batch, half]
            through_list.append(jnp.sum(later * outgoing, axis=0, keepdims=True))
            incoming = incoming.astype(bf16)
            later = later.astype(bf16)
            tail_list.append(mm(b_rows[rows], later))
            flow_list.append(mm(c_rows[rows], incoming))
            b_list.append(nt(weighted[rows], later))
            c_list.append(nt(carried_grad[rows], incoming))
        tail_part = tail * jnp.concatenate(tail_list, axis=0)
        flow_part = inflow * jnp.concatenate(flow_list, axis=0)
        first_head = iota((ROWS, LANES), 1) < HALF
        inner_grad = jnp.zeros((ROWS, ROWS), f32)
        row_sums = jnp.zeros((ROWS, LANES), f32)
        col_list = []
        drive_list = []
        for pair in range(4):
            lanes = slice(pair * LANES, (pair + 1) * LANES)
            y_pair = y_low[:, lanes]
            u_pair = driving_low[:, lanes]
            parts = []
            for k in range(2):
                head = 2 * pair + k
                mine = first_head if k == 0 else ~first_head
                decay = decay_matrix(cumulative, cumulative_t, head, mask)
                product = nt(jnp.where(mine, y_pair, jnp.zeros_like(y_pair)), u_pair)
                decayed = decay * product
                inner_grad = inner_grad + decayed
                both = decayed * inner_cb
                row_sums = row_sums + jnp.where(
                    lane == RATE_AT + head, jnp.sum(both, axis=1, keepdims=True), 0.0
                )
                col_list.append(jnp.sum(both, axis=0, keepdims=True))
                parts.append(tn((decay * inner_cb).astype(bf16), y_pair))
            drive_list.append(jnp.where(first_head, parts[0], parts[1]))
        drive_grad = jnp.concatenate(drive_list, axis=1) + tail_part
        col_rows = jnp.concatenate(
            [jnp.zeros((RATE_AT, ROWS), f32)]
            + col_list
            + [jnp.zeros((LANES - RATE_AT - HPG, ROWS), f32)],
            axis=0,
        )
        cum_grad = (
            row_sums
            - col_rows.T
            + nt_exact(y_grad * flow_part - driving * tail_part, spread)
        )
        through_rows = nt_exact(
            jnp.concatenate(through_list + [jnp.zeros((6, HCH), f32)], axis=0), spread
        )
        decay_grad = mm_exact(lower_t, cum_grad) + per_block(
            through_rows[0:1], through_rows[1:2], (ROWS, LANES)
        )
        step_grad = nt_exact(mixed * drive_grad, spread) - decay_grad * rates
        rate_grad = step_grad * sigmoid(shifted)
        inner_low = inner_grad.astype(bf16)
        b_grad = tn(inner_low, c_rows) + jnp.concatenate(b_list, axis=0)
        c_grad = mm(inner_low, b_rows) + jnp.concatenate(c_list, axis=0)
        is_rate = (lane >= RATE_AT) & (lane < RATE_AT + HPG)
        rate_grad = jnp.where(is_rate, rate_grad, 0.0)
        sr_grad = jnp.concatenate(
            [b_grad, c_grad, rate_grad[:, RATE_AT:LANES]], axis=1
        ).astype(bf16)
        mixed_grad = step_wide * drive_grad + params[5:6] * y_grad
        conv_grad = mixed_grad * conv_slope
        x_scr[...] = x_ref[:, cols].astype(f32)
        grad_scr[...] = jnp.zeros(grad_scr.shape, f32)
        sr_scr[...] = jnp.zeros(sr_scr.shape, bf16)
        gate_scr[...] = jnp.zeros(gate_scr.shape, bf16)
        gate_grad = gate_grad_ref[:, cols]
        for batch in range(2):
            rows = slice(batch * HALF, (batch + 1) * HALF)
            ext_rows = slice(batch * EXT + TAIL, (batch + 1) * EXT)
            grad_scr[batch, TAIL:EXT, :] = conv_grad[rows]
            sr_scr[ext_rows, :] = sr_grad[rows]
            gate_scr[ext_rows, :] = gate_grad[rows]
        x_list = []
        tap_list = [jnp.zeros((1, HCH), f32) for _ in range(CONV)]
        for batch in range(2):
            x_grad = jnp.zeros((EXT, HCH), f32)
            for tap in range(CONV):
                lag = CONV - 1 - tap
                x_grad = x_grad + params[tap : tap + 1] * grad_scr[batch, lag : lag + EXT, :]
                first = batch * EXT + TAIL - lag
                tap_list[tap] = tap_list[tap] + jnp.sum(
                    x_scr[first : first + HALF, :] * grad_scr[batch, TAIL:EXT, :],
                    axis=0,
                    keepdims=True,
                )
            x_list.append(x_grad)
        x_low = jnp.concatenate(x_list, axis=0).astype(bf16)
        small_list.append(
            jnp.concatenate(
                tap_list
                + [
                    jnp.sum(conv_grad, axis=0, keepdims=True),
                    skip_grad_ref[:, cols],
                    jnp.concatenate(
                        [
                            jnp.sum(rate_grad, axis=0, keepdims=True),
                            jnp.sum(decay_grad * log_decay, axis=0, keepdims=True),
                            jnp.zeros((1, HCH - 2 * LANES), f32),
                        ],
                        axis=1,
                    ),
                ],
                axis=0,
            )
        )
        pack_ref[0 : 2 * EXT, 0:HCH] = x_low
        pack_ref[0 : 2 * EXT, HCH : HCH + LANES] = sr_scr[...]
        pack_ref[0 : 2 * EXT, HCH + LANES : 2 * HCH + LANES] = normed
        ext_grad = (
            ext_grad
            + nt(x_low, w_ref[:, 0:HCH])
            + nt(gate_scr[...], w_ref[:, HCH : 2 * HCH])
            + nt(sr_scr[...], w_ref[:, 2 * HCH : 2 * HCH + LANES])
        )
    hidden = tok_ref[...].astype(f32)
    part, gain_grad = rms_back(hidden, gain_ref[0:1], ext_grad)
    deal = deal_ref[...]
    gain_grads = nt_exact(
        jnp.concatenate([gain_grad, attgain_ref[...], mlpgain_ref[...]], axis=0), deal.astype(f32)
    )
    tails = nt(
        jnp.concatenate([part[TAIL - 3 : TAIL], part[EXT + TAIL - 3 : EXT + TAIL]], axis=0).astype(
            bf16
        ),
        deal,
    )
    tails = jnp.concatenate([tails, jnp.zeros((SMALL_ROWS - 6, HCH), f32)], axis=0)
    for small, pack_ref in zip(small_list, (mine_ref, theirs_ref)):
        rows = slice(2 * EXT, 2 * EXT + SMALL_ROWS)
        pack_ref[rows, 0:HCH] = jnp.concatenate(
            [small, gain_grads, jnp.zeros((SMALL_ROWS - 10, HCH), f32)], axis=0
        ).astype(bf16)
        pack_ref[rows, HCH : 2 * HCH] = tails.astype(bf16)
        pack_ref[rows, 2 * HCH :] = jnp.zeros((SMALL_ROWS, LANES), bf16)
    rows_grad = jnp.concatenate([part[TAIL:EXT], part[EXT + TAIL :]], axis=0) + one_grad_ref[...]
    hidden_grad_ref[...] = nt(rows_grad.astype(bf16), deal)


SMEM_SPEC = pl.BlockSpec(memory_space=pltpu.SMEM)
VMEM_SPEC = pl.BlockSpec(memory_space=pltpu.VMEM)
ANY_SPEC = pl.BlockSpec(memory_space=pl.ANY)


def run_kernel(kernel, out_shapes, scalars_n, args, scratch=(), after=(), blocks=None):
    args_n = len(args)
    blocks = blocks or {}

    def body(*refs):
        kernel(*refs[:args_n], *refs[args_n + len(after) :])

    return pl.pallas_call(
        body,
        out_shape=[jax.ShapeDtypeStruct(shape, kind) for shape, kind in out_shapes],
        in_specs=[SMEM_SPEC] * scalars_n
        + [blocks.get(k, VMEM_SPEC) for k in range(scalars_n, args_n)]
        + [ANY_SPEC] * len(after),
        out_specs=[VMEM_SPEC] * len(out_shapes),
        scratch_shapes=list(scratch),
        compiler_params=pltpu.CompilerParams(vmem_limit_bytes=VMEM_LIMIT),
        name=getattr(kernel, "__name__", "stack_kernel"),
        cost_estimate=pl.CostEstimate(flops=0, transcendentals=0, bytes_accessed=0),
    )(*args, *after)


def hold(values, *after):
    def body(*refs):
        pass

    return pl.pallas_call(
        body,
        out_shape=jax.ShapeDtypeStruct(values.shape, values.dtype),
        in_specs=[ANY_SPEC] * (1 + len(after)),
        out_specs=ANY_SPEC,
        input_output_aliases={0: 0},
    )(values, *after)


def flip(bits, ranks):
    return [(index, index ^ bits) for index in range(ranks)]


def swap_cores(values):
    return lax.ppermute(values, "head", [(0, 1), (1, 0)])


def permute_three(pieces, step, ranks):
    return [
        lax.ppermute(piece, "seq", flip(step * (k + 1), ranks)) for k, piece in enumerate(pieces)
    ]


def stack_pieces(pieces, first_col, cols, after):
    shape = (4 * pieces[0].shape[0], cols)
    kernel = functools.partial(stack_kernel, first_col)
    return run_kernel(kernel, [(shape, bf16)], 0, pieces, (), after)[0]


def sum_pieces(mine, moved, after=()):
    rows_n, cols = mine.shape
    return run_kernel(
        sum_kernel, [((rows_n // 4, cols), bf16)] * 4, 0, [mine] + moved, (), after
    )


def sum_last(mine, moved):
    total = mine.astype(f32)
    for piece in moved:
        total = total + piece.astype(f32)
    return total


def exchange(values, axes):
    return lax.all_to_all(values, axes, 0, 0, tiled=True)


def dealt_device(
    tokens, cotangent, lengths, order, mix_gain, in_value, in_gate, in_state, in_rate,
    rate_bias, decay_log, conv_taps, conv_bias, skip_gain, mix_out, att_gain, qkv_proj,
    att_out, mlp_gain, mlp_up, mlp_down,
):
    ranks = lax.axis_size("seq")
    both = ("seq", "head")
    chip = lax.axis_index("seq")
    core = lax.axis_index("head")
    ids = jnp.stack([chip, core]).astype(jnp.int32)
    my_slot = 2 * chip + core
    width = tokens.shape[2]
    slots_n = 2 * ranks
    shard_rows = width // ranks
    slots_scratch = (pltpu.SMEM((slots_n,), jnp.int32),)

    tail_rows = tokens.reshape(2, 2, HALF, width)[:, :, HALF - (CONV - 1) :]
    tail_rows = jnp.where(core == 0, tail_rows[0], tail_rows[1]).reshape(-1, LANES)
    tail_rows = jnp.pad(tail_rows, ((0, shard_rows - tail_rows.shape[0]), (0, 0)))
    first_shard = jnp.concatenate(
        [
            in_value, in_gate, in_state, in_rate, jnp.zeros((shard_rows, LANES - 40), bf16),
            tail_rows,
        ],
        axis=1,
    )
    first_cols = first_shard.shape[1]
    second_cols, third_cols = HCH + 768, 2304
    early_shard = jnp.concatenate(
        [first_shard, mix_out.T, qkv_proj.reshape(shard_rows, -1)], axis=1
    )
    third_shard = jnp.concatenate([mlp_up, mlp_down.T, att_out.T], axis=1)
    early_pieces = [early_shard] + permute_three([early_shard] * 3, 4, ranks)
    first_stack = jnp.concatenate([piece[:, :first_cols] for piece in early_pieces], axis=0)
    first_own = jnp.concatenate(
        [first_stack] + permute_three([first_stack] * 3, 1, ranks), axis=0
    )
    first_other = swap_cores(first_own)
    third_shard = hold(third_shard, first_own)
    third_z = [third_shard] + permute_three([third_shard] * 3, 4, ranks)
    second_stack = jnp.concatenate([piece[:, first_cols:] for piece in early_pieces], axis=0)
    second_pieces = [second_stack] + permute_three([second_stack] * 3, 1, ranks)

    par_own = jnp.concatenate(
        [
            conv_taps,
            conv_bias[None],
            skip_gain[None],
            jnp.pad(rate_bias, (RATE_AT, HCH - RATE_AT - HPG))[None],
            jnp.pad(decay_log, (RATE_AT, HCH - RATE_AT - HPG))[None],
        ],
        axis=0,
    )
    par_other = swap_cores(par_own)
    gains = jnp.stack([mix_gain, att_gain, mlp_gain])

    channels = 2 * HCH
    (
        ext_rows, normed_one, x_in, conv_sum, gate_in, state_rate, cum_wide, inner_y,
        local_state, msg, deal_low, gains,
    ) = run_kernel(
        in_kernel,
        [
            ((2 * EXT, width), bf16),
            ((2 * EXT, width), bf16),
            ((2 * EXT, channels), bf16),
            ((ROWS, channels), f32),
            ((ROWS, channels), f32),
            ((ROWS, 2 * LANES), f32),
            ((ROWS, channels), f32),
            ((ROWS, channels), f32),
            ((2, 2, NSTATE, HCH), f32),
            ((slots_n, 16, LANES), f32),
            ((width, width), bf16),
            ((3, width), f32),
        ],
        2,
        (ids, order, tokens, gains, first_own, first_other, par_own, par_other),
        (pltpu.VMEM((2 * EXT, HCH), f32), pltpu.VMEM((2, TILE_ROWS, LANES), f32)),
    )

    states = exchange(hold(msg, *second_pieces[1:3]), both)
    third_stack = stack_pieces(third_z, 0, third_cols, (states,))
    third_pieces = [third_stack] + permute_three([third_stack] * 3, 1, ranks)
    second_own = stack_pieces(second_pieces, 0, second_cols, (states, *third_z[1:]))
    second_other = swap_cores(second_own)
    (incoming,) = run_kernel(
        forward_scan_kernel,
        [((slots_n, 8, LANES), f32)],
        2,
        (ids, order, states),
        slots_scratch,
        after=[second_pieces[3], third_stack],
    )
    incoming = exchange(incoming, both)

    full_y, gated, hidden_one, normed_two, msg = run_kernel(
        mix_kernel,
        [
            ((ROWS, channels), f32),
            ((ROWS, channels), bf16),
            ((ROWS, width), f32),
            ((ROWS, width), bf16),
            ((ranks, QKV_ROWS, LANES), bf16),
        ],
        1,
        (
            ids, ext_rows, incoming, state_rate, cum_wide, inner_y, conv_sum, gate_in,
            par_own, par_other, second_own, second_other, gains,
        ),
    )
    att_rows = ranks * HALF
    qkv_scratch = (
        pltpu.VMEM((att_rows, AHEAD_DIM), bf16),
        pltpu.VMEM((2, att_rows, AHEAD_DIM), bf16),
        pltpu.VMEM((2, att_rows, AHEAD_DIM), bf16),
    )
    qkv_own = exchange(hold(msg, *third_pieces[1:3]), "seq")
    qkv_other = swap_cores(qkv_own)
    attended, log_total = run_kernel(
        attend_kernel,
        [((ranks, HALF // 2, LANES), bf16), ((att_rows, 1), f32)],
        2,
        (ids, order, qkv_own, qkv_other),
        qkv_scratch,
    )
    third_own = stack_pieces(third_pieces, 0, third_cols, (attended,))
    third_other = swap_cores(third_own)
    attended = exchange(attended, "seq")

    pack_cols = 3328
    (
        down_rows, hidden_two, cot_both, mine, theirs, two_grad, mlpgain_part, msg,
    ) = run_kernel(
        mlp_kernel,
        [
            ((ROWS, width), f32),
            ((ROWS, width), f32),
            ((2 * ROWS, width), bf16),
            ((ROWS, pack_cols), bf16),
            ((ROWS, pack_cols), bf16),
            ((ROWS, width), f32),
            ((1, width), f32),
            ((ranks, HALF // 2, LANES), bf16),
        ],
        1,
        (ids, attended, hidden_one, cotangent, deal_low, gains, third_own, third_other),
        (pltpu.VMEM((2, ROWS, 256), bf16), pltpu.VMEM((2, ROWS, width), f32)),
    )
    att_grad = exchange(msg, "seq")
    third_grads = run_kernel(
        third_grad_kernel,
        [((width // 4, third_cols), bf16)] * 4,
        0,
        (mine, swap_cores(theirs), cot_both),
    )
    mine, theirs = run_kernel(
        attend_back_kernel,
        [((ranks, QKV_ROWS, LANES), f32), ((ranks, QKV_ROWS, LANES), bf16)],
        2,
        (ids, order, qkv_own, qkv_other, att_grad, log_total),
        qkv_scratch
        + (
            pltpu.VMEM((att_rows, AHEAD_DIM), f32),
            pltpu.VMEM((2, att_rows, AHEAD_DIM), f32),
            pltpu.VMEM((2, att_rows, AHEAD_DIM), f32),
        ),
        after=third_grads[:1],
    )
    qkv_grad = (mine + swap_cores(theirs).astype(f32)).astype(bf16)
    qkv_grad = exchange(qkv_grad, "seq")
    third_moved = permute_three(third_grads[1:], 1, ranks)

    mine, theirs, y_grad, gate_grad, one_grad, attgain_part, skip_part, msg = run_kernel(
        mix_back_kernel,
        [
            ((ROWS, pack_cols), bf16),
            ((ROWS, pack_cols), bf16),
            ((ROWS, channels), f32),
            ((ROWS, channels), bf16),
            ((ROWS, width), f32),
            ((1, width), f32),
            ((1, channels), f32),
            ((slots_n, 8, LANES), f32),
        ],
        1,
        (
            ids, qkv_grad, normed_one, normed_two, hidden_one, two_grad, gains, second_own,
            second_other, gated, gate_in, full_y, conv_sum, cum_wide, state_rate,
        ),
        (pltpu.VMEM((ROWS, 768), bf16),),
        after=third_moved[:2],
    )
    back_states = exchange(msg, both)
    second_grads = run_kernel(
        second_grad_kernel,
        [((width // 4, second_cols + HCH), bf16)] * 4,
        0,
        (mine, swap_cores(theirs)),
    )
    (later,) = run_kernel(
        backward_scan_kernel,
        [((slots_n, 8, LANES), f32)],
        2,
        (ids, order, states, back_states),
        slots_scratch,
        after=[second_grads[0], third_moved[2]],
    )
    third_parts = sum_pieces(third_grads[0], third_moved, (later,))
    third_moved = permute_three(third_parts[1:], 4, ranks)
    second_moved = permute_three(second_grads[1:], 1, ranks)
    later = exchange(later, both)

    grad_cols = HCH + LANES
    pack_shape = (2 * EXT + SMALL_ROWS, grad_cols + width)
    mine, theirs, tokens_grad = run_kernel(
        in_back_kernel,
        [(pack_shape, bf16), (pack_shape, bf16), ((ROWS, width), f32)],
        1,
        (
            ids, later, incoming, local_state, state_rate, cum_wide, conv_sum, x_in, y_grad,
            gate_grad, normed_one, ext_rows, gains, one_grad, first_own, first_other,
            par_own, par_other, deal_low, skip_part, attgain_part, mlpgain_part,
        ),
        (
            pltpu.VMEM((2 * EXT, HCH), f32),
            pltpu.VMEM((2, EXT + TAIL, HCH), f32),
            pltpu.VMEM((2 * EXT, LANES), bf16),
            pltpu.VMEM((2 * EXT, HCH), bf16),
        ),
        after=[third_parts[0]],
    )
    last_msg, *first_grads = run_kernel(
        first_grad_kernel,
        [((ranks, SMALL_ROWS, 2 * HCH), bf16)] + [((width // 4, grad_cols), bf16)] * 4,
        1,
        (ids, mine, swap_cores(theirs)),
    )
    first_moved = permute_three(first_grads[1:], 1, ranks)
    last = exchange(last_msg, "seq")
    early_parts = run_kernel(
        sum_both_kernel,
        [((width // 16, grad_cols + second_cols + HCH), bf16)] * 4,
        0,
        [first_grads[0]] + first_moved + [second_grads[0]] + second_moved,
    )
    third_total = sum_last(third_parts[0], third_moved)
    early_total = sum_last(early_parts[0], permute_three(early_parts[1:], 4, ranks))
    first_total, second_total = early_total[:, :grad_cols], early_total[:, grad_cols:]

    my_blocks = jnp.sum(
        jnp.where(jnp.arange(slots_n)[None, :] == my_slot, order, 0), axis=1
    )
    last = last.astype(f32)
    small_total = jnp.sum(last[:, 0:10, 0:HCH], axis=0)
    next_tails = last[:, 0:12, HCH:].reshape(ranks, 2, 2, CONV - 1, width).transpose(2, 0, 1, 3, 4)
    next_tails = next_tails.reshape(2, slots_n, CONV - 1, width)
    pick_next = (order == my_blocks[:, None] + 1).astype(f32)
    tail_add = jnp.sum(pick_next[:, :, None, None] * next_tails, axis=1)
    tokens_grad = tokens_grad.reshape(2, HALF, width)
    tokens_grad = jnp.concatenate(
        [tokens_grad[:, : HALF - (CONV - 1)], tokens_grad[:, HALF - (CONV - 1) :] + tail_add],
        axis=1,
    ).astype(bf16)
    layer_rows = nt((hidden_two + down_rows).astype(bf16), deal_low).astype(bf16)
    outs = jnp.stack([layer_rows.reshape(2, HALF, width), tokens_grad])
    outs_other = swap_cores(outs)
    outs = jnp.where(
        core == 0,
        jnp.concatenate([outs, outs_other], axis=2),
        jnp.concatenate([outs_other, outs], axis=2),
    )
    return (
        outs[0],
        outs[1],
        small_total[7],
        first_total[:, 0:HCH],
        second_total[:, second_cols:],
        first_total[:, HCH : HCH + 32],
        first_total[:, HCH + RATE_AT : HCH + RATE_AT + HPG],
        small_total[6, RATE_AT : RATE_AT + HPG],
        small_total[6, LANES + RATE_AT : LANES + RATE_AT + HPG],
        small_total[0:4],
        small_total[4],
        small_total[5],
        second_total[:, 0:HCH].T,
        small_total[8],
        second_total[:, HCH : HCH + 768].reshape(qkv_proj.shape),
        third_total[:, 2048:2304].T,
        small_total[9],
        third_total[:, 0:1024],
        third_total[:, 1024:2048].T,
    )


def layer(*args):
    tokens, lengths = args[0], args[2]
    fits = lax.axis_size("seq") == 16 and lax.axis_size("head") == 2
    fits = fits and lengths.shape == (2, 1) and tokens.shape[1] == ROWS
    return dealt_device(*args) if fits else on_device(*args)


def solution(mesh):
    return jax.shard_map(
        layer,
        mesh=mesh,
        in_specs=(
            P(None, "seq", None),
            P(None, "seq", None),
            P(),
            P(),
            P(),
            P("seq", "head"),
            P("seq", "head"),
            P("seq", "head"),
            P("seq", "head"),
            P("head"),
            P("head"),
            P(None, "head"),
            P("head"),
            P("head"),
            P("head", "seq"),
            P(),
            P("seq", None, "head"),
            P("head", "seq"),
            P(),
            P("seq", "head"),
            P("head", "seq"),
        ),
        out_specs=(
            P(None, "seq", None),
            P(None, "seq", None),
            P(),
            P("seq", "head"),
            P("seq", "head"),
            P("seq", "head"),
            P("seq", "head"),
            P("head"),
            P("head"),
            P(None, "head"),
            P("head"),
            P("head"),
            P("head", "seq"),
            P(),
            P("seq", None, "head"),
            P("head", "seq"),
            P(),
            P("seq", "head"),
            P("head", "seq"),
        ),
        check_vma=False,
    )
```

```python
import functools
import math

import jax
import jax.numpy as jnp
from jax import lax
from jax.experimental import pallas as pl
from jax.experimental.pallas import tpu as pltpu
from jax.sharding import PartitionSpec as P

NSTATE = 16
CONV = 4
AHEAD_DIM = 64


epsilon = 1e-05
highest = lax.Precision.HIGHEST


def rms_norm(values, gain_row):
    return (
        values * lax.rsqrt(jnp.mean(values * values, axis=-1, keepdims=True) + epsilon) * gain_row
    )


def gelu_tanh(values):
    return jax.nn.gelu(values, approximate=True)


def segment_of(position, seq_ends):
    bounds = seq_ends[:-1]
    return jnp.sum((jnp.asarray(position)[..., None] >= bounds).astype(jnp.int32), axis=-1)


def tap_valid(position, lag_rows, seq_ends):
    source = position - lag_rows
    return (
        (source >= 0) & (segment_of(source, seq_ends) == segment_of(position, seq_ends))
    ).astype(jnp.float32)


def slot_position(order_row, row_ids, half_rows):
    slot = row_ids // half_rows
    slot_table = jnp.arange(order_row.shape[0], dtype=jnp.int32)
    block = jnp.sum(jnp.where(slot[:, None] == slot_table[None, :], order_row[None, :], 0), axis=1)
    return block * half_rows + row_ids % half_rows


def stream_slots(order_row):
    slot_table = jnp.arange(order_row.shape[0], dtype=jnp.int32)
    return jnp.sum(
        jnp.where(order_row[None, :] == slot_table[:, None], slot_table[None, :], 0), axis=1
    )


def matmul(left_op, right_op):
    return jnp.dot(left_op, right_op, preferred_element_type=jnp.float32)


def transposed(left_op, right_op):
    return lax.dot_general(
        left_op, right_op, (((1,), (1,)), ((), ())), preferred_element_type=jnp.float32
    )


def left_gram(left_op, right_op):
    return lax.dot_general(
        left_op, right_op, (((0,), (0,)), ((), ())), preferred_element_type=jnp.float32
    )


def transposed_exact(left_op, right_op):
    return lax.dot_general(
        left_op,
        right_op,
        (((1,), (1,)), ((), ())),
        preferred_element_type=jnp.float32,
        precision=highest,
    )


def left_gram_exact(left_op, right_op):
    return lax.dot_general(
        left_op,
        right_op,
        (((0,), (0,)), ((), ())),
        preferred_element_type=jnp.float32,
        precision=highest,
    )


def keep_same(current):
    return current


def head_total(partial_rows):
    return lax.psum(partial_rows, "head")


def collect(in_value, in_gate, in_state, in_rate, qkv_proj, mlp_up, mix_out, att_out, mlp_down):
    return (
        lax.all_gather(in_value, "seq", axis=0, tiled=True),
        lax.all_gather(in_gate, "seq", axis=0, tiled=True),
        lax.all_gather(in_state, "seq", axis=0, tiled=True),
        lax.all_gather(in_rate, "seq", axis=0, tiled=True),
        lax.all_gather(qkv_proj, "seq", axis=0, tiled=True),
        lax.all_gather(mlp_up, "seq", axis=0, tiled=True),
        lax.all_gather(mix_out, "seq", axis=1, tiled=True),
        lax.all_gather(att_out, "seq", axis=1, tiled=True),
        lax.all_gather(mlp_down, "seq", axis=1, tiled=True),
    )


def reduce_grads(grad_parts):
    return (
        lax.psum_scatter(grad_parts[0], "seq", scatter_dimension=0, tiled=True),
        lax.psum_scatter(grad_parts[1], "seq", scatter_dimension=0, tiled=True),
        lax.psum_scatter(grad_parts[2], "seq", scatter_dimension=0, tiled=True),
        lax.psum_scatter(grad_parts[3], "seq", scatter_dimension=0, tiled=True),
        lax.psum_scatter(grad_parts[4], "seq", scatter_dimension=0, tiled=True),
        lax.psum_scatter(grad_parts[5], "seq", scatter_dimension=0, tiled=True),
        lax.psum_scatter(grad_parts[6], "seq", scatter_dimension=1, tiled=True),
        lax.psum_scatter(grad_parts[7], "seq", scatter_dimension=1, tiled=True),
        lax.psum_scatter(grad_parts[8], "seq", scatter_dimension=1, tiled=True),
    )


def fold_blocks(fold_fn, initial, arrays, block_rows):
    blocks_n = arrays[0].shape[0] // block_rows

    def one_step(block_index, current):
        offset = block_index * block_rows
        shards = tuple(
            (lax.dynamic_slice_in_dim(member, offset, block_rows, 0) for member in arrays)
        )
        return fold_fn(current, shards, offset)

    return lax.fori_loop(0, blocks_n, one_step, initial)


def add_parts(left_op, right_op):
    if left_op is None:
        return right_op
    return tuple((first_part + second_part for first_part, second_part in zip(left_op, right_op)))


def combine_state(earlier, later):
    return (earlier[0] * later[0], later[0][..., None, None] * earlier[1] + later[1])


def attention_probs(
    query_rows, key_rows, query_pos, key_pos, query_seg, key_seg, log_total, scaling
):
    allowed = ((key_pos[None, :] <= query_pos[:, None]) & (key_seg[None, :] == query_seg[:, None]))[
        :, None, :
    ]
    scores = (
        jnp.einsum("qhd,khd->qhk", query_rows, key_rows, preferred_element_type=jnp.float32)
        * scaling
    )
    return jnp.where(allowed, jnp.exp(jnp.where(allowed, scores - log_total[:, :, None], 0.0)), 0.0)


def scan_terms(mixed_x, step_size, bc_rows, decay_log, segment, seg_before):
    rows_n, heads_n = step_size.shape
    log_decay = -step_size * jnp.exp(decay_log)
    cumulative = jnp.cumsum(log_decay, axis=0)
    driving = step_size[:, :, None] * mixed_x.reshape(rows_n, heads_n, -1)
    tail_weight = (
        jnp.exp(cumulative[-1][None, :] - cumulative)
        * (segment == segment[-1]).astype(jnp.float32)[:, None]
    )
    local_state = jnp.einsum(
        "sh,shp,sn->hpn", tail_weight, driving, bc_rows[:, :NSTATE], precision=highest
    )
    through = jnp.exp(cumulative[-1]) * (segment[-1] == seg_before).astype(jnp.float32)
    return (cumulative, driving, through, local_state)


def scan_output(cumulative, driving, bc_rows, incoming, segment, seg_before):
    rows_n = cumulative.shape[0]
    row_ids = jnp.arange(rows_n, dtype=jnp.int32)
    allowed = ((row_ids[:, None] >= row_ids[None, :]) & (segment[:, None] == segment[None, :]))[
        :, :, None
    ]
    decays = jnp.where(
        allowed,
        jnp.exp(jnp.where(allowed, cumulative[:, None, :] - cumulative[None, :, :], 0.0)),
        0.0,
    )
    inner_cb = jnp.dot(bc_rows[:, NSTATE:], bc_rows[:, :NSTATE].T, precision=highest)
    output = jnp.einsum("tsh,shp->thp", decays * inner_cb[:, :, None], driving, precision=highest)
    inflow = jnp.exp(cumulative) * (segment == seg_before).astype(jnp.float32)[:, None]
    output = output + inflow[:, :, None] * jnp.einsum(
        "tn,hpn->thp", bc_rows[:, NSTATE:], incoming, precision=highest
    )
    return output.reshape(rows_n, -1)


def scan_whole(mixed_x, step_size, bc_rows, decay_log, incoming, segment, seg_before):
    cumulative, driving, through, local_state = scan_terms(
        mixed_x, step_size, bc_rows, decay_log, segment, seg_before
    )
    output = scan_output(cumulative, driving, bc_rows, incoming, segment, seg_before)
    return (output, through[:, None, None] * incoming + local_state)


def on_device(
    tokens,
    cotangent,
    lengths,
    order,
    mix_gain,
    in_value,
    in_gate,
    in_state,
    in_rate,
    rate_bias,
    decay_log,
    conv_taps,
    conv_bias,
    skip_gain,
    mix_out,
    att_gain,
    qkv_proj,
    att_out,
    mlp_gain,
    mlp_up,
    mlp_down,
):
    rows_n = tokens.shape[1]
    half_rows = rows_n // 2
    slots_n = 2 * lax.axis_size("seq")
    my_slot = 2 * lax.axis_index("seq")
    total_rows = rows_n * lax.axis_size("seq")
    block_rows = math.gcd(total_rows, 1024)
    scaling = AHEAD_DIM ** (-0.5)
    local_ids = jnp.arange(half_rows, dtype=jnp.int32)
    ext_ids = jnp.arange(half_rows + CONV - 1, dtype=jnp.int32)
    terms_all = jax.vmap(scan_terms, in_axes=(0, 0, 0, None, 0, 0))
    output_all = jax.vmap(scan_output, in_axes=(0, 0, 0, 0, 0, 0))
    whole_all = jax.vmap(scan_whole, in_axes=(0, 0, 0, None, 0, 0, 0))
    layer_list = []
    input_list = []
    big_sums = None
    small_sums = None
    for batch_index in range(tokens.shape[0]):
        (
            value_full,
            gate_full,
            state_full,
            rate_full,
            qkv_full,
            up_full,
            mixout_full,
            attout_full,
            down_full,
        ) = collect(
            in_value, in_gate, in_state, in_rate, qkv_proj, mlp_up, mix_out, att_out, mlp_down
        )
        seq_ends = jnp.cumsum(lengths[batch_index])
        order_row = order[batch_index]
        inverse = stream_slots(order_row)
        my_blocks = lax.dynamic_slice_in_dim(order_row, my_slot, 2)
        position = (my_blocks[:, None] * half_rows + local_ids[None, :]).reshape(rows_n)
        segment = segment_of(position, seq_ends)
        seg_blocks = segment.reshape(2, half_rows)
        seg_before = segment_of(my_blocks * half_rows - 1, seq_ends)
        hidden_in = tokens[batch_index].astype(jnp.float32)
        normed_one = rms_norm(hidden_in, mix_gain).astype(jnp.bfloat16)
        x_in = matmul(normed_one, value_full).astype(jnp.bfloat16)
        gate_in = matmul(normed_one, gate_full)
        bc_rows = matmul(normed_one, state_full)
        rate_in = matmul(normed_one, rate_full)
        step_size = jax.nn.softplus(rate_in + rate_bias)
        x_blocks = x_in.reshape(2, half_rows, -1)
        all_tails = lax.all_gather(x_blocks[:, half_rows - (CONV - 1) :], "seq", axis=0, tiled=True)
        pick_prev = (order_row[None, :] == my_blocks[:, None] - 1).astype(jnp.bfloat16)
        edge_rows = jnp.einsum(
            "bs,srd->brd", pick_prev, all_tails, preferred_element_type=jnp.float32
        )
        extended = jnp.concatenate([edge_rows, x_blocks.astype(jnp.float32)], axis=1)
        valid_taps = [
            tap_valid(position, CONV - 1 - tap_index, seq_ends).reshape(2, half_rows)
            for tap_index in range(CONV)
        ]
        conv_blocks = jnp.zeros(x_blocks.shape, jnp.float32) + conv_bias
        for tap_index in range(CONV):
            conv_blocks = (
                conv_blocks
                + conv_taps[tap_index]
                * extended[:, tap_index : tap_index + half_rows]
                * valid_taps[tap_index][:, :, None]
            )
        conv_sum = conv_blocks.reshape(rows_n, -1)
        mixed_x = jax.nn.silu(conv_sum)
        mixed_b = mixed_x.reshape(2, half_rows, -1)
        step_b = step_size.reshape(2, half_rows, -1)
        bc_b = bc_rows.reshape(2, half_rows, -1)
        cumulative, driving, through, local_state = terms_all(
            mixed_b, step_b, bc_b, decay_log, seg_blocks, seg_before
        )
        all_through, all_state = (
            lax.all_gather(through, "seq", axis=0, tiled=True),
            lax.all_gather(local_state, "seq", axis=0, tiled=True),
        )
        through_stream = all_through[inverse]
        state_stream = all_state[inverse]
        acc_through, acc_state = lax.associative_scan(
            combine_state, (through_stream, state_stream), axis=0
        )
        before = my_blocks - 1
        incoming = (
            acc_state[jnp.maximum(before, 0)]
            * (before >= 0).astype(jnp.float32)[:, None, None, None]
        )
        ssm_out = output_all(cumulative, driving, bc_b, incoming, seg_blocks, seg_before).reshape(
            rows_n, -1
        )
        full_y = ssm_out + skip_gain * mixed_x
        gating = jax.nn.silu(gate_in)
        gated_low = (full_y * gating).astype(jnp.bfloat16)
        hidden_one = hidden_in + head_total(matmul(gated_low, mixout_full))
        normed_two = rms_norm(hidden_one, att_gain).astype(jnp.bfloat16)
        qkv_rows = jnp.einsum(
            "rd,dcn->rcn", normed_two, qkv_full, preferred_element_type=jnp.float32
        ).astype(jnp.bfloat16)
        heads_att = qkv_rows.shape[2] // AHEAD_DIM
        queries = qkv_rows[:, 0].reshape(rows_n, heads_att, AHEAD_DIM)
        key_heads = qkv_rows[:, 1].reshape(rows_n, heads_att, AHEAD_DIM)
        value_heads = qkv_rows[:, 2].reshape(rows_n, heads_att, AHEAD_DIM)

        def forward_fold(totals, shards, offset):
            key_rows, value_rows = shards
            key_pos = slot_position(
                order_row, offset + jnp.arange(key_rows.shape[0], dtype=jnp.int32), half_rows
            )
            allowed = (
                (key_pos[None, :] <= position[:, None])
                & (segment_of(key_pos, seq_ends)[None, :] == segment[:, None])
            )[:, None, :]

            def forward_compute(current):
                running_max, running_sum, weighted = current
                scores = (
                    jnp.einsum(
                        "qhd,khd->qhk", queries, key_rows, preferred_element_type=jnp.float32
                    )
                    * scaling
                )
                scores = jnp.where(allowed, scores, -jnp.inf)
                new_max = jnp.maximum(running_max, jnp.max(scores, axis=-1))
                safe_max = jnp.where(new_max == -jnp.inf, 0.0, new_max)
                exp_scores = jnp.exp(scores - safe_max[:, :, None])
                factor = jnp.exp(running_max - safe_max)
                running_sum = running_sum * factor + jnp.sum(exp_scores, axis=-1)
                weighted = weighted * factor[:, :, None] + jnp.einsum(
                    "qhk,khd->qhd",
                    exp_scores.astype(jnp.bfloat16),
                    value_rows,
                    preferred_element_type=jnp.float32,
                )
                return (new_max, running_sum, weighted)

            return lax.cond(jnp.any(allowed), forward_compute, keep_same, totals)

        init_fwd = (
            jnp.full((rows_n, heads_att), -jnp.inf, jnp.float32),
            jnp.zeros((rows_n, heads_att), jnp.float32),
            jnp.zeros((rows_n, heads_att, AHEAD_DIM), jnp.float32),
        )
        all_keys, all_values = (
            lax.all_gather(key_heads, "seq", axis=0, tiled=True),
            lax.all_gather(value_heads, "seq", axis=0, tiled=True),
        )
        running_max, running_sum, weighted = fold_blocks(
            forward_fold, init_fwd, (all_keys, all_values), block_rows
        )
        attended = weighted / running_sum[:, :, None]
        log_total = running_max + jnp.log(running_sum)
        att_low = attended.reshape(rows_n, -1).astype(jnp.bfloat16)
        hidden_two = hidden_one + head_total(matmul(att_low, attout_full))
        normed_three = rms_norm(hidden_two, mlp_gain).astype(jnp.bfloat16)
        up_rows = matmul(normed_three, up_full)
        act_low = gelu_tanh(up_rows).astype(jnp.bfloat16)
        layer_rows = hidden_two + head_total(matmul(act_low, down_full))
        layer_list.append(layer_rows.astype(jnp.bfloat16))
        cot_low = cotangent[batch_index]
        down_wgrad = left_gram(act_low, cot_low)
        act_grad = transposed(cot_low, down_full)
        up_grad = jax.vjp(gelu_tanh, up_rows)[1](act_grad)[0].astype(jnp.bfloat16)
        up_wgrad = left_gram(normed_three, up_grad)
        three_grad = head_total(transposed(up_grad, up_full))
        hidden_part, mlpgain_part = jax.vjp(rms_norm, hidden_two, mlp_gain)[1](three_grad)
        hidden_two_grad = cot_low.astype(jnp.float32) + hidden_part
        branch_low = hidden_two_grad.astype(jnp.bfloat16)
        attout_wgrad = left_gram(att_low, branch_low)
        attended_grad = (
            transposed(branch_low, attout_full)
            .astype(jnp.bfloat16)
            .reshape(rows_n, heads_att, AHEAD_DIM)
        )
        delta_rows = jnp.sum(attended_grad.astype(jnp.float32) * attended, axis=-1)

        def query_fold(totals, shards, offset):
            key_rows, value_rows = shards
            key_pos = slot_position(
                order_row, offset + jnp.arange(key_rows.shape[0], dtype=jnp.int32), half_rows
            )
            key_seg = segment_of(key_pos, seq_ends)
            any_allowed = jnp.any(
                (key_pos[None, :] <= position[:, None]) & (key_seg[None, :] == segment[:, None])
            )

            def query_compute(current):
                probabilities = attention_probs(
                    queries, key_rows, position, key_pos, segment, key_seg, log_total, scaling
                )
                prob_grad = jnp.einsum(
                    "qhd,khd->qhk", attended_grad, value_rows, preferred_element_type=jnp.float32
                )
                score_grad = (probabilities * (prob_grad - delta_rows[:, :, None])).astype(
                    jnp.bfloat16
                )
                return current + jnp.einsum(
                    "qhk,khd->qhd", score_grad, key_rows, preferred_element_type=jnp.float32
                )

            return lax.cond(any_allowed, query_compute, keep_same, totals)

        zero_heads = jnp.zeros((rows_n, heads_att, AHEAD_DIM), jnp.float32)
        query_sum = fold_blocks(query_fold, zero_heads, (all_keys, all_values), block_rows)
        query_rows = lax.all_gather(queries.astype(jnp.float32), "seq", axis=0, tiled=True)
        grad_rows = lax.all_gather(attended_grad.astype(jnp.float32), "seq", axis=0, tiled=True)
        log_rows = lax.all_gather(log_total, "seq", axis=0, tiled=True)
        delta_part = lax.all_gather(delta_rows, "seq", axis=0, tiled=True)
        query_pos = slot_position(
            order_row, jnp.arange(query_rows.shape[0], dtype=jnp.int32), half_rows
        )
        query_seg = segment_of(query_pos, seq_ends)
        key_any_allowed = jnp.any(
            (position[None, :] <= query_pos[:, None]) & (segment[None, :] == query_seg[:, None])
        )

        def key_compute(current):
            query_low = query_rows.astype(jnp.bfloat16)
            grad_low = grad_rows.astype(jnp.bfloat16)
            probabilities = attention_probs(
                query_low, key_heads, query_pos, position, query_seg, segment, log_rows, scaling
            )
            value_grad = jnp.einsum(
                "qhk,qhd->khd",
                probabilities.astype(jnp.bfloat16),
                grad_low,
                preferred_element_type=jnp.float32,
            )
            prob_grad = jnp.einsum(
                "qhd,khd->qhk", grad_low, value_heads, preferred_element_type=jnp.float32
            )
            score_grad = (probabilities * (prob_grad - delta_part[:, :, None])).astype(jnp.bfloat16)
            key_grad = jnp.einsum(
                "qhk,qhd->khd", score_grad, query_low, preferred_element_type=jnp.float32
            )
            return (key_grad, value_grad)

        key_sum, value_sum = lax.cond(
            key_any_allowed, key_compute, keep_same, (zero_heads, zero_heads)
        )
        qkv_grad = jnp.stack(
            [
                (query_sum * scaling).astype(jnp.bfloat16),
                (key_sum * scaling).astype(jnp.bfloat16),
                value_sum.astype(jnp.bfloat16),
            ],
            axis=1,
        ).reshape(rows_n, 3, -1)
        qkv_wgrad = jnp.einsum(
            "rd,rcn->dcn", normed_two, qkv_grad, preferred_element_type=jnp.float32
        )
        two_grad = head_total(
            jnp.einsum("rcn,dcn->rd", qkv_grad, qkv_full, preferred_element_type=jnp.float32)
        )
        hidden_part, attgain_part = jax.vjp(rms_norm, hidden_one, att_gain)[1](two_grad)
        hidden_one_grad = hidden_two_grad + hidden_part
        mix_low = hidden_one_grad.astype(jnp.bfloat16)
        mixout_wgrad = left_gram(gated_low, mix_low)
        gated_grad = transposed(mix_low, mixout_full)
        y_grad = gated_grad * gating
        gate_grad = jax.vjp(jax.nn.silu, gate_in)[1](gated_grad * full_y)[0].astype(jnp.bfloat16)
        skip_part = jnp.sum(y_grad * mixed_x, axis=0)
        heads_mix = step_size.shape[1]
        y_blocks = y_grad.reshape(2, half_rows, -1)
        inflow = (
            jnp.exp(cumulative)
            * (seg_blocks == seg_before[:, None]).astype(jnp.float32)[:, :, None]
        )
        back_local = jnp.einsum(
            "bth,bthp,btn->bhpn",
            inflow,
            y_blocks.reshape(2, half_rows, heads_mix, -1),
            bc_b[:, :, NSTATE:],
            precision=highest,
        )
        all_back = lax.all_gather(back_local, "seq", axis=0, tiled=True)
        back_stream = all_back[inverse]
        rev_through, rev_state = lax.associative_scan(
            combine_state, (through_stream[::-1], back_stream[::-1]), axis=0
        )
        after_index = slots_n - 2 - my_blocks
        outgoing_grad = (
            rev_state[jnp.maximum(after_index, 0)]
            * (after_index >= 0).astype(jnp.float32)[:, None, None, None]
        )

        def scan_call(mixed_arg, step_arg, bc_arg, decay_arg, incoming_arg):
            return whole_all(
                mixed_arg, step_arg, bc_arg, decay_arg, incoming_arg, seg_blocks, seg_before
            )

        scan_pull = jax.vjp(scan_call, mixed_b, step_b, bc_b, decay_log, incoming)[1]
        x_scan_grad, step_grad, bc_grad, decay_part, incoming_grad = scan_pull(
            (y_blocks, outgoing_grad)
        )
        mixed_grad = y_grad * skip_gain + x_scan_grad.reshape(rows_n, -1)
        conv_grad = jax.vjp(jax.nn.silu, conv_sum)[1](mixed_grad)[0]
        conv_grad_b = conv_grad.reshape(2, half_rows, -1)
        convbias_part = jnp.sum(conv_grad, axis=0)
        convtaps_part = jnp.stack(
            [
                jnp.sum(
                    extended[:, tap_index : tap_index + half_rows]
                    * valid_taps[tap_index][:, :, None]
                    * conv_grad_b,
                    axis=(0, 1),
                )
                for tap_index in range(CONV)
            ]
        )
        all_heads = lax.all_gather(conv_grad_b[:, : CONV - 1], "seq", axis=0, tiled=True)
        pick_next = (order_row[None, :] == my_blocks[:, None] + 1).astype(jnp.float32)
        next_rows = jnp.einsum("bs,srd->brd", pick_next, all_heads, precision=highest)
        grad_ext = jnp.concatenate([conv_grad_b, next_rows], axis=1)
        position_ext = (my_blocks[:, None] * half_rows + ext_ids[None, :]).reshape(-1)
        x_blocks_grad = jnp.zeros(conv_grad_b.shape, jnp.float32)
        for tap_index in range(CONV):
            lag_rows = CONV - 1 - tap_index
            masked_grad = (
                grad_ext
                * tap_valid(position_ext, lag_rows, seq_ends).reshape(2, half_rows + CONV - 1)[
                    :, :, None
                ]
            )
            x_blocks_grad = (
                x_blocks_grad
                + conv_taps[tap_index] * masked_grad[:, lag_rows : lag_rows + half_rows]
            )
        x_low = x_blocks_grad.reshape(rows_n, -1).astype(jnp.bfloat16)
        rate_grad = step_grad.reshape(rows_n, -1) * jax.nn.sigmoid(rate_in + rate_bias)
        ratebias_part = jnp.sum(rate_grad, axis=0)
        bc_flat = bc_grad.reshape(rows_n, -1)
        normed_wide = normed_one.astype(jnp.float32)
        value_wgrad = left_gram(normed_one, x_low)
        gate_wgrad = left_gram(normed_one, gate_grad)
        state_wgrad = left_gram_exact(normed_wide, bc_flat)
        rate_wgrad = left_gram_exact(normed_wide, rate_grad)
        one_grad = head_total(
            transposed(x_low, value_full)
            + transposed(gate_grad, gate_full)
            + transposed_exact(bc_flat, state_full.astype(jnp.float32))
            + transposed_exact(rate_grad, rate_full.astype(jnp.float32))
        )
        hidden_part, mixgain_part = jax.vjp(rms_norm, hidden_in, mix_gain)[1](one_grad)
        input_list.append((hidden_one_grad + hidden_part).astype(jnp.bfloat16))
        big_part = (
            value_wgrad,
            gate_wgrad,
            state_wgrad,
            rate_wgrad,
            qkv_wgrad,
            up_wgrad,
            mixout_wgrad,
            attout_wgrad,
            down_wgrad,
        )
        small_part = (
            mixgain_part,
            attgain_part,
            mlpgain_part,
            ratebias_part,
            decay_part,
            convtaps_part,
            convbias_part,
            skip_part,
        )
        big_part = reduce_grads(big_part)
        big_sums = add_parts(big_sums, big_part)
        small_sums = add_parts(small_sums, small_part)
    small_total = lax.psum(
        (
            small_sums[0],
            small_sums[1],
            small_sums[2],
            small_sums[3],
            small_sums[4],
            small_sums[5],
            small_sums[6],
            small_sums[7],
        ),
        "seq",
    )
    return (
        jnp.stack(layer_list),
        jnp.stack(input_list),
        small_total[0],
        big_sums[0],
        big_sums[1],
        big_sums[2],
        big_sums[3],
        small_total[3],
        small_total[4],
        small_total[5],
        small_total[6],
        small_total[7],
        big_sums[6],
        small_total[1],
        big_sums[4],
        big_sums[7],
        small_total[2],
        big_sums[5],
        big_sums[8],
    )


f32 = jnp.float32
bf16 = jnp.bfloat16
HALF = 64
TAIL = 16
EXT = HALF + TAIL
ROWS = 2 * HALF
HCH = 512
LANES = 128
RATE_AT = 32
HPG = 8
TILE_ROWS = 32
SMALL_ROWS = 16
TAIL_COLS = slice(2 * HCH + LANES, 2 * HCH + 2 * LANES)
QKV_ROWS = HALF + HALF // 2
VMEM_LIMIT = 56 * 1024 * 1024


def mm(left_op, right_op):
    return jnp.dot(left_op, right_op, preferred_element_type=f32)


def two_parts(values):
    coarse = values.astype(bf16)
    return coarse, (values - coarse.astype(f32)).astype(bf16)


def mm_onehot(values, onehot):
    coarse, fine = two_parts(values)
    return mm(coarse, onehot) + mm(fine, onehot)


def nt(left_op, right_op):
    return lax.dot_general(
        left_op, right_op, (((1,), (1,)), ((), ())), preferred_element_type=f32
    )


def nt_onehot(values, onehot):
    coarse, fine = two_parts(values)
    return nt(coarse, onehot) + nt(fine, onehot)


def onehot_mm(onehot, values):
    coarse, fine = two_parts(values)
    return mm(onehot, coarse) + mm(onehot, fine)


def tn(left_op, right_op):
    return lax.dot_general(
        left_op, right_op, (((0,), (0,)), ((), ())), preferred_element_type=f32
    )


def iota(shape, axis):
    return lax.broadcasted_iota(jnp.int32, shape, axis)


def sigmoid(values):
    return 1.0 / (1.0 + jnp.exp(-values))


def softplus(values):
    return jnp.maximum(values, 0.0) + jnp.log1p(jnp.exp(-jnp.abs(values)))


def rms_rows(values):
    return lax.rsqrt(jnp.mean(values * values, axis=-1, keepdims=True) + epsilon)


def rms_back(values, gain_row, grad):
    scale = rms_rows(values)
    inner = grad * gain_row
    dot = jnp.mean(inner * values, axis=-1, keepdims=True)
    part = scale * (inner - values * (scale * scale) * dot)
    return part, jnp.sum(grad * (values * scale), axis=0, keepdims=True)


def same_block(rows_idx, cols_idx):
    return (rows_idx // HALF) == (cols_idx // HALF)


def lower_mask():
    rows_idx, cols_idx = iota((ROWS, ROWS), 0), iota((ROWS, ROWS), 1)
    return same_block(rows_idx, cols_idx) & (rows_idx >= cols_idx)


def spread_matrix():
    return (iota((LANES, HCH), 0) - RATE_AT == iota((LANES, HCH), 1) // HALF).astype(f32).astype(bf16)


def per_block(values_0, values_1, shape):
    return jnp.where(iota(shape, 0) < HALF, values_0, values_1)


def step_terms(state_rate, params):
    lane = iota((1, LANES), 1)
    is_rate = (lane >= RATE_AT) & (lane < RATE_AT + HPG)
    shifted = state_rate + params[6:7, 0:LANES]
    step = jnp.where(is_rate, softplus(shifted), 0.0)
    rates = jnp.where(is_rate, jnp.exp(params[7:8, 0:LANES]), 0.0)
    log_decay = -step * rates
    cumulative = onehot_mm(lower_mask().astype(f32).astype(bf16), log_decay)
    return shifted, step, rates, log_decay, cumulative


def tail_decay(cum_wide):
    last = per_block(cum_wide[HALF - 1 : HALF], cum_wide[ROWS - 1 : ROWS], cum_wide.shape)
    return jnp.exp(last - cum_wide)


def decay_matrix(cumulative, cumulative_t, head, mask):
    at = RATE_AT + head
    gap = cumulative[:, at : at + 1] - cumulative_t[at : at + 1, :]
    return jnp.where(mask, jnp.exp(jnp.where(mask, gap, 0.0)), 0.0)


def silu_parts(values):
    gate = sigmoid(values)
    return values * gate, gate * (1.0 + values * (1.0 - gate))


def put_state(msg_ref, batch, group, state):
    for lane_block in range(4):
        for state_half in range(2):
            msg_ref[batch * 16 + group * 8 + lane_block * 2 + state_half, 0:8, :] = state[
                state_half * 8 : (state_half + 1) * 8,
                lane_block * LANES : (lane_block + 1) * LANES,
            ]


def get_state(msg_ref, batch, group):
    base = batch * 16 + group * 8
    return jnp.concatenate(
        [
            jnp.concatenate(
                [
                    msg_ref[base + lane_block * 2 + state_half, 0:8, :]
                    for lane_block in range(4)
                ],
                axis=1,
            )
            for state_half in range(2)
        ],
        axis=0,
    )


def my_rows(core):
    return pl.ds(pl.multiple_of(core * HALF, HALF), HALF)


def in_kernel(
    ids_ref, order_ref, tok_ref, gain_ref, own_ref, other_ref, par_own_ref, par_other_ref,
    ext_ref, normed_ref, x_ref, conv_ref, gate_ref, sr_ref, cum_ref, inner_ref, local_ref,
    msg_ref, deal_ref, gains_ref, x_scr, tail_scr,
):
    chip, core = ids_ref[0], ids_ref[1]
    width = tok_ref.shape[2]
    place = iota((1, width), 1)
    block = place // TILE_ROWS
    source = (chip ^ (block // 4 + 4 * (block % 4))) * TILE_ROWS + place % TILE_ROWS
    deal = (iota((width, width), 0) == source).astype(f32)
    deal_low = deal.astype(bf16)
    deal_ref[...] = deal_low
    gains = mm_onehot(gain_ref[...], deal_low)
    gains_ref[...] = gains
    ext_list = []
    for batch in range(2):
        my_block = order_ref[batch, 2 * chip + core]
        before = jnp.int32(0)
        for slot in range(order_ref.shape[1]):
            before = jnp.where(order_ref[batch, slot] == my_block - 1, slot, before)
        apart = chip ^ (before // 2)
        tail_at = ((apart % 4) * 4 + apart // 4) * TILE_ROWS
        rows = pl.ds(pl.multiple_of(tail_at, TILE_ROWS), TILE_ROWS)

        @pl.when(core == batch)
        def _():
            tail_scr[batch] = own_ref[rows, TAIL_COLS].astype(f32)

        @pl.when(core != batch)
        def _():
            tail_scr[batch] = other_ref[rows, TAIL_COLS].astype(f32)

        tile = jnp.where(before % 2 == 0, tail_scr[batch, 0:12], tail_scr[batch, 12:24])
        tile = jnp.where(my_block == 0, 0.0, tile)
        tails = [
            jnp.concatenate([tile[4 * k + j : 4 * k + j + 1] for j in range(4)], axis=1)
            for k in range(CONV - 1)
        ]
        lead = jnp.zeros((TAIL - (CONV - 1), width), f32)
        ext_list.append(jnp.concatenate([lead] + tails, axis=0).astype(bf16))
        ext_list.append(tok_ref[batch, my_rows(core), :])
    ext_rows = mm(jnp.concatenate(ext_list, axis=0), deal_low).astype(bf16)
    ext_ref[...] = ext_rows
    hidden = ext_rows.astype(f32)
    normed = (hidden * rms_rows(hidden) * gains[0:1]).astype(bf16)
    normed_ref[...] = normed
    real = jnp.concatenate([normed[TAIL:EXT], normed[EXT + TAIL :]], axis=0)
    mask = lower_mask()
    spread = spread_matrix()
    for half, (w_ref, par_ref) in enumerate(
        ((own_ref, par_own_ref), (other_ref, par_other_ref))
    ):
        at = half * HCH
        params = par_ref[...]
        x_low = mm(normed, w_ref[:, 0:HCH]).astype(bf16)
        x_ref[:, at : at + HCH] = x_low
        x_scr[...] = x_low.astype(f32)
        gate_ref[:, at : at + HCH] = mm(real, w_ref[:, HCH : 2 * HCH])
        state_rate = mm(real, w_ref[:, 2 * HCH : 2 * HCH + LANES])
        sr_ref[:, half * LANES : (half + 1) * LANES] = state_rate
        conv_list = []
        for batch in range(2):
            conv = jnp.zeros((HALF, HCH), f32) + params[4:5]
            for tap in range(CONV):
                first = batch * EXT + TAIL - (CONV - 1) + tap
                conv = conv + params[tap : tap + 1] * x_scr[first : first + HALF, :]
            conv_list.append(conv)
        conv = jnp.concatenate(conv_list, axis=0)
        conv_ref[:, at : at + HCH] = conv
        mixed = conv * sigmoid(conv)
        _, step, _, _, cumulative = step_terms(state_rate, params)
        cum_wide = mm_onehot(cumulative, spread)
        cum_ref[:, at : at + HCH] = cum_wide
        driving = mm_onehot(step, spread) * mixed
        weighted = (driving * tail_decay(cum_wide)).astype(bf16)
        driving = driving.astype(bf16)
        b_rows = state_rate[:, 0:NSTATE].astype(bf16)
        c_rows = state_rate[:, NSTATE : 2 * NSTATE].astype(bf16)
        group = half ^ core
        for batch in range(2):
            rows = slice(batch * HALF, (batch + 1) * HALF)
            state = tn(b_rows[rows], weighted[rows])
            local_ref[batch, half] = state
            last_row = (batch + 1) * HALF - 1
            total = jnp.broadcast_to(cum_wide[last_row : last_row + 1], (4, HCH))
            coarse = total.astype(bf16).astype(f32)
            for state_half in range(2):
                block = jnp.concatenate(
                    [state[state_half * 8 : (state_half + 1) * 8], coarse, total - coarse], axis=0
                ).astype(bf16)
                for lane_block in range(4):
                    msg_ref[batch * 16 + group * 8 + lane_block * 2 + state_half] = block[
                        :, lane_block * LANES : (lane_block + 1) * LANES
                    ]
        inner_cb = nt(c_rows, b_rows)
        cumulative_t = cumulative.T
        first_head = iota((ROWS, LANES), 1) < HALF
        for pair in range(4):
            pair_rows = driving[:, pair * LANES : (pair + 1) * LANES]
            parts = [
                mm(
                    (decay_matrix(cumulative, cumulative_t, 2 * pair + k, mask) * inner_cb).astype(
                        bf16
                    ),
                    pair_rows,
                )
                for k in range(2)
            ]
            inner_ref[:, at + pair * LANES : at + (pair + 1) * LANES] = jnp.where(
                first_head, parts[0], parts[1]
            )


def invert_order(ids_ref, order_ref, slots_scr):
    slots_n = order_ref.shape[1]
    batch = (2 * ids_ref[0] + ids_ref[1]) // (slots_n // 2)
    for slot in range(slots_n):
        slots_scr[order_ref[batch, slot]] = slot


def block_decay(block):
    return jnp.exp(block[8:9] + block[12:13])


def forward_scan_kernel(ids_ref, order_ref, in_ref, out_ref, slots_scr):
    invert_order(ids_ref, order_ref, slots_scr)
    state = jnp.zeros((8, LANES), f32)
    for place in range(order_ref.shape[1]):
        slot = slots_scr[place]
        out_ref[slot] = state
        block = in_ref[slot].astype(f32)
        state = state * block_decay(block) + block[0:8]


def backward_scan_kernel(ids_ref, order_ref, decay_ref, in_ref, out_ref, slots_scr):
    invert_order(ids_ref, order_ref, slots_scr)
    state = jnp.zeros((8, LANES), f32)
    for place in reversed(range(order_ref.shape[1])):
        slot = slots_scr[place]
        out_ref[slot] = state
        state = state * block_decay(decay_ref[slot].astype(f32)) + in_ref[slot]


def mix_kernel(
    ids_ref, tok_ref, state_ref, sr_ref, cum_ref, inner_ref, conv_ref, gate_ref,
    par_own_ref, par_other_ref, own_ref, other_ref, gain_ref,
    full_ref, gated_ref, hidden_ref, normed_ref, msg_ref,
):
    core = ids_ref[1]
    hidden = tok_ref[...].astype(f32)
    hidden = jnp.concatenate([hidden[TAIL:EXT], hidden[EXT + TAIL :]], axis=0)
    for half, (w_ref, par_ref) in enumerate(
        ((own_ref, par_own_ref), (other_ref, par_other_ref))
    ):
        cols = slice(half * HCH, (half + 1) * HCH)
        c_rows = sr_ref[:, half * LANES + NSTATE : half * LANES + 2 * NSTATE].astype(bf16)
        carried = jnp.concatenate(
            [
                mm(
                    c_rows[batch * HALF : (batch + 1) * HALF],
                    get_state(state_ref, batch, half ^ core).astype(bf16),
                )
                for batch in range(2)
            ],
            axis=0,
        )
        conv = conv_ref[:, cols]
        mixed = conv * sigmoid(conv)
        full = inner_ref[:, cols] + jnp.exp(cum_ref[:, cols]) * carried + par_ref[5:6] * mixed
        full_ref[:, cols] = full
        gate = gate_ref[:, cols]
        gated = (full * (gate * sigmoid(gate))).astype(bf16)
        gated_ref[:, cols] = gated
        hidden = hidden + nt(gated, w_ref[:, 0:HCH])
    hidden_ref[...] = hidden
    normed = (hidden * rms_rows(hidden) * gain_ref[1:2]).astype(bf16)
    normed_ref[...] = normed
    for half, w_ref in enumerate((own_ref, other_ref)):
        rows_qkv = mm(normed, w_ref[:, HCH : HCH + 768]).astype(bf16)
        for batch in range(2):
            rows = slice(batch * HALF, (batch + 1) * HALF)
            for head in range(4):
                put_qkv(
                    msg_ref,
                    batch * 8 + (half ^ core) * 4 + head,
                    [
                        rows_qkv[rows, at : at + AHEAD_DIM]
                        for at in range(head * AHEAD_DIM, 768, 256)
                    ],
                )


def put_qkv(ref, at, members):
    ref[at, 0:HALF, 0:AHEAD_DIM] = members[0]
    ref[at, 0:HALF, AHEAD_DIM:LANES] = members[1]
    ref[at, HALF:QKV_ROWS, 0:AHEAD_DIM] = members[2][0 : HALF // 2]
    ref[at, HALF:QKV_ROWS, AHEAD_DIM:LANES] = members[2][HALF // 2 :]


def get_qkv(ref, at):
    return [
        ref[at, 0:HALF, 0:AHEAD_DIM],
        ref[at, 0:HALF, AHEAD_DIM:LANES],
        jnp.concatenate(
            [ref[at, HALF:QKV_ROWS, 0:AHEAD_DIM], ref[at, HALF:QKV_ROWS, AHEAD_DIM:LANES]], axis=0
        ),
    ]


def unpack_qkv(own_ref, other_ref, query_scr, key_scr, value_scr):
    for k, ref in enumerate((own_ref, other_ref)):
        for at in range(ref.shape[0]):
            rows = slice(at * HALF, (at + 1) * HALF)
            queries, keys, values = get_qkv(ref, at)
            if k == 0:
                query_scr[rows, :] = queries
            key_scr[k, rows, :] = keys
            value_scr[k, rows, :] = values


def put_rows(ref, at, member):
    ref[at, :, 0:AHEAD_DIM] = member[0 : HALF // 2]
    ref[at, :, AHEAD_DIM:LANES] = member[HALF // 2 :]


def get_rows(ref, at):
    return jnp.concatenate([ref[at, :, 0:AHEAD_DIM], ref[at, :, AHEAD_DIM:LANES]], axis=0)


QTILE = 256


def block_place(ids_ref, order_ref, block, other):
    chip, core = ids_ref[0], ids_ref[1]
    batch = chip // (order_ref.shape[1] // 4)
    return order_ref[batch, 2 * block + (core ^ other)] * HALF


def query_places(ids_ref, order_ref, tile):
    parts = [
        iota((HALF, 1), 0) + block_place(ids_ref, order_ref, tile * (QTILE // HALF) + k, 0)
        for k in range(QTILE // HALF)
    ]
    return jnp.concatenate(parts, axis=0)


def key_places(ids_ref, order_ref, other):
    lane = iota((1, LANES), 1)
    parts = []
    for pair in range(order_ref.shape[1] // 4):
        first = block_place(ids_ref, order_ref, 2 * pair, other)
        second = block_place(ids_ref, order_ref, 2 * pair + 1, other)
        parts.append(lane + jnp.where(lane < HALF, first, second - HALF))
    return jnp.concatenate(parts, axis=1)


def attend_kernel(
    ids_ref, order_ref, own_ref, other_ref, out_ref, log_ref, full_ref, query_scr, key_scr,
    value_scr,
):
    places = [key_places(ids_ref, order_ref, k) for k in range(2)]
    unpack_qkv(own_ref, other_ref, query_scr, key_scr, value_scr)
    scaling = AHEAD_DIM ** (-0.5)
    for tile in range(query_scr.shape[0] // QTILE):
        rows = slice(tile * QTILE, (tile + 1) * QTILE)
        place = query_places(ids_ref, order_ref, tile)
        queries = (query_scr[rows, :].astype(f32) * scaling).astype(bf16)
        scores = [
            jnp.where(
                places[k] <= place, nt(queries, key_scr[k]), -jnp.inf
            )
            for k in range(2)
        ]
        most = jnp.maximum(
            jnp.max(scores[0], axis=-1, keepdims=True), jnp.max(scores[1], axis=-1, keepdims=True)
        )
        exps = [jnp.exp(member - most) for member in scores]
        total = jnp.sum(exps[0], axis=-1, keepdims=True) + jnp.sum(exps[1], axis=-1, keepdims=True)
        mixed = mm(exps[0].astype(bf16), value_scr[0]) + mm(exps[1].astype(bf16), value_scr[1])
        mixed = mixed / total
        full_ref[rows, :] = mixed
        mixed = mixed.astype(bf16)
        for k in range(QTILE // HALF):
            put_rows(out_ref, tile * (QTILE // HALF) + k, mixed[k * HALF : (k + 1) * HALF])
        log_ref[rows, :] = most + jnp.log(total)


def attend_back_kernel(
    ids_ref, order_ref, own_ref, other_ref, grad_ref, log_ref, full_ref, mine_ref, theirs_ref,
    query_scr, key_scr, value_scr, query_sum, key_sum, value_sum,
):
    places = [key_places(ids_ref, order_ref, k) for k in range(2)]
    unpack_qkv(own_ref, other_ref, query_scr, key_scr, value_scr)
    scaling = AHEAD_DIM ** (-0.5)
    key_sum[...] = jnp.zeros(key_sum.shape, f32)
    value_sum[...] = jnp.zeros(value_sum.shape, f32)
    for tile in range(query_scr.shape[0] // QTILE):
        rows = slice(tile * QTILE, (tile + 1) * QTILE)
        place = query_places(ids_ref, order_ref, tile)
        queries = query_scr[rows, :]
        scaled = (queries.astype(f32) * scaling).astype(bf16)
        grad = jnp.concatenate(
            [get_rows(grad_ref, tile * (QTILE // HALF) + k) for k in range(QTILE // HALF)],
            axis=0,
        )
        log_total = log_ref[rows, :]
        probs = []
        prob_grads = []
        for k in range(2):
            scores = nt(scaled, key_scr[k]) - log_total
            probs.append(jnp.exp(jnp.where(places[k] <= place, scores, -jnp.inf)))
            prob_grads.append(nt(grad, value_scr[k]))
        delta = jnp.sum(grad.astype(f32) * full_ref[rows, :], axis=-1, keepdims=True)
        query_grad = jnp.zeros((QTILE, AHEAD_DIM), f32)
        for k in range(2):
            score_grad = (probs[k] * (prob_grads[k] - delta)).astype(bf16)
            value_sum[k] += tn(probs[k].astype(bf16), grad)
            key_sum[k] += tn(score_grad, queries)
            query_grad = query_grad + mm(score_grad, key_scr[k])
        query_sum[rows, :] = query_grad * scaling
    for at in range(mine_ref.shape[0]):
        rows = slice(at * HALF, (at + 1) * HALF)
        put_qkv(
            mine_ref, at, [query_sum[rows, :], key_sum[0, rows, :] * scaling, value_sum[0, rows, :]]
        )
        put_qkv(
            theirs_ref,
            at,
            [
                jnp.zeros((HALF, AHEAD_DIM), bf16),
                (key_sum[1, rows, :] * scaling).astype(bf16),
                value_sum[1, rows, :].astype(bf16),
            ],
        )


GELU_RATE = math.sqrt(2.0 / math.pi)
GELU_CUBE = 0.044715


def mlp_kernel(
    ids_ref, att_ref, hidden_ref, cot_ref, deal_ref, gain_ref, own_ref, other_ref,
    out_ref, hidden_two_ref, cot_both_ref, mine_ref, theirs_ref, hidden_grad_ref, gain_grad_ref,
    msg_ref,
    att_scr, result_scr,
):
    core = ids_ref[1]
    weights = (own_ref, other_ref)
    packs = (mine_ref, theirs_ref)
    up_cols, down_cols, att_cols = slice(0, 1024), slice(1024, 2048), slice(2048, 2304)
    cot_both = mm(
        jnp.concatenate(
            [cot_ref[batch, my_rows(side), :] for side in (core, 1 - core) for batch in range(2)],
            axis=0,
        ),
        deal_ref[...],
    ).astype(bf16)
    cot_both_ref[...] = cot_both
    cot = cot_both[0:ROWS]
    hidden = hidden_ref[...]
    for half in range(2):
        for batch in range(2):
            for head in range(4):
                att_scr[
                    half,
                    batch * HALF : (batch + 1) * HALF,
                    head * AHEAD_DIM : (head + 1) * AHEAD_DIM,
                ] = get_rows(att_ref, batch * 8 + (half ^ core) * 4 + head)
        packs[half][:, att_cols] = att_scr[half]
        hidden = hidden + nt(att_scr[half], weights[half][:, att_cols])
    gain = gain_ref[2:3]
    normed = (hidden * rms_rows(hidden) * gain).astype(bf16)
    normed_grad = jnp.zeros(hidden.shape, f32)
    for half in range(2):
        up_rows = mm(normed, weights[half][:, up_cols])
        squares = up_rows * up_rows
        bent = jnp.tanh(GELU_RATE * (up_rows + GELU_CUBE * squares * up_rows))
        act = (0.5 * up_rows * (1.0 + bent)).astype(bf16)
        slope = 0.5 * (1.0 + bent) + 0.5 * up_rows * (1.0 - bent * bent) * (
            GELU_RATE * (1.0 + 3.0 * GELU_CUBE * squares)
        )
        result_scr[half] = nt(act, weights[half][:, down_cols])
        packs[half][:, down_cols] = act
        up_grad = (mm(cot, weights[half][:, down_cols]) * slope).astype(bf16)
        packs[half][:, up_cols] = up_grad
        normed_grad = normed_grad + nt(up_grad, weights[half][:, up_cols])
        packs[half][:, 2304 : 2304 + 512] = normed
    hidden_two_ref[...] = hidden
    out_ref[...] = result_scr[0] + result_scr[1]
    part, gain_grad = rms_back(hidden, gain, normed_grad)
    gain_grad_ref[...] = gain_grad
    hidden_grad = cot.astype(f32) + part
    hidden_grad_ref[...] = hidden_grad
    branch = hidden_grad.astype(bf16)
    for half in range(2):
        packs[half][:, 2816 : 2816 + 512] = branch
        att_grad = mm(branch, weights[half][:, att_cols]).astype(bf16)
        for batch in range(2):
            for head in range(4):
                put_rows(
                    msg_ref,
                    batch * 8 + (half ^ core) * 4 + head,
                    att_grad[
                        batch * HALF : (batch + 1) * HALF,
                        head * AHEAD_DIM : (head + 1) * AHEAD_DIM,
                    ],
                )


def both_rows(mine_ref, theirs_ref, cols):
    return jnp.concatenate([mine_ref[:, cols], theirs_ref[:, cols]], axis=0)


def put_pieces(piece_refs, cols, values):
    rows_n = piece_refs[0].shape[0]
    for k, piece_ref in enumerate(piece_refs):
        piece_ref[:, cols] = values[k * rows_n : (k + 1) * rows_n].astype(bf16)


def third_grad_kernel(mine_ref, theirs_ref, cot_ref, *piece_refs):
    up_cols, down_cols, att_cols = slice(0, 1024), slice(1024, 2048), slice(2048, 2304)

    def both(cols):
        return both_rows(mine_ref, theirs_ref, cols)

    put_pieces(piece_refs, up_cols, tn(both(slice(2304, 2816)), both(up_cols)))
    put_pieces(piece_refs, down_cols, tn(cot_ref[...], both(down_cols)))
    put_pieces(piece_refs, att_cols, tn(both(slice(2816, 3328)), both(att_cols)))


def second_grad_kernel(mine_ref, theirs_ref, *piece_refs):
    def both(cols):
        return both_rows(mine_ref, theirs_ref, cols)

    for cols, base in ((slice(0, 512), 2304), (slice(512, 1280), 1792), (slice(1280, 1792), 2816)):
        put_pieces(piece_refs, cols, tn(both(slice(base, base + 512)), both(cols)))


def first_grad_kernel(ids_ref, mine_ref, theirs_ref, msg_ref, *piece_refs):
    cols = slice(0, HCH + LANES)
    rows = slice(0, 2 * EXT)
    packs = (mine_ref, theirs_ref)
    put_pieces(
        piece_refs,
        cols,
        tn(
            jnp.concatenate([ref[rows, HCH + LANES : 2 * HCH + LANES] for ref in packs], axis=0),
            jnp.concatenate([ref[rows, cols] for ref in packs], axis=0),
        ),
    )
    rows = slice(2 * EXT, 2 * EXT + SMALL_ROWS)
    small = mine_ref[rows, 0:HCH].astype(f32) + theirs_ref[rows, 0:HCH].astype(f32)
    tails = [ref[rows, HCH : 2 * HCH].astype(f32) for ref in packs]
    ordered = [jnp.where(ids_ref[1] == k, tails[0], tails[1]) for k in range(2)]
    tails = jnp.concatenate(
        [ordered[0][0:6], ordered[1][0:6], jnp.zeros((SMALL_ROWS - 12, HCH), f32)], axis=0
    )
    block = jnp.concatenate([small, tails], axis=1).astype(bf16)
    for k in range(msg_ref.shape[0]):
        msg_ref[k] = block


def sum_kernel(*refs):
    total = refs[0][...].astype(f32)
    for ref in refs[1:4]:
        total = total + ref[...].astype(f32)
    put_pieces(refs[4:], slice(0, total.shape[1]), total)


def sum_both_kernel(*refs):
    at = 0
    for group in (refs[0:4], refs[4:8]):
        total = group[0][...].astype(f32)
        for ref in group[1:]:
            total = total + ref[...].astype(f32)
        put_pieces(refs[8:], slice(at, at + total.shape[1]), total)
        at += total.shape[1]


def early_out_kernel(*refs):
    total = refs[0][...].astype(f32)
    for ref in refs[1:4]:
        total = total + ref[...].astype(f32)
    value_ref, state_ref, rate_ref, mix_ref, qkv_ref, gate_ref = refs[4:]
    value_ref[...] = total[:, 0:HCH]
    state_ref[...] = total[:, HCH : HCH + 32]
    rate_ref[...] = total[:, HCH : HCH + LANES].T[RATE_AT : RATE_AT + HPG]
    base = HCH + LANES
    mix_ref[...] = total[:, base : base + HCH]
    for kind in range(3):
        qkv_ref[kind] = total[:, base + HCH + kind * 256 : base + HCH + (kind + 1) * 256]
    gate_ref[...] = total[:, base + HCH + 768 :]


def mix_back_kernel(
    ids_ref, qkv_ref, first_ref, normed_ref, hidden_ref, hidden_grad_ref, gain_ref, own_ref,
    other_ref, gated_ref, gate_ref, full_ref, conv_ref, cum_ref, sr_ref,
    mine_ref, theirs_ref, y_grad_ref, gate_grad_ref, one_grad_ref, gain_grad_ref, skip_grad_ref,
    msg_ref, qkv_scr,
):
    core = ids_ref[1]
    weights = (own_ref, other_ref)
    packs = (mine_ref, theirs_ref)
    mix_cols, qkv_cols, gate_cols = slice(0, 512), slice(512, 1280), slice(1280, 1792)
    first = jnp.concatenate([first_ref[TAIL:EXT], first_ref[EXT + TAIL :]], axis=0)
    normed_grad = jnp.zeros(hidden_ref.shape, f32)
    for half in range(2):
        for batch in range(2):
            for head in range(4):
                members = get_qkv(qkv_ref, batch * 8 + (half ^ core) * 4 + head)
                for kind, member in enumerate(members):
                    at = kind * 256 + head * AHEAD_DIM
                    qkv_scr[batch * HALF : (batch + 1) * HALF, at : at + AHEAD_DIM] = member
        rows_grad = qkv_scr[...]
        packs[half][:, qkv_cols] = rows_grad
        normed_grad = normed_grad + nt(rows_grad, weights[half][:, qkv_cols])
    part, gain_grad = rms_back(hidden_ref[...], gain_ref[1:2], normed_grad)
    gain_grad_ref[...] = gain_grad
    one_grad = hidden_grad_ref[...] + part
    one_grad_ref[...] = one_grad
    branch = one_grad.astype(bf16)
    for half in range(2):
        cols = slice(half * HCH, (half + 1) * HCH)
        packs[half][:, mix_cols] = gated_ref[:, cols]
        packs[half][:, 1792:2304] = normed_ref[...]
        packs[half][:, 2304:2816] = branch
        packs[half][:, 2816:3328] = first
        gated_grad = mm(branch, weights[half][:, mix_cols])
        silu, slope = silu_parts(gate_ref[:, cols])
        y_grad = gated_grad * silu
        y_grad_ref[:, cols] = y_grad
        gate_grad = (gated_grad * full_ref[:, cols] * slope).astype(bf16)
        gate_grad_ref[:, cols] = gate_grad
        packs[half][:, gate_cols] = gate_grad
        conv = conv_ref[:, cols]
        skip_grad_ref[:, cols] = jnp.sum(y_grad * (conv * sigmoid(conv)), axis=0, keepdims=True)
        carried = (jnp.exp(cum_ref[:, cols]) * y_grad).astype(bf16)
        c_rows = sr_ref[:, half * LANES + NSTATE : half * LANES + 2 * NSTATE].astype(bf16)
        for batch in range(2):
            rows = slice(batch * HALF, (batch + 1) * HALF)
            put_state(msg_ref, batch, half ^ core, tn(c_rows[rows], carried[rows]))


def in_back_kernel(
    ids_ref, later_ref, state_ref, local_ref, sr_ref, cum_ref, conv_ref, x_ref, y_grad_ref,
    gate_grad_ref, normed_ref, tok_ref, gain_ref, one_grad_ref, own_ref, other_ref,
    par_own_ref, par_other_ref, deal_ref, skip_grad_ref, attgain_ref, mlpgain_ref,
    mine_ref, theirs_ref, hidden_grad_ref,
    x_scr, grad_scr, sr_scr, gate_scr,
):
    core = ids_ref[1]
    mask = lower_mask()
    spread = spread_matrix()
    normed = normed_ref[...]
    ext_grad = jnp.zeros((2 * EXT, normed.shape[1]), f32)
    lower_t = (
        same_block(iota((ROWS, ROWS), 0), iota((ROWS, ROWS), 1))
        & (iota((ROWS, ROWS), 0) <= iota((ROWS, ROWS), 1))
    ).astype(f32).astype(bf16)
    lane = iota((1, LANES), 1)
    small_list = []
    for half, (w_ref, par_ref, pack_ref) in enumerate(
        ((own_ref, par_own_ref, mine_ref), (other_ref, par_other_ref, theirs_ref))
    ):
        cols = slice(half * HCH, (half + 1) * HCH)
        group = half ^ core
        params = par_ref[...]
        state_rate = sr_ref[:, half * LANES : (half + 1) * LANES]
        shifted, step, rates, log_decay, cumulative = step_terms(state_rate, params)
        cumulative_t = cumulative.T
        cum_wide = cum_ref[:, cols]
        step_wide = mm_onehot(step, spread)
        conv = conv_ref[:, cols]
        mixed, conv_slope = silu_parts(conv)
        driving = step_wide * mixed
        tail = tail_decay(cum_wide)
        inflow = jnp.exp(cum_wide)
        y_grad = y_grad_ref[:, cols]
        y_low = y_grad.astype(bf16)
        driving_low = driving.astype(bf16)
        b_rows = state_rate[:, 0:NSTATE].astype(bf16)
        c_rows = state_rate[:, NSTATE : 2 * NSTATE].astype(bf16)
        inner_cb = nt(c_rows, b_rows)
        weighted = (driving * tail).astype(bf16)
        carried_grad = (inflow * y_grad).astype(bf16)
        through_list = []
        tail_list = []
        flow_list = []
        b_list = []
        c_list = []
        for batch in range(2):
            rows = slice(batch * HALF, (batch + 1) * HALF)
            incoming = get_state(state_ref, batch, group)
            later = get_state(later_ref, batch, group)
            total = cum_wide[(batch + 1) * HALF - 1 : (batch + 1) * HALF, :]
            outgoing = jnp.exp(total) * incoming + local_ref[batch, half]
            through_list.append(jnp.sum(later * outgoing, axis=0, keepdims=True))
            incoming = incoming.astype(bf16)
            later = later.astype(bf16)
            tail_list.append(mm(b_rows[rows], later))
            flow_list.append(mm(c_rows[rows], incoming))
            b_list.append(nt(weighted[rows], later))
            c_list.append(nt(carried_grad[rows], incoming))
        tail_part = tail * jnp.concatenate(tail_list, axis=0)
        flow_part = inflow * jnp.concatenate(flow_list, axis=0)
        first_head = iota((ROWS, LANES), 1) < HALF
        inner_grad = jnp.zeros((ROWS, ROWS), f32)
        row_sums = jnp.zeros((ROWS, LANES), f32)
        col_list = []
        drive_list = []
        for pair in range(4):
            lanes = slice(pair * LANES, (pair + 1) * LANES)
            y_pair = y_low[:, lanes]
            u_pair = driving_low[:, lanes]
            parts = []
            for k in range(2):
                head = 2 * pair + k
                mine = first_head if k == 0 else ~first_head
                decay = decay_matrix(cumulative, cumulative_t, head, mask)
                product = nt(jnp.where(mine, y_pair, jnp.zeros_like(y_pair)), u_pair)
                decayed = decay * product
                inner_grad = inner_grad + decayed
                both = decayed * inner_cb
                row_sums = row_sums + jnp.where(
                    lane == RATE_AT + head, jnp.sum(both, axis=1, keepdims=True), 0.0
                )
                col_list.append(jnp.sum(both, axis=0, keepdims=True))
                parts.append(tn((decay * inner_cb).astype(bf16), y_pair))
            drive_list.append(jnp.where(first_head, parts[0], parts[1]))
        drive_grad = jnp.concatenate(drive_list, axis=1) + tail_part
        col_rows = jnp.concatenate(
            [jnp.zeros((RATE_AT, ROWS), f32)]
            + col_list
            + [jnp.zeros((LANES - RATE_AT - HPG, ROWS), f32)],
            axis=0,
        )
        cum_grad = (
            row_sums
            - col_rows.T
            + nt_onehot(y_grad * flow_part - driving * tail_part, spread)
        )
        through_rows = nt_onehot(
            jnp.concatenate(through_list + [jnp.zeros((6, HCH), f32)], axis=0), spread
        )
        decay_grad = onehot_mm(lower_t, cum_grad) + per_block(
            through_rows[0:1], through_rows[1:2], (ROWS, LANES)
        )
        step_grad = nt_onehot(mixed * drive_grad, spread) - decay_grad * rates
        rate_grad = step_grad * sigmoid(shifted)
        inner_low = inner_grad.astype(bf16)
        b_grad = tn(inner_low, c_rows) + jnp.concatenate(b_list, axis=0)
        c_grad = mm(inner_low, b_rows) + jnp.concatenate(c_list, axis=0)
        is_rate = (lane >= RATE_AT) & (lane < RATE_AT + HPG)
        rate_grad = jnp.where(is_rate, rate_grad, 0.0)
        sr_grad = jnp.concatenate(
            [b_grad, c_grad, rate_grad[:, RATE_AT:LANES]], axis=1
        ).astype(bf16)
        mixed_grad = step_wide * drive_grad + params[5:6] * y_grad
        conv_grad = mixed_grad * conv_slope
        x_scr[...] = x_ref[:, cols].astype(f32)
        grad_scr[...] = jnp.zeros(grad_scr.shape, f32)
        sr_scr[...] = jnp.zeros(sr_scr.shape, bf16)
        gate_scr[...] = jnp.zeros(gate_scr.shape, bf16)
        gate_grad = gate_grad_ref[:, cols]
        for batch in range(2):
            rows = slice(batch * HALF, (batch + 1) * HALF)
            ext_rows = slice(batch * EXT + TAIL, (batch + 1) * EXT)
            grad_scr[batch, TAIL:EXT, :] = conv_grad[rows]
            sr_scr[ext_rows, :] = sr_grad[rows]
            gate_scr[ext_rows, :] = gate_grad[rows]
        x_list = []
        tap_list = [jnp.zeros((1, HCH), f32) for _ in range(CONV)]
        for batch in range(2):
            x_grad = jnp.zeros((EXT, HCH), f32)
            for tap in range(CONV):
                lag = CONV - 1 - tap
                x_grad = x_grad + params[tap : tap + 1] * grad_scr[batch, lag : lag + EXT, :]
                first = batch * EXT + TAIL - lag
                tap_list[tap] = tap_list[tap] + jnp.sum(
                    x_scr[first : first + HALF, :] * grad_scr[batch, TAIL:EXT, :],
                    axis=0,
                    keepdims=True,
                )
            x_list.append(x_grad)
        x_low = jnp.concatenate(x_list, axis=0).astype(bf16)
        small_list.append(
            jnp.concatenate(
                tap_list
                + [
                    jnp.sum(conv_grad, axis=0, keepdims=True),
                    skip_grad_ref[:, cols],
                    jnp.concatenate(
                        [
                            jnp.sum(rate_grad, axis=0, keepdims=True),
                            jnp.sum(decay_grad * log_decay, axis=0, keepdims=True),
                            jnp.zeros((1, HCH - 2 * LANES), f32),
                        ],
                        axis=1,
                    ),
                ],
                axis=0,
            )
        )
        pack_ref[0 : 2 * EXT, 0:HCH] = x_low
        pack_ref[0 : 2 * EXT, HCH : HCH + LANES] = sr_scr[...]
        pack_ref[0 : 2 * EXT, HCH + LANES : 2 * HCH + LANES] = normed
        ext_grad = (
            ext_grad
            + nt(x_low, w_ref[:, 0:HCH])
            + nt(gate_scr[...], w_ref[:, HCH : 2 * HCH])
            + nt(sr_scr[...], w_ref[:, 2 * HCH : 2 * HCH + LANES])
        )
    hidden = tok_ref[...].astype(f32)
    part, gain_grad = rms_back(hidden, gain_ref[0:1], ext_grad)
    deal = deal_ref[...]
    gain_grads = nt_onehot(
        jnp.concatenate([gain_grad, attgain_ref[...], mlpgain_ref[...]], axis=0), deal
    )
    tails = nt(
        jnp.concatenate([part[TAIL - 3 : TAIL], part[EXT + TAIL - 3 : EXT + TAIL]], axis=0).astype(
            bf16
        ),
        deal,
    )
    tails = jnp.concatenate([tails, jnp.zeros((SMALL_ROWS - 6, HCH), f32)], axis=0)
    for small, pack_ref in zip(small_list, (mine_ref, theirs_ref)):
        rows = slice(2 * EXT, 2 * EXT + SMALL_ROWS)
        pack_ref[rows, 0:HCH] = jnp.concatenate(
            [small, gain_grads, jnp.zeros((SMALL_ROWS - 10, HCH), f32)], axis=0
        ).astype(bf16)
        pack_ref[rows, HCH : 2 * HCH] = tails.astype(bf16)
        pack_ref[rows, 2 * HCH :] = jnp.zeros((SMALL_ROWS, LANES), bf16)
    rows_grad = jnp.concatenate([part[TAIL:EXT], part[EXT + TAIL :]], axis=0) + one_grad_ref[...]
    hidden_grad_ref[...] = nt(rows_grad.astype(bf16), deal)


SMEM_SPEC = pl.BlockSpec(memory_space=pltpu.SMEM)
VMEM_SPEC = pl.BlockSpec(memory_space=pltpu.VMEM)
ANY_SPEC = pl.BlockSpec(memory_space=pl.ANY)


def run_kernel(kernel, out_shapes, scalars_n, args, scratch=(), after=(), pieces=None, at=0):
    args_n = len(args)
    pieces = [] if pieces is None else list(pieces[0]) + list(pieces[1])
    scratch = list(scratch)
    if pieces:
        rows_n, cols = pieces[0].shape
        scratch += [pltpu.VMEM((4 * rows_n, cols), bf16)] * 2
        scratch.append(pltpu.SemaphoreType.DMA((8,)))

    def body(*refs):
        ins, rest = list(refs[:args_n]), list(refs[args_n + len(pieces) + len(after) :])
        if pieces:
            *rest, own_scr, other_scr, sems = rest
            copies = [
                pltpu.make_async_copy(
                    refs[args_n + k],
                    (own_scr, other_scr)[k // 4].at[pl.ds((k % 4) * rows_n, rows_n), :],
                    sems.at[k],
                )
                for k in range(8)
            ]
            for copy in copies:
                copy.start()
            for copy in copies:
                copy.wait()
            ins[at:at] = [own_scr, other_scr]
        kernel(*ins, *rest)

    return pl.pallas_call(
        body,
        out_shape=[jax.ShapeDtypeStruct(shape, kind) for shape, kind in out_shapes],
        in_specs=[SMEM_SPEC] * scalars_n
        + [VMEM_SPEC] * (args_n - scalars_n)
        + [ANY_SPEC] * (len(pieces) + len(after)),
        out_specs=[VMEM_SPEC] * len(out_shapes),
        scratch_shapes=scratch,
        compiler_params=pltpu.CompilerParams(vmem_limit_bytes=VMEM_LIMIT),
        name=kernel.__name__,
        cost_estimate=pl.CostEstimate(flops=0, transcendentals=0, bytes_accessed=0),
    )(*args, *pieces, *after)


def hold(values, *after):
    def body(*refs):
        pass

    return pl.pallas_call(
        body,
        out_shape=jax.ShapeDtypeStruct(values.shape, values.dtype),
        in_specs=[ANY_SPEC] * (1 + len(after)),
        out_specs=ANY_SPEC,
        input_output_aliases={0: 0},
    )(values, *after)


def flip(bits, ranks):
    return [(index, index ^ bits) for index in range(ranks)]


def swap_cores(values):
    return lax.ppermute(values, "head", [(0, 1), (1, 0)])


def permute_three(pieces, step, ranks):
    return [
        lax.ppermute(piece, "seq", flip(step * (k + 1), ranks)) for k, piece in enumerate(pieces)
    ]


def sum_pieces(mine, moved, after=()):
    rows_n, cols = mine.shape
    return run_kernel(
        sum_kernel, [((rows_n // 4, cols), bf16)] * 4, 0, [mine] + moved, (), after
    )


def exchange(values, axes):
    return lax.all_to_all(values, axes, 0, 0, tiled=True)


def dealt_device(
    tokens, cotangent, lengths, order, mix_gain, in_value, in_gate, in_state, in_rate,
    rate_bias, decay_log, conv_taps, conv_bias, skip_gain, mix_out, att_gain, qkv_proj,
    att_out, mlp_gain, mlp_up, mlp_down,
):
    ranks = lax.axis_size("seq")
    both = ("seq", "head")
    chip = lax.axis_index("seq")
    core = lax.axis_index("head")
    ids = jnp.stack([chip, core]).astype(jnp.int32)
    my_slot = 2 * chip + core
    width = tokens.shape[2]
    slots_n = 2 * ranks
    shard_rows = width // ranks
    slots_scratch = (pltpu.SMEM((slots_n,), jnp.int32),)

    tail_rows = tokens.reshape(2, 2, HALF, width)[:, :, HALF - (CONV - 1) :]
    tail_rows = jnp.where(core == 0, tail_rows[0], tail_rows[1]).reshape(-1, LANES)
    tail_rows = jnp.pad(tail_rows, ((0, shard_rows - tail_rows.shape[0]), (0, 0)))
    first_shard = jnp.concatenate(
        [
            in_value, in_gate, in_state, in_rate, jnp.zeros((shard_rows, LANES - 40), bf16),
            tail_rows,
        ],
        axis=1,
    )
    first_cols = first_shard.shape[1]
    second_cols, third_cols = HCH + 768, 2304
    early_shard = jnp.concatenate(
        [first_shard, mix_out.T, qkv_proj.reshape(shard_rows, -1)], axis=1
    )
    third_shard = jnp.concatenate([mlp_up, mlp_down.T, att_out.T], axis=1)
    early_pieces = [early_shard] + permute_three([early_shard] * 3, 4, ranks)
    first_stack = jnp.concatenate([piece[:, :first_cols] for piece in early_pieces], axis=0)
    third_shard = hold(third_shard, first_stack)
    third_z = [third_shard] + permute_three([third_shard] * 3, 4, ranks)
    third_stack = jnp.concatenate(third_z, axis=0)
    first_own = [first_stack] + permute_three([first_stack] * 3, 1, ranks)
    first_own[3] = hold(first_own[3], *third_z[1:])
    first_pieces = (first_own, [swap_cores(piece) for piece in first_own])
    second_stack = jnp.concatenate([piece[:, first_cols:] for piece in early_pieces], axis=0)
    second_own = [second_stack] + permute_three([second_stack] * 3, 1, ranks)
    second_pieces = (second_own, [swap_cores(piece) for piece in second_own])

    par_own = jnp.concatenate(
        [
            conv_taps,
            conv_bias[None],
            skip_gain[None],
            jnp.pad(rate_bias, (RATE_AT, HCH - RATE_AT - HPG))[None],
            jnp.pad(decay_log, (RATE_AT, HCH - RATE_AT - HPG))[None],
        ],
        axis=0,
    )
    par_other = swap_cores(par_own)
    gains = jnp.stack([mix_gain, att_gain, mlp_gain])

    channels = 2 * HCH
    (
        ext_rows, normed_one, x_in, conv_sum, gate_in, state_rate, cum_wide, inner_y,
        local_state, msg, deal_low, gains,
    ) = run_kernel(
        in_kernel,
        [
            ((2 * EXT, width), bf16),
            ((2 * EXT, width), bf16),
            ((2 * EXT, channels), bf16),
            ((ROWS, channels), f32),
            ((ROWS, channels), f32),
            ((ROWS, 2 * LANES), f32),
            ((ROWS, channels), f32),
            ((ROWS, channels), f32),
            ((2, 2, NSTATE, HCH), f32),
            ((slots_n, 16, LANES), bf16),
            ((width, width), bf16),
            ((3, width), f32),
        ],
        2,
        (ids, order, tokens, gains, par_own, par_other),
        (pltpu.VMEM((2 * EXT, HCH), f32), pltpu.VMEM((2, TILE_ROWS, LANES), f32)),
        pieces=first_pieces,
        at=4,
    )

    states = exchange(hold(msg, *second_own[1:3]), both)
    (incoming,) = run_kernel(
        forward_scan_kernel,
        [((slots_n, 8, LANES), f32)],
        2,
        (ids, order, states),
        slots_scratch,
        after=second_own[3:],
    )
    incoming = exchange(incoming, both)

    full_y, gated, hidden_one, normed_two, msg = run_kernel(
        mix_kernel,
        [
            ((ROWS, channels), f32),
            ((ROWS, channels), bf16),
            ((ROWS, width), f32),
            ((ROWS, width), bf16),
            ((ranks, QKV_ROWS, LANES), bf16),
        ],
        1,
        (
            ids, ext_rows, incoming, state_rate, cum_wide, inner_y, conv_sum, gate_in,
            par_own, par_other, gains,
        ),
        after=[third_stack],
        pieces=second_pieces,
        at=10,
    )
    third_own = [third_stack] + permute_three([third_stack] * 3, 1, ranks)
    att_rows = ranks * HALF
    qkv_scratch = (
        pltpu.VMEM((att_rows, AHEAD_DIM), bf16),
        pltpu.VMEM((2, att_rows, AHEAD_DIM), bf16),
        pltpu.VMEM((2, att_rows, AHEAD_DIM), bf16),
    )
    qkv_own = exchange(hold(msg, *third_own[1:3]), "seq")
    qkv_other = swap_cores(qkv_own)
    attended, log_total, att_full = run_kernel(
        attend_kernel,
        [((ranks, HALF // 2, LANES), bf16), ((att_rows, 1), f32), ((att_rows, AHEAD_DIM), f32)],
        2,
        (ids, order, qkv_own, qkv_other),
        qkv_scratch,
    )
    third_own[3] = hold(third_own[3], log_total)
    third_pieces = (third_own, [swap_cores(piece) for piece in third_own])
    attended = exchange(attended, "seq")

    pack_cols = 3328
    (
        down_rows, hidden_two, cot_both, mine, theirs, two_grad, mlpgain_part, msg,
    ) = run_kernel(
        mlp_kernel,
        [
            ((ROWS, width), f32),
            ((ROWS, width), f32),
            ((2 * ROWS, width), bf16),
            ((ROWS, pack_cols), bf16),
            ((ROWS, pack_cols), bf16),
            ((ROWS, width), f32),
            ((1, width), f32),
            ((ranks, HALF // 2, LANES), bf16),
        ],
        1,
        (ids, attended, hidden_one, cotangent, deal_low, gains),
        (pltpu.VMEM((2, ROWS, 256), bf16), pltpu.VMEM((2, ROWS, width), f32)),
        pieces=third_pieces,
        at=6,
    )
    att_grad = exchange(msg, "seq")
    third_grads = run_kernel(
        third_grad_kernel,
        [((width // 4, third_cols), bf16)] * 4,
        0,
        (mine, swap_cores(theirs), cot_both),
    )
    mine, theirs = run_kernel(
        attend_back_kernel,
        [((ranks, QKV_ROWS, LANES), f32), ((ranks, QKV_ROWS, LANES), bf16)],
        2,
        (ids, order, qkv_own, qkv_other, att_grad, log_total, att_full),
        qkv_scratch
        + (
            pltpu.VMEM((att_rows, AHEAD_DIM), f32),
            pltpu.VMEM((2, att_rows, AHEAD_DIM), f32),
            pltpu.VMEM((2, att_rows, AHEAD_DIM), f32),
        ),
        after=third_grads[:1],
    )
    qkv_grad = (mine + swap_cores(theirs).astype(f32)).astype(bf16)
    qkv_grad = exchange(qkv_grad, "seq")
    third_moved = permute_three(third_grads[1:], 1, ranks)

    mine, theirs, y_grad, gate_grad, one_grad, attgain_part, skip_part, msg = run_kernel(
        mix_back_kernel,
        [
            ((ROWS, pack_cols), bf16),
            ((ROWS, pack_cols), bf16),
            ((ROWS, channels), f32),
            ((ROWS, channels), bf16),
            ((ROWS, width), f32),
            ((1, width), f32),
            ((1, channels), f32),
            ((slots_n, 8, LANES), f32),
        ],
        1,
        (
            ids, qkv_grad, normed_one, normed_two, hidden_one, two_grad, gains, gated, gate_in,
            full_y, conv_sum, cum_wide, state_rate,
        ),
        (pltpu.VMEM((ROWS, 768), bf16),),
        pieces=second_pieces,
        at=7,
        after=third_moved[:2],
    )
    back_states = exchange(msg, both)
    second_grads = run_kernel(
        second_grad_kernel,
        [((width // 4, second_cols + HCH), bf16)] * 4,
        0,
        (mine, swap_cores(theirs)),
    )
    (later,) = run_kernel(
        backward_scan_kernel,
        [((slots_n, 8, LANES), f32)],
        2,
        (ids, order, states, back_states),
        slots_scratch,
        after=[second_grads[0], third_moved[2]],
    )
    third_parts = sum_pieces(third_grads[0], third_moved, (later,))
    third_moved = permute_three(third_parts[1:], 4, ranks)
    second_moved = permute_three(second_grads[1:], 1, ranks)
    later = exchange(later, both)

    grad_cols = HCH + LANES
    pack_shape = (2 * EXT + SMALL_ROWS, grad_cols + width)
    mine, theirs, tokens_grad = run_kernel(
        in_back_kernel,
        [(pack_shape, bf16), (pack_shape, bf16), ((ROWS, width), f32)],
        1,
        (
            ids, later, incoming, local_state, state_rate, cum_wide, conv_sum, x_in, y_grad,
            gate_grad, normed_one, ext_rows, gains, one_grad, par_own, par_other, deal_low,
            skip_part, attgain_part, mlpgain_part,
        ),
        (
            pltpu.VMEM((2 * EXT, HCH), f32),
            pltpu.VMEM((2, EXT + TAIL, HCH), f32),
            pltpu.VMEM((2 * EXT, LANES), bf16),
            pltpu.VMEM((2 * EXT, HCH), bf16),
        ),
        after=[third_parts[0]],
        pieces=first_pieces,
        at=14,
    )
    last_msg, *first_grads = run_kernel(
        first_grad_kernel,
        [((ranks, SMALL_ROWS, 2 * HCH), bf16)] + [((width // 4, grad_cols), bf16)] * 4,
        1,
        (ids, mine, swap_cores(theirs)),
        after=second_moved,
    )
    first_moved = permute_three(first_grads[1:], 1, ranks)
    last = exchange(hold(last_msg, *first_moved), "seq")
    early_parts = run_kernel(
        sum_both_kernel,
        [((width // 16, grad_cols + second_cols + HCH), bf16)] * 4,
        0,
        [first_grads[0]] + first_moved + [second_grads[0]] + second_moved,
    )
    third_total = third_parts[0].astype(f32)
    for piece in third_moved:
        third_total = third_total + piece.astype(f32)
    early_outs = run_kernel(
        early_out_kernel,
        [
            (shape, f32)
            for shape in (
                in_value.shape,
                in_state.shape,
                in_rate.shape[::-1],
                mix_out.shape[::-1],
                (qkv_proj.shape[1], qkv_proj.shape[0], qkv_proj.shape[2]),
                in_gate.shape,
            )
        ],
        0,
        [early_parts[0]] + permute_three(early_parts[1:], 4, ranks),
    )

    my_blocks = jnp.sum(
        jnp.where(jnp.arange(slots_n)[None, :] == my_slot, order, 0), axis=1
    )
    last = last.astype(f32)
    small_total = jnp.sum(last[:, 0:10, 0:HCH], axis=0)
    next_tails = last[:, 0:12, HCH:].reshape(ranks, 2, 2, CONV - 1, width).transpose(2, 0, 1, 3, 4)
    next_tails = next_tails.reshape(2, slots_n, CONV - 1, width)
    pick_next = (order == my_blocks[:, None] + 1).astype(f32)
    tail_add = jnp.sum(pick_next[:, :, None, None] * next_tails, axis=1)
    tokens_grad = tokens_grad.reshape(2, HALF, width)
    tokens_grad = jnp.concatenate(
        [tokens_grad[:, : HALF - (CONV - 1)], tokens_grad[:, HALF - (CONV - 1) :] + tail_add],
        axis=1,
    ).astype(bf16)
    layer_rows = nt((hidden_two + down_rows).astype(bf16), deal_low).astype(bf16)
    outs = jnp.stack([layer_rows.reshape(2, HALF, width), tokens_grad])
    outs_other = swap_cores(outs)
    outs = jnp.where(
        core == 0,
        jnp.concatenate([outs, outs_other], axis=2),
        jnp.concatenate([outs_other, outs], axis=2),
    )
    return (
        outs[0],
        outs[1],
        small_total[7],
        early_outs[0],
        early_outs[5],
        early_outs[1],
        early_outs[2].T,
        small_total[6, RATE_AT : RATE_AT + HPG],
        small_total[6, LANES + RATE_AT : LANES + RATE_AT + HPG],
        small_total[0:4],
        small_total[4],
        small_total[5],
        early_outs[3].T,
        small_total[8],
        early_outs[4].transpose(1, 0, 2),
        third_total[:, 2048:2304].T,
        small_total[9],
        third_total[:, 0:1024],
        third_total[:, 1024:2048].T,
    )


def layer(*args):
    tokens, lengths = args[0], args[2]
    fits = lax.axis_size("seq") == 16 and lax.axis_size("head") == 2
    fits = fits and lengths.shape == (2, 1) and tokens.shape[1] == ROWS
    return dealt_device(*args) if fits else on_device(*args)


def solution(mesh):
    return jax.shard_map(
        layer,
        mesh=mesh,
        in_specs=(
            P(None, "seq", None),
            P(None, "seq", None),
            P(),
            P(),
            P(),
            P("seq", "head"),
            P("seq", "head"),
            P("seq", "head"),
            P("seq", "head"),
            P("head"),
            P("head"),
            P(None, "head"),
            P("head"),
            P("head"),
            P("head", "seq"),
            P(),
            P("seq", None, "head"),
            P("head", "seq"),
            P(),
            P("seq", "head"),
            P("head", "seq"),
        ),
        out_specs=(
            P(None, "seq", None),
            P(None, "seq", None),
            P(),
            P("seq", "head"),
            P("seq", "head"),
            P("seq", "head"),
            P("seq", "head"),
            P("head"),
            P("head"),
            P(None, "head"),
            P("head"),
            P("head"),
            P("head", "seq"),
            P(),
            P("seq", None, "head"),
            P("head", "seq"),
            P(),
            P("seq", "head"),
            P("head", "seq"),
        ),
        check_vma=False,
    )
```

```python
import functools
import math

import jax
import jax.numpy as jnp
from jax import lax
from jax.experimental import pallas as pl
from jax.experimental.pallas import tpu as pltpu
from jax.sharding import PartitionSpec as P

NSTATE = 16
CONV = 4
AHEAD_DIM = 64


epsilon = 1e-05
highest = lax.Precision.HIGHEST


def rms_norm(values, gain_row):
    return (
        values * lax.rsqrt(jnp.mean(values * values, axis=-1, keepdims=True) + epsilon) * gain_row
    )


def gelu_tanh(values):
    return jax.nn.gelu(values, approximate=True)


def segment_of(position, seq_ends):
    bounds = seq_ends[:-1]
    return jnp.sum((jnp.asarray(position)[..., None] >= bounds).astype(jnp.int32), axis=-1)


def tap_valid(position, lag_rows, seq_ends):
    source = position - lag_rows
    return (
        (source >= 0) & (segment_of(source, seq_ends) == segment_of(position, seq_ends))
    ).astype(jnp.float32)


def slot_position(order_row, row_ids, half_rows):
    slot = row_ids // half_rows
    slot_table = jnp.arange(order_row.shape[0], dtype=jnp.int32)
    block = jnp.sum(jnp.where(slot[:, None] == slot_table[None, :], order_row[None, :], 0), axis=1)
    return block * half_rows + row_ids % half_rows


def stream_slots(order_row):
    slot_table = jnp.arange(order_row.shape[0], dtype=jnp.int32)
    return jnp.sum(
        jnp.where(order_row[None, :] == slot_table[:, None], slot_table[None, :], 0), axis=1
    )


def matmul(left_op, right_op):
    return jnp.dot(left_op, right_op, preferred_element_type=jnp.float32)


def transposed(left_op, right_op):
    return lax.dot_general(
        left_op, right_op, (((1,), (1,)), ((), ())), preferred_element_type=jnp.float32
    )


def left_gram(left_op, right_op):
    return lax.dot_general(
        left_op, right_op, (((0,), (0,)), ((), ())), preferred_element_type=jnp.float32
    )


def transposed_exact(left_op, right_op):
    return lax.dot_general(
        left_op,
        right_op,
        (((1,), (1,)), ((), ())),
        preferred_element_type=jnp.float32,
        precision=highest,
    )


def left_gram_exact(left_op, right_op):
    return lax.dot_general(
        left_op,
        right_op,
        (((0,), (0,)), ((), ())),
        preferred_element_type=jnp.float32,
        precision=highest,
    )


def keep_same(current):
    return current


def head_total(partial_rows):
    return lax.psum(partial_rows, "head")


def collect(in_value, in_gate, in_state, in_rate, qkv_proj, mlp_up, mix_out, att_out, mlp_down):
    return (
        lax.all_gather(in_value, "seq", axis=0, tiled=True),
        lax.all_gather(in_gate, "seq", axis=0, tiled=True),
        lax.all_gather(in_state, "seq", axis=0, tiled=True),
        lax.all_gather(in_rate, "seq", axis=0, tiled=True),
        lax.all_gather(qkv_proj, "seq", axis=0, tiled=True),
        lax.all_gather(mlp_up, "seq", axis=0, tiled=True),
        lax.all_gather(mix_out, "seq", axis=1, tiled=True),
        lax.all_gather(att_out, "seq", axis=1, tiled=True),
        lax.all_gather(mlp_down, "seq", axis=1, tiled=True),
    )


def reduce_grads(grad_parts):
    return (
        lax.psum_scatter(grad_parts[0], "seq", scatter_dimension=0, tiled=True),
        lax.psum_scatter(grad_parts[1], "seq", scatter_dimension=0, tiled=True),
        lax.psum_scatter(grad_parts[2], "seq", scatter_dimension=0, tiled=True),
        lax.psum_scatter(grad_parts[3], "seq", scatter_dimension=0, tiled=True),
        lax.psum_scatter(grad_parts[4], "seq", scatter_dimension=0, tiled=True),
        lax.psum_scatter(grad_parts[5], "seq", scatter_dimension=0, tiled=True),
        lax.psum_scatter(grad_parts[6], "seq", scatter_dimension=1, tiled=True),
        lax.psum_scatter(grad_parts[7], "seq", scatter_dimension=1, tiled=True),
        lax.psum_scatter(grad_parts[8], "seq", scatter_dimension=1, tiled=True),
    )


def fold_blocks(fold_fn, initial, arrays, block_rows):
    blocks_n = arrays[0].shape[0] // block_rows

    def one_step(block_index, current):
        offset = block_index * block_rows
        shards = tuple(
            (lax.dynamic_slice_in_dim(member, offset, block_rows, 0) for member in arrays)
        )
        return fold_fn(current, shards, offset)

    return lax.fori_loop(0, blocks_n, one_step, initial)


def add_parts(left_op, right_op):
    if left_op is None:
        return right_op
    return tuple((first_part + second_part for first_part, second_part in zip(left_op, right_op)))


def combine_state(earlier, later):
    return (earlier[0] * later[0], later[0][..., None, None] * earlier[1] + later[1])


def attention_probs(
    query_rows, key_rows, query_pos, key_pos, query_seg, key_seg, log_total, scaling
):
    allowed = ((key_pos[None, :] <= query_pos[:, None]) & (key_seg[None, :] == query_seg[:, None]))[
        :, None, :
    ]
    scores = (
        jnp.einsum("qhd,khd->qhk", query_rows, key_rows, preferred_element_type=jnp.float32)
        * scaling
    )
    return jnp.where(allowed, jnp.exp(jnp.where(allowed, scores - log_total[:, :, None], 0.0)), 0.0)


def scan_terms(mixed_x, step_size, bc_rows, decay_log, segment, seg_before):
    rows_n, heads_n = step_size.shape
    log_decay = -step_size * jnp.exp(decay_log)
    cumulative = jnp.cumsum(log_decay, axis=0)
    driving = step_size[:, :, None] * mixed_x.reshape(rows_n, heads_n, -1)
    tail_weight = (
        jnp.exp(cumulative[-1][None, :] - cumulative)
        * (segment == segment[-1]).astype(jnp.float32)[:, None]
    )
    local_state = jnp.einsum(
        "sh,shp,sn->hpn", tail_weight, driving, bc_rows[:, :NSTATE], precision=highest
    )
    through = jnp.exp(cumulative[-1]) * (segment[-1] == seg_before).astype(jnp.float32)
    return (cumulative, driving, through, local_state)


def scan_output(cumulative, driving, bc_rows, incoming, segment, seg_before):
    rows_n = cumulative.shape[0]
    row_ids = jnp.arange(rows_n, dtype=jnp.int32)
    allowed = ((row_ids[:, None] >= row_ids[None, :]) & (segment[:, None] == segment[None, :]))[
        :, :, None
    ]
    decays = jnp.where(
        allowed,
        jnp.exp(jnp.where(allowed, cumulative[:, None, :] - cumulative[None, :, :], 0.0)),
        0.0,
    )
    inner_cb = jnp.dot(bc_rows[:, NSTATE:], bc_rows[:, :NSTATE].T, precision=highest)
    output = jnp.einsum("tsh,shp->thp", decays * inner_cb[:, :, None], driving, precision=highest)
    inflow = jnp.exp(cumulative) * (segment == seg_before).astype(jnp.float32)[:, None]
    output = output + inflow[:, :, None] * jnp.einsum(
        "tn,hpn->thp", bc_rows[:, NSTATE:], incoming, precision=highest
    )
    return output.reshape(rows_n, -1)


def scan_whole(mixed_x, step_size, bc_rows, decay_log, incoming, segment, seg_before):
    cumulative, driving, through, local_state = scan_terms(
        mixed_x, step_size, bc_rows, decay_log, segment, seg_before
    )
    output = scan_output(cumulative, driving, bc_rows, incoming, segment, seg_before)
    return (output, through[:, None, None] * incoming + local_state)


def on_device(
    tokens,
    cotangent,
    lengths,
    order,
    mix_gain,
    in_value,
    in_gate,
    in_state,
    in_rate,
    rate_bias,
    decay_log,
    conv_taps,
    conv_bias,
    skip_gain,
    mix_out,
    att_gain,
    qkv_proj,
    att_out,
    mlp_gain,
    mlp_up,
    mlp_down,
):
    rows_n = tokens.shape[1]
    half_rows = rows_n // 2
    slots_n = 2 * lax.axis_size("seq")
    my_slot = 2 * lax.axis_index("seq")
    total_rows = rows_n * lax.axis_size("seq")
    block_rows = math.gcd(total_rows, 1024)
    scaling = AHEAD_DIM ** (-0.5)
    local_ids = jnp.arange(half_rows, dtype=jnp.int32)
    ext_ids = jnp.arange(half_rows + CONV - 1, dtype=jnp.int32)
    terms_all = jax.vmap(scan_terms, in_axes=(0, 0, 0, None, 0, 0))
    output_all = jax.vmap(scan_output, in_axes=(0, 0, 0, 0, 0, 0))
    whole_all = jax.vmap(scan_whole, in_axes=(0, 0, 0, None, 0, 0, 0))
    layer_list = []
    input_list = []
    big_sums = None
    small_sums = None
    for batch_index in range(tokens.shape[0]):
        (
            value_full,
            gate_full,
            state_full,
            rate_full,
            qkv_full,
            up_full,
            mixout_full,
            attout_full,
            down_full,
        ) = collect(
            in_value, in_gate, in_state, in_rate, qkv_proj, mlp_up, mix_out, att_out, mlp_down
        )
        seq_ends = jnp.cumsum(lengths[batch_index])
        order_row = order[batch_index]
        inverse = stream_slots(order_row)
        my_blocks = lax.dynamic_slice_in_dim(order_row, my_slot, 2)
        position = (my_blocks[:, None] * half_rows + local_ids[None, :]).reshape(rows_n)
        segment = segment_of(position, seq_ends)
        seg_blocks = segment.reshape(2, half_rows)
        seg_before = segment_of(my_blocks * half_rows - 1, seq_ends)
        hidden_in = tokens[batch_index].astype(jnp.float32)
        normed_one = rms_norm(hidden_in, mix_gain).astype(jnp.bfloat16)
        x_in = matmul(normed_one, value_full).astype(jnp.bfloat16)
        gate_in = matmul(normed_one, gate_full)
        bc_rows = matmul(normed_one, state_full)
        rate_in = matmul(normed_one, rate_full)
        step_size = jax.nn.softplus(rate_in + rate_bias)
        x_blocks = x_in.reshape(2, half_rows, -1)
        all_tails = lax.all_gather(x_blocks[:, half_rows - (CONV - 1) :], "seq", axis=0, tiled=True)
        pick_prev = (order_row[None, :] == my_blocks[:, None] - 1).astype(jnp.bfloat16)
        edge_rows = jnp.einsum(
            "bs,srd->brd", pick_prev, all_tails, preferred_element_type=jnp.float32
        )
        extended = jnp.concatenate([edge_rows, x_blocks.astype(jnp.float32)], axis=1)
        valid_taps = [
            tap_valid(position, CONV - 1 - tap_index, seq_ends).reshape(2, half_rows)
            for tap_index in range(CONV)
        ]
        conv_blocks = jnp.zeros(x_blocks.shape, jnp.float32) + conv_bias
        for tap_index in range(CONV):
            conv_blocks = (
                conv_blocks
                + conv_taps[tap_index]
                * extended[:, tap_index : tap_index + half_rows]
                * valid_taps[tap_index][:, :, None]
            )
        conv_sum = conv_blocks.reshape(rows_n, -1)
        mixed_x = jax.nn.silu(conv_sum)
        mixed_b = mixed_x.reshape(2, half_rows, -1)
        step_b = step_size.reshape(2, half_rows, -1)
        bc_b = bc_rows.reshape(2, half_rows, -1)
        cumulative, driving, through, local_state = terms_all(
            mixed_b, step_b, bc_b, decay_log, seg_blocks, seg_before
        )
        all_through, all_state = (
            lax.all_gather(through, "seq", axis=0, tiled=True),
            lax.all_gather(local_state, "seq", axis=0, tiled=True),
        )
        through_stream = all_through[inverse]
        state_stream = all_state[inverse]
        acc_through, acc_state = lax.associative_scan(
            combine_state, (through_stream, state_stream), axis=0
        )
        before = my_blocks - 1
        incoming = (
            acc_state[jnp.maximum(before, 0)]
            * (before >= 0).astype(jnp.float32)[:, None, None, None]
        )
        ssm_out = output_all(cumulative, driving, bc_b, incoming, seg_blocks, seg_before).reshape(
            rows_n, -1
        )
        full_y = ssm_out + skip_gain * mixed_x
        gating = jax.nn.silu(gate_in)
        gated_low = (full_y * gating).astype(jnp.bfloat16)
        hidden_one = hidden_in + head_total(matmul(gated_low, mixout_full))
        normed_two = rms_norm(hidden_one, att_gain).astype(jnp.bfloat16)
        qkv_rows = jnp.einsum(
            "rd,dcn->rcn", normed_two, qkv_full, preferred_element_type=jnp.float32
        ).astype(jnp.bfloat16)
        heads_att = qkv_rows.shape[2] // AHEAD_DIM
        queries = qkv_rows[:, 0].reshape(rows_n, heads_att, AHEAD_DIM)
        key_heads = qkv_rows[:, 1].reshape(rows_n, heads_att, AHEAD_DIM)
        value_heads = qkv_rows[:, 2].reshape(rows_n, heads_att, AHEAD_DIM)

        def forward_fold(totals, shards, offset):
            key_rows, value_rows = shards
            key_pos = slot_position(
                order_row, offset + jnp.arange(key_rows.shape[0], dtype=jnp.int32), half_rows
            )
            allowed = (
                (key_pos[None, :] <= position[:, None])
                & (segment_of(key_pos, seq_ends)[None, :] == segment[:, None])
            )[:, None, :]

            def forward_compute(current):
                running_max, running_sum, weighted = current
                scores = (
                    jnp.einsum(
                        "qhd,khd->qhk", queries, key_rows, preferred_element_type=jnp.float32
                    )
                    * scaling
                )
                scores = jnp.where(allowed, scores, -jnp.inf)
                new_max = jnp.maximum(running_max, jnp.max(scores, axis=-1))
                safe_max = jnp.where(new_max == -jnp.inf, 0.0, new_max)
                exp_scores = jnp.exp(scores - safe_max[:, :, None])
                factor = jnp.exp(running_max - safe_max)
                running_sum = running_sum * factor + jnp.sum(exp_scores, axis=-1)
                weighted = weighted * factor[:, :, None] + jnp.einsum(
                    "qhk,khd->qhd",
                    exp_scores.astype(jnp.bfloat16),
                    value_rows,
                    preferred_element_type=jnp.float32,
                )
                return (new_max, running_sum, weighted)

            return lax.cond(jnp.any(allowed), forward_compute, keep_same, totals)

        init_fwd = (
            jnp.full((rows_n, heads_att), -jnp.inf, jnp.float32),
            jnp.zeros((rows_n, heads_att), jnp.float32),
            jnp.zeros((rows_n, heads_att, AHEAD_DIM), jnp.float32),
        )
        all_keys, all_values = (
            lax.all_gather(key_heads, "seq", axis=0, tiled=True),
            lax.all_gather(value_heads, "seq", axis=0, tiled=True),
        )
        running_max, running_sum, weighted = fold_blocks(
            forward_fold, init_fwd, (all_keys, all_values), block_rows
        )
        attended = weighted / running_sum[:, :, None]
        log_total = running_max + jnp.log(running_sum)
        att_low = attended.reshape(rows_n, -1).astype(jnp.bfloat16)
        hidden_two = hidden_one + head_total(matmul(att_low, attout_full))
        normed_three = rms_norm(hidden_two, mlp_gain).astype(jnp.bfloat16)
        up_rows = matmul(normed_three, up_full)
        act_low = gelu_tanh(up_rows).astype(jnp.bfloat16)
        layer_rows = hidden_two + head_total(matmul(act_low, down_full))
        layer_list.append(layer_rows.astype(jnp.bfloat16))
        cot_low = cotangent[batch_index]
        down_wgrad = left_gram(act_low, cot_low)
        act_grad = transposed(cot_low, down_full)
        up_grad = jax.vjp(gelu_tanh, up_rows)[1](act_grad)[0].astype(jnp.bfloat16)
        up_wgrad = left_gram(normed_three, up_grad)
        three_grad = head_total(transposed(up_grad, up_full))
        hidden_part, mlpgain_part = jax.vjp(rms_norm, hidden_two, mlp_gain)[1](three_grad)
        hidden_two_grad = cot_low.astype(jnp.float32) + hidden_part
        branch_low = hidden_two_grad.astype(jnp.bfloat16)
        attout_wgrad = left_gram(att_low, branch_low)
        attended_grad = (
            transposed(branch_low, attout_full)
            .astype(jnp.bfloat16)
            .reshape(rows_n, heads_att, AHEAD_DIM)
        )
        delta_rows = jnp.sum(attended_grad.astype(jnp.float32) * attended, axis=-1)

        def query_fold(totals, shards, offset):
            key_rows, value_rows = shards
            key_pos = slot_position(
                order_row, offset + jnp.arange(key_rows.shape[0], dtype=jnp.int32), half_rows
            )
            key_seg = segment_of(key_pos, seq_ends)
            any_allowed = jnp.any(
                (key_pos[None, :] <= position[:, None]) & (key_seg[None, :] == segment[:, None])
            )

            def query_compute(current):
                probabilities = attention_probs(
                    queries, key_rows, position, key_pos, segment, key_seg, log_total, scaling
                )
                prob_grad = jnp.einsum(
                    "qhd,khd->qhk", attended_grad, value_rows, preferred_element_type=jnp.float32
                )
                score_grad = (probabilities * (prob_grad - delta_rows[:, :, None])).astype(
                    jnp.bfloat16
                )
                return current + jnp.einsum(
                    "qhk,khd->qhd", score_grad, key_rows, preferred_element_type=jnp.float32
                )

            return lax.cond(any_allowed, query_compute, keep_same, totals)

        zero_heads = jnp.zeros((rows_n, heads_att, AHEAD_DIM), jnp.float32)
        query_sum = fold_blocks(query_fold, zero_heads, (all_keys, all_values), block_rows)
        query_rows = lax.all_gather(queries.astype(jnp.float32), "seq", axis=0, tiled=True)
        grad_rows = lax.all_gather(attended_grad.astype(jnp.float32), "seq", axis=0, tiled=True)
        log_rows = lax.all_gather(log_total, "seq", axis=0, tiled=True)
        delta_part = lax.all_gather(delta_rows, "seq", axis=0, tiled=True)
        query_pos = slot_position(
            order_row, jnp.arange(query_rows.shape[0], dtype=jnp.int32), half_rows
        )
        query_seg = segment_of(query_pos, seq_ends)
        key_any_allowed = jnp.any(
            (position[None, :] <= query_pos[:, None]) & (segment[None, :] == query_seg[:, None])
        )

        def key_compute(current):
            query_low = query_rows.astype(jnp.bfloat16)
            grad_low = grad_rows.astype(jnp.bfloat16)
            probabilities = attention_probs(
                query_low, key_heads, query_pos, position, query_seg, segment, log_rows, scaling
            )
            value_grad = jnp.einsum(
                "qhk,qhd->khd",
                probabilities.astype(jnp.bfloat16),
                grad_low,
                preferred_element_type=jnp.float32,
            )
            prob_grad = jnp.einsum(
                "qhd,khd->qhk", grad_low, value_heads, preferred_element_type=jnp.float32
            )
            score_grad = (probabilities * (prob_grad - delta_part[:, :, None])).astype(jnp.bfloat16)
            key_grad = jnp.einsum(
                "qhk,qhd->khd", score_grad, query_low, preferred_element_type=jnp.float32
            )
            return (key_grad, value_grad)

        key_sum, value_sum = lax.cond(
            key_any_allowed, key_compute, keep_same, (zero_heads, zero_heads)
        )
        qkv_grad = jnp.stack(
            [
                (query_sum * scaling).astype(jnp.bfloat16),
                (key_sum * scaling).astype(jnp.bfloat16),
                value_sum.astype(jnp.bfloat16),
            ],
            axis=1,
        ).reshape(rows_n, 3, -1)
        qkv_wgrad = jnp.einsum(
            "rd,rcn->dcn", normed_two, qkv_grad, preferred_element_type=jnp.float32
        )
        two_grad = head_total(
            jnp.einsum("rcn,dcn->rd", qkv_grad, qkv_full, preferred_element_type=jnp.float32)
        )
        hidden_part, attgain_part = jax.vjp(rms_norm, hidden_one, att_gain)[1](two_grad)
        hidden_one_grad = hidden_two_grad + hidden_part
        mix_low = hidden_one_grad.astype(jnp.bfloat16)
        mixout_wgrad = left_gram(gated_low, mix_low)
        gated_grad = transposed(mix_low, mixout_full)
        y_grad = gated_grad * gating
        gate_grad = jax.vjp(jax.nn.silu, gate_in)[1](gated_grad * full_y)[0].astype(jnp.bfloat16)
        skip_part = jnp.sum(y_grad * mixed_x, axis=0)
        heads_mix = step_size.shape[1]
        y_blocks = y_grad.reshape(2, half_rows, -1)
        inflow = (
            jnp.exp(cumulative)
            * (seg_blocks == seg_before[:, None]).astype(jnp.float32)[:, :, None]
        )
        back_local = jnp.einsum(
            "bth,bthp,btn->bhpn",
            inflow,
            y_blocks.reshape(2, half_rows, heads_mix, -1),
            bc_b[:, :, NSTATE:],
            precision=highest,
        )
        all_back = lax.all_gather(back_local, "seq", axis=0, tiled=True)
        back_stream = all_back[inverse]
        rev_through, rev_state = lax.associative_scan(
            combine_state, (through_stream[::-1], back_stream[::-1]), axis=0
        )
        after_index = slots_n - 2 - my_blocks
        outgoing_grad = (
            rev_state[jnp.maximum(after_index, 0)]
            * (after_index >= 0).astype(jnp.float32)[:, None, None, None]
        )

        def scan_call(mixed_arg, step_arg, bc_arg, decay_arg, incoming_arg):
            return whole_all(
                mixed_arg, step_arg, bc_arg, decay_arg, incoming_arg, seg_blocks, seg_before
            )

        scan_pull = jax.vjp(scan_call, mixed_b, step_b, bc_b, decay_log, incoming)[1]
        x_scan_grad, step_grad, bc_grad, decay_part, incoming_grad = scan_pull(
            (y_blocks, outgoing_grad)
        )
        mixed_grad = y_grad * skip_gain + x_scan_grad.reshape(rows_n, -1)
        conv_grad = jax.vjp(jax.nn.silu, conv_sum)[1](mixed_grad)[0]
        conv_grad_b = conv_grad.reshape(2, half_rows, -1)
        convbias_part = jnp.sum(conv_grad, axis=0)
        convtaps_part = jnp.stack(
            [
                jnp.sum(
                    extended[:, tap_index : tap_index + half_rows]
                    * valid_taps[tap_index][:, :, None]
                    * conv_grad_b,
                    axis=(0, 1),
                )
                for tap_index in range(CONV)
            ]
        )
        all_heads = lax.all_gather(conv_grad_b[:, : CONV - 1], "seq", axis=0, tiled=True)
        pick_next = (order_row[None, :] == my_blocks[:, None] + 1).astype(jnp.float32)
        next_rows = jnp.einsum("bs,srd->brd", pick_next, all_heads, precision=highest)
        grad_ext = jnp.concatenate([conv_grad_b, next_rows], axis=1)
        position_ext = (my_blocks[:, None] * half_rows + ext_ids[None, :]).reshape(-1)
        x_blocks_grad = jnp.zeros(conv_grad_b.shape, jnp.float32)
        for tap_index in range(CONV):
            lag_rows = CONV - 1 - tap_index
            masked_grad = (
                grad_ext
                * tap_valid(position_ext, lag_rows, seq_ends).reshape(2, half_rows + CONV - 1)[
                    :, :, None
                ]
            )
            x_blocks_grad = (
                x_blocks_grad
                + conv_taps[tap_index] * masked_grad[:, lag_rows : lag_rows + half_rows]
            )
        x_low = x_blocks_grad.reshape(rows_n, -1).astype(jnp.bfloat16)
        rate_grad = step_grad.reshape(rows_n, -1) * jax.nn.sigmoid(rate_in + rate_bias)
        ratebias_part = jnp.sum(rate_grad, axis=0)
        bc_flat = bc_grad.reshape(rows_n, -1)
        normed_wide = normed_one.astype(jnp.float32)
        value_wgrad = left_gram(normed_one, x_low)
        gate_wgrad = left_gram(normed_one, gate_grad)
        state_wgrad = left_gram_exact(normed_wide, bc_flat)
        rate_wgrad = left_gram_exact(normed_wide, rate_grad)
        one_grad = head_total(
            transposed(x_low, value_full)
            + transposed(gate_grad, gate_full)
            + transposed_exact(bc_flat, state_full.astype(jnp.float32))
            + transposed_exact(rate_grad, rate_full.astype(jnp.float32))
        )
        hidden_part, mixgain_part = jax.vjp(rms_norm, hidden_in, mix_gain)[1](one_grad)
        input_list.append((hidden_one_grad + hidden_part).astype(jnp.bfloat16))
        big_part = (
            value_wgrad,
            gate_wgrad,
            state_wgrad,
            rate_wgrad,
            qkv_wgrad,
            up_wgrad,
            mixout_wgrad,
            attout_wgrad,
            down_wgrad,
        )
        small_part = (
            mixgain_part,
            attgain_part,
            mlpgain_part,
            ratebias_part,
            decay_part,
            convtaps_part,
            convbias_part,
            skip_part,
        )
        big_part = reduce_grads(big_part)
        big_sums = add_parts(big_sums, big_part)
        small_sums = add_parts(small_sums, small_part)
    small_total = lax.psum(
        (
            small_sums[0],
            small_sums[1],
            small_sums[2],
            small_sums[3],
            small_sums[4],
            small_sums[5],
            small_sums[6],
            small_sums[7],
        ),
        "seq",
    )
    return (
        jnp.stack(layer_list),
        jnp.stack(input_list),
        small_total[0],
        big_sums[0],
        big_sums[1],
        big_sums[2],
        big_sums[3],
        small_total[3],
        small_total[4],
        small_total[5],
        small_total[6],
        small_total[7],
        big_sums[6],
        small_total[1],
        big_sums[4],
        big_sums[7],
        small_total[2],
        big_sums[5],
        big_sums[8],
    )


f32 = jnp.float32
bf16 = jnp.bfloat16
HALF = 64
TAIL = 16
EXT = HALF + TAIL
ROWS = 2 * HALF
HCH = 512
LANES = 128
RATE_AT = 32
HPG = 8
TILE_ROWS = 32
SMALL_ROWS = 16
TAIL_COLS = slice(2 * HCH + LANES, 2 * HCH + 2 * LANES)
QKV_ROWS = HALF + HALF // 2
VMEM_LIMIT = 56 * 1024 * 1024


def mm(left_op, right_op):
    return jnp.dot(left_op, right_op, preferred_element_type=f32)


def two_parts(values):
    coarse = values.astype(bf16)
    return coarse, (values - coarse.astype(f32)).astype(bf16)


def mm_onehot(values, onehot):
    coarse, fine = two_parts(values)
    return mm(coarse, onehot) + mm(fine, onehot)


def nt(left_op, right_op):
    return lax.dot_general(
        left_op, right_op, (((1,), (1,)), ((), ())), preferred_element_type=f32
    )


def nt_onehot(values, onehot):
    coarse, fine = two_parts(values)
    return nt(coarse, onehot) + nt(fine, onehot)


def onehot_mm(onehot, values):
    coarse, fine = two_parts(values)
    return mm(onehot, coarse) + mm(onehot, fine)


def tn(left_op, right_op):
    return lax.dot_general(
        left_op, right_op, (((0,), (0,)), ((), ())), preferred_element_type=f32
    )


def iota(shape, axis):
    return lax.broadcasted_iota(jnp.int32, shape, axis)


def sigmoid(values):
    return 1.0 / (1.0 + jnp.exp(-values))


def softplus(values):
    return jnp.maximum(values, 0.0) + jnp.log1p(jnp.exp(-jnp.abs(values)))


def rms_rows(values):
    return lax.rsqrt(jnp.mean(values * values, axis=-1, keepdims=True) + epsilon)


def rms_back(values, gain_row, grad):
    scale = rms_rows(values)
    inner = grad * gain_row
    dot = jnp.mean(inner * values, axis=-1, keepdims=True)
    part = scale * (inner - values * (scale * scale) * dot)
    return part, jnp.sum(grad * (values * scale), axis=0, keepdims=True)


def same_block(rows_idx, cols_idx):
    return (rows_idx // HALF) == (cols_idx // HALF)


def lower_mask():
    rows_idx, cols_idx = iota((ROWS, ROWS), 0), iota((ROWS, ROWS), 1)
    return same_block(rows_idx, cols_idx) & (rows_idx >= cols_idx)


def spread_matrix():
    return (iota((LANES, HCH), 0) - RATE_AT == iota((LANES, HCH), 1) // HALF).astype(f32).astype(bf16)


def per_block(values_0, values_1, shape):
    return jnp.where(iota(shape, 0) < HALF, values_0, values_1)


def step_terms(state_rate, params):
    lane = iota((1, LANES), 1)
    is_rate = (lane >= RATE_AT) & (lane < RATE_AT + HPG)
    shifted = state_rate + params[6:7, 0:LANES]
    step = jnp.where(is_rate, softplus(shifted), 0.0)
    rates = jnp.where(is_rate, jnp.exp(params[7:8, 0:LANES]), 0.0)
    log_decay = -step * rates
    cumulative = onehot_mm(lower_mask().astype(f32).astype(bf16), log_decay)
    return shifted, step, rates, log_decay, cumulative


def tail_decay(cum_wide):
    last = per_block(cum_wide[HALF - 1 : HALF], cum_wide[ROWS - 1 : ROWS], cum_wide.shape)
    return jnp.exp(last - cum_wide)


def decay_matrix(cumulative, cumulative_t, head, mask):
    at = RATE_AT + head
    gap = cumulative[:, at : at + 1] - cumulative_t[at : at + 1, :]
    return jnp.where(mask, jnp.exp(jnp.where(mask, gap, 0.0)), 0.0)


def silu_parts(values):
    gate = sigmoid(values)
    return values * gate, gate * (1.0 + values * (1.0 - gate))


def put_state(msg_ref, batch, group, state):
    for lane_block in range(4):
        for state_half in range(2):
            msg_ref[batch * 16 + group * 8 + lane_block * 2 + state_half, 0:8, :] = state[
                state_half * 8 : (state_half + 1) * 8,
                lane_block * LANES : (lane_block + 1) * LANES,
            ]


def get_state(msg_ref, batch, group):
    base = batch * 16 + group * 8
    return jnp.concatenate(
        [
            jnp.concatenate(
                [
                    msg_ref[base + lane_block * 2 + state_half, 0:8, :]
                    for lane_block in range(4)
                ],
                axis=1,
            )
            for state_half in range(2)
        ],
        axis=0,
    )


def my_rows(core):
    return pl.ds(pl.multiple_of(core * HALF, HALF), HALF)


def in_kernel(
    ids_ref, order_ref, tok_ref, gain_ref, own_ref, other_ref, par_own_ref, par_other_ref,
    ext_ref, normed_ref, x_ref, conv_ref, gate_ref, sr_ref, cum_ref, inner_ref, local_ref,
    msg_ref, deal_ref, gains_ref, x_scr, tail_scr,
):
    chip, core = ids_ref[0], ids_ref[1]
    width = tok_ref.shape[2]
    place = iota((1, width), 1)
    block = place // TILE_ROWS
    source = (chip ^ (block // 4 + 4 * (block % 4))) * TILE_ROWS + place % TILE_ROWS
    deal = (iota((width, width), 0) == source).astype(f32)
    deal_low = deal.astype(bf16)
    deal_ref[...] = deal_low
    gains = mm_onehot(gain_ref[...], deal_low)
    gains_ref[...] = gains
    ext_list = []
    for batch in range(2):
        my_block = order_ref[batch, 2 * chip + core]
        before = jnp.int32(0)
        for slot in range(order_ref.shape[1]):
            before = jnp.where(order_ref[batch, slot] == my_block - 1, slot, before)
        apart = chip ^ (before // 2)
        tail_at = ((apart % 4) * 4 + apart // 4) * TILE_ROWS
        rows = pl.ds(pl.multiple_of(tail_at, TILE_ROWS), TILE_ROWS)

        @pl.when(core == batch)
        def _():
            tail_scr[batch] = own_ref[rows, TAIL_COLS].astype(f32)

        @pl.when(core != batch)
        def _():
            tail_scr[batch] = other_ref[rows, TAIL_COLS].astype(f32)

        tile = jnp.where(before % 2 == 0, tail_scr[batch, 0:12], tail_scr[batch, 12:24])
        tile = jnp.where(my_block == 0, 0.0, tile)
        tails = [
            jnp.concatenate([tile[4 * k + j : 4 * k + j + 1] for j in range(4)], axis=1)
            for k in range(CONV - 1)
        ]
        lead = jnp.zeros((TAIL - (CONV - 1), width), f32)
        ext_list.append(jnp.concatenate([lead] + tails, axis=0).astype(bf16))
        ext_list.append(tok_ref[batch, my_rows(core), :])
    ext_rows = mm(jnp.concatenate(ext_list, axis=0), deal_low).astype(bf16)
    ext_ref[...] = ext_rows
    hidden = ext_rows.astype(f32)
    normed = (hidden * rms_rows(hidden) * gains[0:1]).astype(bf16)
    normed_ref[...] = normed
    real = jnp.concatenate([normed[TAIL:EXT], normed[EXT + TAIL :]], axis=0)
    mask = lower_mask()
    spread = spread_matrix()
    for half, (w_ref, par_ref) in enumerate(
        ((own_ref, par_own_ref), (other_ref, par_other_ref))
    ):
        at = half * HCH
        params = par_ref[...]
        x_low = mm(normed, w_ref[:, 0:HCH]).astype(bf16)
        x_ref[:, at : at + HCH] = x_low
        x_scr[...] = x_low.astype(f32)
        gate_ref[:, at : at + HCH] = mm(real, w_ref[:, HCH : 2 * HCH])
        state_rate = mm(real, w_ref[:, 2 * HCH : 2 * HCH + LANES])
        sr_ref[:, half * LANES : (half + 1) * LANES] = state_rate
        conv_list = []
        for batch in range(2):
            conv = jnp.zeros((HALF, HCH), f32) + params[4:5]
            for tap in range(CONV):
                first = batch * EXT + TAIL - (CONV - 1) + tap
                conv = conv + params[tap : tap + 1] * x_scr[first : first + HALF, :]
            conv_list.append(conv)
        conv = jnp.concatenate(conv_list, axis=0)
        conv_ref[:, at : at + HCH] = conv
        mixed = conv * sigmoid(conv)
        _, step, _, _, cumulative = step_terms(state_rate, params)
        cum_wide = mm_onehot(cumulative, spread)
        cum_ref[:, at : at + HCH] = cum_wide
        driving = mm_onehot(step, spread) * mixed
        weighted = (driving * tail_decay(cum_wide)).astype(bf16)
        driving = driving.astype(bf16)
        b_rows = state_rate[:, 0:NSTATE].astype(bf16)
        c_rows = state_rate[:, NSTATE : 2 * NSTATE].astype(bf16)
        group = half ^ core
        for batch in range(2):
            rows = slice(batch * HALF, (batch + 1) * HALF)
            state = tn(b_rows[rows], weighted[rows])
            local_ref[batch, half] = state
            last_row = (batch + 1) * HALF - 1
            total = jnp.broadcast_to(cum_wide[last_row : last_row + 1], (4, HCH))
            coarse = total.astype(bf16).astype(f32)
            for state_half in range(2):
                block = jnp.concatenate(
                    [state[state_half * 8 : (state_half + 1) * 8], coarse, total - coarse], axis=0
                ).astype(bf16)
                for lane_block in range(4):
                    msg_ref[batch * 16 + group * 8 + lane_block * 2 + state_half] = block[
                        :, lane_block * LANES : (lane_block + 1) * LANES
                    ]
        inner_cb = nt(c_rows, b_rows)
        cumulative_t = cumulative.T
        first_head = iota((ROWS, LANES), 1) < HALF
        for pair in range(4):
            pair_rows = driving[:, pair * LANES : (pair + 1) * LANES]
            parts = [
                mm(
                    (decay_matrix(cumulative, cumulative_t, 2 * pair + k, mask) * inner_cb).astype(
                        bf16
                    ),
                    pair_rows,
                )
                for k in range(2)
            ]
            inner_ref[:, at + pair * LANES : at + (pair + 1) * LANES] = jnp.where(
                first_head, parts[0], parts[1]
            )


def invert_order(ids_ref, order_ref, slots_scr):
    slots_n = order_ref.shape[1]
    batch = (2 * ids_ref[0] + ids_ref[1]) // (slots_n // 2)
    for slot in range(slots_n):
        slots_scr[order_ref[batch, slot]] = slot


def block_decay(block):
    return jnp.exp(block[8:9] + block[12:13])


def forward_scan_kernel(ids_ref, order_ref, in_ref, out_ref, slots_scr):
    invert_order(ids_ref, order_ref, slots_scr)
    state = jnp.zeros((8, LANES), f32)
    for place in range(order_ref.shape[1]):
        slot = slots_scr[place]
        out_ref[slot] = state
        block = in_ref[slot].astype(f32)
        state = state * block_decay(block) + block[0:8]


def backward_scan_kernel(ids_ref, order_ref, decay_ref, in_ref, out_ref, slots_scr):
    invert_order(ids_ref, order_ref, slots_scr)
    state = jnp.zeros((8, LANES), f32)
    for place in reversed(range(order_ref.shape[1])):
        slot = slots_scr[place]
        out_ref[slot] = state
        state = state * block_decay(decay_ref[slot].astype(f32)) + in_ref[slot]


def mix_kernel(
    ids_ref, tok_ref, state_ref, sr_ref, cum_ref, inner_ref, conv_ref, gate_ref,
    par_own_ref, par_other_ref, own_ref, other_ref, gain_ref,
    full_ref, gated_ref, hidden_ref, normed_ref, msg_ref,
):
    core = ids_ref[1]
    hidden = tok_ref[...].astype(f32)
    hidden = jnp.concatenate([hidden[TAIL:EXT], hidden[EXT + TAIL :]], axis=0)
    for half, (w_ref, par_ref) in enumerate(
        ((own_ref, par_own_ref), (other_ref, par_other_ref))
    ):
        cols = slice(half * HCH, (half + 1) * HCH)
        c_rows = sr_ref[:, half * LANES + NSTATE : half * LANES + 2 * NSTATE].astype(bf16)
        carried = jnp.concatenate(
            [
                mm(
                    c_rows[batch * HALF : (batch + 1) * HALF],
                    get_state(state_ref, batch, half ^ core).astype(bf16),
                )
                for batch in range(2)
            ],
            axis=0,
        )
        conv = conv_ref[:, cols]
        mixed = conv * sigmoid(conv)
        full = inner_ref[:, cols] + jnp.exp(cum_ref[:, cols]) * carried + par_ref[5:6] * mixed
        full_ref[:, cols] = full
        gate = gate_ref[:, cols]
        gated = (full * (gate * sigmoid(gate))).astype(bf16)
        gated_ref[:, cols] = gated
        hidden = hidden + nt(gated, w_ref[:, 0:HCH])
    hidden_ref[...] = hidden
    normed = (hidden * rms_rows(hidden) * gain_ref[1:2]).astype(bf16)
    normed_ref[...] = normed
    for half, w_ref in enumerate((own_ref, other_ref)):
        rows_qkv = mm(normed, w_ref[:, HCH : HCH + 768]).astype(bf16)
        for batch in range(2):
            rows = slice(batch * HALF, (batch + 1) * HALF)
            for head in range(4):
                put_qkv(
                    msg_ref,
                    batch * 8 + (half ^ core) * 4 + head,
                    [
                        rows_qkv[rows, at : at + AHEAD_DIM]
                        for at in range(head * AHEAD_DIM, 768, 256)
                    ],
                )


def put_qkv(ref, at, members):
    ref[at, 0:HALF, 0:AHEAD_DIM] = members[0]
    ref[at, 0:HALF, AHEAD_DIM:LANES] = members[1]
    ref[at, HALF:QKV_ROWS, 0:AHEAD_DIM] = members[2][0 : HALF // 2]
    ref[at, HALF:QKV_ROWS, AHEAD_DIM:LANES] = members[2][HALF // 2 :]


def get_qkv(ref, at):
    return [
        ref[at, 0:HALF, 0:AHEAD_DIM],
        ref[at, 0:HALF, AHEAD_DIM:LANES],
        jnp.concatenate(
            [ref[at, HALF:QKV_ROWS, 0:AHEAD_DIM], ref[at, HALF:QKV_ROWS, AHEAD_DIM:LANES]], axis=0
        ),
    ]


def unpack_qkv(own_ref, other_ref, query_scr, key_scr, value_scr):
    for k, ref in enumerate((own_ref, other_ref)):
        for at in range(ref.shape[0]):
            rows = slice(at * HALF, (at + 1) * HALF)
            queries, keys, values = get_qkv(ref, at)
            if k == 0:
                query_scr[rows, :] = queries
            key_scr[k, rows, :] = keys
            value_scr[k, rows, :] = values


def put_rows(ref, at, member):
    ref[at, :, 0:AHEAD_DIM] = member[0 : HALF // 2]
    ref[at, :, AHEAD_DIM:LANES] = member[HALF // 2 :]


def get_rows(ref, at):
    return jnp.concatenate([ref[at, :, 0:AHEAD_DIM], ref[at, :, AHEAD_DIM:LANES]], axis=0)


QTILE = 256


def block_place(ids_ref, order_ref, block, other):
    chip, core = ids_ref[0], ids_ref[1]
    batch = chip // (order_ref.shape[1] // 4)
    return order_ref[batch, 2 * block + (core ^ other)] * HALF


def query_places(ids_ref, order_ref, tile):
    parts = [
        iota((HALF, 1), 0) + block_place(ids_ref, order_ref, tile * (QTILE // HALF) + k, 0)
        for k in range(QTILE // HALF)
    ]
    return jnp.concatenate(parts, axis=0)


def key_places(ids_ref, order_ref, other):
    lane = iota((1, LANES), 1)
    parts = []
    for pair in range(order_ref.shape[1] // 4):
        first = block_place(ids_ref, order_ref, 2 * pair, other)
        second = block_place(ids_ref, order_ref, 2 * pair + 1, other)
        parts.append(lane + jnp.where(lane < HALF, first, second - HALF))
    return jnp.concatenate(parts, axis=1)


def attend_kernel(
    ids_ref, order_ref, own_ref, other_ref, out_ref, log_ref, full_ref, query_scr, key_scr,
    value_scr,
):
    places = [key_places(ids_ref, order_ref, k) for k in range(2)]
    unpack_qkv(own_ref, other_ref, query_scr, key_scr, value_scr)
    scaling = AHEAD_DIM ** (-0.5)
    for tile in range(query_scr.shape[0] // QTILE):
        rows = slice(tile * QTILE, (tile + 1) * QTILE)
        place = query_places(ids_ref, order_ref, tile)
        queries = (query_scr[rows, :].astype(f32) * scaling).astype(bf16)
        scores = [
            jnp.where(
                places[k] <= place, nt(queries, key_scr[k]), -jnp.inf
            )
            for k in range(2)
        ]
        most = jnp.maximum(
            jnp.max(scores[0], axis=-1, keepdims=True), jnp.max(scores[1], axis=-1, keepdims=True)
        )
        exps = [jnp.exp(member - most) for member in scores]
        total = jnp.sum(exps[0], axis=-1, keepdims=True) + jnp.sum(exps[1], axis=-1, keepdims=True)
        mixed = mm(exps[0].astype(bf16), value_scr[0]) + mm(exps[1].astype(bf16), value_scr[1])
        mixed = mixed / total
        full_ref[rows, :] = mixed
        mixed = mixed.astype(bf16)
        for k in range(QTILE // HALF):
            put_rows(out_ref, tile * (QTILE // HALF) + k, mixed[k * HALF : (k + 1) * HALF])
        log_ref[rows, :] = most + jnp.log(total)


def attend_back_kernel(
    ids_ref, order_ref, own_ref, other_ref, grad_ref, log_ref, full_ref, mine_ref, theirs_ref,
    query_scr, key_scr, value_scr, query_sum, key_sum, value_sum,
):
    places = [key_places(ids_ref, order_ref, k) for k in range(2)]
    unpack_qkv(own_ref, other_ref, query_scr, key_scr, value_scr)
    scaling = AHEAD_DIM ** (-0.5)
    key_sum[...] = jnp.zeros(key_sum.shape, f32)
    value_sum[...] = jnp.zeros(value_sum.shape, f32)
    for tile in range(query_scr.shape[0] // QTILE):
        rows = slice(tile * QTILE, (tile + 1) * QTILE)
        place = query_places(ids_ref, order_ref, tile)
        queries = query_scr[rows, :]
        scaled = (queries.astype(f32) * scaling).astype(bf16)
        grad = jnp.concatenate(
            [get_rows(grad_ref, tile * (QTILE // HALF) + k) for k in range(QTILE // HALF)],
            axis=0,
        )
        log_total = log_ref[rows, :]
        probs = []
        prob_grads = []
        for k in range(2):
            scores = nt(scaled, key_scr[k]) - log_total
            probs.append(jnp.exp(jnp.where(places[k] <= place, scores, -jnp.inf)))
            prob_grads.append(nt(grad, value_scr[k]))
        delta = jnp.sum(grad.astype(f32) * full_ref[rows, :], axis=-1, keepdims=True)
        query_grad = jnp.zeros((QTILE, AHEAD_DIM), f32)
        for k in range(2):
            score_grad = (probs[k] * (prob_grads[k] - delta)).astype(bf16)
            value_sum[k] += tn(probs[k].astype(bf16), grad)
            key_sum[k] += tn(score_grad, queries)
            query_grad = query_grad + mm(score_grad, key_scr[k])
        query_sum[rows, :] = query_grad * scaling
    for at in range(mine_ref.shape[0]):
        rows = slice(at * HALF, (at + 1) * HALF)
        put_qkv(
            mine_ref, at, [query_sum[rows, :], key_sum[0, rows, :] * scaling, value_sum[0, rows, :]]
        )
        put_qkv(
            theirs_ref,
            at,
            [
                jnp.zeros((HALF, AHEAD_DIM), bf16),
                (key_sum[1, rows, :] * scaling).astype(bf16),
                value_sum[1, rows, :].astype(bf16),
            ],
        )


GELU_RATE = math.sqrt(2.0 / math.pi)
GELU_CUBE = 0.044715


def mlp_kernel(
    ids_ref, att_ref, hidden_ref, cot_ref, deal_ref, gain_ref, own_ref, other_ref,
    out_ref, hidden_two_ref, cot_both_ref, mine_ref, theirs_ref, hidden_grad_ref, gain_grad_ref,
    msg_ref,
    att_scr, result_scr,
):
    core = ids_ref[1]
    weights = (own_ref, other_ref)
    packs = (mine_ref, theirs_ref)
    up_cols, down_cols, att_cols = slice(0, 1024), slice(1024, 2048), slice(2048, 2304)
    cot_both = mm(
        jnp.concatenate(
            [cot_ref[batch, my_rows(side), :] for side in (core, 1 - core) for batch in range(2)],
            axis=0,
        ),
        deal_ref[...],
    ).astype(bf16)
    cot_both_ref[...] = cot_both
    cot = cot_both[0:ROWS]
    hidden = hidden_ref[...]
    for half in range(2):
        for batch in range(2):
            for head in range(4):
                att_scr[
                    half,
                    batch * HALF : (batch + 1) * HALF,
                    head * AHEAD_DIM : (head + 1) * AHEAD_DIM,
                ] = get_rows(att_ref, batch * 8 + (half ^ core) * 4 + head)
        packs[half][:, att_cols] = att_scr[half]
        hidden = hidden + nt(att_scr[half], weights[half][:, att_cols])
    gain = gain_ref[2:3]
    normed = (hidden * rms_rows(hidden) * gain).astype(bf16)
    normed_grad = jnp.zeros(hidden.shape, f32)
    for half in range(2):
        up_rows = mm(normed, weights[half][:, up_cols])
        squares = up_rows * up_rows
        bent = jnp.tanh(GELU_RATE * (up_rows + GELU_CUBE * squares * up_rows))
        act = (0.5 * up_rows * (1.0 + bent)).astype(bf16)
        slope = 0.5 * (1.0 + bent) + 0.5 * up_rows * (1.0 - bent * bent) * (
            GELU_RATE * (1.0 + 3.0 * GELU_CUBE * squares)
        )
        result_scr[half] = nt(act, weights[half][:, down_cols])
        packs[half][:, down_cols] = act
        up_grad = (mm(cot, weights[half][:, down_cols]) * slope).astype(bf16)
        packs[half][:, up_cols] = up_grad
        normed_grad = normed_grad + nt(up_grad, weights[half][:, up_cols])
        packs[half][:, 2304 : 2304 + 512] = normed
    hidden_two_ref[...] = hidden
    out_ref[...] = result_scr[0] + result_scr[1]
    part, gain_grad = rms_back(hidden, gain, normed_grad)
    gain_grad_ref[...] = gain_grad
    hidden_grad = cot.astype(f32) + part
    hidden_grad_ref[...] = hidden_grad
    branch = hidden_grad.astype(bf16)
    for half in range(2):
        packs[half][:, 2816 : 2816 + 512] = branch
        att_grad = mm(branch, weights[half][:, att_cols]).astype(bf16)
        for batch in range(2):
            for head in range(4):
                put_rows(
                    msg_ref,
                    batch * 8 + (half ^ core) * 4 + head,
                    att_grad[
                        batch * HALF : (batch + 1) * HALF,
                        head * AHEAD_DIM : (head + 1) * AHEAD_DIM,
                    ],
                )


def both_rows(mine_ref, theirs_ref, cols):
    return jnp.concatenate([mine_ref[:, cols], theirs_ref[:, cols]], axis=0)


def put_pieces(piece_refs, cols, values):
    rows_n = piece_refs[0].shape[0]
    for k, piece_ref in enumerate(piece_refs):
        piece_ref[:, cols] = values[k * rows_n : (k + 1) * rows_n].astype(bf16)


def third_grad_kernel(mine_ref, theirs_ref, cot_ref, *piece_refs):
    up_cols, down_cols, att_cols = slice(0, 1024), slice(1024, 2048), slice(2048, 2304)

    def both(cols):
        return both_rows(mine_ref, theirs_ref, cols)

    put_pieces(piece_refs, up_cols, tn(both(slice(2304, 2816)), both(up_cols)))
    put_pieces(piece_refs, down_cols, tn(cot_ref[...], both(down_cols)))
    put_pieces(piece_refs, att_cols, tn(both(slice(2816, 3328)), both(att_cols)))


def second_grad_kernel(mine_ref, theirs_ref, *piece_refs):
    def both(cols):
        return both_rows(mine_ref, theirs_ref, cols)

    for cols, base in ((slice(0, 512), 2304), (slice(512, 1280), 1792), (slice(1280, 1792), 2816)):
        put_pieces(piece_refs, cols, tn(both(slice(base, base + 512)), both(cols)))


def first_grad_kernel(ids_ref, mine_ref, theirs_ref, msg_ref, *piece_refs):
    cols = slice(0, HCH + LANES)
    rows = slice(0, 2 * EXT)
    packs = (mine_ref, theirs_ref)
    put_pieces(
        piece_refs,
        cols,
        tn(
            jnp.concatenate([ref[rows, HCH + LANES : 2 * HCH + LANES] for ref in packs], axis=0),
            jnp.concatenate([ref[rows, cols] for ref in packs], axis=0),
        ),
    )
    rows = slice(2 * EXT, 2 * EXT + SMALL_ROWS)
    small = mine_ref[rows, 0:HCH].astype(f32) + theirs_ref[rows, 0:HCH].astype(f32)
    tails = [ref[rows, HCH : 2 * HCH].astype(f32) for ref in packs]
    ordered = [jnp.where(ids_ref[1] == k, tails[0], tails[1]) for k in range(2)]
    tails = jnp.concatenate(
        [ordered[0][0:6], ordered[1][0:6], jnp.zeros((SMALL_ROWS - 12, HCH), f32)], axis=0
    )
    block = jnp.concatenate([small, tails], axis=1).astype(bf16)
    for k in range(msg_ref.shape[0]):
        msg_ref[k] = block


def sum_kernel(*refs):
    total = refs[0][...].astype(f32)
    for ref in refs[1:4]:
        total = total + ref[...].astype(f32)
    put_pieces(refs[4:], slice(0, total.shape[1]), total)


def sum_both_kernel(*refs):
    at = 0
    for group in (refs[0:4], refs[4:8]):
        total = group[0][...].astype(f32)
        for ref in group[1:]:
            total = total + ref[...].astype(f32)
        put_pieces(refs[8:], slice(at, at + total.shape[1]), total)
        at += total.shape[1]


def early_out_kernel(*refs):
    total = refs[0][...].astype(f32)
    for ref in refs[1:4]:
        total = total + ref[...].astype(f32)
    value_ref, state_ref, rate_ref, mix_ref, qkv_ref, gate_ref = refs[4:]
    value_ref[...] = total[:, 0:HCH]
    state_ref[...] = total[:, HCH : HCH + 32]
    rate_ref[...] = total[:, HCH : HCH + LANES].T[RATE_AT : RATE_AT + HPG]
    base = HCH + LANES
    mix_ref[...] = total[:, base : base + HCH]
    for kind in range(3):
        qkv_ref[kind] = total[:, base + HCH + kind * 256 : base + HCH + (kind + 1) * 256]
    gate_ref[...] = total[:, base + HCH + 768 :]


def mix_back_kernel(
    ids_ref, qkv_ref, first_ref, normed_ref, hidden_ref, hidden_grad_ref, gain_ref, own_ref,
    other_ref, gated_ref, gate_ref, full_ref, conv_ref, cum_ref, sr_ref,
    mine_ref, theirs_ref, y_grad_ref, gate_grad_ref, one_grad_ref, gain_grad_ref, skip_grad_ref,
    msg_ref, qkv_scr,
):
    core = ids_ref[1]
    weights = (own_ref, other_ref)
    packs = (mine_ref, theirs_ref)
    mix_cols, qkv_cols, gate_cols = slice(0, 512), slice(512, 1280), slice(1280, 1792)
    first = jnp.concatenate([first_ref[TAIL:EXT], first_ref[EXT + TAIL :]], axis=0)
    normed_grad = jnp.zeros(hidden_ref.shape, f32)
    for half in range(2):
        for batch in range(2):
            for head in range(4):
                members = get_qkv(qkv_ref, batch * 8 + (half ^ core) * 4 + head)
                for kind, member in enumerate(members):
                    at = kind * 256 + head * AHEAD_DIM
                    qkv_scr[batch * HALF : (batch + 1) * HALF, at : at + AHEAD_DIM] = member
        rows_grad = qkv_scr[...]
        packs[half][:, qkv_cols] = rows_grad
        normed_grad = normed_grad + nt(rows_grad, weights[half][:, qkv_cols])
    part, gain_grad = rms_back(hidden_ref[...], gain_ref[1:2], normed_grad)
    gain_grad_ref[...] = gain_grad
    one_grad = hidden_grad_ref[...] + part
    one_grad_ref[...] = one_grad
    branch = one_grad.astype(bf16)
    for half in range(2):
        cols = slice(half * HCH, (half + 1) * HCH)
        packs[half][:, mix_cols] = gated_ref[:, cols]
        packs[half][:, 1792:2304] = normed_ref[...]
        packs[half][:, 2304:2816] = branch
        packs[half][:, 2816:3328] = first
        gated_grad = mm(branch, weights[half][:, mix_cols])
        silu, slope = silu_parts(gate_ref[:, cols])
        y_grad = gated_grad * silu
        y_grad_ref[:, cols] = y_grad
        gate_grad = (gated_grad * full_ref[:, cols] * slope).astype(bf16)
        gate_grad_ref[:, cols] = gate_grad
        packs[half][:, gate_cols] = gate_grad
        conv = conv_ref[:, cols]
        skip_grad_ref[:, cols] = jnp.sum(y_grad * (conv * sigmoid(conv)), axis=0, keepdims=True)
        carried = (jnp.exp(cum_ref[:, cols]) * y_grad).astype(bf16)
        c_rows = sr_ref[:, half * LANES + NSTATE : half * LANES + 2 * NSTATE].astype(bf16)
        for batch in range(2):
            rows = slice(batch * HALF, (batch + 1) * HALF)
            put_state(msg_ref, batch, half ^ core, tn(c_rows[rows], carried[rows]))


def in_back_kernel(
    ids_ref, later_ref, state_ref, local_ref, sr_ref, cum_ref, conv_ref, x_ref, y_grad_ref,
    gate_grad_ref, normed_ref, tok_ref, gain_ref, one_grad_ref, own_ref, other_ref,
    par_own_ref, par_other_ref, deal_ref, skip_grad_ref, attgain_ref, mlpgain_ref,
    mine_ref, theirs_ref, hidden_grad_ref,
    x_scr, grad_scr, sr_scr, gate_scr,
):
    core = ids_ref[1]
    mask = lower_mask()
    spread = spread_matrix()
    normed = normed_ref[...]
    ext_grad = jnp.zeros((2 * EXT, normed.shape[1]), f32)
    lower_t = (
        same_block(iota((ROWS, ROWS), 0), iota((ROWS, ROWS), 1))
        & (iota((ROWS, ROWS), 0) <= iota((ROWS, ROWS), 1))
    ).astype(f32).astype(bf16)
    lane = iota((1, LANES), 1)
    small_list = []
    for half, (w_ref, par_ref, pack_ref) in enumerate(
        ((own_ref, par_own_ref, mine_ref), (other_ref, par_other_ref, theirs_ref))
    ):
        cols = slice(half * HCH, (half + 1) * HCH)
        group = half ^ core
        params = par_ref[...]
        state_rate = sr_ref[:, half * LANES : (half + 1) * LANES]
        shifted, step, rates, log_decay, cumulative = step_terms(state_rate, params)
        cumulative_t = cumulative.T
        cum_wide = cum_ref[:, cols]
        step_wide = mm_onehot(step, spread)
        conv = conv_ref[:, cols]
        mixed, conv_slope = silu_parts(conv)
        driving = step_wide * mixed
        tail = tail_decay(cum_wide)
        inflow = jnp.exp(cum_wide)
        y_grad = y_grad_ref[:, cols]
        y_low = y_grad.astype(bf16)
        driving_low = driving.astype(bf16)
        b_rows = state_rate[:, 0:NSTATE].astype(bf16)
        c_rows = state_rate[:, NSTATE : 2 * NSTATE].astype(bf16)
        inner_cb = nt(c_rows, b_rows)
        weighted = (driving * tail).astype(bf16)
        carried_grad = (inflow * y_grad).astype(bf16)
        through_list = []
        tail_list = []
        flow_list = []
        b_list = []
        c_list = []
        for batch in range(2):
            rows = slice(batch * HALF, (batch + 1) * HALF)
            incoming = get_state(state_ref, batch, group)
            later = get_state(later_ref, batch, group)
            total = cum_wide[(batch + 1) * HALF - 1 : (batch + 1) * HALF, :]
            outgoing = jnp.exp(total) * incoming + local_ref[batch, half]
            through_list.append(jnp.sum(later * outgoing, axis=0, keepdims=True))
            incoming = incoming.astype(bf16)
            later = later.astype(bf16)
            tail_list.append(mm(b_rows[rows], later))
            flow_list.append(mm(c_rows[rows], incoming))
            b_list.append(nt(weighted[rows], later))
            c_list.append(nt(carried_grad[rows], incoming))
        tail_part = tail * jnp.concatenate(tail_list, axis=0)
        flow_part = inflow * jnp.concatenate(flow_list, axis=0)
        first_head = iota((ROWS, LANES), 1) < HALF
        inner_grad = jnp.zeros((ROWS, ROWS), f32)
        row_sums = jnp.zeros((ROWS, LANES), f32)
        col_list = []
        drive_list = []
        for pair in range(4):
            lanes = slice(pair * LANES, (pair + 1) * LANES)
            y_pair = y_low[:, lanes]
            u_pair = driving_low[:, lanes]
            parts = []
            for k in range(2):
                head = 2 * pair + k
                mine = first_head if k == 0 else ~first_head
                decay = decay_matrix(cumulative, cumulative_t, head, mask)
                product = nt(jnp.where(mine, y_pair, jnp.zeros_like(y_pair)), u_pair)
                decayed = decay * product
                inner_grad = inner_grad + decayed
                both = decayed * inner_cb
                row_sums = row_sums + jnp.where(
                    lane == RATE_AT + head, jnp.sum(both, axis=1, keepdims=True), 0.0
                )
                col_list.append(jnp.sum(both, axis=0, keepdims=True))
                parts.append(tn((decay * inner_cb).astype(bf16), y_pair))
            drive_list.append(jnp.where(first_head, parts[0], parts[1]))
        drive_grad = jnp.concatenate(drive_list, axis=1) + tail_part
        col_rows = jnp.concatenate(
            [jnp.zeros((RATE_AT, ROWS), f32)]
            + col_list
            + [jnp.zeros((LANES - RATE_AT - HPG, ROWS), f32)],
            axis=0,
        )
        cum_grad = (
            row_sums
            - col_rows.T
            + nt_onehot(y_grad * flow_part - driving * tail_part, spread)
        )
        through_rows = nt_onehot(
            jnp.concatenate(through_list + [jnp.zeros((6, HCH), f32)], axis=0), spread
        )
        decay_grad = onehot_mm(lower_t, cum_grad) + per_block(
            through_rows[0:1], through_rows[1:2], (ROWS, LANES)
        )
        step_grad = nt_onehot(mixed * drive_grad, spread) - decay_grad * rates
        rate_grad = step_grad * sigmoid(shifted)
        inner_low = inner_grad.astype(bf16)
        b_grad = tn(inner_low, c_rows) + jnp.concatenate(b_list, axis=0)
        c_grad = mm(inner_low, b_rows) + jnp.concatenate(c_list, axis=0)
        is_rate = (lane >= RATE_AT) & (lane < RATE_AT + HPG)
        rate_grad = jnp.where(is_rate, rate_grad, 0.0)
        sr_grad = jnp.concatenate(
            [b_grad, c_grad, rate_grad[:, RATE_AT:LANES]], axis=1
        ).astype(bf16)
        mixed_grad = step_wide * drive_grad + params[5:6] * y_grad
        conv_grad = mixed_grad * conv_slope
        x_scr[...] = x_ref[:, cols].astype(f32)
        grad_scr[...] = jnp.zeros(grad_scr.shape, f32)
        sr_scr[...] = jnp.zeros(sr_scr.shape, bf16)
        gate_scr[...] = jnp.zeros(gate_scr.shape, bf16)
        gate_grad = gate_grad_ref[:, cols]
        for batch in range(2):
            rows = slice(batch * HALF, (batch + 1) * HALF)
            ext_rows = slice(batch * EXT + TAIL, (batch + 1) * EXT)
            grad_scr[batch, TAIL:EXT, :] = conv_grad[rows]
            sr_scr[ext_rows, :] = sr_grad[rows]
            gate_scr[ext_rows, :] = gate_grad[rows]
        x_list = []
        tap_list = [jnp.zeros((1, HCH), f32) for _ in range(CONV)]
        for batch in range(2):
            x_grad = jnp.zeros((EXT, HCH), f32)
            for tap in range(CONV):
                lag = CONV - 1 - tap
                x_grad = x_grad + params[tap : tap + 1] * grad_scr[batch, lag : lag + EXT, :]
                first = batch * EXT + TAIL - lag
                tap_list[tap] = tap_list[tap] + jnp.sum(
                    x_scr[first : first + HALF, :] * grad_scr[batch, TAIL:EXT, :],
                    axis=0,
                    keepdims=True,
                )
            x_list.append(x_grad)
        x_low = jnp.concatenate(x_list, axis=0).astype(bf16)
        small_list.append(
            jnp.concatenate(
                tap_list
                + [
                    jnp.sum(conv_grad, axis=0, keepdims=True),
                    skip_grad_ref[:, cols],
                    jnp.concatenate(
                        [
                            jnp.sum(rate_grad, axis=0, keepdims=True),
                            jnp.sum(decay_grad * log_decay, axis=0, keepdims=True),
                            jnp.zeros((1, HCH - 2 * LANES), f32),
                        ],
                        axis=1,
                    ),
                ],
                axis=0,
            )
        )
        pack_ref[0 : 2 * EXT, 0:HCH] = x_low
        pack_ref[0 : 2 * EXT, HCH : HCH + LANES] = sr_scr[...]
        pack_ref[0 : 2 * EXT, HCH + LANES : 2 * HCH + LANES] = normed
        ext_grad = (
            ext_grad
            + nt(x_low, w_ref[:, 0:HCH])
            + nt(gate_scr[...], w_ref[:, HCH : 2 * HCH])
            + nt(sr_scr[...], w_ref[:, 2 * HCH : 2 * HCH + LANES])
        )
    hidden = tok_ref[...].astype(f32)
    part, gain_grad = rms_back(hidden, gain_ref[0:1], ext_grad)
    deal = deal_ref[...]
    gain_grads = nt_onehot(
        jnp.concatenate([gain_grad, attgain_ref[...], mlpgain_ref[...]], axis=0), deal
    )
    tails = nt(
        jnp.concatenate([part[TAIL - 3 : TAIL], part[EXT + TAIL - 3 : EXT + TAIL]], axis=0).astype(
            bf16
        ),
        deal,
    )
    tails = jnp.concatenate([tails, jnp.zeros((SMALL_ROWS - 6, HCH), f32)], axis=0)
    for small, pack_ref in zip(small_list, (mine_ref, theirs_ref)):
        rows = slice(2 * EXT, 2 * EXT + SMALL_ROWS)
        pack_ref[rows, 0:HCH] = jnp.concatenate(
            [small, gain_grads, jnp.zeros((SMALL_ROWS - 10, HCH), f32)], axis=0
        ).astype(bf16)
        pack_ref[rows, HCH : 2 * HCH] = tails.astype(bf16)
        pack_ref[rows, 2 * HCH :] = jnp.zeros((SMALL_ROWS, LANES), bf16)
    rows_grad = jnp.concatenate([part[TAIL:EXT], part[EXT + TAIL :]], axis=0) + one_grad_ref[...]
    hidden_grad_ref[...] = nt(rows_grad.astype(bf16), deal)


SMEM_SPEC = pl.BlockSpec(memory_space=pltpu.SMEM)
VMEM_SPEC = pl.BlockSpec(memory_space=pltpu.VMEM)
ANY_SPEC = pl.BlockSpec(memory_space=pl.ANY)


def run_kernel(kernel, out_shapes, scalars_n, args, scratch=(), after=(), pieces=None, at=0):
    args_n = len(args)
    pieces = [] if pieces is None else list(pieces[0]) + list(pieces[1])
    scratch = list(scratch)
    if pieces:
        rows_n, cols = pieces[0].shape
        scratch += [pltpu.VMEM((4 * rows_n, cols), bf16)] * 2
        scratch.append(pltpu.SemaphoreType.DMA((8,)))

    def body(*refs):
        ins, rest = list(refs[:args_n]), list(refs[args_n + len(pieces) + len(after) :])
        if pieces:
            *rest, own_scr, other_scr, sems = rest
            copies = [
                pltpu.make_async_copy(
                    refs[args_n + k],
                    (own_scr, other_scr)[k // 4].at[pl.ds((k % 4) * rows_n, rows_n), :],
                    sems.at[k],
                )
                for k in range(8)
            ]
            for copy in copies:
                copy.start()
            for copy in copies:
                copy.wait()
            ins[at:at] = [own_scr, other_scr]
        kernel(*ins, *rest)

    return pl.pallas_call(
        body,
        out_shape=[jax.ShapeDtypeStruct(shape, kind) for shape, kind in out_shapes],
        in_specs=[SMEM_SPEC] * scalars_n
        + [VMEM_SPEC] * (args_n - scalars_n)
        + [ANY_SPEC] * (len(pieces) + len(after)),
        out_specs=[VMEM_SPEC] * len(out_shapes),
        scratch_shapes=scratch,
        compiler_params=pltpu.CompilerParams(vmem_limit_bytes=VMEM_LIMIT),
        name=kernel.__name__,
        cost_estimate=pl.CostEstimate(flops=0, transcendentals=0, bytes_accessed=0),
    )(*args, *pieces, *after)


def hold(values, *after):
    def body(*refs):
        pass

    return pl.pallas_call(
        body,
        out_shape=jax.ShapeDtypeStruct(values.shape, values.dtype),
        in_specs=[ANY_SPEC] * (1 + len(after)),
        out_specs=ANY_SPEC,
        input_output_aliases={0: 0},
    )(values, *after)


def flip(bits, ranks):
    return [(index, index ^ bits) for index in range(ranks)]


def swap_cores(values):
    return lax.ppermute(values, "head", [(0, 1), (1, 0)])


def permute_three(pieces, step, ranks):
    return [
        lax.ppermute(piece, "seq", flip(step * (k + 1), ranks)) for k, piece in enumerate(pieces)
    ]


def sum_pieces(mine, moved, after=()):
    rows_n, cols = mine.shape
    return run_kernel(
        sum_kernel, [((rows_n // 4, cols), bf16)] * 4, 0, [mine] + moved, (), after
    )


def exchange(values, axes):
    return lax.all_to_all(values, axes, 0, 0, tiled=True)


def dealt_device(
    tokens, cotangent, lengths, order, mix_gain, in_value, in_gate, in_state, in_rate,
    rate_bias, decay_log, conv_taps, conv_bias, skip_gain, mix_out, att_gain, qkv_proj,
    att_out, mlp_gain, mlp_up, mlp_down,
):
    ranks = lax.axis_size("seq")
    both = ("seq", "head")
    chip = lax.axis_index("seq")
    core = lax.axis_index("head")
    ids = jnp.stack([chip, core]).astype(jnp.int32)
    my_slot = 2 * chip + core
    width = tokens.shape[2]
    slots_n = 2 * ranks
    shard_rows = width // ranks
    slots_scratch = (pltpu.SMEM((slots_n,), jnp.int32),)

    tail_rows = tokens.reshape(2, 2, HALF, width)[:, :, HALF - (CONV - 1) :]
    tail_rows = jnp.where(core == 0, tail_rows[0], tail_rows[1]).reshape(-1, LANES)
    tail_rows = jnp.pad(tail_rows, ((0, shard_rows - tail_rows.shape[0]), (0, 0)))
    first_shard = jnp.concatenate(
        [
            in_value, in_gate, in_state, in_rate, jnp.zeros((shard_rows, LANES - 40), bf16),
            tail_rows,
        ],
        axis=1,
    )
    first_cols = first_shard.shape[1]
    second_cols, third_cols = HCH + 768, 2304
    early_shard = jnp.concatenate(
        [first_shard, mix_out.T, qkv_proj.reshape(shard_rows, -1)], axis=1
    )
    third_shard = jnp.concatenate([mlp_up, mlp_down.T, att_out.T], axis=1)
    early_pieces = [early_shard] + permute_three([early_shard] * 3, 4, ranks)
    first_stack = jnp.concatenate([piece[:, :first_cols] for piece in early_pieces], axis=0)
    third_shard = hold(third_shard, first_stack)
    third_z = [third_shard] + permute_three([third_shard] * 3, 4, ranks)
    third_stack = jnp.concatenate(third_z, axis=0)
    first_own = [first_stack] + permute_three([first_stack] * 3, 1, ranks)
    first_own[3] = hold(first_own[3], *third_z[1:])
    first_pieces = (first_own, [swap_cores(piece) for piece in first_own])
    second_stack = jnp.concatenate([piece[:, first_cols:] for piece in early_pieces], axis=0)
    second_own = [second_stack] + permute_three([second_stack] * 3, 1, ranks)
    second_pieces = (second_own, [swap_cores(piece) for piece in second_own])

    par_own = jnp.concatenate(
        [
            conv_taps,
            conv_bias[None],
            skip_gain[None],
            jnp.pad(rate_bias, (RATE_AT, HCH - RATE_AT - HPG))[None],
            jnp.pad(decay_log, (RATE_AT, HCH - RATE_AT - HPG))[None],
        ],
        axis=0,
    )
    par_other = swap_cores(par_own)
    gains = jnp.stack([mix_gain, att_gain, mlp_gain])

    channels = 2 * HCH
    (
        ext_rows, normed_one, x_in, conv_sum, gate_in, state_rate, cum_wide, inner_y,
        local_state, msg, deal_low, gains,
    ) = run_kernel(
        in_kernel,
        [
            ((2 * EXT, width), bf16),
            ((2 * EXT, width), bf16),
            ((2 * EXT, channels), bf16),
            ((ROWS, channels), f32),
            ((ROWS, channels), f32),
            ((ROWS, 2 * LANES), f32),
            ((ROWS, channels), f32),
            ((ROWS, channels), f32),
            ((2, 2, NSTATE, HCH), f32),
            ((slots_n, 16, LANES), bf16),
            ((width, width), bf16),
            ((3, width), f32),
        ],
        2,
        (ids, order, tokens, gains, par_own, par_other),
        (pltpu.VMEM((2 * EXT, HCH), f32), pltpu.VMEM((2, TILE_ROWS, LANES), f32)),
        pieces=first_pieces,
        at=4,
    )

    states = exchange(hold(msg, *second_own[1:3]), both)
    (incoming,) = run_kernel(
        forward_scan_kernel,
        [((slots_n, 8, LANES), f32)],
        2,
        (ids, order, states),
        slots_scratch,
        after=second_own[3:],
    )
    incoming = exchange(incoming, both)

    full_y, gated, hidden_one, normed_two, msg = run_kernel(
        mix_kernel,
        [
            ((ROWS, channels), f32),
            ((ROWS, channels), bf16),
            ((ROWS, width), f32),
            ((ROWS, width), bf16),
            ((ranks, QKV_ROWS, LANES), bf16),
        ],
        1,
        (
            ids, ext_rows, incoming, state_rate, cum_wide, inner_y, conv_sum, gate_in,
            par_own, par_other, gains,
        ),
        after=[third_stack],
        pieces=second_pieces,
        at=10,
    )
    third_own = [third_stack] + permute_three([third_stack] * 3, 1, ranks)
    att_rows = ranks * HALF
    qkv_scratch = (
        pltpu.VMEM((att_rows, AHEAD_DIM), bf16),
        pltpu.VMEM((2, att_rows, AHEAD_DIM), bf16),
        pltpu.VMEM((2, att_rows, AHEAD_DIM), bf16),
    )
    qkv_own = exchange(hold(msg, *third_own[1:3]), "seq")
    qkv_other = swap_cores(qkv_own)
    attended, log_total, att_full = run_kernel(
        attend_kernel,
        [((ranks, HALF // 2, LANES), bf16), ((att_rows, 1), f32), ((att_rows, AHEAD_DIM), f32)],
        2,
        (ids, order, qkv_own, qkv_other),
        qkv_scratch,
    )
    third_own[3] = hold(third_own[3], log_total)
    third_pieces = (third_own, [swap_cores(piece) for piece in third_own])
    attended = exchange(attended, "seq")

    pack_cols = 3328
    (
        down_rows, hidden_two, cot_both, mine, theirs, two_grad, mlpgain_part, msg,
    ) = run_kernel(
        mlp_kernel,
        [
            ((ROWS, width), f32),
            ((ROWS, width), f32),
            ((2 * ROWS, width), bf16),
            ((ROWS, pack_cols), bf16),
            ((ROWS, pack_cols), bf16),
            ((ROWS, width), f32),
            ((1, width), f32),
            ((ranks, HALF // 2, LANES), bf16),
        ],
        1,
        (ids, attended, hidden_one, cotangent, deal_low, gains),
        (pltpu.VMEM((2, ROWS, 256), bf16), pltpu.VMEM((2, ROWS, width), f32)),
        pieces=third_pieces,
        at=6,
    )
    att_grad = exchange(msg, "seq")
    third_grads = run_kernel(
        third_grad_kernel,
        [((width // 4, third_cols), bf16)] * 4,
        0,
        (mine, swap_cores(theirs), cot_both),
    )
    mine, theirs = run_kernel(
        attend_back_kernel,
        [((ranks, QKV_ROWS, LANES), f32), ((ranks, QKV_ROWS, LANES), bf16)],
        2,
        (ids, order, qkv_own, qkv_other, att_grad, log_total, att_full),
        qkv_scratch
        + (
            pltpu.VMEM((att_rows, AHEAD_DIM), f32),
            pltpu.VMEM((2, att_rows, AHEAD_DIM), f32),
            pltpu.VMEM((2, att_rows, AHEAD_DIM), f32),
        ),
        after=third_grads[:1],
    )
    qkv_grad = (mine + swap_cores(theirs).astype(f32)).astype(bf16)
    qkv_grad = exchange(qkv_grad, "seq")
    third_moved = permute_three(third_grads[1:], 1, ranks)

    mine, theirs, y_grad, gate_grad, one_grad, attgain_part, skip_part, msg = run_kernel(
        mix_back_kernel,
        [
            ((ROWS, pack_cols), bf16),
            ((ROWS, pack_cols), bf16),
            ((ROWS, channels), f32),
            ((ROWS, channels), bf16),
            ((ROWS, width), f32),
            ((1, width), f32),
            ((1, channels), f32),
            ((slots_n, 8, LANES), f32),
        ],
        1,
        (
            ids, qkv_grad, normed_one, normed_two, hidden_one, two_grad, gains, gated, gate_in,
            full_y, conv_sum, cum_wide, state_rate,
        ),
        (pltpu.VMEM((ROWS, 768), bf16),),
        pieces=second_pieces,
        at=7,
        after=third_moved[:2],
    )
    back_states = exchange(msg, both)
    second_grads = run_kernel(
        second_grad_kernel,
        [((width // 4, second_cols + HCH), bf16)] * 4,
        0,
        (mine, swap_cores(theirs)),
    )
    (later,) = run_kernel(
        backward_scan_kernel,
        [((slots_n, 8, LANES), f32)],
        2,
        (ids, order, states, back_states),
        slots_scratch,
        after=[second_grads[0], third_moved[2]],
    )
    third_parts = sum_pieces(third_grads[0], third_moved, (later,))
    third_moved = permute_three(third_parts[1:], 4, ranks)
    second_moved = permute_three(second_grads[1:], 1, ranks)
    later = exchange(later, both)

    grad_cols = HCH + LANES
    pack_shape = (2 * EXT + SMALL_ROWS, grad_cols + width)
    mine, theirs, tokens_grad = run_kernel(
        in_back_kernel,
        [(pack_shape, bf16), (pack_shape, bf16), ((ROWS, width), f32)],
        1,
        (
            ids, later, incoming, local_state, state_rate, cum_wide, conv_sum, x_in, y_grad,
            gate_grad, normed_one, ext_rows, gains, one_grad, par_own, par_other, deal_low,
            skip_part, attgain_part, mlpgain_part,
        ),
        (
            pltpu.VMEM((2 * EXT, HCH), f32),
            pltpu.VMEM((2, EXT + TAIL, HCH), f32),
            pltpu.VMEM((2 * EXT, LANES), bf16),
            pltpu.VMEM((2 * EXT, HCH), bf16),
        ),
        after=[third_parts[0]],
        pieces=first_pieces,
        at=14,
    )
    last_msg, *first_grads = run_kernel(
        first_grad_kernel,
        [((ranks, SMALL_ROWS, 2 * HCH), bf16)] + [((width // 4, grad_cols), bf16)] * 4,
        1,
        (ids, mine, swap_cores(theirs)),
        after=second_moved,
    )
    first_moved = permute_three(first_grads[1:], 1, ranks)
    last = exchange(hold(last_msg, *first_moved), "seq")
    early_parts = run_kernel(
        sum_both_kernel,
        [((width // 16, grad_cols + second_cols + HCH), bf16)] * 4,
        0,
        [first_grads[0]] + first_moved + [second_grads[0]] + second_moved,
    )
    third_total = third_parts[0].astype(f32)
    for piece in third_moved:
        third_total = third_total + piece.astype(f32)
    my_blocks = jnp.sum(
        jnp.where(jnp.arange(slots_n)[None, :] == my_slot, order, 0), axis=1
    )
    last = last.astype(f32)
    small_total = jnp.sum(last[:, 0:10, 0:HCH], axis=0)
    next_tails = last[:, 0:12, HCH:].reshape(ranks, 2, 2, CONV - 1, width).transpose(2, 0, 1, 3, 4)
    next_tails = next_tails.reshape(2, slots_n, CONV - 1, width)
    pick_next = (order == my_blocks[:, None] + 1).astype(f32)
    tail_add = jnp.sum(pick_next[:, :, None, None] * next_tails, axis=1)
    tokens_grad = tokens_grad.reshape(2, HALF, width)
    tokens_grad = jnp.concatenate(
        [tokens_grad[:, : HALF - (CONV - 1)], tokens_grad[:, HALF - (CONV - 1) :] + tail_add],
        axis=1,
    ).astype(bf16)
    layer_rows = nt((hidden_two + down_rows).astype(bf16), deal_low).astype(bf16)
    outs = jnp.stack([layer_rows.reshape(2, HALF, width), tokens_grad])
    outs_other = swap_cores(outs)
    outs = jnp.where(
        core == 0,
        jnp.concatenate([outs, outs_other], axis=2),
        jnp.concatenate([outs_other, outs], axis=2),
    )
    small_outs = [
        small_total[7],
        small_total[6, RATE_AT : RATE_AT + HPG],
        small_total[6, LANES + RATE_AT : LANES + RATE_AT + HPG],
        small_total[0:4],
        small_total[4],
        small_total[5],
        small_total[8],
        small_total[9],
    ]
    early_outs = run_kernel(
        early_out_kernel,
        [
            (shape, f32)
            for shape in (
                in_value.shape,
                in_state.shape,
                in_rate.shape[::-1],
                mix_out.shape[::-1],
                (qkv_proj.shape[1], qkv_proj.shape[0], qkv_proj.shape[2]),
                in_gate.shape,
            )
        ],
        0,
        [early_parts[0]] + permute_three(early_parts[1:], 4, ranks),
        after=[outs] + small_outs,
    )
    return (
        outs[0],
        outs[1],
        small_outs[0],
        early_outs[0],
        early_outs[5],
        early_outs[1],
        early_outs[2].T,
        small_outs[1],
        small_outs[2],
        small_outs[3],
        small_outs[4],
        small_outs[5],
        early_outs[3].T,
        small_outs[6],
        early_outs[4].transpose(1, 0, 2),
        third_total[:, 2048:2304].T,
        small_outs[7],
        third_total[:, 0:1024],
        third_total[:, 1024:2048].T,
    )


def layer(*args):
    tokens, lengths = args[0], args[2]
    fits = lax.axis_size("seq") == 16 and lax.axis_size("head") == 2
    fits = fits and lengths.shape == (2, 1) and tokens.shape[1] == ROWS
    return dealt_device(*args) if fits else on_device(*args)


def solution(mesh):
    return jax.shard_map(
        layer,
        mesh=mesh,
        in_specs=(
            P(None, "seq", None),
            P(None, "seq", None),
            P(),
            P(),
            P(),
            P("seq", "head"),
            P("seq", "head"),
            P("seq", "head"),
            P("seq", "head"),
            P("head"),
            P("head"),
            P(None, "head"),
            P("head"),
            P("head"),
            P("head", "seq"),
            P(),
            P("seq", None, "head"),
            P("head", "seq"),
            P(),
            P("seq", "head"),
            P("head", "seq"),
        ),
        out_specs=(
            P(None, "seq", None),
            P(None, "seq", None),
            P(),
            P("seq", "head"),
            P("seq", "head"),
            P("seq", "head"),
            P("seq", "head"),
            P("head"),
            P("head"),
            P(None, "head"),
            P("head"),
            P("head"),
            P("head", "seq"),
            P(),
            P("seq", None, "head"),
            P("head", "seq"),
            P(),
            P("seq", "head"),
            P("head", "seq"),
        ),
        check_vma=False,
    )
```

```python
import functools
import math

import jax
import jax.numpy as jnp
from jax import lax
from jax.experimental import pallas as pl
from jax.experimental.pallas import tpu as pltpu
from jax.sharding import PartitionSpec as P

NSTATE = 16
CONV = 4
AHEAD_DIM = 64


epsilon = 1e-05
highest = lax.Precision.HIGHEST


def rms_norm(values, gain_row):
    return (
        values * lax.rsqrt(jnp.mean(values * values, axis=-1, keepdims=True) + epsilon) * gain_row
    )


def gelu_tanh(values):
    return jax.nn.gelu(values, approximate=True)


def segment_of(position, seq_ends):
    bounds = seq_ends[:-1]
    return jnp.sum((jnp.asarray(position)[..., None] >= bounds).astype(jnp.int32), axis=-1)


def tap_valid(position, lag_rows, seq_ends):
    source = position - lag_rows
    return (
        (source >= 0) & (segment_of(source, seq_ends) == segment_of(position, seq_ends))
    ).astype(jnp.float32)


def slot_position(order_row, row_ids, half_rows):
    slot = row_ids // half_rows
    slot_table = jnp.arange(order_row.shape[0], dtype=jnp.int32)
    block = jnp.sum(jnp.where(slot[:, None] == slot_table[None, :], order_row[None, :], 0), axis=1)
    return block * half_rows + row_ids % half_rows


def stream_slots(order_row):
    slot_table = jnp.arange(order_row.shape[0], dtype=jnp.int32)
    return jnp.sum(
        jnp.where(order_row[None, :] == slot_table[:, None], slot_table[None, :], 0), axis=1
    )


def matmul(left_op, right_op):
    return jnp.dot(left_op, right_op, preferred_element_type=jnp.float32)


def transposed(left_op, right_op):
    return lax.dot_general(
        left_op, right_op, (((1,), (1,)), ((), ())), preferred_element_type=jnp.float32
    )


def left_gram(left_op, right_op):
    return lax.dot_general(
        left_op, right_op, (((0,), (0,)), ((), ())), preferred_element_type=jnp.float32
    )


def transposed_exact(left_op, right_op):
    return lax.dot_general(
        left_op,
        right_op,
        (((1,), (1,)), ((), ())),
        preferred_element_type=jnp.float32,
        precision=highest,
    )


def left_gram_exact(left_op, right_op):
    return lax.dot_general(
        left_op,
        right_op,
        (((0,), (0,)), ((), ())),
        preferred_element_type=jnp.float32,
        precision=highest,
    )


def keep_same(current):
    return current


def head_total(partial_rows):
    return lax.psum(partial_rows, "head")


def collect(in_value, in_gate, in_state, in_rate, qkv_proj, mlp_up, mix_out, att_out, mlp_down):
    return (
        lax.all_gather(in_value, "seq", axis=0, tiled=True),
        lax.all_gather(in_gate, "seq", axis=0, tiled=True),
        lax.all_gather(in_state, "seq", axis=0, tiled=True),
        lax.all_gather(in_rate, "seq", axis=0, tiled=True),
        lax.all_gather(qkv_proj, "seq", axis=0, tiled=True),
        lax.all_gather(mlp_up, "seq", axis=0, tiled=True),
        lax.all_gather(mix_out, "seq", axis=1, tiled=True),
        lax.all_gather(att_out, "seq", axis=1, tiled=True),
        lax.all_gather(mlp_down, "seq", axis=1, tiled=True),
    )


def reduce_grads(grad_parts):
    return (
        lax.psum_scatter(grad_parts[0], "seq", scatter_dimension=0, tiled=True),
        lax.psum_scatter(grad_parts[1], "seq", scatter_dimension=0, tiled=True),
        lax.psum_scatter(grad_parts[2], "seq", scatter_dimension=0, tiled=True),
        lax.psum_scatter(grad_parts[3], "seq", scatter_dimension=0, tiled=True),
        lax.psum_scatter(grad_parts[4], "seq", scatter_dimension=0, tiled=True),
        lax.psum_scatter(grad_parts[5], "seq", scatter_dimension=0, tiled=True),
        lax.psum_scatter(grad_parts[6], "seq", scatter_dimension=1, tiled=True),
        lax.psum_scatter(grad_parts[7], "seq", scatter_dimension=1, tiled=True),
        lax.psum_scatter(grad_parts[8], "seq", scatter_dimension=1, tiled=True),
    )


def fold_blocks(fold_fn, initial, arrays, block_rows):
    blocks_n = arrays[0].shape[0] // block_rows

    def one_step(block_index, current):
        offset = block_index * block_rows
        shards = tuple(
            (lax.dynamic_slice_in_dim(member, offset, block_rows, 0) for member in arrays)
        )
        return fold_fn(current, shards, offset)

    return lax.fori_loop(0, blocks_n, one_step, initial)


def add_parts(left_op, right_op):
    if left_op is None:
        return right_op
    return tuple((first_part + second_part for first_part, second_part in zip(left_op, right_op)))


def combine_state(earlier, later):
    return (earlier[0] * later[0], later[0][..., None, None] * earlier[1] + later[1])


def attention_probs(
    query_rows, key_rows, query_pos, key_pos, query_seg, key_seg, log_total, scaling
):
    allowed = ((key_pos[None, :] <= query_pos[:, None]) & (key_seg[None, :] == query_seg[:, None]))[
        :, None, :
    ]
    scores = (
        jnp.einsum("qhd,khd->qhk", query_rows, key_rows, preferred_element_type=jnp.float32)
        * scaling
    )
    return jnp.where(allowed, jnp.exp(jnp.where(allowed, scores - log_total[:, :, None], 0.0)), 0.0)


def scan_terms(mixed_x, step_size, bc_rows, decay_log, segment, seg_before):
    rows_n, heads_n = step_size.shape
    log_decay = -step_size * jnp.exp(decay_log)
    cumulative = jnp.cumsum(log_decay, axis=0)
    driving = step_size[:, :, None] * mixed_x.reshape(rows_n, heads_n, -1)
    tail_weight = (
        jnp.exp(cumulative[-1][None, :] - cumulative)
        * (segment == segment[-1]).astype(jnp.float32)[:, None]
    )
    local_state = jnp.einsum(
        "sh,shp,sn->hpn", tail_weight, driving, bc_rows[:, :NSTATE], precision=highest
    )
    through = jnp.exp(cumulative[-1]) * (segment[-1] == seg_before).astype(jnp.float32)
    return (cumulative, driving, through, local_state)


def scan_output(cumulative, driving, bc_rows, incoming, segment, seg_before):
    rows_n = cumulative.shape[0]
    row_ids = jnp.arange(rows_n, dtype=jnp.int32)
    allowed = ((row_ids[:, None] >= row_ids[None, :]) & (segment[:, None] == segment[None, :]))[
        :, :, None
    ]
    decays = jnp.where(
        allowed,
        jnp.exp(jnp.where(allowed, cumulative[:, None, :] - cumulative[None, :, :], 0.0)),
        0.0,
    )
    inner_cb = jnp.dot(bc_rows[:, NSTATE:], bc_rows[:, :NSTATE].T, precision=highest)
    output = jnp.einsum("tsh,shp->thp", decays * inner_cb[:, :, None], driving, precision=highest)
    inflow = jnp.exp(cumulative) * (segment == seg_before).astype(jnp.float32)[:, None]
    output = output + inflow[:, :, None] * jnp.einsum(
        "tn,hpn->thp", bc_rows[:, NSTATE:], incoming, precision=highest
    )
    return output.reshape(rows_n, -1)


def scan_whole(mixed_x, step_size, bc_rows, decay_log, incoming, segment, seg_before):
    cumulative, driving, through, local_state = scan_terms(
        mixed_x, step_size, bc_rows, decay_log, segment, seg_before
    )
    output = scan_output(cumulative, driving, bc_rows, incoming, segment, seg_before)
    return (output, through[:, None, None] * incoming + local_state)


def on_device(
    tokens,
    cotangent,
    lengths,
    order,
    mix_gain,
    in_value,
    in_gate,
    in_state,
    in_rate,
    rate_bias,
    decay_log,
    conv_taps,
    conv_bias,
    skip_gain,
    mix_out,
    att_gain,
    qkv_proj,
    att_out,
    mlp_gain,
    mlp_up,
    mlp_down,
):
    rows_n = tokens.shape[1]
    half_rows = rows_n // 2
    slots_n = 2 * lax.axis_size("seq")
    my_slot = 2 * lax.axis_index("seq")
    total_rows = rows_n * lax.axis_size("seq")
    block_rows = math.gcd(total_rows, 1024)
    scaling = AHEAD_DIM ** (-0.5)
    local_ids = jnp.arange(half_rows, dtype=jnp.int32)
    ext_ids = jnp.arange(half_rows + CONV - 1, dtype=jnp.int32)
    terms_all = jax.vmap(scan_terms, in_axes=(0, 0, 0, None, 0, 0))
    output_all = jax.vmap(scan_output, in_axes=(0, 0, 0, 0, 0, 0))
    whole_all = jax.vmap(scan_whole, in_axes=(0, 0, 0, None, 0, 0, 0))
    layer_list = []
    input_list = []
    big_sums = None
    small_sums = None
    for batch_index in range(tokens.shape[0]):
        (
            value_full,
            gate_full,
            state_full,
            rate_full,
            qkv_full,
            up_full,
            mixout_full,
            attout_full,
            down_full,
        ) = collect(
            in_value, in_gate, in_state, in_rate, qkv_proj, mlp_up, mix_out, att_out, mlp_down
        )
        seq_ends = jnp.cumsum(lengths[batch_index])
        order_row = order[batch_index]
        inverse = stream_slots(order_row)
        my_blocks = lax.dynamic_slice_in_dim(order_row, my_slot, 2)
        position = (my_blocks[:, None] * half_rows + local_ids[None, :]).reshape(rows_n)
        segment = segment_of(position, seq_ends)
        seg_blocks = segment.reshape(2, half_rows)
        seg_before = segment_of(my_blocks * half_rows - 1, seq_ends)
        hidden_in = tokens[batch_index].astype(jnp.float32)
        normed_one = rms_norm(hidden_in, mix_gain).astype(jnp.bfloat16)
        x_in = matmul(normed_one, value_full).astype(jnp.bfloat16)
        gate_in = matmul(normed_one, gate_full)
        bc_rows = matmul(normed_one, state_full)
        rate_in = matmul(normed_one, rate_full)
        step_size = jax.nn.softplus(rate_in + rate_bias)
        x_blocks = x_in.reshape(2, half_rows, -1)
        all_tails = lax.all_gather(x_blocks[:, half_rows - (CONV - 1) :], "seq", axis=0, tiled=True)
        pick_prev = (order_row[None, :] == my_blocks[:, None] - 1).astype(jnp.bfloat16)
        edge_rows = jnp.einsum(
            "bs,srd->brd", pick_prev, all_tails, preferred_element_type=jnp.float32
        )
        extended = jnp.concatenate([edge_rows, x_blocks.astype(jnp.float32)], axis=1)
        valid_taps = [
            tap_valid(position, CONV - 1 - tap_index, seq_ends).reshape(2, half_rows)
            for tap_index in range(CONV)
        ]
        conv_blocks = jnp.zeros(x_blocks.shape, jnp.float32) + conv_bias
        for tap_index in range(CONV):
            conv_blocks = (
                conv_blocks
                + conv_taps[tap_index]
                * extended[:, tap_index : tap_index + half_rows]
                * valid_taps[tap_index][:, :, None]
            )
        conv_sum = conv_blocks.reshape(rows_n, -1)
        mixed_x = jax.nn.silu(conv_sum)
        mixed_b = mixed_x.reshape(2, half_rows, -1)
        step_b = step_size.reshape(2, half_rows, -1)
        bc_b = bc_rows.reshape(2, half_rows, -1)
        cumulative, driving, through, local_state = terms_all(
            mixed_b, step_b, bc_b, decay_log, seg_blocks, seg_before
        )
        all_through, all_state = (
            lax.all_gather(through, "seq", axis=0, tiled=True),
            lax.all_gather(local_state, "seq", axis=0, tiled=True),
        )
        through_stream = all_through[inverse]
        state_stream = all_state[inverse]
        acc_through, acc_state = lax.associative_scan(
            combine_state, (through_stream, state_stream), axis=0
        )
        before = my_blocks - 1
        incoming = (
            acc_state[jnp.maximum(before, 0)]
            * (before >= 0).astype(jnp.float32)[:, None, None, None]
        )
        ssm_out = output_all(cumulative, driving, bc_b, incoming, seg_blocks, seg_before).reshape(
            rows_n, -1
        )
        full_y = ssm_out + skip_gain * mixed_x
        gating = jax.nn.silu(gate_in)
        gated_low = (full_y * gating).astype(jnp.bfloat16)
        hidden_one = hidden_in + head_total(matmul(gated_low, mixout_full))
        normed_two = rms_norm(hidden_one, att_gain).astype(jnp.bfloat16)
        qkv_rows = jnp.einsum(
            "rd,dcn->rcn", normed_two, qkv_full, preferred_element_type=jnp.float32
        ).astype(jnp.bfloat16)
        heads_att = qkv_rows.shape[2] // AHEAD_DIM
        queries = qkv_rows[:, 0].reshape(rows_n, heads_att, AHEAD_DIM)
        key_heads = qkv_rows[:, 1].reshape(rows_n, heads_att, AHEAD_DIM)
        value_heads = qkv_rows[:, 2].reshape(rows_n, heads_att, AHEAD_DIM)

        def forward_fold(totals, shards, offset):
            key_rows, value_rows = shards
            key_pos = slot_position(
                order_row, offset + jnp.arange(key_rows.shape[0], dtype=jnp.int32), half_rows
            )
            allowed = (
                (key_pos[None, :] <= position[:, None])
                & (segment_of(key_pos, seq_ends)[None, :] == segment[:, None])
            )[:, None, :]

            def forward_compute(current):
                running_max, running_sum, weighted = current
                scores = (
                    jnp.einsum(
                        "qhd,khd->qhk", queries, key_rows, preferred_element_type=jnp.float32
                    )
                    * scaling
                )
                scores = jnp.where(allowed, scores, -jnp.inf)
                new_max = jnp.maximum(running_max, jnp.max(scores, axis=-1))
                safe_max = jnp.where(new_max == -jnp.inf, 0.0, new_max)
                exp_scores = jnp.exp(scores - safe_max[:, :, None])
                factor = jnp.exp(running_max - safe_max)
                running_sum = running_sum * factor + jnp.sum(exp_scores, axis=-1)
                weighted = weighted * factor[:, :, None] + jnp.einsum(
                    "qhk,khd->qhd",
                    exp_scores.astype(jnp.bfloat16),
                    value_rows,
                    preferred_element_type=jnp.float32,
                )
                return (new_max, running_sum, weighted)

            return lax.cond(jnp.any(allowed), forward_compute, keep_same, totals)

        init_fwd = (
            jnp.full((rows_n, heads_att), -jnp.inf, jnp.float32),
            jnp.zeros((rows_n, heads_att), jnp.float32),
            jnp.zeros((rows_n, heads_att, AHEAD_DIM), jnp.float32),
        )
        all_keys, all_values = (
            lax.all_gather(key_heads, "seq", axis=0, tiled=True),
            lax.all_gather(value_heads, "seq", axis=0, tiled=True),
        )
        running_max, running_sum, weighted = fold_blocks(
            forward_fold, init_fwd, (all_keys, all_values), block_rows
        )
        attended = weighted / running_sum[:, :, None]
        log_total = running_max + jnp.log(running_sum)
        att_low = attended.reshape(rows_n, -1).astype(jnp.bfloat16)
        hidden_two = hidden_one + head_total(matmul(att_low, attout_full))
        normed_three = rms_norm(hidden_two, mlp_gain).astype(jnp.bfloat16)
        up_rows = matmul(normed_three, up_full)
        act_low = gelu_tanh(up_rows).astype(jnp.bfloat16)
        layer_rows = hidden_two + head_total(matmul(act_low, down_full))
        layer_list.append(layer_rows.astype(jnp.bfloat16))
        cot_low = cotangent[batch_index]
        down_wgrad = left_gram(act_low, cot_low)
        act_grad = transposed(cot_low, down_full)
        up_grad = jax.vjp(gelu_tanh, up_rows)[1](act_grad)[0].astype(jnp.bfloat16)
        up_wgrad = left_gram(normed_three, up_grad)
        three_grad = head_total(transposed(up_grad, up_full))
        hidden_part, mlpgain_part = jax.vjp(rms_norm, hidden_two, mlp_gain)[1](three_grad)
        hidden_two_grad = cot_low.astype(jnp.float32) + hidden_part
        branch_low = hidden_two_grad.astype(jnp.bfloat16)
        attout_wgrad = left_gram(att_low, branch_low)
        attended_grad = (
            transposed(branch_low, attout_full)
            .astype(jnp.bfloat16)
            .reshape(rows_n, heads_att, AHEAD_DIM)
        )
        delta_rows = jnp.sum(attended_grad.astype(jnp.float32) * attended, axis=-1)

        def query_fold(totals, shards, offset):
            key_rows, value_rows = shards
            key_pos = slot_position(
                order_row, offset + jnp.arange(key_rows.shape[0], dtype=jnp.int32), half_rows
            )
            key_seg = segment_of(key_pos, seq_ends)
            any_allowed = jnp.any(
                (key_pos[None, :] <= position[:, None]) & (key_seg[None, :] == segment[:, None])
            )

            def query_compute(current):
                probabilities = attention_probs(
                    queries, key_rows, position, key_pos, segment, key_seg, log_total, scaling
                )
                prob_grad = jnp.einsum(
                    "qhd,khd->qhk", attended_grad, value_rows, preferred_element_type=jnp.float32
                )
                score_grad = (probabilities * (prob_grad - delta_rows[:, :, None])).astype(
                    jnp.bfloat16
                )
                return current + jnp.einsum(
                    "qhk,khd->qhd", score_grad, key_rows, preferred_element_type=jnp.float32
                )

            return lax.cond(any_allowed, query_compute, keep_same, totals)

        zero_heads = jnp.zeros((rows_n, heads_att, AHEAD_DIM), jnp.float32)
        query_sum = fold_blocks(query_fold, zero_heads, (all_keys, all_values), block_rows)
        query_rows = lax.all_gather(queries.astype(jnp.float32), "seq", axis=0, tiled=True)
        grad_rows = lax.all_gather(attended_grad.astype(jnp.float32), "seq", axis=0, tiled=True)
        log_rows = lax.all_gather(log_total, "seq", axis=0, tiled=True)
        delta_part = lax.all_gather(delta_rows, "seq", axis=0, tiled=True)
        query_pos = slot_position(
            order_row, jnp.arange(query_rows.shape[0], dtype=jnp.int32), half_rows
        )
        query_seg = segment_of(query_pos, seq_ends)
        key_any_allowed = jnp.any(
            (position[None, :] <= query_pos[:, None]) & (segment[None, :] == query_seg[:, None])
        )

        def key_compute(current):
            query_low = query_rows.astype(jnp.bfloat16)
            grad_low = grad_rows.astype(jnp.bfloat16)
            probabilities = attention_probs(
                query_low, key_heads, query_pos, position, query_seg, segment, log_rows, scaling
            )
            value_grad = jnp.einsum(
                "qhk,qhd->khd",
                probabilities.astype(jnp.bfloat16),
                grad_low,
                preferred_element_type=jnp.float32,
            )
            prob_grad = jnp.einsum(
                "qhd,khd->qhk", grad_low, value_heads, preferred_element_type=jnp.float32
            )
            score_grad = (probabilities * (prob_grad - delta_part[:, :, None])).astype(jnp.bfloat16)
            key_grad = jnp.einsum(
                "qhk,qhd->khd", score_grad, query_low, preferred_element_type=jnp.float32
            )
            return (key_grad, value_grad)

        key_sum, value_sum = lax.cond(
            key_any_allowed, key_compute, keep_same, (zero_heads, zero_heads)
        )
        qkv_grad = jnp.stack(
            [
                (query_sum * scaling).astype(jnp.bfloat16),
                (key_sum * scaling).astype(jnp.bfloat16),
                value_sum.astype(jnp.bfloat16),
            ],
            axis=1,
        ).reshape(rows_n, 3, -1)
        qkv_wgrad = jnp.einsum(
            "rd,rcn->dcn", normed_two, qkv_grad, preferred_element_type=jnp.float32
        )
        two_grad = head_total(
            jnp.einsum("rcn,dcn->rd", qkv_grad, qkv_full, preferred_element_type=jnp.float32)
        )
        hidden_part, attgain_part = jax.vjp(rms_norm, hidden_one, att_gain)[1](two_grad)
        hidden_one_grad = hidden_two_grad + hidden_part
        mix_low = hidden_one_grad.astype(jnp.bfloat16)
        mixout_wgrad = left_gram(gated_low, mix_low)
        gated_grad = transposed(mix_low, mixout_full)
        y_grad = gated_grad * gating
        gate_grad = jax.vjp(jax.nn.silu, gate_in)[1](gated_grad * full_y)[0].astype(jnp.bfloat16)
        skip_part = jnp.sum(y_grad * mixed_x, axis=0)
        heads_mix = step_size.shape[1]
        y_blocks = y_grad.reshape(2, half_rows, -1)
        inflow = (
            jnp.exp(cumulative)
            * (seg_blocks == seg_before[:, None]).astype(jnp.float32)[:, :, None]
        )
        back_local = jnp.einsum(
            "bth,bthp,btn->bhpn",
            inflow,
            y_blocks.reshape(2, half_rows, heads_mix, -1),
            bc_b[:, :, NSTATE:],
            precision=highest,
        )
        all_back = lax.all_gather(back_local, "seq", axis=0, tiled=True)
        back_stream = all_back[inverse]
        rev_through, rev_state = lax.associative_scan(
            combine_state, (through_stream[::-1], back_stream[::-1]), axis=0
        )
        after_index = slots_n - 2 - my_blocks
        outgoing_grad = (
            rev_state[jnp.maximum(after_index, 0)]
            * (after_index >= 0).astype(jnp.float32)[:, None, None, None]
        )

        def scan_call(mixed_arg, step_arg, bc_arg, decay_arg, incoming_arg):
            return whole_all(
                mixed_arg, step_arg, bc_arg, decay_arg, incoming_arg, seg_blocks, seg_before
            )

        scan_pull = jax.vjp(scan_call, mixed_b, step_b, bc_b, decay_log, incoming)[1]
        x_scan_grad, step_grad, bc_grad, decay_part, incoming_grad = scan_pull(
            (y_blocks, outgoing_grad)
        )
        mixed_grad = y_grad * skip_gain + x_scan_grad.reshape(rows_n, -1)
        conv_grad = jax.vjp(jax.nn.silu, conv_sum)[1](mixed_grad)[0]
        conv_grad_b = conv_grad.reshape(2, half_rows, -1)
        convbias_part = jnp.sum(conv_grad, axis=0)
        convtaps_part = jnp.stack(
            [
                jnp.sum(
                    extended[:, tap_index : tap_index + half_rows]
                    * valid_taps[tap_index][:, :, None]
                    * conv_grad_b,
                    axis=(0, 1),
                )
                for tap_index in range(CONV)
            ]
        )
        all_heads = lax.all_gather(conv_grad_b[:, : CONV - 1], "seq", axis=0, tiled=True)
        pick_next = (order_row[None, :] == my_blocks[:, None] + 1).astype(jnp.float32)
        next_rows = jnp.einsum("bs,srd->brd", pick_next, all_heads, precision=highest)
        grad_ext = jnp.concatenate([conv_grad_b, next_rows], axis=1)
        position_ext = (my_blocks[:, None] * half_rows + ext_ids[None, :]).reshape(-1)
        x_blocks_grad = jnp.zeros(conv_grad_b.shape, jnp.float32)
        for tap_index in range(CONV):
            lag_rows = CONV - 1 - tap_index
            masked_grad = (
                grad_ext
                * tap_valid(position_ext, lag_rows, seq_ends).reshape(2, half_rows + CONV - 1)[
                    :, :, None
                ]
            )
            x_blocks_grad = (
                x_blocks_grad
                + conv_taps[tap_index] * masked_grad[:, lag_rows : lag_rows + half_rows]
            )
        x_low = x_blocks_grad.reshape(rows_n, -1).astype(jnp.bfloat16)
        rate_grad = step_grad.reshape(rows_n, -1) * jax.nn.sigmoid(rate_in + rate_bias)
        ratebias_part = jnp.sum(rate_grad, axis=0)
        bc_flat = bc_grad.reshape(rows_n, -1)
        normed_wide = normed_one.astype(jnp.float32)
        value_wgrad = left_gram(normed_one, x_low)
        gate_wgrad = left_gram(normed_one, gate_grad)
        state_wgrad = left_gram_exact(normed_wide, bc_flat)
        rate_wgrad = left_gram_exact(normed_wide, rate_grad)
        one_grad = head_total(
            transposed(x_low, value_full)
            + transposed(gate_grad, gate_full)
            + transposed_exact(bc_flat, state_full.astype(jnp.float32))
            + transposed_exact(rate_grad, rate_full.astype(jnp.float32))
        )
        hidden_part, mixgain_part = jax.vjp(rms_norm, hidden_in, mix_gain)[1](one_grad)
        input_list.append((hidden_one_grad + hidden_part).astype(jnp.bfloat16))
        big_part = (
            value_wgrad,
            gate_wgrad,
            state_wgrad,
            rate_wgrad,
            qkv_wgrad,
            up_wgrad,
            mixout_wgrad,
            attout_wgrad,
            down_wgrad,
        )
        small_part = (
            mixgain_part,
            attgain_part,
            mlpgain_part,
            ratebias_part,
            decay_part,
            convtaps_part,
            convbias_part,
            skip_part,
        )
        big_part = reduce_grads(big_part)
        big_sums = add_parts(big_sums, big_part)
        small_sums = add_parts(small_sums, small_part)
    small_total = lax.psum(
        (
            small_sums[0],
            small_sums[1],
            small_sums[2],
            small_sums[3],
            small_sums[4],
            small_sums[5],
            small_sums[6],
            small_sums[7],
        ),
        "seq",
    )
    return (
        jnp.stack(layer_list),
        jnp.stack(input_list),
        small_total[0],
        big_sums[0],
        big_sums[1],
        big_sums[2],
        big_sums[3],
        small_total[3],
        small_total[4],
        small_total[5],
        small_total[6],
        small_total[7],
        big_sums[6],
        small_total[1],
        big_sums[4],
        big_sums[7],
        small_total[2],
        big_sums[5],
        big_sums[8],
    )


f32 = jnp.float32
bf16 = jnp.bfloat16
HALF = 64
TAIL = 16
EXT = HALF + TAIL
ROWS = 2 * HALF
HCH = 512
LANES = 128
RATE_AT = 32
HPG = 8
TILE_ROWS = 32
SMALL_ROWS = 16
TAIL_COLS = slice(2 * HCH + LANES, 2 * HCH + 2 * LANES)
QKV_ROWS = HALF + HALF // 2
VMEM_LIMIT = 56 * 1024 * 1024


def mm(left_op, right_op):
    return jnp.dot(left_op, right_op, preferred_element_type=f32)


def two_parts(values):
    coarse = values.astype(bf16)
    return coarse, (values - coarse.astype(f32)).astype(bf16)


def mm_onehot(values, onehot):
    coarse, fine = two_parts(values)
    return mm(coarse, onehot) + mm(fine, onehot)


def nt(left_op, right_op):
    return lax.dot_general(
        left_op, right_op, (((1,), (1,)), ((), ())), preferred_element_type=f32
    )


def nt_onehot(values, onehot):
    coarse, fine = two_parts(values)
    return nt(coarse, onehot) + nt(fine, onehot)


def onehot_mm(onehot, values):
    coarse, fine = two_parts(values)
    return mm(onehot, coarse) + mm(onehot, fine)


def tn(left_op, right_op):
    return lax.dot_general(
        left_op, right_op, (((0,), (0,)), ((), ())), preferred_element_type=f32
    )


def iota(shape, axis):
    return lax.broadcasted_iota(jnp.int32, shape, axis)


def sigmoid(values):
    return 1.0 / (1.0 + jnp.exp(-values))


def softplus(values):
    return jnp.maximum(values, 0.0) + jnp.log1p(jnp.exp(-jnp.abs(values)))


def rms_rows(values):
    return lax.rsqrt(jnp.mean(values * values, axis=-1, keepdims=True) + epsilon)


def rms_back(values, gain_row, grad):
    scale = rms_rows(values)
    inner = grad * gain_row
    dot = jnp.mean(inner * values, axis=-1, keepdims=True)
    part = scale * (inner - values * (scale * scale) * dot)
    return part, jnp.sum(grad * (values * scale), axis=0, keepdims=True)


def same_block(rows_idx, cols_idx):
    return (rows_idx // HALF) == (cols_idx // HALF)


def lower_mask():
    rows_idx, cols_idx = iota((ROWS, ROWS), 0), iota((ROWS, ROWS), 1)
    return same_block(rows_idx, cols_idx) & (rows_idx >= cols_idx)


def spread_matrix():
    return (iota((LANES, HCH), 0) - RATE_AT == iota((LANES, HCH), 1) // HALF).astype(f32).astype(bf16)


def per_block(values_0, values_1, shape):
    return jnp.where(iota(shape, 0) < HALF, values_0, values_1)


def step_terms(state_rate, params):
    lane = iota((1, LANES), 1)
    is_rate = (lane >= RATE_AT) & (lane < RATE_AT + HPG)
    shifted = state_rate + params[6:7, 0:LANES]
    step = jnp.where(is_rate, softplus(shifted), 0.0)
    rates = jnp.where(is_rate, jnp.exp(params[7:8, 0:LANES]), 0.0)
    log_decay = -step * rates
    cumulative = onehot_mm(lower_mask().astype(f32).astype(bf16), log_decay)
    return shifted, step, rates, log_decay, cumulative


def tail_decay(cum_wide):
    last = per_block(cum_wide[HALF - 1 : HALF], cum_wide[ROWS - 1 : ROWS], cum_wide.shape)
    return jnp.exp(last - cum_wide)


def decay_matrix(cumulative, cumulative_t, head, mask):
    at = RATE_AT + head
    gap = cumulative[:, at : at + 1] - cumulative_t[at : at + 1, :]
    return jnp.where(mask, jnp.exp(jnp.where(mask, gap, 0.0)), 0.0)


def silu_parts(values):
    gate = sigmoid(values)
    return values * gate, gate * (1.0 + values * (1.0 - gate))


def put_state(msg_ref, batch, group, state):
    for lane_block in range(4):
        for state_half in range(2):
            msg_ref[batch * 16 + group * 8 + lane_block * 2 + state_half, 0:8, :] = state[
                state_half * 8 : (state_half + 1) * 8,
                lane_block * LANES : (lane_block + 1) * LANES,
            ]


def get_state(msg_ref, batch, group):
    base = batch * 16 + group * 8
    return jnp.concatenate(
        [
            jnp.concatenate(
                [
                    msg_ref[base + lane_block * 2 + state_half, 0:8, :]
                    for lane_block in range(4)
                ],
                axis=1,
            )
            for state_half in range(2)
        ],
        axis=0,
    )


def my_rows(core):
    return pl.ds(pl.multiple_of(core * HALF, HALF), HALF)


def in_kernel(
    ids_ref, order_ref, tok_ref, gain_ref, own_ref, other_ref, par_own_ref, par_other_ref,
    ext_ref, normed_ref, x_ref, conv_ref, gate_ref, sr_ref, cum_ref, inner_ref, local_ref,
    msg_ref, deal_ref, gains_ref, x_scr, tail_scr,
):
    chip, core = ids_ref[0], ids_ref[1]
    width = tok_ref.shape[2]
    place = iota((1, width), 1)
    block = place // TILE_ROWS
    source = (chip ^ (block // 4 + 4 * (block % 4))) * TILE_ROWS + place % TILE_ROWS
    deal = (iota((width, width), 0) == source).astype(f32)
    deal_low = deal.astype(bf16)
    deal_ref[...] = deal_low
    gains = mm_onehot(gain_ref[...], deal_low)
    gains_ref[...] = gains
    ext_list = []
    for batch in range(2):
        my_block = order_ref[batch, 2 * chip + core]
        before = jnp.int32(0)
        for slot in range(order_ref.shape[1]):
            before = jnp.where(order_ref[batch, slot] == my_block - 1, slot, before)
        apart = chip ^ (before // 2)
        tail_at = ((apart % 4) * 4 + apart // 4) * TILE_ROWS
        rows = pl.ds(pl.multiple_of(tail_at, TILE_ROWS), TILE_ROWS)

        @pl.when(core == batch)
        def _():
            tail_scr[batch] = own_ref[rows, TAIL_COLS].astype(f32)

        @pl.when(core != batch)
        def _():
            tail_scr[batch] = other_ref[rows, TAIL_COLS].astype(f32)

        tile = jnp.where(before % 2 == 0, tail_scr[batch, 0:12], tail_scr[batch, 12:24])
        tile = jnp.where(my_block == 0, 0.0, tile)
        tails = [
            jnp.concatenate([tile[4 * k + j : 4 * k + j + 1] for j in range(4)], axis=1)
            for k in range(CONV - 1)
        ]
        lead = jnp.zeros((TAIL - (CONV - 1), width), f32)
        ext_list.append(jnp.concatenate([lead] + tails, axis=0).astype(bf16))
        ext_list.append(tok_ref[batch, my_rows(core), :])
    ext_rows = mm(jnp.concatenate(ext_list, axis=0), deal_low).astype(bf16)
    ext_ref[...] = ext_rows
    hidden = ext_rows.astype(f32)
    normed = (hidden * rms_rows(hidden) * gains[0:1]).astype(bf16)
    normed_ref[...] = normed
    real = jnp.concatenate([normed[TAIL:EXT], normed[EXT + TAIL :]], axis=0)
    mask = lower_mask()
    spread = spread_matrix()
    for half, (w_ref, par_ref) in enumerate(
        ((own_ref, par_own_ref), (other_ref, par_other_ref))
    ):
        at = half * HCH
        params = par_ref[...]
        x_low = mm(normed, w_ref[:, 0:HCH]).astype(bf16)
        x_ref[:, at : at + HCH] = x_low
        x_scr[...] = x_low.astype(f32)
        gate_ref[:, at : at + HCH] = mm(real, w_ref[:, HCH : 2 * HCH])
        state_rate = mm(real, w_ref[:, 2 * HCH : 2 * HCH + LANES])
        sr_ref[:, half * LANES : (half + 1) * LANES] = state_rate
        conv_list = []
        for batch in range(2):
            conv = jnp.zeros((HALF, HCH), f32) + params[4:5]
            for tap in range(CONV):
                first = batch * EXT + TAIL - (CONV - 1) + tap
                conv = conv + params[tap : tap + 1] * x_scr[first : first + HALF, :]
            conv_list.append(conv)
        conv = jnp.concatenate(conv_list, axis=0)
        conv_ref[:, at : at + HCH] = conv
        mixed = conv * sigmoid(conv)
        _, step, _, _, cumulative = step_terms(state_rate, params)
        cum_wide = mm_onehot(cumulative, spread)
        cum_ref[:, at : at + HCH] = cum_wide
        driving = mm_onehot(step, spread) * mixed
        weighted = (driving * tail_decay(cum_wide)).astype(bf16)
        driving = driving.astype(bf16)
        b_rows = state_rate[:, 0:NSTATE].astype(bf16)
        c_rows = state_rate[:, NSTATE : 2 * NSTATE].astype(bf16)
        group = half ^ core
        for batch in range(2):
            rows = slice(batch * HALF, (batch + 1) * HALF)
            state = tn(b_rows[rows], weighted[rows])
            local_ref[batch, half] = state
            last_row = (batch + 1) * HALF - 1
            total = jnp.broadcast_to(cum_wide[last_row : last_row + 1], (4, HCH))
            coarse = total.astype(bf16).astype(f32)
            for state_half in range(2):
                block = jnp.concatenate(
                    [state[state_half * 8 : (state_half + 1) * 8], coarse, total - coarse], axis=0
                ).astype(bf16)
                for lane_block in range(4):
                    msg_ref[batch * 16 + group * 8 + lane_block * 2 + state_half] = block[
                        :, lane_block * LANES : (lane_block + 1) * LANES
                    ]
        inner_cb = nt(c_rows, b_rows)
        cumulative_t = cumulative.T
        first_head = iota((ROWS, LANES), 1) < HALF
        for pair in range(4):
            pair_rows = driving[:, pair * LANES : (pair + 1) * LANES]
            parts = [
                mm(
                    (decay_matrix(cumulative, cumulative_t, 2 * pair + k, mask) * inner_cb).astype(
                        bf16
                    ),
                    pair_rows,
                )
                for k in range(2)
            ]
            inner_ref[:, at + pair * LANES : at + (pair + 1) * LANES] = jnp.where(
                first_head, parts[0], parts[1]
            )


def invert_order(ids_ref, order_ref, slots_scr):
    slots_n = order_ref.shape[1]
    batch = (2 * ids_ref[0] + ids_ref[1]) // (slots_n // 2)
    for slot in range(slots_n):
        slots_scr[order_ref[batch, slot]] = slot


def block_decay(block):
    return jnp.exp(block[8:9] + block[12:13])


def forward_scan_kernel(ids_ref, order_ref, in_ref, out_ref, slots_scr):
    invert_order(ids_ref, order_ref, slots_scr)
    state = jnp.zeros((8, LANES), f32)
    for place in range(order_ref.shape[1]):
        slot = slots_scr[place]
        out_ref[slot] = state
        block = in_ref[slot].astype(f32)
        state = state * block_decay(block) + block[0:8]


def backward_scan_kernel(ids_ref, order_ref, decay_ref, in_ref, out_ref, slots_scr):
    invert_order(ids_ref, order_ref, slots_scr)
    state = jnp.zeros((8, LANES), f32)
    for place in reversed(range(order_ref.shape[1])):
        slot = slots_scr[place]
        out_ref[slot] = state
        state = state * block_decay(decay_ref[slot].astype(f32)) + in_ref[slot]


def mix_kernel(
    ids_ref, tok_ref, state_ref, sr_ref, cum_ref, inner_ref, conv_ref, gate_ref,
    par_own_ref, par_other_ref, own_ref, other_ref, gain_ref,
    full_ref, gated_ref, hidden_ref, normed_ref, msg_ref,
):
    core = ids_ref[1]
    hidden = tok_ref[...].astype(f32)
    hidden = jnp.concatenate([hidden[TAIL:EXT], hidden[EXT + TAIL :]], axis=0)
    for half, (w_ref, par_ref) in enumerate(
        ((own_ref, par_own_ref), (other_ref, par_other_ref))
    ):
        cols = slice(half * HCH, (half + 1) * HCH)
        c_rows = sr_ref[:, half * LANES + NSTATE : half * LANES + 2 * NSTATE].astype(bf16)
        carried = jnp.concatenate(
            [
                mm(
                    c_rows[batch * HALF : (batch + 1) * HALF],
                    get_state(state_ref, batch, half ^ core).astype(bf16),
                )
                for batch in range(2)
            ],
            axis=0,
        )
        conv = conv_ref[:, cols]
        mixed = conv * sigmoid(conv)
        full = inner_ref[:, cols] + jnp.exp(cum_ref[:, cols]) * carried + par_ref[5:6] * mixed
        full_ref[:, cols] = full
        gate = gate_ref[:, cols]
        gated = (full * (gate * sigmoid(gate))).astype(bf16)
        gated_ref[:, cols] = gated
        hidden = hidden + nt(gated, w_ref[:, 0:HCH])
    hidden_ref[...] = hidden
    normed = (hidden * rms_rows(hidden) * gain_ref[1:2]).astype(bf16)
    normed_ref[...] = normed
    for half, w_ref in enumerate((own_ref, other_ref)):
        rows_qkv = mm(normed, w_ref[:, HCH : HCH + 768]).astype(bf16)
        for batch in range(2):
            rows = slice(batch * HALF, (batch + 1) * HALF)
            for head in range(4):
                put_qkv(
                    msg_ref,
                    batch * 8 + (half ^ core) * 4 + head,
                    [
                        rows_qkv[rows, at : at + AHEAD_DIM]
                        for at in range(head * AHEAD_DIM, 768, 256)
                    ],
                )


def put_qkv(ref, at, members):
    ref[at, 0:HALF, 0:AHEAD_DIM] = members[0]
    ref[at, 0:HALF, AHEAD_DIM:LANES] = members[1]
    ref[at, HALF:QKV_ROWS, 0:AHEAD_DIM] = members[2][0 : HALF // 2]
    ref[at, HALF:QKV_ROWS, AHEAD_DIM:LANES] = members[2][HALF // 2 :]


def get_qkv(ref, at):
    return [
        ref[at, 0:HALF, 0:AHEAD_DIM],
        ref[at, 0:HALF, AHEAD_DIM:LANES],
        jnp.concatenate(
            [ref[at, HALF:QKV_ROWS, 0:AHEAD_DIM], ref[at, HALF:QKV_ROWS, AHEAD_DIM:LANES]], axis=0
        ),
    ]


def unpack_qkv(own_ref, other_ref, query_scr, key_scr, value_scr):
    for k, ref in enumerate((own_ref, other_ref)):
        for at in range(ref.shape[0]):
            rows = slice(at * HALF, (at + 1) * HALF)
            queries, keys, values = get_qkv(ref, at)
            if k == 0:
                query_scr[rows, :] = queries
            key_scr[k, rows, :] = keys
            value_scr[k, rows, :] = values


def put_rows(ref, at, member):
    ref[at, :, 0:AHEAD_DIM] = member[0 : HALF // 2]
    ref[at, :, AHEAD_DIM:LANES] = member[HALF // 2 :]


def get_rows(ref, at):
    return jnp.concatenate([ref[at, :, 0:AHEAD_DIM], ref[at, :, AHEAD_DIM:LANES]], axis=0)


QTILE = 256


def block_place(ids_ref, order_ref, block, other):
    chip, core = ids_ref[0], ids_ref[1]
    batch = chip // (order_ref.shape[1] // 4)
    return order_ref[batch, 2 * block + (core ^ other)] * HALF


def query_places(ids_ref, order_ref, tile):
    parts = [
        iota((HALF, 1), 0) + block_place(ids_ref, order_ref, tile * (QTILE // HALF) + k, 0)
        for k in range(QTILE // HALF)
    ]
    return jnp.concatenate(parts, axis=0)


def key_places(ids_ref, order_ref, other):
    lane = iota((1, LANES), 1)
    parts = []
    for pair in range(order_ref.shape[1] // 4):
        first = block_place(ids_ref, order_ref, 2 * pair, other)
        second = block_place(ids_ref, order_ref, 2 * pair + 1, other)
        parts.append(lane + jnp.where(lane < HALF, first, second - HALF))
    return jnp.concatenate(parts, axis=1)


def attend_kernel(
    ids_ref, order_ref, own_ref, other_ref, out_ref, log_ref, full_ref, query_scr, key_scr,
    value_scr,
):
    places = [key_places(ids_ref, order_ref, k) for k in range(2)]
    unpack_qkv(own_ref, other_ref, query_scr, key_scr, value_scr)
    scaling = AHEAD_DIM ** (-0.5)
    for tile in range(query_scr.shape[0] // QTILE):
        rows = slice(tile * QTILE, (tile + 1) * QTILE)
        place = query_places(ids_ref, order_ref, tile)
        queries = (query_scr[rows, :].astype(f32) * scaling).astype(bf16)
        scores = [
            jnp.where(
                places[k] <= place, nt(queries, key_scr[k]), -jnp.inf
            )
            for k in range(2)
        ]
        most = jnp.maximum(
            jnp.max(scores[0], axis=-1, keepdims=True), jnp.max(scores[1], axis=-1, keepdims=True)
        )
        exps = [jnp.exp(member - most) for member in scores]
        total = jnp.sum(exps[0], axis=-1, keepdims=True) + jnp.sum(exps[1], axis=-1, keepdims=True)
        mixed = mm(exps[0].astype(bf16), value_scr[0]) + mm(exps[1].astype(bf16), value_scr[1])
        mixed = mixed / total
        full_ref[rows, :] = mixed
        mixed = mixed.astype(bf16)
        for k in range(QTILE // HALF):
            put_rows(out_ref, tile * (QTILE // HALF) + k, mixed[k * HALF : (k + 1) * HALF])
        log_ref[rows, :] = most + jnp.log(total)


def attend_back_kernel(
    ids_ref, order_ref, own_ref, other_ref, grad_ref, log_ref, full_ref, mine_ref, theirs_ref,
    query_scr, key_scr, value_scr, query_sum, key_sum, value_sum,
):
    places = [key_places(ids_ref, order_ref, k) for k in range(2)]
    unpack_qkv(own_ref, other_ref, query_scr, key_scr, value_scr)
    scaling = AHEAD_DIM ** (-0.5)
    key_sum[...] = jnp.zeros(key_sum.shape, f32)
    value_sum[...] = jnp.zeros(value_sum.shape, f32)
    for tile in range(query_scr.shape[0] // QTILE):
        rows = slice(tile * QTILE, (tile + 1) * QTILE)
        place = query_places(ids_ref, order_ref, tile)
        queries = query_scr[rows, :]
        scaled = (queries.astype(f32) * scaling).astype(bf16)
        grad = jnp.concatenate(
            [get_rows(grad_ref, tile * (QTILE // HALF) + k) for k in range(QTILE // HALF)],
            axis=0,
        )
        log_total = log_ref[rows, :]
        probs = []
        prob_grads = []
        for k in range(2):
            scores = nt(scaled, key_scr[k]) - log_total
            probs.append(jnp.exp(jnp.where(places[k] <= place, scores, -jnp.inf)))
            prob_grads.append(nt(grad, value_scr[k]))
        delta = jnp.sum(grad.astype(f32) * full_ref[rows, :], axis=-1, keepdims=True)
        query_grad = jnp.zeros((QTILE, AHEAD_DIM), f32)
        for k in range(2):
            score_grad = (probs[k] * (prob_grads[k] - delta)).astype(bf16)
            value_sum[k] += tn(probs[k].astype(bf16), grad)
            key_sum[k] += tn(score_grad, queries)
            query_grad = query_grad + mm(score_grad, key_scr[k])
        query_sum[rows, :] = query_grad * scaling
    for at in range(mine_ref.shape[0]):
        rows = slice(at * HALF, (at + 1) * HALF)
        put_qkv(
            mine_ref, at, [query_sum[rows, :], key_sum[0, rows, :] * scaling, value_sum[0, rows, :]]
        )
        put_qkv(
            theirs_ref,
            at,
            [
                jnp.zeros((HALF, AHEAD_DIM), bf16),
                (key_sum[1, rows, :] * scaling).astype(bf16),
                value_sum[1, rows, :].astype(bf16),
            ],
        )


GELU_RATE = math.sqrt(2.0 / math.pi)
GELU_CUBE = 0.044715


def mlp_kernel(
    ids_ref, att_ref, hidden_ref, cot_ref, deal_ref, gain_ref, own_ref, other_ref,
    out_ref, hidden_two_ref, cot_both_ref, mine_ref, theirs_ref, hidden_grad_ref, gain_grad_ref,
    msg_ref,
    att_scr, result_scr,
):
    core = ids_ref[1]
    weights = (own_ref, other_ref)
    packs = (mine_ref, theirs_ref)
    up_cols, down_cols, att_cols = slice(0, 1024), slice(1024, 2048), slice(2048, 2304)
    cot_both = mm(
        jnp.concatenate(
            [cot_ref[batch, my_rows(side), :] for side in (core, 1 - core) for batch in range(2)],
            axis=0,
        ),
        deal_ref[...],
    ).astype(bf16)
    cot_both_ref[...] = cot_both
    cot = cot_both[0:ROWS]
    hidden = hidden_ref[...]
    for half in range(2):
        for batch in range(2):
            for head in range(4):
                att_scr[
                    half,
                    batch * HALF : (batch + 1) * HALF,
                    head * AHEAD_DIM : (head + 1) * AHEAD_DIM,
                ] = get_rows(att_ref, batch * 8 + (half ^ core) * 4 + head)
        packs[half][:, att_cols] = att_scr[half]
        hidden = hidden + nt(att_scr[half], weights[half][:, att_cols])
    gain = gain_ref[2:3]
    normed = (hidden * rms_rows(hidden) * gain).astype(bf16)
    normed_grad = jnp.zeros(hidden.shape, f32)
    for half in range(2):
        up_rows = mm(normed, weights[half][:, up_cols])
        squares = up_rows * up_rows
        bent = jnp.tanh(GELU_RATE * (up_rows + GELU_CUBE * squares * up_rows))
        act = (0.5 * up_rows * (1.0 + bent)).astype(bf16)
        slope = 0.5 * (1.0 + bent) + 0.5 * up_rows * (1.0 - bent * bent) * (
            GELU_RATE * (1.0 + 3.0 * GELU_CUBE * squares)
        )
        result_scr[half] = nt(act, weights[half][:, down_cols])
        packs[half][:, down_cols] = act
        up_grad = (mm(cot, weights[half][:, down_cols]) * slope).astype(bf16)
        packs[half][:, up_cols] = up_grad
        normed_grad = normed_grad + nt(up_grad, weights[half][:, up_cols])
        packs[half][:, 2304 : 2304 + 512] = normed
    hidden_two_ref[...] = hidden
    out_ref[...] = result_scr[0] + result_scr[1]
    part, gain_grad = rms_back(hidden, gain, normed_grad)
    gain_grad_ref[...] = gain_grad
    hidden_grad = cot.astype(f32) + part
    hidden_grad_ref[...] = hidden_grad
    branch = hidden_grad.astype(bf16)
    for half in range(2):
        packs[half][:, 2816 : 2816 + 512] = branch
        att_grad = mm(branch, weights[half][:, att_cols]).astype(bf16)
        for batch in range(2):
            for head in range(4):
                put_rows(
                    msg_ref,
                    batch * 8 + (half ^ core) * 4 + head,
                    att_grad[
                        batch * HALF : (batch + 1) * HALF,
                        head * AHEAD_DIM : (head + 1) * AHEAD_DIM,
                    ],
                )


def both_rows(mine_ref, theirs_ref, cols):
    return jnp.concatenate([mine_ref[:, cols], theirs_ref[:, cols]], axis=0)


def put_pieces(piece_refs, cols, values):
    rows_n = piece_refs[0].shape[0]
    for k, piece_ref in enumerate(piece_refs):
        piece_ref[:, cols] = values[k * rows_n : (k + 1) * rows_n].astype(bf16)


def third_grad_kernel(mine_ref, theirs_ref, cot_ref, *piece_refs):
    up_cols, down_cols, att_cols = slice(0, 1024), slice(1024, 2048), slice(2048, 2304)

    def both(cols):
        return both_rows(mine_ref, theirs_ref, cols)

    put_pieces(piece_refs, up_cols, tn(both(slice(2304, 2816)), both(up_cols)))
    put_pieces(piece_refs, down_cols, tn(cot_ref[...], both(down_cols)))
    put_pieces(piece_refs, att_cols, tn(both(slice(2816, 3328)), both(att_cols)))


def second_grad_kernel(mine_ref, theirs_ref, *piece_refs):
    def both(cols):
        return both_rows(mine_ref, theirs_ref, cols)

    for cols, base in ((slice(0, 512), 2304), (slice(512, 1280), 1792), (slice(1280, 1792), 2816)):
        put_pieces(piece_refs, cols, tn(both(slice(base, base + 512)), both(cols)))


def first_grad_kernel(ids_ref, mine_ref, theirs_ref, msg_ref, *piece_refs):
    cols = slice(0, HCH + LANES)
    rows = slice(0, 2 * EXT)
    packs = (mine_ref, theirs_ref)
    put_pieces(
        piece_refs,
        cols,
        tn(
            jnp.concatenate([ref[rows, HCH + LANES : 2 * HCH + LANES] for ref in packs], axis=0),
            jnp.concatenate([ref[rows, cols] for ref in packs], axis=0),
        ),
    )
    rows = slice(2 * EXT, 2 * EXT + SMALL_ROWS)
    small = mine_ref[rows, 0:HCH].astype(f32) + theirs_ref[rows, 0:HCH].astype(f32)
    tails = [ref[rows, HCH : 2 * HCH].astype(f32) for ref in packs]
    ordered = [jnp.where(ids_ref[1] == k, tails[0], tails[1]) for k in range(2)]
    tails = jnp.concatenate(
        [ordered[0][0:6], ordered[1][0:6], jnp.zeros((SMALL_ROWS - 12, HCH), f32)], axis=0
    )
    block = jnp.concatenate([small, tails], axis=1).astype(bf16)
    for k in range(msg_ref.shape[0]):
        msg_ref[k] = block


def sum_kernel(*refs):
    total = refs[0][...].astype(f32)
    for ref in refs[1:4]:
        total = total + ref[...].astype(f32)
    put_pieces(refs[4:], slice(0, total.shape[1]), total)


def sum_both_kernel(*refs):
    at = 0
    for group in (refs[0:4], refs[4:8]):
        total = group[0][...].astype(f32)
        for ref in group[1:]:
            total = total + ref[...].astype(f32)
        put_pieces(refs[8:], slice(at, at + total.shape[1]), total)
        at += total.shape[1]


def early_out_kernel(*refs):
    total = refs[0][...].astype(f32)
    for ref in refs[1:4]:
        total = total + ref[...].astype(f32)
    value_ref, state_ref, rate_ref, mix_ref, qkv_ref, gate_ref = refs[4:]
    value_ref[...] = total[:, 0:HCH]
    state_ref[...] = total[:, HCH : HCH + 32]
    rate_ref[...] = total[:, HCH : HCH + LANES].T[RATE_AT : RATE_AT + HPG]
    base = HCH + LANES
    mix_ref[...] = total[:, base : base + HCH]
    for kind in range(3):
        qkv_ref[kind] = total[:, base + HCH + kind * 256 : base + HCH + (kind + 1) * 256]
    gate_ref[...] = total[:, base + HCH + 768 :]


def mix_back_kernel(
    ids_ref, qkv_ref, first_ref, normed_ref, hidden_ref, hidden_grad_ref, gain_ref, own_ref,
    other_ref, gated_ref, gate_ref, full_ref, conv_ref, cum_ref, sr_ref,
    mine_ref, theirs_ref, y_grad_ref, gate_grad_ref, one_grad_ref, gain_grad_ref, skip_grad_ref,
    msg_ref, qkv_scr,
):
    core = ids_ref[1]
    weights = (own_ref, other_ref)
    packs = (mine_ref, theirs_ref)
    mix_cols, qkv_cols, gate_cols = slice(0, 512), slice(512, 1280), slice(1280, 1792)
    first = jnp.concatenate([first_ref[TAIL:EXT], first_ref[EXT + TAIL :]], axis=0)
    normed_grad = jnp.zeros(hidden_ref.shape, f32)
    for half in range(2):
        for batch in range(2):
            for head in range(4):
                members = get_qkv(qkv_ref, batch * 8 + (half ^ core) * 4 + head)
                for kind, member in enumerate(members):
                    at = kind * 256 + head * AHEAD_DIM
                    qkv_scr[batch * HALF : (batch + 1) * HALF, at : at + AHEAD_DIM] = member
        rows_grad = qkv_scr[...]
        packs[half][:, qkv_cols] = rows_grad
        normed_grad = normed_grad + nt(rows_grad, weights[half][:, qkv_cols])
    part, gain_grad = rms_back(hidden_ref[...], gain_ref[1:2], normed_grad)
    gain_grad_ref[...] = gain_grad
    one_grad = hidden_grad_ref[...] + part
    one_grad_ref[...] = one_grad
    branch = one_grad.astype(bf16)
    for half in range(2):
        cols = slice(half * HCH, (half + 1) * HCH)
        packs[half][:, mix_cols] = gated_ref[:, cols]
        packs[half][:, 1792:2304] = normed_ref[...]
        packs[half][:, 2304:2816] = branch
        packs[half][:, 2816:3328] = first
        gated_grad = mm(branch, weights[half][:, mix_cols])
        silu, slope = silu_parts(gate_ref[:, cols])
        y_grad = gated_grad * silu
        y_grad_ref[:, cols] = y_grad
        gate_grad = (gated_grad * full_ref[:, cols] * slope).astype(bf16)
        gate_grad_ref[:, cols] = gate_grad
        packs[half][:, gate_cols] = gate_grad
        conv = conv_ref[:, cols]
        skip_grad_ref[:, cols] = jnp.sum(y_grad * (conv * sigmoid(conv)), axis=0, keepdims=True)
        carried = (jnp.exp(cum_ref[:, cols]) * y_grad).astype(bf16)
        c_rows = sr_ref[:, half * LANES + NSTATE : half * LANES + 2 * NSTATE].astype(bf16)
        for batch in range(2):
            rows = slice(batch * HALF, (batch + 1) * HALF)
            put_state(msg_ref, batch, half ^ core, tn(c_rows[rows], carried[rows]))


def in_back_kernel(
    ids_ref, later_ref, state_ref, local_ref, sr_ref, cum_ref, conv_ref, x_ref, y_grad_ref,
    gate_grad_ref, normed_ref, tok_ref, gain_ref, one_grad_ref, own_ref, other_ref,
    par_own_ref, par_other_ref, deal_ref, skip_grad_ref, attgain_ref, mlpgain_ref,
    mine_ref, theirs_ref, hidden_grad_ref,
    x_scr, grad_scr, sr_scr, gate_scr,
):
    core = ids_ref[1]
    mask = lower_mask()
    spread = spread_matrix()
    normed = normed_ref[...]
    ext_grad = jnp.zeros((2 * EXT, normed.shape[1]), f32)
    lower_t = (
        same_block(iota((ROWS, ROWS), 0), iota((ROWS, ROWS), 1))
        & (iota((ROWS, ROWS), 0) <= iota((ROWS, ROWS), 1))
    ).astype(f32).astype(bf16)
    lane = iota((1, LANES), 1)
    small_list = []
    for half, (w_ref, par_ref, pack_ref) in enumerate(
        ((own_ref, par_own_ref, mine_ref), (other_ref, par_other_ref, theirs_ref))
    ):
        cols = slice(half * HCH, (half + 1) * HCH)
        group = half ^ core
        params = par_ref[...]
        state_rate = sr_ref[:, half * LANES : (half + 1) * LANES]
        shifted, step, rates, log_decay, cumulative = step_terms(state_rate, params)
        cumulative_t = cumulative.T
        cum_wide = cum_ref[:, cols]
        step_wide = mm_onehot(step, spread)
        conv = conv_ref[:, cols]
        mixed, conv_slope = silu_parts(conv)
        driving = step_wide * mixed
        tail = tail_decay(cum_wide)
        inflow = jnp.exp(cum_wide)
        y_grad = y_grad_ref[:, cols]
        y_low = y_grad.astype(bf16)
        driving_low = driving.astype(bf16)
        b_rows = state_rate[:, 0:NSTATE].astype(bf16)
        c_rows = state_rate[:, NSTATE : 2 * NSTATE].astype(bf16)
        inner_cb = nt(c_rows, b_rows)
        weighted = (driving * tail).astype(bf16)
        carried_grad = (inflow * y_grad).astype(bf16)
        through_list = []
        tail_list = []
        flow_list = []
        b_list = []
        c_list = []
        for batch in range(2):
            rows = slice(batch * HALF, (batch + 1) * HALF)
            incoming = get_state(state_ref, batch, group)
            later = get_state(later_ref, batch, group)
            total = cum_wide[(batch + 1) * HALF - 1 : (batch + 1) * HALF, :]
            outgoing = jnp.exp(total) * incoming + local_ref[batch, half]
            through_list.append(jnp.sum(later * outgoing, axis=0, keepdims=True))
            incoming = incoming.astype(bf16)
            later = later.astype(bf16)
            tail_list.append(mm(b_rows[rows], later))
            flow_list.append(mm(c_rows[rows], incoming))
            b_list.append(nt(weighted[rows], later))
            c_list.append(nt(carried_grad[rows], incoming))
        tail_part = tail * jnp.concatenate(tail_list, axis=0)
        flow_part = inflow * jnp.concatenate(flow_list, axis=0)
        first_head = iota((ROWS, LANES), 1) < HALF
        inner_grad = jnp.zeros((ROWS, ROWS), f32)
        row_sums = jnp.zeros((ROWS, LANES), f32)
        col_list = []
        drive_list = []
        for pair in range(4):
            lanes = slice(pair * LANES, (pair + 1) * LANES)
            y_pair = y_low[:, lanes]
            u_pair = driving_low[:, lanes]
            parts = []
            for k in range(2):
                head = 2 * pair + k
                mine = first_head if k == 0 else ~first_head
                decay = decay_matrix(cumulative, cumulative_t, head, mask)
                product = nt(jnp.where(mine, y_pair, jnp.zeros_like(y_pair)), u_pair)
                decayed = decay * product
                inner_grad = inner_grad + decayed
                both = decayed * inner_cb
                row_sums = row_sums + jnp.where(
                    lane == RATE_AT + head, jnp.sum(both, axis=1, keepdims=True), 0.0
                )
                col_list.append(jnp.sum(both, axis=0, keepdims=True))
                parts.append(tn((decay * inner_cb).astype(bf16), y_pair))
            drive_list.append(jnp.where(first_head, parts[0], parts[1]))
        drive_grad = jnp.concatenate(drive_list, axis=1) + tail_part
        col_rows = jnp.concatenate(
            [jnp.zeros((RATE_AT, ROWS), f32)]
            + col_list
            + [jnp.zeros((LANES - RATE_AT - HPG, ROWS), f32)],
            axis=0,
        )
        cum_grad = (
            row_sums
            - col_rows.T
            + nt_onehot(y_grad * flow_part - driving * tail_part, spread)
        )
        through_rows = nt_onehot(
            jnp.concatenate(through_list + [jnp.zeros((6, HCH), f32)], axis=0), spread
        )
        decay_grad = onehot_mm(lower_t, cum_grad) + per_block(
            through_rows[0:1], through_rows[1:2], (ROWS, LANES)
        )
        step_grad = nt_onehot(mixed * drive_grad, spread) - decay_grad * rates
        rate_grad = step_grad * sigmoid(shifted)
        inner_low = inner_grad.astype(bf16)
        b_grad = tn(inner_low, c_rows) + jnp.concatenate(b_list, axis=0)
        c_grad = mm(inner_low, b_rows) + jnp.concatenate(c_list, axis=0)
        is_rate = (lane >= RATE_AT) & (lane < RATE_AT + HPG)
        rate_grad = jnp.where(is_rate, rate_grad, 0.0)
        sr_grad = jnp.concatenate(
            [b_grad, c_grad, rate_grad[:, RATE_AT:LANES]], axis=1
        ).astype(bf16)
        mixed_grad = step_wide * drive_grad + params[5:6] * y_grad
        conv_grad = mixed_grad * conv_slope
        x_scr[...] = x_ref[:, cols].astype(f32)
        grad_scr[...] = jnp.zeros(grad_scr.shape, f32)
        sr_scr[...] = jnp.zeros(sr_scr.shape, bf16)
        gate_scr[...] = jnp.zeros(gate_scr.shape, bf16)
        gate_grad = gate_grad_ref[:, cols]
        for batch in range(2):
            rows = slice(batch * HALF, (batch + 1) * HALF)
            ext_rows = slice(batch * EXT + TAIL, (batch + 1) * EXT)
            grad_scr[batch, TAIL:EXT, :] = conv_grad[rows]
            sr_scr[ext_rows, :] = sr_grad[rows]
            gate_scr[ext_rows, :] = gate_grad[rows]
        x_list = []
        tap_list = [jnp.zeros((1, HCH), f32) for _ in range(CONV)]
        for batch in range(2):
            x_grad = jnp.zeros((EXT, HCH), f32)
            for tap in range(CONV):
                lag = CONV - 1 - tap
                x_grad = x_grad + params[tap : tap + 1] * grad_scr[batch, lag : lag + EXT, :]
                first = batch * EXT + TAIL - lag
                tap_list[tap] = tap_list[tap] + jnp.sum(
                    x_scr[first : first + HALF, :] * grad_scr[batch, TAIL:EXT, :],
                    axis=0,
                    keepdims=True,
                )
            x_list.append(x_grad)
        x_low = jnp.concatenate(x_list, axis=0).astype(bf16)
        small_list.append(
            jnp.concatenate(
                tap_list
                + [
                    jnp.sum(conv_grad, axis=0, keepdims=True),
                    skip_grad_ref[:, cols],
                    jnp.concatenate(
                        [
                            jnp.sum(rate_grad, axis=0, keepdims=True),
                            jnp.sum(decay_grad * log_decay, axis=0, keepdims=True),
                            jnp.zeros((1, HCH - 2 * LANES), f32),
                        ],
                        axis=1,
                    ),
                ],
                axis=0,
            )
        )
        pack_ref[0 : 2 * EXT, 0:HCH] = x_low
        pack_ref[0 : 2 * EXT, HCH : HCH + LANES] = sr_scr[...]
        pack_ref[0 : 2 * EXT, HCH + LANES : 2 * HCH + LANES] = normed
        ext_grad = (
            ext_grad
            + nt(x_low, w_ref[:, 0:HCH])
            + nt(gate_scr[...], w_ref[:, HCH : 2 * HCH])
            + nt(sr_scr[...], w_ref[:, 2 * HCH : 2 * HCH + LANES])
        )
    hidden = tok_ref[...].astype(f32)
    part, gain_grad = rms_back(hidden, gain_ref[0:1], ext_grad)
    deal = deal_ref[...]
    gain_grads = nt_onehot(
        jnp.concatenate([gain_grad, attgain_ref[...], mlpgain_ref[...]], axis=0), deal
    )
    tails = nt(
        jnp.concatenate([part[TAIL - 3 : TAIL], part[EXT + TAIL - 3 : EXT + TAIL]], axis=0).astype(
            bf16
        ),
        deal,
    )
    tails = jnp.concatenate([tails, jnp.zeros((SMALL_ROWS - 6, HCH), f32)], axis=0)
    for small, pack_ref in zip(small_list, (mine_ref, theirs_ref)):
        rows = slice(2 * EXT, 2 * EXT + SMALL_ROWS)
        pack_ref[rows, 0:HCH] = jnp.concatenate(
            [small, gain_grads, jnp.zeros((SMALL_ROWS - 10, HCH), f32)], axis=0
        ).astype(bf16)
        pack_ref[rows, HCH : 2 * HCH] = tails.astype(bf16)
        pack_ref[rows, 2 * HCH :] = jnp.zeros((SMALL_ROWS, LANES), bf16)
    rows_grad = jnp.concatenate([part[TAIL:EXT], part[EXT + TAIL :]], axis=0) + one_grad_ref[...]
    hidden_grad_ref[...] = nt(rows_grad.astype(bf16), deal)


SMEM_SPEC = pl.BlockSpec(memory_space=pltpu.SMEM)
VMEM_SPEC = pl.BlockSpec(memory_space=pltpu.VMEM)
ANY_SPEC = pl.BlockSpec(memory_space=pl.ANY)


def run_kernel(kernel, out_shapes, scalars_n, args, scratch=(), after=(), pieces=None, at=0):
    args_n = len(args)
    pieces = [] if pieces is None else list(pieces[0]) + list(pieces[1])
    scratch = list(scratch)
    if pieces:
        rows_n, cols = pieces[0].shape
        scratch += [pltpu.VMEM((4 * rows_n, cols), bf16)] * 2
        scratch.append(pltpu.SemaphoreType.DMA((8,)))

    def body(*refs):
        ins, rest = list(refs[:args_n]), list(refs[args_n + len(pieces) + len(after) :])
        if pieces:
            *rest, own_scr, other_scr, sems = rest
            copies = [
                pltpu.make_async_copy(
                    refs[args_n + k],
                    (own_scr, other_scr)[k // 4].at[pl.ds((k % 4) * rows_n, rows_n), :],
                    sems.at[k],
                )
                for k in range(8)
            ]
            for copy in copies:
                copy.start()
            for copy in copies:
                copy.wait()
            ins[at:at] = [own_scr, other_scr]
        kernel(*ins, *rest)

    return pl.pallas_call(
        body,
        out_shape=[jax.ShapeDtypeStruct(shape, kind) for shape, kind in out_shapes],
        in_specs=[SMEM_SPEC] * scalars_n
        + [VMEM_SPEC] * (args_n - scalars_n)
        + [ANY_SPEC] * (len(pieces) + len(after)),
        out_specs=[VMEM_SPEC] * len(out_shapes),
        scratch_shapes=scratch,
        compiler_params=pltpu.CompilerParams(vmem_limit_bytes=VMEM_LIMIT),
        name=kernel.__name__,
        cost_estimate=pl.CostEstimate(flops=0, transcendentals=0, bytes_accessed=0),
    )(*args, *pieces, *after)


def hold(values, *after):
    def body(*refs):
        pass

    return pl.pallas_call(
        body,
        out_shape=jax.ShapeDtypeStruct(values.shape, values.dtype),
        in_specs=[ANY_SPEC] * (1 + len(after)),
        out_specs=ANY_SPEC,
        input_output_aliases={0: 0},
    )(values, *after)


def flip(bits, ranks):
    return [(index, index ^ bits) for index in range(ranks)]


def swap_cores(values):
    return lax.ppermute(values, "head", [(0, 1), (1, 0)])


def permute_three(pieces, step, ranks):
    return [
        lax.ppermute(piece, "seq", flip(step * (k + 1), ranks)) for k, piece in enumerate(pieces)
    ]


def sum_pieces(mine, moved, after=()):
    rows_n, cols = mine.shape
    return run_kernel(
        sum_kernel, [((rows_n // 4, cols), bf16)] * 4, 0, [mine] + moved, (), after
    )


def exchange(values, axes):
    return lax.all_to_all(values, axes, 0, 0, tiled=True)


def dealt_device(
    tokens, cotangent, lengths, order, mix_gain, in_value, in_gate, in_state, in_rate,
    rate_bias, decay_log, conv_taps, conv_bias, skip_gain, mix_out, att_gain, qkv_proj,
    att_out, mlp_gain, mlp_up, mlp_down,
):
    ranks = lax.axis_size("seq")
    both = ("seq", "head")
    chip = lax.axis_index("seq")
    core = lax.axis_index("head")
    ids = jnp.stack([chip, core]).astype(jnp.int32)
    my_slot = 2 * chip + core
    width = tokens.shape[2]
    slots_n = 2 * ranks
    shard_rows = width // ranks
    slots_scratch = (pltpu.SMEM((slots_n,), jnp.int32),)

    tail_rows = tokens.reshape(2, 2, HALF, width)[:, :, HALF - (CONV - 1) :]
    tail_rows = jnp.where(core == 0, tail_rows[0], tail_rows[1]).reshape(-1, LANES)
    tail_rows = jnp.pad(tail_rows, ((0, shard_rows - tail_rows.shape[0]), (0, 0)))
    first_shard = jnp.concatenate(
        [
            in_value, in_gate, in_state, in_rate, jnp.zeros((shard_rows, LANES - 40), bf16),
            tail_rows,
        ],
        axis=1,
    )
    first_cols = first_shard.shape[1]
    second_cols, third_cols = HCH + 768, 2304
    early_shard = jnp.concatenate(
        [first_shard, mix_out.T, qkv_proj.reshape(shard_rows, -1)], axis=1
    )
    third_shard = jnp.concatenate([mlp_up, mlp_down.T, att_out.T], axis=1)
    early_pieces = [early_shard] + permute_three([early_shard] * 3, 4, ranks)
    first_stack = jnp.concatenate([piece[:, :first_cols] for piece in early_pieces], axis=0)
    third_shard = hold(third_shard, first_stack)
    third_z = [third_shard] + permute_three([third_shard] * 3, 4, ranks)
    third_stack = jnp.concatenate(third_z, axis=0)
    first_own = [first_stack] + permute_three([first_stack] * 3, 1, ranks)
    first_own[3] = hold(first_own[3], *third_z[1:])
    first_pieces = (first_own, [swap_cores(piece) for piece in first_own])
    second_stack = jnp.concatenate([piece[:, first_cols:] for piece in early_pieces], axis=0)
    second_own = [second_stack] + permute_three([second_stack] * 3, 1, ranks)
    second_pieces = (second_own, [swap_cores(piece) for piece in second_own])

    par_own = jnp.concatenate(
        [
            conv_taps,
            conv_bias[None],
            skip_gain[None],
            jnp.pad(rate_bias, (RATE_AT, HCH - RATE_AT - HPG))[None],
            jnp.pad(decay_log, (RATE_AT, HCH - RATE_AT - HPG))[None],
        ],
        axis=0,
    )
    par_other = swap_cores(par_own)
    gains = jnp.stack([mix_gain, att_gain, mlp_gain])

    channels = 2 * HCH
    (
        ext_rows, normed_one, x_in, conv_sum, gate_in, state_rate, cum_wide, inner_y,
        local_state, msg, deal_low, gains,
    ) = run_kernel(
        in_kernel,
        [
            ((2 * EXT, width), bf16),
            ((2 * EXT, width), bf16),
            ((2 * EXT, channels), bf16),
            ((ROWS, channels), f32),
            ((ROWS, channels), f32),
            ((ROWS, 2 * LANES), f32),
            ((ROWS, channels), f32),
            ((ROWS, channels), f32),
            ((2, 2, NSTATE, HCH), f32),
            ((slots_n, 16, LANES), bf16),
            ((width, width), bf16),
            ((3, width), f32),
        ],
        2,
        (ids, order, tokens, gains, par_own, par_other),
        (pltpu.VMEM((2 * EXT, HCH), f32), pltpu.VMEM((2, TILE_ROWS, LANES), f32)),
        pieces=first_pieces,
        at=4,
    )

    states = exchange(hold(msg, *second_own[1:3]), both)
    (incoming,) = run_kernel(
        forward_scan_kernel,
        [((slots_n, 8, LANES), f32)],
        2,
        (ids, order, states),
        slots_scratch,
        after=second_own[3:],
    )
    incoming = exchange(incoming, both)

    full_y, gated, hidden_one, normed_two, msg = run_kernel(
        mix_kernel,
        [
            ((ROWS, channels), f32),
            ((ROWS, channels), bf16),
            ((ROWS, width), f32),
            ((ROWS, width), bf16),
            ((ranks, QKV_ROWS, LANES), bf16),
        ],
        1,
        (
            ids, ext_rows, incoming, state_rate, cum_wide, inner_y, conv_sum, gate_in,
            par_own, par_other, gains,
        ),
        after=[third_stack],
        pieces=second_pieces,
        at=10,
    )
    third_own = [third_stack] + permute_three([third_stack] * 3, 1, ranks)
    att_rows = ranks * HALF
    qkv_scratch = (
        pltpu.VMEM((att_rows, AHEAD_DIM), bf16),
        pltpu.VMEM((2, att_rows, AHEAD_DIM), bf16),
        pltpu.VMEM((2, att_rows, AHEAD_DIM), bf16),
    )
    qkv_own = exchange(hold(msg, *third_own[1:3]), "seq")
    qkv_other = swap_cores(qkv_own)
    attended, log_total, att_full = run_kernel(
        attend_kernel,
        [((ranks, HALF // 2, LANES), bf16), ((att_rows, 1), f32), ((att_rows, AHEAD_DIM), f32)],
        2,
        (ids, order, qkv_own, qkv_other),
        qkv_scratch,
    )
    third_own[3] = hold(third_own[3], log_total)
    third_pieces = (third_own, [swap_cores(piece) for piece in third_own])
    attended = exchange(attended, "seq")

    pack_cols = 3328
    (
        down_rows, hidden_two, cot_both, mine, theirs, two_grad, mlpgain_part, msg,
    ) = run_kernel(
        mlp_kernel,
        [
            ((ROWS, width), f32),
            ((ROWS, width), f32),
            ((2 * ROWS, width), bf16),
            ((ROWS, pack_cols), bf16),
            ((ROWS, pack_cols), bf16),
            ((ROWS, width), f32),
            ((1, width), f32),
            ((ranks, HALF // 2, LANES), bf16),
        ],
        1,
        (ids, attended, hidden_one, cotangent, deal_low, gains),
        (pltpu.VMEM((2, ROWS, 256), bf16), pltpu.VMEM((2, ROWS, width), f32)),
        pieces=third_pieces,
        at=6,
    )
    att_grad = exchange(msg, "seq")
    third_grads = run_kernel(
        third_grad_kernel,
        [((width // 4, third_cols), bf16)] * 4,
        0,
        (mine, swap_cores(theirs), cot_both),
    )
    mine, theirs = run_kernel(
        attend_back_kernel,
        [((ranks, QKV_ROWS, LANES), f32), ((ranks, QKV_ROWS, LANES), bf16)],
        2,
        (ids, order, qkv_own, qkv_other, att_grad, log_total, att_full),
        qkv_scratch
        + (
            pltpu.VMEM((att_rows, AHEAD_DIM), f32),
            pltpu.VMEM((2, att_rows, AHEAD_DIM), f32),
            pltpu.VMEM((2, att_rows, AHEAD_DIM), f32),
        ),
        after=third_grads[:1],
    )
    qkv_grad = (mine + swap_cores(theirs).astype(f32)).astype(bf16)
    qkv_grad = exchange(qkv_grad, "seq")
    third_moved = permute_three(third_grads[1:], 1, ranks)

    mine, theirs, y_grad, gate_grad, one_grad, attgain_part, skip_part, msg = run_kernel(
        mix_back_kernel,
        [
            ((ROWS, pack_cols), bf16),
            ((ROWS, pack_cols), bf16),
            ((ROWS, channels), f32),
            ((ROWS, channels), bf16),
            ((ROWS, width), f32),
            ((1, width), f32),
            ((1, channels), f32),
            ((slots_n, 8, LANES), f32),
        ],
        1,
        (
            ids, qkv_grad, normed_one, normed_two, hidden_one, two_grad, gains, gated, gate_in,
            full_y, conv_sum, cum_wide, state_rate,
        ),
        (pltpu.VMEM((ROWS, 768), bf16),),
        pieces=second_pieces,
        at=7,
        after=third_moved[:2],
    )
    back_states = exchange(msg, both)
    second_grads = run_kernel(
        second_grad_kernel,
        [((width // 4, second_cols + HCH), bf16)] * 4,
        0,
        (mine, swap_cores(theirs)),
    )
    (later,) = run_kernel(
        backward_scan_kernel,
        [((slots_n, 8, LANES), f32)],
        2,
        (ids, order, states, back_states),
        slots_scratch,
        after=[second_grads[0], third_moved[2]],
    )
    third_parts = sum_pieces(third_grads[0], third_moved, (later,))
    third_moved = permute_three(third_parts[1:], 4, ranks)
    second_moved = permute_three(second_grads[1:], 1, ranks)
    later = exchange(later, both)

    grad_cols = HCH + LANES
    pack_shape = (2 * EXT + SMALL_ROWS, grad_cols + width)
    mine, theirs, tokens_grad = run_kernel(
        in_back_kernel,
        [(pack_shape, bf16), (pack_shape, bf16), ((ROWS, width), f32)],
        1,
        (
            ids, later, incoming, local_state, state_rate, cum_wide, conv_sum, x_in, y_grad,
            gate_grad, normed_one, ext_rows, gains, one_grad, par_own, par_other, deal_low,
            skip_part, attgain_part, mlpgain_part,
        ),
        (
            pltpu.VMEM((2 * EXT, HCH), f32),
            pltpu.VMEM((2, EXT + TAIL, HCH), f32),
            pltpu.VMEM((2 * EXT, LANES), bf16),
            pltpu.VMEM((2 * EXT, HCH), bf16),
        ),
        after=[third_parts[0]],
        pieces=first_pieces,
        at=14,
    )
    last_msg, *first_grads = run_kernel(
        first_grad_kernel,
        [((ranks, SMALL_ROWS, 2 * HCH), bf16)] + [((width // 4, grad_cols), bf16)] * 4,
        1,
        (ids, mine, swap_cores(theirs)),
        after=second_moved,
    )
    first_moved = permute_three(first_grads[1:], 1, ranks)
    last = exchange(hold(last_msg, *first_moved), "seq")
    early_parts = run_kernel(
        sum_both_kernel,
        [((width // 16, grad_cols + second_cols + HCH), bf16)] * 4,
        0,
        [first_grads[0]] + first_moved + [second_grads[0]] + second_moved,
    )
    third_total = third_parts[0].astype(f32)
    for piece in [hold(member, early_parts[0]) for member in third_moved]:
        third_total = third_total + piece.astype(f32)
    my_blocks = jnp.sum(
        jnp.where(jnp.arange(slots_n)[None, :] == my_slot, order, 0), axis=1
    )
    last = last.astype(f32)
    small_total = jnp.sum(last[:, 0:10, 0:HCH], axis=0)
    next_tails = last[:, 0:12, HCH:].reshape(ranks, 2, 2, CONV - 1, width).transpose(2, 0, 1, 3, 4)
    next_tails = next_tails.reshape(2, slots_n, CONV - 1, width)
    pick_next = (order == my_blocks[:, None] + 1).astype(f32)
    tail_add = jnp.sum(pick_next[:, :, None, None] * next_tails, axis=1)
    tokens_grad = tokens_grad.reshape(2, HALF, width)
    tokens_grad = jnp.concatenate(
        [tokens_grad[:, : HALF - (CONV - 1)], tokens_grad[:, HALF - (CONV - 1) :] + tail_add],
        axis=1,
    ).astype(bf16)
    layer_rows = nt((hidden_two + down_rows).astype(bf16), deal_low).astype(bf16)
    outs = jnp.stack([layer_rows.reshape(2, HALF, width), tokens_grad])
    outs_other = swap_cores(outs)
    outs = jnp.where(
        core == 0,
        jnp.concatenate([outs, outs_other], axis=2),
        jnp.concatenate([outs_other, outs], axis=2),
    )
    small_outs = [
        small_total[7],
        small_total[6, RATE_AT : RATE_AT + HPG],
        small_total[6, LANES + RATE_AT : LANES + RATE_AT + HPG],
        small_total[0:4],
        small_total[4],
        small_total[5],
        small_total[8],
        small_total[9],
    ]
    early_outs = run_kernel(
        early_out_kernel,
        [
            (shape, f32)
            for shape in (
                in_value.shape,
                in_state.shape,
                in_rate.shape[::-1],
                mix_out.shape[::-1],
                (qkv_proj.shape[1], qkv_proj.shape[0], qkv_proj.shape[2]),
                in_gate.shape,
            )
        ],
        0,
        [early_parts[0]] + permute_three(early_parts[1:], 4, ranks),
        after=[outs] + small_outs,
    )
    return (
        outs[0],
        outs[1],
        small_outs[0],
        early_outs[0],
        early_outs[5],
        early_outs[1],
        early_outs[2].T,
        small_outs[1],
        small_outs[2],
        small_outs[3],
        small_outs[4],
        small_outs[5],
        early_outs[3].T,
        small_outs[6],
        early_outs[4].transpose(1, 0, 2),
        third_total[:, 2048:2304].T,
        small_outs[7],
        third_total[:, 0:1024],
        third_total[:, 1024:2048].T,
    )


def layer(*args):
    tokens, lengths = args[0], args[2]
    fits = lax.axis_size("seq") == 16 and lax.axis_size("head") == 2
    fits = fits and lengths.shape == (2, 1) and tokens.shape[1] == ROWS
    return dealt_device(*args) if fits else on_device(*args)


def solution(mesh):
    return jax.shard_map(
        layer,
        mesh=mesh,
        in_specs=(
            P(None, "seq", None),
            P(None, "seq", None),
            P(),
            P(),
            P(),
            P("seq", "head"),
            P("seq", "head"),
            P("seq", "head"),
            P("seq", "head"),
            P("head"),
            P("head"),
            P(None, "head"),
            P("head"),
            P("head"),
            P("head", "seq"),
            P(),
            P("seq", None, "head"),
            P("head", "seq"),
            P(),
            P("seq", "head"),
            P("head", "seq"),
        ),
        out_specs=(
            P(None, "seq", None),
            P(None, "seq", None),
            P(),
            P("seq", "head"),
            P("seq", "head"),
            P("seq", "head"),
            P("seq", "head"),
            P("head"),
            P("head"),
            P(None, "head"),
            P("head"),
            P("head"),
            P("head", "seq"),
            P(),
            P("seq", None, "head"),
            P("head", "seq"),
            P(),
            P("seq", "head"),
            P("head", "seq"),
        ),
        check_vma=False,
    )
```
